32 devices in a mesh: seg: 8 (over y, x, core), stretch: 4 (over z).
Axes of the slice: x: 2, y: 2, z: 4, core: 2. Of those that a mesh axis runs over, the one named last changes fastest.
Arguments:
- stream_in: bfloat16 [2, 8, 512, 1024], P(None, 'seg', 'stretch'), may hold values from -6 to 6
- cotangent: bfloat16 [2, 8, 512, 1024], P(None, 'seg', 'stretch'), may hold values from -6 to 6
- previous_mix: float32 [2, 8, 1024], P(None, 'seg'), may hold values from -6 to 6
- previous_ffn: float32 [2, 8, 1024], P(None, 'seg'), may hold values from -6 to 6
- state_num: float32 [2, 8, 1024], P(None, 'seg'), may hold values from -6 to 6
- state_den: float32 [2, 8, 1024], P(None, 'seg'), may hold values from 1 to 4
- state_exp: float32 [2, 8, 1024], P(None, 'seg'), may hold values from 1 to 5
- gain_one: bfloat16 [1024], P('seg'), may hold values from 0.5 to 1.5
- bias_one: bfloat16 [1024], P('seg'), may hold values from -1.5 to 1.5
- gain_two: bfloat16 [1024], P('seg'), may hold values from 0.5 to 1.5
- bias_two: bfloat16 [1024], P('seg'), may hold values from -1.5 to 1.5
- mix_key: bfloat16 [1024], P('seg'), may hold values from 0 to 1
- mix_value: bfloat16 [1024], P('seg'), may hold values from 0 to 1
- mix_recept: bfloat16 [1024], P('seg'), may hold values from 0 to 1
- time_decay: bfloat16 [1024], P('seg'), may hold values from -11 to -3.390625
- time_first: bfloat16 [1024], P('seg'), may hold values from -1 to 1
- chan_mix_key: bfloat16 [1024], P('seg'), may hold values from 0 to 1
- chan_mix_recept: bfloat16 [1024], P('seg'), may hold values from 0 to 1
- att_key: bfloat16 [1024, 1024], P('seg'), may hold values from -0.1875 to 0.1875
- att_value: bfloat16 [1024, 1024], P('seg'), may hold values from -0.1875 to 0.1875
- att_recept: bfloat16 [1024, 1024], P('seg'), may hold values from -0.1875 to 0.1875
- att_output: bfloat16 [1024, 1024], P('seg'), may hold values from -2 to 2
- chan_key: bfloat16 [1024, 4096], P('seg'), may hold values from -0.1875 to 0.1875
- chan_value: bfloat16 [4096, 1024], P('seg'), may hold values from -0.09375 to 0.09375
- chan_recept: bfloat16 [1024, 1024], P('seg'), may hold values from -0.1875 to 0.1875
Outputs:
- block_out: bfloat16 [2, 8, 512, 1024], P(None, 'seg', 'stretch')
- grad_stream: bfloat16 [2, 8, 512, 1024], P(None, 'seg', 'stretch')
- grad_gain_one: float32 [1024], P(('seg', 'stretch'))
- grad_bias_one: float32 [1024], P(('seg', 'stretch'))
- grad_gain_two: float32 [1024], P(('seg', 'stretch'))
- grad_bias_two: float32 [1024], P(('seg', 'stretch'))
- grad_mix_key: float32 [1024], P(('seg', 'stretch'))
- grad_mix_value: float32 [1024], P(('seg', 'stretch'))
- grad_mix_recept: float32 [1024], P(('seg', 'stretch'))
- grad_time_decay: float32 [1024], P(('seg', 'stretch'))
- grad_time_first: float32 [1024], P(('seg', 'stretch'))
- grad_chan_mix_key: float32 [1024], P(('seg', 'stretch'))
- grad_chan_mix_recept: float32 [1024], P(('seg', 'stretch'))
- grad_att_key: float32 [1024, 1024], P(('seg', 'stretch'))
- grad_att_value: float32 [1024, 1024], P(('seg', 'stretch'))
- grad_att_recept: float32 [1024, 1024], P(('seg', 'stretch'))
- grad_att_output: float32 [1024, 1024], P(('seg', 'stretch'))
- grad_chan_key: float32 [1024, 4096], P(('seg', 'stretch'))
- grad_chan_value: float32 [4096, 1024], P(('seg', 'stretch'))
- grad_chan_recept: float32 [1024, 1024], P(('seg', 'stretch'))
- grad_state_num: float32 [2, 8, 1024], P(None, 'seg')
- grad_state_den: float32 [2, 8, 1024], P(None, 'seg')
- grad_state_exp: float32 [2, 8, 1024], P(None, 'seg')
- grad_previous_mix: float32 [2, 8, 1024], P(None, 'seg')
- grad_previous_ffn: float32 [2, 8, 1024], P(None, 'seg')
- final_mean: float32 [2, 8, 1024], P(None, 'seg')
- final_log: float32 [2, 8, 1024], P(None, 'seg')
The draws below stay inside these ranges and needn't reach their ends.
All inputs are finite; a program needn't handle non-finite values.
Results may differ from the reference program's by a relative error of at most 0.025.
Values may be sent and summed in bfloat16 or wider, within the bound.
No kernel may reach another device: no remote copies, remote signals or barrier semaphores. Data moves between devices by JAX's collectives and lax.ppermute only.
A program may use at most 192 MiB of HBM per device.

```python
from functools import partial
import jax
import jax.numpy as jnp
from jax import lax

D = 1024
FF = 4096
TOK_DEV = 128
MB = 2
SEGS = 8
LENGTH = 512


def shard_levels(rng, dims, pieces, smallest, largest):
    def one(axis_at, shards_of):
        draws = jax.random.uniform(jax.random.fold_in(jax.random.fold_in(rng, 6), axis_at), (shards_of,), jnp.float32, smallest / len(pieces), largest / len(pieces))
        return jnp.repeat(jnp.exp(draws), dims[axis_at] // shards_of).reshape((-1,) + (1,) * (len(dims) - axis_at - 1))

    loudness = one(*pieces[0])
    for cut in pieces[1:]:
        loudness = loudness * one(*cut)
    return loudness


def centred(own_key, shape, deviation, limit, cuts=(), held_as=jnp.bfloat16):
    factor_of = shard_levels(own_key, shape, cuts, -0.22, 0.18) if cuts else 1.0
    entries = jax.random.normal(own_key, shape, jnp.float32) * deviation * factor_of
    return jnp.minimum(jnp.maximum(entries, -limit), limit).astype(held_as)


def setup_inputs(seed: int = 0) -> dict:
    arg_keys = jax.random.split(jax.random.key(seed), 26)
    stream_in = centred(arg_keys[0], (MB, SEGS, LENGTH, D), 1.0, 6.0, ((1, 8), (2, 4)))
    cotangent = centred(arg_keys[1], (MB, SEGS, LENGTH, D), 1.0, 6.0, ((1, 8), (2, 4)))
    previous_mix = centred(arg_keys[2], (MB, SEGS, D), 1.0, 6.0, ((1, 8),), jnp.float32)
    previous_ffn = centred(arg_keys[3], (MB, SEGS, D), 1.0, 6.0, ((1, 8),), jnp.float32)
    state_num = centred(arg_keys[4], (MB, SEGS, D), 1.0, 6.0, ((1, 8),), jnp.float32)
    state_den = jnp.clip(1.0 + 3.0 * jax.random.uniform(arg_keys[5], (MB, SEGS, D), jnp.float32) ** shard_levels(arg_keys[5], (MB, SEGS, D), ((1, 8),), -0.2, 0.2), 1.0, 4.0)
    state_exp = jnp.clip(1.0 + 4.0 * jax.random.uniform(arg_keys[6], (MB, SEGS, D), jnp.float32) ** shard_levels(arg_keys[6], (MB, SEGS, D), ((1, 8),), -0.2, 0.2), 1.0, 5.0)
    gain_one = jnp.clip(1.0 + 0.1 * jax.random.normal(arg_keys[7], (D,), jnp.float32), 0.5, 1.5).astype(jnp.bfloat16)
    bias_one = centred(arg_keys[8], (D,), 0.3, 1.5, ((0, 8),))
    gain_two = jnp.clip(1.0 + 0.1 * jax.random.normal(arg_keys[9], (D,), jnp.float32), 0.5, 1.5).astype(jnp.bfloat16)
    bias_two = centred(arg_keys[10], (D,), 0.3, 1.5, ((0, 8),))
    mix_key = jnp.clip(1.0 * jax.random.uniform(arg_keys[11], (D,), jnp.float32) ** shard_levels(arg_keys[11], (D,), ((0, 8),), -0.2, 0.2), 0.0, 1.0).astype(jnp.bfloat16)
    mix_value = jnp.clip(1.0 * jax.random.uniform(arg_keys[12], (D,), jnp.float32) ** shard_levels(arg_keys[12], (D,), ((0, 8),), -0.2, 0.2), 0.0, 1.0).astype(jnp.bfloat16)
    mix_recept = jnp.clip(1.0 * jax.random.uniform(arg_keys[13], (D,), jnp.float32) ** shard_levels(arg_keys[13], (D,), ((0, 8),), -0.2, 0.2), 0.0, 1.0).astype(jnp.bfloat16)
    time_decay = jnp.clip(-11.0 + 7.609375 * jax.random.uniform(arg_keys[14], (D,), jnp.float32) ** shard_levels(arg_keys[14], (D,), ((0, 8),), -0.2, 0.2), -11.0, -3.390625).astype(jnp.bfloat16)
    time_first = jnp.clip(jax.random.uniform(arg_keys[15], (D,), jnp.float32, -1.0, 1.0) * shard_levels(arg_keys[15], (D,), ((0, 8),), -0.4, 0.0), -1.0, 1.0).astype(jnp.bfloat16)
    chan_mix_key = jnp.clip(1.0 * jax.random.uniform(arg_keys[16], (D,), jnp.float32) ** shard_levels(arg_keys[16], (D,), ((0, 8),), -0.2, 0.2), 0.0, 1.0).astype(jnp.bfloat16)
    chan_mix_recept = jnp.clip(1.0 * jax.random.uniform(arg_keys[17], (D,), jnp.float32) ** shard_levels(arg_keys[17], (D,), ((0, 8),), -0.2, 0.2), 0.0, 1.0).astype(jnp.bfloat16)
    att_key = centred(arg_keys[18], (D, D), D ** -0.5, 0.1875, ((0, 8),))
    att_value = centred(arg_keys[19], (D, D), D ** -0.5, 0.1875, ((0, 8),))
    att_recept = centred(arg_keys[20], (D, D), D ** -0.5, 0.1875, ((0, 8),))
    att_output = centred(arg_keys[21], (D, D), 8 ** -0.5, 2.0, ((0, 8),))
    chan_key = centred(arg_keys[22], (D, FF), D ** -0.5, 0.1875, ((0, 8),))
    chan_value = centred(arg_keys[23], (FF, D), FF ** -0.5, 0.09375, ((0, 8),))
    chan_recept = centred(arg_keys[24], (D, D), D ** -0.5, 0.1875, ((0, 8),))
    return dict(stream_in=stream_in, cotangent=cotangent, previous_mix=previous_mix, previous_ffn=previous_ffn, state_num=state_num, state_den=state_den, state_exp=state_exp, gain_one=gain_one, bias_one=bias_one, gain_two=gain_two, bias_two=bias_two, mix_key=mix_key, mix_value=mix_value, mix_recept=mix_recept, time_decay=time_decay, time_first=time_first, chan_mix_key=chan_mix_key, chan_mix_recept=chan_mix_recept, att_key=att_key, att_value=att_value, att_recept=att_recept, att_output=att_output, chan_key=chan_key, chan_value=chan_value, chan_recept=chan_recept)


@jax.custom_vjp
def low(v):
    return lax.optimization_barrier(v.astype(jnp.bfloat16)).astype(jnp.float32)

@jax.custom_vjp
def low_back(v):
    return v

def low_keep(v):
    return (low(v), None)

def low_pass(kept, grad):
    return (grad,)

def back_keep(v):
    return (v, None)

def back_low(kept, grad):
    return (low(grad),)
low.defvjp(low_keep, low_pass)
low_back.defvjp(back_keep, back_low)
epsilon = 1e-05
highest = lax.Precision.HIGHEST

def product(left, right):
    return jnp.dot(left, right, precision=highest, preferred_element_type=jnp.float32)

def normalize(matrix_rows, gain_vec, bias_vec):
    centre = matrix_rows - lax.optimization_barrier(jnp.mean(matrix_rows, axis=-1, keepdims=True))
    spread = lax.optimization_barrier(jnp.mean(centre * centre, axis=-1, keepdims=True))
    return centre * lax.rsqrt(spread + epsilon) * gain_vec + bias_vec

def recurrence_advance(fading_rate_param, reward_channels, current_carry, lone_position_item):
    numerator, denominator, largest_logit = current_carry
    lone_lookup_line, value_row = lone_position_item
    elevated_routine = reward_channels + lone_lookup_line
    ceiling = jnp.maximum(largest_logit, elevated_routine)
    fading = jnp.exp(largest_logit - ceiling)
    fresh_part = jnp.exp(elevated_routine - ceiling)
    blended = (fading * numerator + fresh_part * value_row) / (fading * denominator + fresh_part)
    decayed = largest_logit + fading_rate_param
    ceiling = jnp.maximum(decayed, lone_lookup_line)
    fading = jnp.exp(decayed - ceiling)
    fresh_part = jnp.exp(lone_lookup_line - ceiling)
    return ((fading * numerator + fresh_part * value_row, fading * denominator + fresh_part, ceiling), blended)

def scaled_payload_tile(fading_rate_param, reward_channels, current_carry, position_items):
    return lax.scan(partial(recurrence_advance, fading_rate_param, reward_channels), current_carry, position_items)

def sequence_blending(all_lookup_lines, all_payload_lines, fading_rate_param, reward_channels, opening_carry):
    blocks = LENGTH // TOK_DEV
    shaped = (all_lookup_lines.reshape(blocks, TOK_DEV, D), all_payload_lines.reshape(blocks, TOK_DEV, D))
    piece_traversal = jax.checkpoint(partial(scaled_payload_tile, fading_rate_param, reward_channels))
    closing, blended = lax.scan(piece_traversal, opening_carry, shaped)
    return (blended.reshape(LENGTH, D), closing)

def segment(params, item_now):
    gain_one, bias_one, gain_two, bias_two, mix_key, mix_value, mix_recept, time_decay, time_first, chan_mix_key, chan_mix_recept, att_key, att_value, att_recept, att_output, chan_key, chan_value, chan_recept = params
    stream_rows, previous_row, previous_chan, start_num, start_den, opening_logit = item_now
    normed = normalize(stream_rows, gain_one, bias_one)
    before = jnp.concatenate([previous_row[None], normed[:-1]], axis=0)
    all_lookup_lines = low_back(product(low(normed * mix_key + before * (1.0 - mix_key)), att_key))
    all_payload_lines = low_back(product(low(normed * mix_value + before * (1.0 - mix_value)), att_value))
    recept_all = low_back(product(low(normed * mix_recept + before * (1.0 - mix_recept)), att_recept))
    fading_rate_param = -jnp.exp(time_decay)
    blended, closing = sequence_blending(all_lookup_lines, all_payload_lines, fading_rate_param, time_first, (start_num, start_den, opening_logit))
    branch = low_back(product(low(jax.nn.sigmoid(recept_all) * blended), att_output))
    middle = stream_rows + branch
    normed_two = normalize(middle, gain_two, bias_two)
    before_two = jnp.concatenate([previous_chan[None], normed_two[:-1]], axis=0)
    hidden_pre = low_back(product(low(normed_two * chan_mix_key + before_two * (1.0 - chan_mix_key)), chan_key))
    hidden = low(jnp.square(jax.nn.relu(hidden_pre)))
    chan_out = low_back(product(hidden, chan_value))
    chan_gate = low_back(product(low(normed_two * chan_mix_recept + before_two * (1.0 - chan_mix_recept)), chan_recept))
    result = middle + jax.nn.sigmoid(chan_gate) * chan_out
    return (result, (closing[0] / closing[1], closing[2] + jnp.log(closing[1])))

def forward(params, stream, previous_mix, previous_ffn, state_num, state_den, state_exp):
    segment_count = MB * SEGS
    flattened = (stream.reshape(segment_count, LENGTH, D), previous_mix.reshape(segment_count, D), previous_ffn.reshape(segment_count, D), state_num.reshape(segment_count, D), state_den.reshape(segment_count, D), state_exp.reshape(segment_count, D))

    def visit_segment(running, item_now):
        result, closing = segment(params, item_now)
        return (running, (result, closing[0], closing[1]))
    running, (results, final_means, final_logs) = lax.scan(jax.checkpoint(visit_segment), jnp.zeros((), jnp.float32), flattened)
    return (results.reshape(MB, SEGS, LENGTH, D), (final_means.reshape(MB, SEGS, D), final_logs.reshape(MB, SEGS, D)))

def reference(stream_in, cotangent, previous_mix, previous_ffn, state_num, state_den, state_exp, gain_one, bias_one, gain_two, bias_two, mix_key, mix_value, mix_recept, time_decay, time_first, chan_mix_key, chan_mix_recept, att_key, att_value, att_recept, att_output, chan_key, chan_value, chan_recept):
    params = tuple((weight.astype(jnp.float32) for weight in (gain_one, bias_one, gain_two, bias_two, mix_key, mix_value, mix_recept, time_decay, time_first, chan_mix_key, chan_mix_recept, att_key, att_value, att_recept, att_output, chan_key, chan_value, chan_recept)))
    output, pullback, finals = jax.vjp(forward, params, stream_in.astype(jnp.float32), previous_mix, previous_ffn, state_num, state_den, state_exp, has_aux=True)
    gradients = pullback(cotangent.astype(jnp.float32))
    dparams = gradients[0]
    return (output.astype(jnp.bfloat16), gradients[1].astype(jnp.bfloat16), dparams[0], dparams[1], dparams[2], dparams[3], dparams[4], dparams[5], dparams[6], dparams[7], dparams[8], dparams[9], dparams[10], dparams[11], dparams[12], dparams[13], dparams[14], dparams[15], dparams[16], dparams[17], gradients[4], gradients[5], gradients[6], gradients[2], gradients[3], finals[0], finals[1])
```

```python
import jax
import jax.numpy as jnp
from jax import lax
from jax.sharding import PartitionSpec as P

epsilon = 1e-05
bf16 = jnp.bfloat16
f32 = jnp.float32


def hop(value, bit):
    count = lax.axis_size("seg")
    return lax.ppermute(value, "seg", [(i, i ^ bit) for i in range(count)])


def along(value, steps):
    count = lax.axis_size("stretch")
    first, last = (max(0, -steps), min(count, count - steps))
    return lax.ppermute(value, "stretch", [(i, i + steps) for i in range(first, last)])


def far_bits():
    bits, b = [], 2
    while b < lax.axis_size("seg"):
        bits.append(b)
        b *= 2
    return bits


def gather_pieces(own):
    half = own.shape[0] // 2
    held = {0: [own[:half], own[half:]]}
    whole = {0: own}
    rest = far_bits()
    for b in rest:
        whole[b] = hop(own, b)
        held[b] = [whole[b][:half], whole[b][half:]]
    for m in sorted(range(0, lax.axis_size("seg"), 2), key=lambda m: (bin(m).count("1"), m)):
        if m in held:
            continue
        bits = [b for b in rest if m & b]
        held[m] = [hop(held[m ^ bits[-1]][0], bits[-1]), hop(held[m ^ bits[0]][1], bits[0])]
    out = {}
    for m in sorted(held):
        pieces = [whole[m]] if m in whole else held[m]
        out[m] = pieces
        out[m ^ 1] = [hop(p, 1) for p in pieces]
    return out


def placed(pieces, first, rows, me):
    count = lax.axis_size("seg")
    some = next(iter(pieces.values()))
    buf = jnp.zeros((count * rows, some[0].shape[1]), some[0].dtype)
    for m, parts in pieces.items():
        base = (me ^ m) * rows
        at = 0
        for part in parts:
            lo, hi = max(first, at), min(first + rows, at + part.shape[0])
            if lo < hi:
                buf = lax.dynamic_update_slice_in_dim(
                    buf, part[lo - at : hi - at], base + (lo - first), 0
                )
            at += part.shape[0]
    return buf


def dot_nn(a, b):
    return jnp.dot(a, b, preferred_element_type=f32)


def dot_nt(a, b):
    return lax.dot_general(a, b, (((1,), (1,)), ((), ())), preferred_element_type=f32)


def dot_tn(a, b):
    return lax.dot_general(a, b, (((0,), (0,)), ((), ())), preferred_element_type=f32)


def paired(a, axis=0):
    return jnp.concatenate([a, hop(a, 1)], axis=axis)


def group_sum(items, me):
    count = lax.axis_size("seg")
    rest = far_bits()
    evens = list(range(0, count, 2))
    keep = {}
    parts = []
    for x, dy in items:
        w = x.shape[1] // count
        mine, other = [], []
        for m in evens:
            mine.append(lax.dynamic_slice_in_dim(x, (me ^ m) * w, w, 1))
            other.append(lax.dynamic_slice_in_dim(x, (me ^ m ^ 1) * w, w, 1))
        got = hop(jnp.concatenate(other, axis=1), 1)
        cols = {m: jnp.concatenate([mine[i], got[:, i * w : (i + 1) * w]], axis=0)
                for i, m in enumerate(evens)}
        half = dy.shape[1] // 2
        parts.append((cols, [paired(dy[:, :half]), paired(dy[:, half:])]))
    result = []
    for side in range(2):
        order = rest if side == 0 else rest[::-1]
        now = evens
        acc = None
        for b in order:
            send = [m for m in now if m & b]
            stay = [m for m in now if not m & b]
            def term(ms):
                outs = []
                for cols, dys in parts:
                    left = jnp.concatenate([cols[m] for m in ms], axis=1)
                    g = dot_tn(left, dys[side])
                    outs.append(g.reshape(len(ms), -1, dys[side].shape[1]))
                return jnp.concatenate(outs, axis=1) if len(outs) > 1 else outs[0]
            if acc is None:
                out = term(send).astype(bf16)
                kept = term(stay)
            else:
                out = jnp.stack([acc[now.index(m)] for m in send]).astype(bf16)
                kept = jnp.stack([acc[now.index(m)] for m in stay])
            got = hop(out, b)
            acc = kept + got.astype(f32)
            now = stay
        result.append(acc[0].astype(bf16))
    return jnp.concatenate(result, axis=1)


def stretch_sum(part):
    return lax.psum_scatter(part, "stretch", scatter_dimension=0, tiled=True).astype(f32)


def norm(rows):
    centre = rows - jnp.mean(rows, axis=-1, keepdims=True)
    inverse = lax.rsqrt(jnp.mean(centre * centre, axis=-1, keepdims=True) + epsilon)
    return centre * inverse, inverse


def norm_back(d, unit, inverse, gain):
    q = d * gain
    return inverse * (
        q
        - jnp.mean(q, axis=-1, keepdims=True)
        - unit * jnp.mean(q * unit, axis=-1, keepdims=True)
    )


def split(a):
    hi = a.astype(bf16)
    mid = (a - hi.astype(f32)).astype(bf16)
    return hi, mid


def tri(mat, a):
    hi, mid = split(a)
    def one(v):
        return jnp.einsum("ts,bsd->btd", mat, v, preferred_element_type=f32)
    return one(hi) + one(mid)


def body(
    stream_in, cotangent, previous_mix, previous_ffn, state_num, state_den, state_exp,
    gain_one, bias_one, gain_two, bias_two, mix_key, mix_value, mix_recept,
    time_decay, time_first, chan_mix_key, chan_mix_recept,
    att_key, att_value, att_recept, att_output, chan_key, chan_value, chan_recept,
):
    me = lax.axis_index("seg")
    position = lax.axis_index("stretch")
    stretches = lax.axis_size("stretch")
    at_start = position == 0
    batches, _, length, width = stream_in.shape
    tokens = batches * length
    shard = att_key.shape[0]
    fshard = chan_value.shape[0]

    def flat(a):
        return a.reshape(tokens, a.shape[-1])

    def cube(a):
        return a.reshape(batches, length, a.shape[-1])

    vecs = lax.all_gather(
        jnp.stack([gain_one, bias_one, gain_two, bias_two, mix_key, mix_value, mix_recept,
                   time_decay, time_first, chan_mix_key, chan_mix_recept]),
        "seg", axis=1, tiled=True).astype(f32)
    (g1, b1, g2, b2, mk, mv, mr, decay, first, cmk, cmr) = [vecs[i] for i in range(11)]

    stream = stream_in[:, 0].astype(f32)
    last_in = along(stream_in[:, 0, length - 1], 1)

    p_kvr = gather_pieces(jnp.concatenate([att_key, att_value, att_recept], axis=0))
    p_or = gather_pieces(jnp.concatenate([att_output, chan_recept], axis=0))
    p_ck = gather_pieces(chan_key)
    p_cv = gather_pieces(chan_value)
    w_k = placed(p_kvr, 0, shard, me)
    w_v = placed(p_kvr, shard, shard, me)
    w_r = placed(p_kvr, 2 * shard, shard, me)
    w_o = placed(p_or, 0, shard, me)
    w_c = placed(p_or, shard, shard, me)
    w_ck = placed(p_ck, 0, shard, me)
    w_cv = placed(p_cv, 0, fshard, me)

    na, inv_a = norm(stream)
    xa = na * g1 + b1
    edge_unit, _ = norm(last_in.astype(f32))
    entry = jnp.where(at_start, previous_mix[:, 0], edge_unit * g1 + b1)
    xs = jnp.concatenate([entry[:, None], xa[:, :-1]], axis=1)

    def mixed(a, shifted, mix):
        return flat((a * mix + shifted * (1.0 - mix)).astype(bf16))

    key_in, value_in, recept_in = mixed(xa, xs, mk), mixed(xa, xs, mv), mixed(xa, xs, mr)
    keys = cube(dot_nn(key_in, w_k))
    vals = cube(dot_nn(value_in, w_v))
    recs = cube(dot_nn(recept_in, w_r))

    rate = -jnp.exp(decay)
    span = rate * length
    places = lax.broadcasted_iota(jnp.int32, (length, 1), 0).astype(f32)
    row = lax.broadcasted_iota(jnp.int32, (length, length), 0)
    col = lax.broadcasted_iota(jnp.int32, (length, length), 1)
    lower = (col < row).astype(bf16)
    upper = (col > row).astype(bf16)
    shifted = keys - places * rate
    peak = jnp.max(shifted, axis=1, keepdims=True)
    factor = jnp.exp(shifted - peak)
    fv = factor * vals
    sum_num, sum_den = jnp.sum(fv, axis=1), jnp.sum(factor, axis=1)
    sum_exp = peak[:, 0] + (length - 1.0) * rate
    everyone = lax.all_gather(jnp.stack([sum_num, sum_den, sum_exp]), "stretch")

    def merge(upto):
        ids = jnp.arange(stretches)[:, None, None]
        gaps = (upto - 1 - ids).astype(f32)
        used = ids < upto
        logit = jnp.where(used, everyone[:, 2] + gaps * span, -jnp.inf)
        opening = state_exp[:, 0] + upto * span
        top = jnp.maximum(opening, jnp.max(logit, axis=0))
        weight = jnp.exp(logit - top)
        start = jnp.exp(opening - top)
        return (
            state_num[:, 0] * start + jnp.sum(weight * everyone[:, 0], axis=0),
            state_den[:, 0] * start + jnp.sum(weight * everyone[:, 1], axis=0),
            top,
        )

    ent_num, ent_den, ent_exp = merge(position)
    fin_num, fin_den, fin_exp = merge(jnp.int32(stretches))
    final_mean = (fin_num / fin_den)[:, None]
    final_log = (fin_exp + jnp.log(fin_den))[:, None]

    cum_num, cum_den = tri(lower, fv), tri(lower, factor)
    near = (places - 1.0) * rate + peak
    opening = places * rate + ent_exp[:, None]
    reward = first + keys
    top = jnp.maximum(jnp.maximum(near, opening), reward)
    p, o, e = jnp.exp(near - top), jnp.exp(opening - top), jnp.exp(reward - top)
    den = cum_den * p + ent_den[:, None] * o + e
    wkv = (cum_num * p + ent_num[:, None] * o + vals * e) / den
    sig = jax.nn.sigmoid(recs)
    gated = flat((sig * wkv).astype(bf16))
    middle = stream + cube(dot_nn(gated, w_o))

    nb, inv_b = norm(middle)
    xb = nb * g2 + b2
    edge_b = along(xb[:, length - 1], 1)
    entry_b = jnp.where(at_start, previous_ffn[:, 0], edge_b)
    xt = jnp.concatenate([entry_b[:, None], xb[:, :-1]], axis=1)
    fkey_in, frec_in = mixed(xb, xt, cmk), mixed(xb, xt, cmr)
    active = jax.nn.relu(dot_nn(fkey_in, w_ck))
    hidden = (active * active).astype(bf16)
    frec = cube(dot_nn(frec_in, w_c))
    fval = cube(dot_nn(hidden, w_cv))
    sigf = jax.nn.sigmoid(frec)
    block_out = (middle + sigf * fval).astype(bf16)[:, None]

    cot = cotangent[:, 0].astype(f32)
    d_fval = flat((cot * sigf).astype(bf16))
    d_frec = flat((cot * fval * sigf * (1.0 - sigf)).astype(bf16))
    d_pre = (dot_nt(d_fval, w_cv) * 2.0 * active).astype(bf16)
    part_cv = group_sum([(hidden, d_fval)], me)
    part_ck = group_sum([(fkey_in, d_pre)], me)
    d_fkey_in = cube(dot_nt(d_pre, w_ck))
    d_frec_in = cube(dot_nt(d_frec, w_c))
    gap_b = xb - xt
    gr_cmk = jnp.sum(d_fkey_in * gap_b, axis=(0, 1))
    gr_cmr = jnp.sum(d_frec_in * gap_b, axis=(0, 1))
    d_xt = d_fkey_in * (1.0 - cmk) + d_frec_in * (1.0 - cmr)
    next_b = along(d_xt[:, 0], -1)
    d_xb = d_fkey_in * cmk + d_frec_in * cmr + jnp.concatenate([d_xt[:, 1:], next_b[:, None]], axis=1)
    gr_g2 = jnp.sum(d_xb * nb, axis=(0, 1))
    gr_b2 = jnp.sum(d_xb, axis=(0, 1))
    d_middle = cot + norm_back(d_xb, nb, inv_b, g2)

    d_branch = flat(d_middle.astype(bf16))
    d_gated = cube(dot_nt(d_branch, w_o))
    d_recs = flat((d_gated * wkv * sig * (1.0 - sig)).astype(bf16))
    part_or = group_sum([(gated, d_branch), (frec_in, d_frec)], me)
    gn = d_gated * sig / den
    gd = -gn * wkv
    direct = e * (gn * vals + gd)
    gr_first = jnp.sum(direct, axis=(0, 1))
    go_n, go_d = gn * o, gd * o
    d_ent_num, d_ent_den = jnp.sum(go_n, axis=1), jnp.sum(go_d, axis=1)
    back = lax.all_gather(jnp.stack([d_ent_num, d_ent_den, ent_exp, d_xt[:, 0]]), "stretch")
    ids = jnp.arange(stretches)[:, None, None]
    lift = jnp.where(ids > position, jnp.exp(jnp.minimum(
        sum_exp - back[:, 2] + (ids - position - 1).astype(f32) * span, 0.0)), 0.0)
    s_num = jnp.sum(back[:, 0] * lift, axis=0)
    s_den = jnp.sum(back[:, 1] * lift, axis=0)
    carry = jnp.where(ids > position, jnp.exp(jnp.minimum(
        ent_exp + (ids - position).astype(f32) * span - back[:, 2], 0.0)), 0.0)
    d_rate = length * jnp.sum(
        ent_num * jnp.sum(back[:, 0] * carry, axis=0) + ent_den * jnp.sum(back[:, 1] * carry, axis=0),
        axis=0)
    raise_0 = jnp.exp(jnp.minimum(state_exp[:, 0] + ids.astype(f32) * span - back[:, 2], 0.0))
    grad_num = jnp.sum(back[:, 0] * raise_0, axis=0)
    grad_den = jnp.sum(back[:, 1] * raise_0, axis=0)
    grad_exp = state_num[:, 0] * grad_num + state_den[:, 0] * grad_den
    grad_previous_ffn = back[0, 3]

    pn, pd = gn * p, gd * p
    rn = tri(upper, pn) + s_num[:, None]
    rd = tri(upper, pd) + s_den[:, None]
    chain = factor * (rn * vals + rd)
    d_keys = flat((chain + direct).astype(bf16))
    d_vals = flat((factor * rn + gn * e).astype(bf16))
    d_rate = d_rate + jnp.sum(
        (places - 1.0) * (pn * cum_num + pd * cum_den)
        + places * (go_n * ent_num[:, None] + go_d * ent_den[:, None])
        - places * chain, axis=(0, 1))
    d_rate = d_rate + (length - 1.0) * jnp.sum(s_num * sum_num + s_den * sum_den, axis=0)
    gr_decay = d_rate * rate

    part_kvr = group_sum([(key_in, d_keys), (value_in, d_vals), (recept_in, d_recs)], me)
    d_key_in = cube(dot_nt(d_keys, w_k))
    d_value_in = cube(dot_nt(d_vals, w_v))
    d_recept_in = cube(dot_nt(d_recs, w_r))
    gap_a = xa - xs
    gr_mk = jnp.sum(d_key_in * gap_a, axis=(0, 1))
    gr_mv = jnp.sum(d_value_in * gap_a, axis=(0, 1))
    gr_mr = jnp.sum(d_recept_in * gap_a, axis=(0, 1))
    d_xs = d_key_in * (1.0 - mk) + d_value_in * (1.0 - mv) + d_recept_in * (1.0 - mr)
    heads = lax.all_gather(d_xs[:, 0], "stretch")
    grad_previous_mix = heads[0]
    next_a = jnp.where(position == stretches - 1, 0.0,
                       heads[jnp.minimum(position + 1, stretches - 1)])
    d_xa = (d_key_in * mk + d_value_in * mv + d_recept_in * mr
            + jnp.concatenate([d_xs[:, 1:], next_a[:, None]], axis=1))
    gr_g1 = jnp.sum(d_xa * na, axis=(0, 1))
    gr_b1 = jnp.sum(d_xa, axis=(0, 1))
    grad_stream = (d_middle + norm_back(d_xa, na, inv_a, g1)).astype(bf16)[:, None]

    out_cv = stretch_sum(part_cv)
    out_ck = stretch_sum(part_ck)
    out_or = [stretch_sum(part_or[:shard]), stretch_sum(part_or[shard:])]
    out_kvr = [stretch_sum(part_kvr[i * shard : (i + 1) * shard]) for i in range(3)]

    small = jnp.stack([gr_g1, gr_b1, gr_g2, gr_b2, gr_mk, gr_mv, gr_mr, gr_decay, gr_first,
                       gr_cmk, gr_cmr])
    small = lax.psum_scatter(small, "seg", scatter_dimension=1, tiled=True)
    small = lax.psum_scatter(small, "stretch", scatter_dimension=1, tiled=True)

    return (
        block_out, grad_stream, *[small[i] for i in range(11)],
        out_kvr[0], out_kvr[1], out_kvr[2], out_or[0], out_ck, out_cv, out_or[1],
        grad_num[:, None], grad_den[:, None], grad_exp[:, None],
        grad_previous_mix[:, None], grad_previous_ffn[:, None], final_mean, final_log,
    )


def solution(mesh):
    rows = P(None, "seg", "stretch", None)
    state = P(None, "seg", None)
    both = P(("seg", "stretch"))
    wide = P(("seg", "stretch"), None)
    return jax.shard_map(
        body,
        mesh=mesh,
        in_specs=(rows,) * 2 + (state,) * 5 + (P("seg"),) * 11 + (P("seg", None),) * 7,
        out_specs=(rows,) * 2 + (both,) * 11 + (wide,) * 7 + (state,) * 7,
        check_vma=False,
    )
```

```python
import jax
import jax.numpy as jnp
from jax import lax
from jax.experimental import pallas as pl
from jax.experimental.pallas import tpu as pltpu
from jax.sharding import PartitionSpec as P

epsilon = 1e-05
bf16 = jnp.bfloat16
f32 = jnp.float32
ROWS = 64
STEP = 512
LANES = 512
LIMIT = 60
MIB = 2**20
G1, B1, G2, B2, MK, MV, MR, DECAY, FIRST, CMK, CMR = range(11)


def hop(value, bit):
    count = lax.axis_size("seg")
    return lax.ppermute(value, "seg", [(i, i ^ bit) for i in range(count)])


def along(value, steps):
    count = lax.axis_size("stretch")
    first, last = (max(0, -steps), min(count, count - steps))
    return lax.ppermute(value, "stretch", [(i, i + steps) for i in range(first, last)])


class Live:
    def __init__(self):
        self.__dict__["held"] = {}

    def __getattr__(self, name):
        return self.held[name]

    def __setattr__(self, name, value):
        self.held[name] = value

    def drop(self, *names):
        for name in names:
            del self.held[name]

    def sync(self):
        self.__dict__["held"] = lax.optimization_barrier(self.held)


def far_bits():
    bits, b = [], 2
    while b < lax.axis_size("seg"):
        bits.append(b)
        b *= 2
    return bits


def relative_order():
    count = lax.axis_size("seg")
    return list(range(0, count, 2)) + list(range(1, count, 2))


def first_stage(own):
    return {b: [hop(part, b) for part in own] for b in far_bits()}


def halves(parts):
    if len(parts) == 2:
        return parts
    half = parts[0].shape[0] // 2
    return [parts[0][:half], parts[0][half:]]


def second_stage(direct, held):
    rest = far_bits()
    held = dict(held)
    for m in sorted(range(0, lax.axis_size("seg"), 2), key=lambda m: (bin(m).count("1"), m)):
        if m == 0 or m in held:
            continue
        bits = [b for b in rest if m & b]
        held[m] = [hop(held[m ^ bits[-1]][0], bits[-1]), hop(held[m ^ bits[0]][1], bits[0])]
    return {m: held[m] for m in held if m not in direct}


def sibling(pieces):
    return {m ^ 1: [hop(p, 1) for p in parts] for m, parts in pieces.items()}


def plan(pieces, first, rows):
    steps, at = [], 0
    for m in relative_order():
        base = 0
        for part in pieces[m]:
            lo, hi = max(first, base), min(first + rows, base + part.shape[0])
            if lo < hi:
                steps.append((at, lo - base, hi - lo, m, lo - first))
            base += part.shape[0]
            at += 1
    return steps


def flat_pieces(pieces):
    return [part for m in relative_order() for part in pieces[m]]


class Loads:
    def __init__(self, sems):
        self.sems, self.used = sems, 0

    def start(self, src, dst):
        copy = pltpu.make_async_copy(src, dst, self.sems.at[self.used])
        self.used += 1
        copy.start()
        return copy

    def pieces(self, steps, refs, target, place):
        return [
            self.start(refs[piece].at[pl.ds(row, count)], target.at[pl.ds(place(m) + within, count)])
            for piece, row, count, m, within in steps
        ]


def wait(copies):
    for c in copies:
        c.wait()


def call(body, info, small, large, raw, outs, big_outs, scratch, copies, us, limit):
    n_small, n_large, n_raw = len(small), len(large), len(raw)
    n_out, n_big = len(outs), len(big_outs)

    def shape_of(array, index):
        return array.shape if index is None else array.shape[1:]

    def kernel(*refs):
        at = 0

        def take(n):
            nonlocal at
            at += n
            return refs[at - n : at]

        (info_ref,), small_refs, large_refs, raw_refs = take(1), take(n_small), take(n_large), take(n_raw)
        out_refs, big_refs = take(n_out), take(n_big)
        buffers, big_buffers, (sems,) = take(n_large), take(n_big), take(1)
        rest = take(len(refs) - at)
        loads = Loads(sems)
        pending = []
        for (array, index), ref, buf in zip(large, large_refs, buffers):
            pending.append(loads.start(ref if index is None else ref.at[index], buf))
        stored = {}

        def get(k):
            if pending[k] is not None:
                pending[k].wait()
                pending[k] = None
            return buffers[k]

        def put(k):
            stored[k] = loads.start(big_buffers[k], big_refs[k])

        body(info_ref, small_refs, get, raw_refs, out_refs, big_buffers, put, rest, loads)
        for k in range(n_large):
            get(k)
        for k in range(n_big):
            if k not in stored:
                put(k)
        wait(stored.values())

    hbm = pl.BlockSpec(memory_space=pltpu.HBM)
    vmem = pl.BlockSpec(memory_space=pltpu.VMEM)
    return pl.pallas_call(
        kernel,
        out_shape=[jax.ShapeDtypeStruct(s, d) for s, d in (*outs, *big_outs)],
        in_specs=[pl.BlockSpec(memory_space=pltpu.SMEM)] + [vmem] * n_small + [hbm] * (n_large + n_raw),
        out_specs=[vmem] * n_out + [hbm] * n_big,
        scratch_shapes=[pltpu.VMEM(shape_of(a, i), a.dtype) for a, i in large]
        + [pltpu.VMEM(s, d) for s, d in big_outs]
        + [pltpu.SemaphoreType.DMA((max(1, n_large + n_big + copies),))]
        + list(scratch),
        compiler_params=pltpu.CompilerParams(vmem_limit_bytes=LIMIT * MIB),
        cost_estimate=pl.CostEstimate(
            flops=0, bytes_accessed=int(us * 1e3), transcendentals=0),
    )(info, *small, *[a for a, _ in large], *raw)


def natural(me, rows):
    return lambda m: pl.multiple_of(jnp.bitwise_xor(me, m) * rows, rows)


def dot_nn(a, b):
    return jnp.dot(a, b, preferred_element_type=f32)


def dot_nt(a, b):
    return lax.dot_general(a, b, (((1,), (1,)), ((), ())), preferred_element_type=f32)


def dot_tn(a, b):
    return lax.dot_general(a, b, (((0,), (0,)), ((), ())), preferred_element_type=f32)


def norm(rows):
    centre = rows - jnp.mean(rows, axis=-1, keepdims=True)
    inverse = lax.rsqrt(jnp.mean(centre * centre, axis=-1, keepdims=True) + epsilon)
    return centre * inverse, inverse


def norm_back(d, unit, inverse, gain):
    q = d * gain
    return inverse * (
        q
        - jnp.mean(q, axis=-1, keepdims=True)
        - unit * jnp.mean(q * unit, axis=-1, keepdims=True)
    )


def down_one(rows, entering):
    at = lax.broadcasted_iota(jnp.int32, rows.shape, 0)
    return jnp.where(at == 0, entering, pltpu.roll(rows, 1, 0))


def up_one(rows, entering):
    at = lax.broadcasted_iota(jnp.int32, rows.shape, 0)
    last = rows.shape[0] - 1
    return jnp.where(at == last, entering, pltpu.roll(rows, last, 0))


def fold(rows):
    total = rows[:8]
    for k in range(8, rows.shape[0], 8):
        total = total + rows[k : k + 8]
    return total


def columns(width, step):
    step = min(step, width)

    def run(body):
        @pl.loop(0, width // step)
        def _(n):
            body(pl.ds(pl.multiple_of(n * step, step), step))

    return run


def row_chunk(b, i, length):
    return pl.ds(pl.multiple_of(b * length + i * ROWS, ROWS), ROWS)


def two_part(mat, value):
    hi = value.astype(bf16)
    lo = (value - hi.astype(f32)).astype(bf16)
    return dot_nn(mat, hi) + dot_nn(mat, lo)


def triangle(length, strictly_before):
    row = lax.broadcasted_iota(jnp.int32, (length, length), 0)
    col = lax.broadcasted_iota(jnp.int32, (length, length), 1)
    keep = (col < row) if strictly_before else (col > row)
    return keep.astype(f32).astype(bf16)


def column_sums(out_ref, sum_ref):
    for k in range(sum_ref.shape[0]):
        out_ref[k : k + 1, :] = jnp.sum(sum_ref[k], axis=0, keepdims=True)


def pack(info, parts_a, parts_b, width):
    arrays = [p[0] for p in (*parts_a, *parts_b)]

    def kernel(*refs):
        ins, outs, sems = refs[: len(arrays)], refs[len(arrays) : -1], refs[-1]
        copies, n = [], 0
        for out, parts in zip(outs, (parts_a, parts_b)):
            at = 0
            for _, first, count in parts:
                copies.append(pltpu.make_async_copy(
                    ins[n].at[pl.ds(first, count)], out.at[pl.ds(at, count)], sems.at[n]))
                at += count
                n += 1
        for c in copies:
            c.start()
        wait(copies)

    return pl.pallas_call(
        kernel,
        out_shape=[jax.ShapeDtypeStruct((sum(p[2] for p in parts), width), bf16)
                   for parts in (parts_a, parts_b)],
        in_specs=[pl.BlockSpec(memory_space=pltpu.HBM)] * len(arrays),
        out_specs=[pl.BlockSpec(memory_space=pltpu.VMEM)] * 2,
        compiler_params=pltpu.CompilerParams(vmem_limit_bytes=LIMIT * MIB),
        scratch_shapes=[pltpu.SemaphoreType.DMA((len(arrays),))],
        cost_estimate=pl.CostEstimate(flops=0, bytes_accessed=3 * MIB, transcendentals=0),
    )(*arrays)


def time_in(info, stream, last, previous, given, pieces, spots, length, shard):
    tokens, width = stream.shape
    batches = tokens // length
    plans = [plan(pieces, spots[k], shard) for k in "kvr"]
    vplan = plan(pieces, spots["vec"], 16)
    order = relative_order()

    def body(info, small, get, raw, outs, big, put, scratch, loads):
        last_ref, prev_ref = small[:2]
        sum_ref, vec_ref, entry_ref = outs
        in_ref, kvr_ref = big
        w, vt = scratch
        place = natural(info[0], shard)
        vcopies = loads.pieces(vplan, raw, vt, lambda m: order.index(m) * 16)
        copies = [loads.pieces(plans[k], raw, w.at[k], place) for k in range(3)]
        wait(vcopies)
        if given is not None:
            vec_ref[...] = small[2][...]
        else:
            for at, m in enumerate(order):
                vec_ref[:, pl.ds(place(m), shard)] = vt[at * 16 : at * 16 + 16, :shard].astype(f32)
        unit, _ = norm(last_ref[...].astype(f32))
        edge = unit * vec_ref[G1 : G1 + 1] + vec_ref[B1 : B1 + 1]
        for b in range(batches):
            entry_ref[b : b + 1, :] = jnp.where(info[1] == 1, prev_ref[b], edge[b : b + 1])
        stream_ref = get(0)

        for b in range(batches):
            def step(i, before):
                r = row_chunk(b, i, length)
                na, _ = norm(stream_ref[r, :].astype(f32))
                xa = na * vec_ref[G1 : G1 + 1] + vec_ref[B1 : B1 + 1]
                xs = down_one(xa, before)
                for k, row in enumerate((MK, MV, MR)):
                    mix = vec_ref[row : row + 1]
                    in_ref[k, r, :] = (xa * mix + xs * (1.0 - mix)).astype(bf16)
                return xa[ROWS - 1 :]
            lax.fori_loop(0, length // ROWS, step, entry_ref[b : b + 1])
        put(0)
        for k in range(3):
            wait(copies[k])
            @columns(width, STEP)
            def _(n):
                kvr_ref[k, :, n] = dot_nn(in_ref[k], w[k, :, n])
        put(1)
        for b in range(batches):
            t = slice(b * length, (b + 1) * length)
            @columns(width, LANES)
            def _(n):
                rate = -jnp.exp(vec_ref[DECAY : DECAY + 1, n])
                at = lax.broadcasted_iota(jnp.int32, (length, 1), 0).astype(f32)
                shifted = kvr_ref[0, t, n] - at * rate
                peak = jnp.max(shifted, axis=0, keepdims=True)
                factor = jnp.exp(shifted - peak)
                sum_ref[b : b + 1, n] = jnp.sum(factor * kvr_ref[1, t, n], axis=0, keepdims=True)
                sum_ref[batches + b : batches + b + 1, n] = jnp.sum(factor, axis=0, keepdims=True)
                sum_ref[2 * batches + b : 2 * batches + b + 1, n] = peak + (length - 1.0) * rate

    extra = [] if given is None else [given]
    return call(
        body, info, [last, previous, *extra], [(stream, None)], flat_pieces(pieces),
        [((3 * batches, width), f32), ((16, width), f32), ((batches, width), f32)],
        [((3, tokens, width), bf16), ((3, tokens, width), f32)],
        [pltpu.VMEM((3, width, width), bf16), pltpu.VMEM((16 * len(order), width), bf16)],
        len(vplan) + sum(map(len, plans)), 9, 40)


def wkv_terms(kvr_ref, ent_ref, vec_ref, b, t, n, batches, length):
    rate = -jnp.exp(vec_ref[DECAY : DECAY + 1, n])
    at = lax.broadcasted_iota(jnp.int32, (length, 1), 0).astype(f32)
    keys = kvr_ref[0, t, n]
    shifted = keys - at * rate
    peak = jnp.max(shifted, axis=0, keepdims=True)
    factor = jnp.exp(shifted - peak)
    near = (at - 1.0) * rate + peak
    opening = at * rate + ent_ref[2 * batches + b : 2 * batches + b + 1, n]
    reward = vec_ref[FIRST : FIRST + 1, n] + keys
    top = jnp.maximum(jnp.maximum(near, opening), reward)
    return at, factor, jnp.exp(near - top), jnp.exp(opening - top), jnp.exp(reward - top)


def time_out(info, kvr, everyone, state, vec, stream, pieces, spots, length, shard):
    tokens, width = stream.shape
    batches = tokens // length
    stretches = everyone.shape[0]
    steps = plan(pieces, spots["o"], shard)

    def body(info, small, get, raw, outs, big, put, scratch, loads):
        every_ref, num_ref, den_ref, exp_ref, vec_ref = small
        ent_ref, mean_ref, log_ref, edge_ref = outs
        gated_ref, wkv_ref, rden_ref, mid_ref, xb_ref = big
        (w,) = scratch
        copies = loads.pieces(steps, raw, w, natural(info[0], shard))
        span = -jnp.exp(vec_ref[DECAY : DECAY + 1, :]) * float(length)

        def merge(upto, b):
            upto_f = upto.astype(f32) if upto is not stretches else float(stretches)
            logits = []
            for z in range(stretches):
                row = 2 * batches + b
                logit = every_ref[z, row : row + 1, :] + (upto_f - 1.0 - z) * span
                logits.append(logit if upto is stretches else jnp.where(z < upto, logit, -jnp.inf))
            opening = exp_ref[b] + upto_f * span
            top = opening
            for logit in logits:
                top = jnp.maximum(top, logit)
            start = jnp.exp(opening - top)
            num, den = num_ref[b] * start, den_ref[b] * start
            for z, logit in enumerate(logits):
                weight = jnp.exp(logit - top)
                num = num + weight * every_ref[z, b : b + 1, :]
                den = den + weight * every_ref[z, batches + b : batches + b + 1, :]
            return num, den, top

        for b in range(batches):
            for k, part in enumerate(merge(info[2], b)):
                ent_ref[k * batches + b : k * batches + b + 1, :] = part
            num, den, top = merge(stretches, b)
            mean_ref[b] = num / den
            log_ref[b] = top + jnp.log(den)

        lower = triangle(length, True)
        kvr_ref = get(0)
        for b in range(batches):
            t = slice(b * length, (b + 1) * length)
            @columns(width, LANES)
            def _(n):
                _, factor, p, o, e = wkv_terms(kvr_ref, ent_ref, vec_ref, b, t, n, batches, length)
                vals = kvr_ref[1, t, n]
                num = (two_part(lower, factor * vals) * p
                       + ent_ref[b : b + 1, n] * o + vals * e)
                den = (two_part(lower, factor) * p
                       + ent_ref[batches + b : batches + b + 1, n] * o + e)
                rden = 1.0 / den
                wkv = num * rden
                wkv_ref[t, n] = wkv
                rden_ref[t, n] = rden
                gated_ref[t, n] = (jax.nn.sigmoid(kvr_ref[2, t, n]) * wkv).astype(bf16)
        put(0)
        put(1)
        put(2)
        wait(copies)
        stream_ref = get(1)
        @columns(width, STEP)
        def _(n):
            mid_ref[:, n] = stream_ref[:, n].astype(f32) + dot_nn(gated_ref[...], w[:, n])
        put(3)
        @pl.loop(0, tokens // ROWS)
        def _(i):
            r = row_chunk(0, i, 0)
            nb, _ = norm(mid_ref[r, :])
            xb_ref[r, :] = nb * vec_ref[G2 : G2 + 1] + vec_ref[B2 : B2 + 1]
        for b in range(batches):
            last = (b + 1) * length - 1
            edge_ref[b : b + 1, :] = xb_ref[last : last + 1, :]

    one = ((tokens, width), f32)
    return call(
        body, info, [everyone, *state, vec], [(kvr, None), (stream, None)], flat_pieces(pieces),
        [((3 * batches, width), f32), ((batches, 1, width), f32), ((batches, 1, width), f32),
         ((batches, width), f32)],
        [((tokens, width), bf16), one, one, one, one],
        [pltpu.VMEM((width, width), bf16)], len(steps), 7, 40)


def chan_in(info, xb, edge, previous, vec, pieces_c, pieces_ck, spots, length, shard, fshard):
    tokens, width = xb.shape
    batches = tokens // length
    order = relative_order()
    wide = fshard * len(order)
    flat_c, flat_k = flat_pieces(pieces_c), flat_pieces(pieces_ck)
    steps_c, steps_k = plan(pieces_c, spots["c"], shard), plan(pieces_ck, 0, shard)

    def body(info, small, get, raw, outs, big, put, scratch, loads):
        edge_ref, prev_ref, vec_ref = small
        (entry_ref,) = outs
        in_ref, near_ref, far_ref, act_ref, frec_ref = big
        wk, wc = scratch
        raw_c, raw_k = raw[: len(flat_c)], raw[len(flat_c) :]
        place = natural(info[0], shard)
        copies_c = loads.pieces(steps_c, raw_c, wc, place)
        copies_k = loads.pieces(steps_k, raw_k, wk, place)
        for b in range(batches):
            entry_ref[b : b + 1, :] = jnp.where(info[1] == 1, prev_ref[b], edge_ref[b : b + 1, :])
        xb_ref = get(0)
        for b in range(batches):
            def step(i, before):
                r = row_chunk(b, i, length)
                x = xb_ref[r, :]
                xt = down_one(x, before)
                for k, row in enumerate((CMK, CMR)):
                    mix = vec_ref[row : row + 1]
                    in_ref[k, r, :] = (x * mix + xt * (1.0 - mix)).astype(bf16)
                return x[ROWS - 1 :]
            lax.fori_loop(0, length // ROWS, step, entry_ref[b : b + 1])
        put(0)
        wait(copies_c)
        @columns(width, STEP)
        def _(n):
            frec_ref[:, n] = dot_nn(in_ref[1], wc[:, n])
        put(4)
        wait(copies_k)
        part = min(STEP, fshard)
        for hid_ref, first in ((far_ref, len(order) // 2), (near_ref, 0)):
            for k in range(len(order) // 2):
                base = natural(info[0], fshard)(order[first + k])
                for q in range(fshard // part):
                    src = pl.ds(pl.multiple_of(base + q * part, part), part)
                    lo = k * fshard + q * part
                    act = jnp.maximum(dot_nn(in_ref[0], wk[:, src]), 0.0)
                    act_ref[:, first * fshard + lo : first * fshard + lo + part] = act.astype(bf16)
                    hid_ref[:, lo : lo + part] = (act * act).astype(bf16)
            put(2 if first else 1)

    return call(
        body, info, [edge, previous, vec], [(xb, None)], [*flat_c, *flat_k],
        [((batches, width), f32)],
        [((2, tokens, width), bf16), ((tokens, wide // 2), bf16), ((tokens, wide // 2), bf16),
         ((tokens, wide), bf16), ((tokens, width), f32)],
        [pltpu.VMEM((width, wide), bf16), pltpu.VMEM((width, width), bf16)],
        len(steps_c) + len(steps_k), 11, 40)


def chan_out(info, near, far, act, frec, mid, cot, pieces, fshard):
    tokens, width = mid.shape
    order = relative_order()
    wide = fshard * len(order)
    steps = plan(pieces, 0, fshard)

    def body(info, small, get, raw, outs, big, put, scratch, loads):
        out_ref, df_ref, dr_ref, dpre_ref = big
        w, fval = scratch
        copies = loads.pieces(steps, raw, w, lambda m: order.index(m) * fshard)
        near_ref, far_ref = get(0), get(1)
        wait(copies)
        @columns(width, STEP)
        def _(n):
            fval[:, n] = (dot_nn(near_ref[...], w[: wide // 2, n])
                          + dot_nn(far_ref[...], w[wide // 2 :, n]))
        frec_ref, mid_ref, cot_ref, act_ref = get(2), get(3), get(4), get(5)
        @pl.loop(0, tokens // ROWS)
        def _(i):
            r = row_chunk(0, i, 0)
            sig = jax.nn.sigmoid(frec_ref[r, :])
            cots, value = cot_ref[r, :].astype(f32), fval[r, :]
            out_ref[r, :] = (mid_ref[r, :] + sig * value).astype(bf16)
            df_ref[r, :] = (cots * sig).astype(bf16)
            dr_ref[r, :] = (cots * value * sig * (1.0 - sig)).astype(bf16)
        for k in range(3):
            put(k)
        part = min(STEP, fshard)
        for at, m in enumerate(order):
            base = natural(info[0], fshard)(m)
            for q in range(fshard // part):
                src = slice(at * fshard + q * part, at * fshard + (q + 1) * part)
                dst = pl.ds(pl.multiple_of(base + q * part, part), part)
                d = dot_nt(df_ref[...], w[src, :]) * (2.0 * act_ref[:, src].astype(f32))
                dpre_ref[:, dst] = d.astype(bf16)

    low = ((tokens, width), bf16)
    return call(
        body, info, [], [(a, None) for a in (near, far, frec, mid, cot, act)], flat_pieces(pieces), [],
        [low, low, low, ((tokens, wide), bf16)],
        [pltpu.VMEM((wide, width), bf16), pltpu.VMEM((tokens, width), f32)], len(steps), 13, 40)


def chan_back(info, dpre, dfrec, xb, entry, vec, pieces_c, pieces_ck, spots, length, shard, wide):
    tokens, width = xb.shape
    batches = tokens // length
    flat_c, flat_k = flat_pieces(pieces_c), flat_pieces(pieces_ck)
    steps_c, steps_k = plan(pieces_c, spots["c"], shard), plan(pieces_ck, 0, shard)

    def body(info, small, get, raw, outs, big, put, scratch, loads):
        entry_ref, vec_ref = small
        head_ref, total_ref = outs
        dxt_ref, dxb_ref = big
        wk, wc, df, dr, sum_ref = scratch
        raw_c, raw_k = raw[: len(flat_c)], raw[len(flat_c) :]
        place = natural(info[0], shard)
        copies_c = loads.pieces(steps_c, raw_c, wc, place)
        copies_k = loads.pieces(steps_k, raw_k, wk, place)
        dfrec_ref = get(0)
        wait(copies_c)
        @columns(width, STEP)
        def _(n):
            dr[:, n] = dot_nt(dfrec_ref[...], wc[n, :])
        dpre_ref = get(1)
        wait(copies_k)
        @columns(width, STEP)
        def _(n):
            df[:, n] = dot_nt(dpre_ref[...], wk[n, :])
        sum_ref[...] = jnp.zeros_like(sum_ref)
        xb_ref = get(2)
        for b in range(batches):
            def step(i, before):
                r = row_chunk(b, i, length)
                x = xb_ref[r, :]
                gap = x - down_one(x, before)
                a, c = df[r, :], dr[r, :]
                ck, cr = vec_ref[CMK : CMK + 1], vec_ref[CMR : CMR + 1]
                dxt_ref[r, :] = a * (1.0 - ck) + c * (1.0 - cr)
                dxb_ref[r, :] = a * ck + c * cr
                sum_ref[0] += fold(a * gap)
                sum_ref[1] += fold(c * gap)
                return x[ROWS - 1 :]
            lax.fori_loop(0, length // ROWS, step, entry_ref[b : b + 1])
            head_ref[b : b + 1, :] = dxt_ref[b * length : b * length + 1, :]
        column_sums(total_ref, sum_ref)

    one = ((tokens, width), f32)
    return call(
        body, info, [entry, vec], [(dfrec, None), (dpre, None), (xb, None)], [*flat_c, *flat_k],
        [((batches, width), f32), ((2, width), f32)], [one, one],
        [pltpu.VMEM((width, wide), bf16), pltpu.VMEM((width, width), bf16),
         pltpu.VMEM((tokens, width), f32), pltpu.VMEM((tokens, width), f32),
         pltpu.VMEM((2, 8, width), f32)],
        len(steps_c) + len(steps_k), 11, 40)


def mid_back(info, dxt, dxb, after, mid, cot, vec, kvr, wkv, rden, ent, pieces, spots, length, shard):
    tokens, width = mid.shape
    batches = tokens // length
    steps = plan(pieces, spots["o"], shard)

    def body(info, small, get, raw, outs, big, put, scratch, loads):
        after_ref, vec_ref, ent_ref = small
        dent_ref, total_ref = outs
        dmid_ref, dbr_ref, drec_ref, gn_ref = big
        w, sum_ref = scratch
        copies = loads.pieces(steps, raw, w, natural(info[0], shard))
        sum_ref[...] = jnp.zeros_like(sum_ref)
        dxt_ref, dxb_ref, mid_ref, cot_ref = get(0), get(1), get(2), get(3)
        for b in range(batches):
            def step(k, after_row):
                r = row_chunk(b, length // ROWS - 1 - k, length)
                nb, inverse = norm(mid_ref[r, :])
                dx = dxt_ref[r, :]
                d = dxb_ref[r, :] + up_one(dx, after_row)
                back = cot_ref[r, :].astype(f32) + norm_back(d, nb, inverse, vec_ref[G2 : G2 + 1])
                dmid_ref[r, :] = back
                dbr_ref[r, :] = back.astype(bf16)
                sum_ref[0] += fold(d * nb)
                sum_ref[1] += fold(d)
                return dx[:1]
            lax.fori_loop(0, length // ROWS, step, after_ref[b : b + 1])
        put(0)
        put(1)
        column_sums(total_ref, sum_ref)
        wait(copies)
        @columns(width, STEP)
        def _(n):
            gn_ref[:, n] = dot_nt(dbr_ref[...], w[n, :])
        kvr_ref, wkv_ref, rden_ref = get(4), get(5), get(6)
        for b in range(batches):
            t = slice(b * length, (b + 1) * length)
            @columns(width, LANES)
            def _(n):
                _, _, _, o, _ = wkv_terms(kvr_ref, ent_ref, vec_ref, b, t, n, batches, length)
                sig = jax.nn.sigmoid(kvr_ref[2, t, n])
                d = gn_ref[t, n] * sig
                wkvs = wkv_ref[t, n]
                drec_ref[t, n] = (d * wkvs * (1.0 - sig)).astype(bf16)
                gn = d * rden_ref[t, n]
                gn_ref[t, n] = gn
                go = gn * o
                dent_ref[b : b + 1, n] = jnp.sum(go, axis=0, keepdims=True)
                dent_ref[batches + b : batches + b + 1, n] = -jnp.sum(go * wkvs, axis=0, keepdims=True)

    one, low = ((tokens, width), f32), ((tokens, width), bf16)
    return call(
        body, info, [after, vec, ent], [(a, None) for a in (dxt, dxb, mid, cot, kvr, wkv, rden)],
        flat_pieces(pieces), [((2 * batches, width), f32), ((2, width), f32)], [one, low, low, one],
        [pltpu.VMEM((width, width), bf16), pltpu.VMEM((2, 8, width), f32)], len(steps), 9, 40)


def time_back(info, gn, wkv, kvr, ent, back, sums, state, drec, stream, entry, vec, pieces, spots,
              length, shard):
    tokens, width = stream.shape
    batches = tokens // length
    stretches = back.shape[0]
    plans = [plan(pieces, spots[k], shard) for k in "kvr"]

    def body(info, small, get, raw, outs, big, put, scratch, loads):
        ent_ref, back_ref, sums_ref, num_ref, den_ref, exp_ref, entry_ref, vec_ref = small
        gnum_ref, gden_ref, gexp_ref, gffn_ref, head_ref, total_ref, extra_ref = outs
        d_ref, dxs_ref, dxa_ref = big
        w, dins, sum_ref, later_ref, loc_ref = scratch
        place = natural(info[0], shard)
        copies = [loads.pieces(plans[k], raw, w.at[k], place) for k in range(3)]
        span = -jnp.exp(vec_ref[DECAY : DECAY + 1, :]) * float(length)
        pos = info[2].astype(f32)
        nums, dens, exps = (slice(k * batches, (k + 1) * batches) for k in range(3))
        zero = jnp.zeros((batches, width), f32)

        def state(ref):
            return jnp.concatenate([ref[b] for b in range(batches)], axis=0)

        later_n = later_d = carry_n = carry_d = grad_n = grad_d = zero
        for z in range(stretches):
            there = back_ref[z, exps, :]
            after = z > info[2]
            lift = jnp.where(after, jnp.exp(jnp.minimum(
                sums_ref[exps, :] - there + (z - 1.0 - pos) * span, 0.0)), 0.0)
            carry = jnp.where(after, jnp.exp(jnp.minimum(
                ent_ref[exps, :] - there + (z - pos) * span, 0.0)), 0.0)
            raised = jnp.exp(jnp.minimum(state(exp_ref) - there + float(z) * span, 0.0))
            dn, dd = back_ref[z, nums, :], back_ref[z, dens, :]
            later_n, later_d = later_n + dn * lift, later_d + dd * lift
            carry_n, carry_d = carry_n + dn * carry, carry_d + dd * carry
            grad_n, grad_d = grad_n + dn * raised, grad_d + dd * raised
        later_ref[nums, :], later_ref[dens, :] = later_n, later_d
        grad_e = state(num_ref) * grad_n + state(den_ref) * grad_d
        for b in range(batches):
            gnum_ref[b], gden_ref[b] = grad_n[b : b + 1], grad_d[b : b + 1]
            gexp_ref[b] = grad_e[b : b + 1]
            gffn_ref[b] = back_ref[0, 3 * batches + b : 3 * batches + b + 1, :]
        rate_part = (
            float(length) * (ent_ref[nums, :] * carry_n + ent_ref[dens, :] * carry_d)
            + (length - 1.0) * (later_n * sums_ref[nums, :] + later_d * sums_ref[dens, :]))

        upper = triangle(length, False)
        gn_ref, wkv_ref, kvr_ref, drec_ref = get(0), get(1), get(2), get(3)
        for b in range(batches):
            t = slice(b * length, (b + 1) * length)
            @columns(width, LANES)
            def _(n):
                at, factor, p, o, e = wkv_terms(kvr_ref, ent_ref, vec_ref, b, t, n, batches, length)
                vals, g = kvr_ref[1, t, n], gn_ref[t, n]
                gd = -g * wkv_ref[t, n]
                direct = e * (g * vals + gd)
                opened = o * (g * ent_ref[b : b + 1, n] + gd * ent_ref[batches + b : batches + b + 1, n])
                rn = two_part(upper, g * p) + later_ref[b : b + 1, n]
                rd = two_part(upper, gd * p) + later_ref[batches + b : batches + b + 1, n]
                chain = factor * (rn * vals + rd)
                d_ref[0, t, n] = (chain + direct).astype(bf16)
                d_ref[1, t, n] = (factor * rn + g * e).astype(bf16)
                d_ref[2, t, n] = drec_ref[t, n]
                loc_ref[b : b + 1, n] = jnp.sum(
                    opened - (at - 1.0) * direct - at * chain, axis=0, keepdims=True)
                loc_ref[batches + b : batches + b + 1, n] = jnp.sum(direct, axis=0, keepdims=True)
        put(0)
        rate_rows = rate_part + loc_ref[:batches, :]
        extra_ref[0:1, :] = jnp.sum(rate_rows, axis=0, keepdims=True) * -jnp.exp(
            vec_ref[DECAY : DECAY + 1, :])
        extra_ref[1:2, :] = jnp.sum(loc_ref[batches:, :], axis=0, keepdims=True)
        for k in range(3):
            wait(copies[k])
            @columns(width, STEP)
            def _(n):
                dins[k, :, n] = dot_nt(d_ref[k], w[k, n, :])
        sum_ref[...] = jnp.zeros_like(sum_ref)
        stream_ref = get(4)
        for b in range(batches):
            def step(i, before):
                r = row_chunk(b, i, length)
                na, _ = norm(stream_ref[r, :].astype(f32))
                xa = na * vec_ref[G1 : G1 + 1] + vec_ref[B1 : B1 + 1]
                gap = xa - down_one(xa, before)
                dxs = jnp.zeros((ROWS, width), f32)
                dxa = jnp.zeros((ROWS, width), f32)
                for k, row in enumerate((MK, MV, MR)):
                    d, mix = dins[k, r, :], vec_ref[row : row + 1]
                    dxs = dxs + d * (1.0 - mix)
                    dxa = dxa + d * mix
                    sum_ref[k] += fold(d * gap)
                dxs_ref[r, :] = dxs
                dxa_ref[r, :] = dxa
                return xa[ROWS - 1 :]
            lax.fori_loop(0, length // ROWS, step, entry_ref[b : b + 1])
            head_ref[b : b + 1, :] = dxs_ref[b * length : b * length + 1, :]
        column_sums(total_ref, sum_ref)

    one = ((tokens, width), f32)
    return call(
        body, info, [ent, back, sums, *state, entry, vec],
        [(a, None) for a in (gn, wkv, kvr, drec, stream)], flat_pieces(pieces),
        [((batches, 1, width), f32)] * 4
        + [((batches, width), f32), ((3, width), f32), ((2, width), f32)],
        [((3, tokens, width), bf16), one, one],
        [pltpu.VMEM((3, width, width), bf16), pltpu.VMEM((3, tokens, width), f32),
         pltpu.VMEM((3, 8, width), f32), pltpu.VMEM((2 * batches, width), f32),
         pltpu.VMEM((2 * batches, width), f32)],
        sum(map(len, plans)), 14, 40)


def in_back(info, dxs, dxa, after, dmid, stream, vec, length):
    tokens, width = stream.shape
    batches = tokens // length

    def body(info, small, get, raw, outs, big, put, scratch, loads):
        after_ref, vec_ref = small
        (out_ref,) = big
        (sum_ref,) = scratch
        dxs_ref, dxa_ref, dmid_ref, stream_ref = (get(k) for k in range(4))
        sum_ref[...] = jnp.zeros_like(sum_ref)
        for b in range(batches):
            def step(k, after_row):
                r = row_chunk(b, length // ROWS - 1 - k, length)
                na, inverse = norm(stream_ref[r, :].astype(f32))
                dx = dxs_ref[r, :]
                d = dxa_ref[r, :] + up_one(dx, after_row)
                back = norm_back(d, na, inverse, vec_ref[G1 : G1 + 1])
                out_ref[r, :] = (dmid_ref[r, :] + back).astype(bf16)
                sum_ref[0] += fold(d * na)
                sum_ref[1] += fold(d)
                return dx[:1]
            lax.fori_loop(0, length // ROWS, step, after_ref[b : b + 1])
        column_sums(outs[0], sum_ref)

    return call(
        body, info, [after, vec], [(a, None) for a in (dxs, dxa, dmid, stream)], [],
        [((2, width), f32)], [((tokens, width), bf16)],
        [pltpu.VMEM((2, 8, width), f32)], 0, 6, 40)


def grad_orders():
    rest = far_bits()
    evens = list(range(0, lax.axis_size("seg"), 2))
    return evens, [[[m for m in evens if m & b], [m for m in evens if not m & b]]
                   for b in (rest[0], rest[-1])]


def weight_grad(info, arrays, items, layout, us):
    count = lax.axis_size("seg")
    evens, orders = grad_orders()
    tokens, n_wide = arrays[items[0][2][0]].shape[-2:]
    half = n_wide // 2
    per = len(evens) // 2
    w = arrays[items[0][0][0]].shape[-1] // {"natural": count, "blocks": len(evens), "groups": 4 * per}[layout]
    joined = w < 256
    loaded = 4 if joined else len(evens)
    group = per * w

    def body(info, small, get, raw, outs, big, put, scratch, loads):
        x_all, dy_all = scratch

        def view(spec):
            which, lead = spec
            return raw[which] if lead is None else raw[which].at[lead]

        def columns_of(ref, which, m):
            if layout == "natural":
                return ref.at[:, pl.ds(natural(info[0], w)(m), w)]
            return ref.at[:, pl.ds(evens.index(m) * w, w)]

        copies = []
        for k, (x, x_sib, dy, dy_sib) in enumerate(items):
            now = []
            for at, part in ((0, dy), (tokens, dy_sib)):
                now.append(loads.start(view(part), dy_all.at[k, pl.ds(at, tokens)]))
            for at, part in ((0, x), (tokens, x_sib)):
                ref = view(part)
                rows = pl.ds(at, tokens)
                if not joined:
                    for n, m in enumerate(evens):
                        now.append(loads.start(columns_of(ref, n, m), x_all.at[k, n, rows]))
                elif layout == "groups":
                    for g in range(4):
                        now.append(loads.start(
                            ref.at[:, pl.ds(g * group, group)], x_all.at[k, g, rows]))
                else:
                    for g in range(4):
                        for n, m in enumerate(orders[g // 2][g % 2]):
                            now.append(loads.start(
                                columns_of(ref, n, m), x_all.at[k, g, rows, pl.ds(n * w, w)]))
            copies.append(now)
        step = min(512, half)
        for k in range(len(items)):
            wait(copies[k])
        for stay in range(2):
            for side in range(2):
                out = big[2 * side + stay]
                for k in range(len(items)):
                    for q in range(half // step):
                        dst = slice(q * step, (q + 1) * step)
                        dys = dy_all[k, :, side * half + q * step : side * half + (q + 1) * step]
                        if joined:
                            g = dot_tn(x_all[k, 2 * side + stay], dys).astype(bf16)
                            for at in range(per):
                                out[at, k * w : (k + 1) * w, dst] = g[at * w : (at + 1) * w]
                        else:
                            for at, m in enumerate(orders[side][stay]):
                                out[at, k * w : (k + 1) * w, dst] = dot_tn(
                                    x_all[k, evens.index(m)], dys).astype(bf16)
                put(2 * side + stay)

    shape = (per, len(items) * w, half)
    return call(
        body, info, [], [], arrays, [], [(shape, bf16)] * 4,
        [pltpu.VMEM((len(items), loaded, 2 * tokens, group if joined else w), bf16),
         pltpu.VMEM((len(items), 2 * tokens, n_wide), bf16)],
        len(items) * (2 + 2 * max(len(evens), 4 * per)), us, 40)


def grad_first(parts):
    rest = far_bits()
    return hop(parts[0], rest[0]), hop(parts[2], rest[-1])


def total(terms):
    out = terms[0].astype(f32)
    for t in terms[1:]:
        out = out + t.astype(f32)
    return out


def own_rows(parts, items):
    return parts[0].shape[1] // items // lax.axis_size("stretch")


def by_kernel(parts, items):
    return len(far_bits()) == 2 and own_rows(parts, items) % 16 == 0


def grad_sends(info, parts, got, items):
    if by_kernel(parts, items):
        large = [(parts[1], 1), (got[0], 1), (parts[3], 1), (got[1], 1)]
        shape = parts[0].shape[1:]

        def body(info, small, get, raw, outs, big, put, scratch, loads):
            for side in range(2):
                a, b = get(2 * side), get(2 * side + 1)
                big[side][...] = total([a[...], b[...]]).astype(bf16)
                put(side)

        return call(body, info, [], large, [], [], [(shape, bf16)] * 2, [], 0, 2, 24)
    out = []
    for side, order in enumerate((far_bits(), far_bits()[::-1])):
        stay = grad_orders()[1][side][1]
        out.append(jnp.stack([
            total([parts[2 * side + 1][k], got[side][k]])
            for k, m in enumerate(stay) if m & order[1]]).astype(bf16))
    return out


def grad_second(parts, sends, items):
    rest = far_bits()
    if by_kernel(parts, items):
        return [hop(sends[0], rest[1]), hop(sends[1], rest[0])]
    return sends


def grad_finish(info, parts, got, last, items):
    stretches = lax.axis_size("stretch")
    own = own_rows(parts, items)
    rows, half = parts[0].shape[1:]
    rest = far_bits()
    if by_kernel(parts, items):
        large = [(parts[1], 0), (got[0], 0), (last[0], None), (parts[3], 0), (got[1], 0), (last[1], None)]

        def body(info, small, get, raw, outs, big, put, scratch, loads):
            for side in range(2):
                refs = [get(3 * side + j) for j in range(3)]
                for z in range(stretches):
                    for k in range(items):
                        src = slice((k * stretches + z) * own, (k * stretches + z + 1) * own)
                        dst = slice((z * items + k) * own, (z * items + k + 1) * own)
                        big[0][dst, side * half : (side + 1) * half] = total(
                            [r[src, :] for r in refs]).astype(bf16)

        return call(body, info, [], large, [], [], [((rows, 2 * half), bf16)], [], 0, 2, 24)[0]
    sides = []
    for side, order in enumerate((rest, rest[::-1])):
        stay = grad_orders()[1][side][1]
        terms = {m: [parts[2 * side + 1][k], got[side][k]] for k, m in enumerate(stay)}
        out = last[side]
        for b in order[1:]:
            if out is None:
                out = jnp.stack([total(v) for m, v in terms.items() if m & b]).astype(bf16)
            back = hop(out, b)
            terms = {m: v for m, v in terms.items() if not m & b}
            terms = {m: [*v, back[k]] for k, (m, v) in enumerate(terms.items())}
            out = None
        sides.append(total(terms[0]))
    whole = jnp.concatenate(sides, axis=1).astype(bf16).reshape(items, stretches, own, 2 * half)
    return jnp.swapaxes(whole, 0, 1).reshape(rows, 2 * half)


def stretch_part(part):
    return lax.psum_scatter(part, "stretch", scatter_dimension=0, tiled=True)


def stretch_items(out, items):
    own = out.shape[0] // items
    return [out[k * own : (k + 1) * own].astype(f32) for k in range(items)]


def vector_sum(table):
    for axis in ("seg", "stretch"):
        at = lax.axis_index(axis)
        bit = lax.axis_size(axis) // 2
        while bit:
            lo, hi = jnp.split(table, 2, axis=1)
            upper = (at & bit) != 0
            count = lax.axis_size(axis)
            got = lax.ppermute(jnp.where(upper, lo, hi), axis, [(i, i ^ bit) for i in range(count)])
            table = jnp.where(upper, hi, lo) + got
            bit //= 2
    return table


def grouped_columns(x, me, w):
    return jnp.concatenate([
        lax.dynamic_slice_in_dim(x, (me ^ m) * w, w, 1)
        for side in grad_orders()[1] for blocks in side for m in blocks], axis=1)


def body(
    stream_in, cotangent, previous_mix, previous_ffn, state_num, state_den, state_exp,
    gain_one, bias_one, gain_two, bias_two, mix_key, mix_value, mix_recept,
    time_decay, time_first, chan_mix_key, chan_mix_recept,
    att_key, att_value, att_recept, att_output, chan_key, chan_value, chan_recept,
):
    mine = lax.axis_index("seg")
    position = lax.axis_index("stretch")
    stretches = lax.axis_size("stretch")
    batches, _, length, width = stream_in.shape
    tokens = batches * length
    shard = att_key.shape[0]
    fshard = chan_value.shape[0]
    wide = chan_key.shape[1]
    aligned = shard % 128 == 0
    info = jnp.stack([mine, (position == 0).astype(jnp.int32), position])

    stream = stream_in.reshape(tokens, width)
    cot = cotangent.reshape(tokens, width)
    state = (state_num, state_den, state_exp)
    vectors = [gain_one, bias_one, gain_two, bias_two, mix_key, mix_value, mix_recept,
               time_decay, time_first, chan_mix_key, chan_mix_recept]

    v = Live()
    vec_rows = jnp.pad(jnp.stack(vectors), ((0, 16 - len(vectors)), (0, width - shard)))
    spots = {"k": 0, "v": shard, "vec": 2 * shard, "c": 2 * shard + 16, "r": 3 * shard + 16,
             "o": 4 * shard + 16}
    cut = shard // 2
    v.own_tm = pack(
        info, [(att_key, 0, shard), (att_value, 0, shard), (vec_rows, 0, 16), (chan_recept, 0, cut)],
        [(chan_recept, cut, cut), (att_recept, 0, shard), (att_output, 0, shard)], width)
    v.ck, v.cv = chan_key, chan_value
    v.last_in = stream_in[:, 0, length - 1]
    v.sync()
    v.one_tm = first_stage(v.own_tm)
    v.last_in = along(v.last_in, 1)
    v.tm0 = sibling({0: v.own_tm})
    v.sync()
    v.tm6 = second_stage(v.one_tm, v.one_tm)
    v.tm2 = sibling(v.one_tm)
    v.sync()

    v.one_ck = first_stage([v.ck])
    tm = {0: v.own_tm, **v.one_tm, **v.tm6, **v.tm0, **v.tm2, **sibling(v.tm6)}
    given = None
    if not aligned:
        given = lax.all_gather(jnp.stack(vectors), "seg", axis=1, tiled=True).astype(f32)
        given = jnp.pad(given, ((0, 5), (0, 0)))
    v.sums, v.vec, v.entry, v.kvr_in, v.kvr = time_in(
        info, stream, v.last_in, previous_mix, given, tm, spots, length, shard)
    v.everyone = lax.all_gather(v.sums, "stretch")
    v.tm = tm
    v.held_ck = {m: halves(p) for m, p in v.one_ck.items()}
    v.drop("own_tm", "one_tm", "tm6", "tm0", "tm2")
    v.sync()

    v.ck6 = second_stage(v.one_ck, v.held_ck)
    v.one_cv = first_stage([v.cv])
    v.ent, v.mean, v.log, edge_b, v.gated, v.wkv, v.rden, v.mid, v.xb = time_out(
        info, v.kvr, v.everyone, state, v.vec, stream, v.tm, spots, length, shard)
    v.edge_b = along(edge_b, 1)
    v.ck0 = sibling({0: [v.ck]})
    v.ck2 = sibling(v.one_ck)
    v.held_cv = {m: halves(p) for m, p in v.one_cv.items()}
    v.drop("held_ck")
    v.sync()

    v.cv6 = second_stage(v.one_cv, v.held_cv)
    ck = {0: [v.ck], **v.one_ck, **v.ck6, **v.ck0, **v.ck2, **sibling(v.ck6)}
    v.entry_b, v.f_in, v.near, v.far, v.act, v.frec = chan_in(
        info, v.xb, v.edge_b, previous_ffn, v.vec, v.tm, ck, spots, length, shard, fshard)
    v.cv0 = sibling({0: [v.cv]})
    v.cv2 = sibling(v.one_cv)
    v.all_ck = ck
    v.drop("held_cv", "ck", "one_ck", "ck6", "ck0", "ck2")
    v.sync()
    cv = {0: [v.cv], **v.one_cv, **v.cv6, **v.cv0, **v.cv2, **sibling(v.cv6)}
    v.far_sib = hop(v.far, 1)
    v.f_sib = hop(v.f_in, 1)
    v.block_out, v.d_fval, v.d_frec, v.dpre = chan_out(
        info, v.near, v.far, v.act, v.frec, v.mid, cot, cv, fshard)
    v.g_sib = hop(v.gated, 1)
    v.kvr_sib = hop(v.kvr_in, 1)
    v.drop("cv", "one_cv", "cv6", "cv0", "cv2", "act", "frec", "far")
    v.sync()

    def pairs(*arrays):
        if aligned:
            return [a for pair in arrays for a in pair]
        return [grouped_columns(a, mine, shard) for pair in arrays for a in pair]

    layout = "natural" if aligned else "groups"
    flat = tuple((j, None) for j in range(4))
    v.parts_cv = weight_grad(info, [v.near, v.far_sib, v.d_fval, hop(v.d_fval, 1)], [flat], "blocks", 6)
    v.drop("near", "far_sib", "d_fval")
    v.sync()

    v.got_cv = grad_first(v.parts_cv)
    v.head_b, v.sums_c, v.dxt, v.dxb = chan_back(
        info, v.dpre, v.d_frec, v.xb, v.entry_b, v.vec, v.tm, v.all_ck, spots, length, shard, wide)
    v.next_b = along(v.head_b, -1)
    dpre_sib = hop(v.dpre, 1)
    if aligned:
        v.parts_ck = weight_grad(
            info, [v.f_in, v.f_sib, v.dpre, dpre_sib], [((0, 0), (1, 0), (2, None), (3, None))], layout, 7)
    else:
        v.parts_ck = weight_grad(
            info, [*pairs((v.f_in[0], v.f_sib[0])), v.dpre, dpre_sib], [flat], layout, 7)
    v.dfrec_sib = hop(v.d_frec, 1)
    v.drop("all_ck", "dpre", "xb", "entry_b")
    v.sync()
    v.sends_cv = grad_sends(info, v.parts_cv, v.got_cv, 1)
    v.sync()

    v.last_cv = grad_second(v.parts_cv, v.sends_cv, 1)
    v.got_ck = grad_first(v.parts_ck)
    dent, v.sums_m, v.dmid, dbr, v.drec, v.gn = mid_back(
        info, v.dxt, v.dxb, v.next_b, v.mid, cot, v.vec, v.kvr, v.wkv, v.rden, v.ent, v.tm, spots,
        length, shard)
    v.back = lax.all_gather(jnp.concatenate([dent, v.ent[2 * batches :], v.head_b], axis=0), "stretch")
    dbr_sib = hop(dbr, 1)
    if aligned:
        v.parts_oc = weight_grad(
            info, [v.gated, v.g_sib, dbr, dbr_sib, v.f_in, v.f_sib, v.d_frec, v.dfrec_sib],
            [flat, ((4, 1), (5, 1), (6, None), (7, None))], layout, 6)
    else:
        xs = pairs((v.gated, v.g_sib), (v.f_in[1], v.f_sib[1]))
        v.parts_oc = weight_grad(
            info, [*xs, dbr, dbr_sib, v.d_frec, v.dfrec_sib],
            [((2 * k, None), (2 * k + 1, None), (4 + 2 * k, None), (5 + 2 * k, None)) for k in range(2)],
            layout, 6)
    v.drop("dxt", "dxb", "mid", "next_b", "rden", "head_b", "gated", "g_sib", "f_in", "f_sib", "d_frec",
           "dfrec_sib", "sends_cv")
    v.sync()
    v.part_cv = grad_finish(info, v.parts_cv, v.got_cv, v.last_cv, 1)
    v.sends_ck = grad_sends(info, v.parts_ck, v.got_ck, 1)
    v.drop("parts_cv", "got_cv", "last_cv")
    v.sync()

    v.z_cv = stretch_part(v.part_cv)
    v.last_ck = grad_second(v.parts_ck, v.sends_ck, 1)
    v.got_oc = grad_first(v.parts_oc)
    *v.grads, v.head_a, v.sums_t, v.extra, v.d_kvr, v.dxs, v.dxa = time_back(
        info, v.gn, v.wkv, v.kvr, v.ent, v.back, v.sums, state, v.drec, stream, v.entry, v.vec,
        v.tm, spots, length, shard)
    dkvr_sib = hop(v.d_kvr, 1)
    if aligned:
        v.parts_kvr = weight_grad(
            info, [v.kvr_in, v.kvr_sib, v.d_kvr, dkvr_sib],
            [tuple((j, k) for j in range(4)) for k in range(3)], layout, 7)
    else:
        xs = pairs(*[(v.kvr_in[k], v.kvr_sib[k]) for k in range(3)])
        v.parts_kvr = weight_grad(
            info, [*xs, v.d_kvr, dkvr_sib],
            [((2 * k, None), (2 * k + 1, None), (6, k), (7, k)) for k in range(3)], layout, 7)
    v.drop("gn", "wkv", "kvr", "ent", "sums", "drec", "entry", "tm", "kvr_in", "kvr_sib", "d_kvr",
           "sends_ck", "part_cv")
    v.sync()
    v.part_ck = grad_finish(info, v.parts_ck, v.got_ck, v.last_ck, 1)
    v.sends_oc = grad_sends(info, v.parts_oc, v.got_oc, 2)
    v.drop("parts_ck", "got_ck", "last_ck")
    v.sync()

    v.z_ck = stretch_part(v.part_ck)
    v.got_kvr = grad_first(v.parts_kvr)
    v.last_oc = grad_second(v.parts_oc, v.sends_oc, 2)
    next_a = along(v.head_a, -1)
    v.sums_i, v.grad_stream = in_back(info, v.dxs, v.dxa, next_a, v.dmid, stream, v.vec, length)
    v.out_cv = stretch_items(v.z_cv, 1)
    v.drop("dxs", "dxa", "dmid", "part_ck", "z_cv")
    v.sync()
    v.part_oc = grad_finish(info, v.parts_oc, v.got_oc, v.last_oc, 2)
    v.sends_kvr = grad_sends(info, v.parts_kvr, v.got_kvr, 3)
    v.drop("parts_oc", "got_oc", "last_oc")
    v.sync()
    v.z_oc = stretch_part(v.part_oc)
    v.last_kvr = grad_second(v.parts_kvr, v.sends_kvr, 3)
    v.small = vector_sum(jnp.concatenate([v.sums_i, v.sums_m, v.sums_t, v.extra, v.sums_c], axis=0))
    v.out_ck = stretch_items(v.z_ck, 1)
    v.drop("part_oc", "z_ck")
    v.sync()
    v.part_kvr = grad_finish(info, v.parts_kvr, v.got_kvr, v.last_kvr, 3)
    v.sync()
    out_kvr = stretch_items(stretch_part(v.part_kvr), 3)
    out_oc = stretch_items(v.z_oc, 2)
    out_cv, out_ck, small = v.out_cv, v.out_ck, v.small
    grad_previous_mix = lax.all_gather(v.head_a, "stretch")[0]
    block_out, grad_stream = v.block_out, v.grad_stream

    shape = stream_in.shape
    return (
        block_out.reshape(shape), grad_stream.reshape(shape), *[small[i] for i in range(11)],
        *out_kvr, out_oc[0], *out_ck, *out_cv, out_oc[1],
        *v.grads[:3], grad_previous_mix[:, None], v.grads[3], v.mean, v.log,
    )


def solution(mesh):
    rows = P(None, "seg", "stretch", None)
    state = P(None, "seg", None)
    both = P(("seg", "stretch"))
    table = P(("seg", "stretch"), None)
    return jax.shard_map(
        body,
        mesh=mesh,
        in_specs=(rows,) * 2 + (state,) * 5 + (P("seg"),) * 11 + (P("seg", None),) * 7,
        out_specs=(rows,) * 2 + (both,) * 11 + (table,) * 7 + (state,) * 7,
        check_vma=False,
    )
```

```python
import jax
import jax.numpy as jnp
from jax import lax
from jax.experimental import pallas as pl
from jax.experimental.pallas import tpu as pltpu
from jax.sharding import PartitionSpec as P

epsilon = 1e-05
bf16 = jnp.bfloat16
f32 = jnp.float32
ROWS = 64
STEP = 512
LANES = 512
LIMIT = 60
MIB = 2**20
G1, B1, G2, B2, MK, MV, MR, DECAY, FIRST, CMK, CMR = range(11)


def hop(value, bit):
    count = lax.axis_size("seg")
    return lax.ppermute(value, "seg", [(i, i ^ bit) for i in range(count)])


def along(value, steps):
    count = lax.axis_size("stretch")
    first, last = (max(0, -steps), min(count, count - steps))
    return lax.ppermute(value, "stretch", [(i, i + steps) for i in range(first, last)])


def across(value, j):
    count = lax.axis_size("stretch")
    return lax.ppermute(value, "stretch", [(i, i ^ j) for i in range(count)])


def exchange(value):
    count = lax.axis_size("stretch")
    if count == 4:
        near, far = across(value, 1), across(value, 2)
        return [value, near, far, across(near, 2)]
    return lax.all_gather(value, "stretch")


def tie(value, *others):
    return lax.optimization_barrier((value, *others))[0]


class Live:
    def __init__(self):
        self.__dict__["held"] = {}

    def __getattr__(self, name):
        return self.held[name]

    def __setattr__(self, name, value):
        self.held[name] = value

    def drop(self, *names):
        for name in names:
            del self.held[name]

    def sync(self):
        self.__dict__["held"] = lax.optimization_barrier(self.held)


def far_bits():
    bits, b = [], 2
    while b < lax.axis_size("seg"):
        bits.append(b)
        b *= 2
    return bits


def relative_order():
    count = lax.axis_size("seg")
    return list(range(0, count, 2)) + list(range(1, count, 2))


def first_stage(own):
    return {b: [hop(part, b) for part in own] for b in far_bits()}


def second_stage(direct, held):
    rest = far_bits()
    held = dict(held)
    for m in sorted(range(0, lax.axis_size("seg"), 2), key=lambda m: (bin(m).count("1"), m)):
        if m == 0 or m in held:
            continue
        bits = [b for b in rest if m & b]
        held[m] = [hop(held[m ^ bits[-1]][0], bits[-1]), hop(held[m ^ bits[0]][1], bits[0])]
    return {m: held[m] for m in held if m not in direct}


def sibling(pieces):
    return {m ^ 1: [hop(p, 1) for p in parts] for m, parts in pieces.items()}


def plan(pieces, first, rows):
    steps, at = [], 0
    for m in relative_order():
        base = 0
        for part in pieces[m]:
            lo, hi = max(first, base), min(first + rows, base + part.shape[0])
            if lo < hi:
                steps.append((at, lo - base, hi - lo, m, lo - first))
            base += part.shape[0]
            at += 1
    return steps


def flat_pieces(pieces):
    return [part for m in relative_order() for part in pieces[m]]


class Loads:
    def __init__(self, sems):
        self.sems, self.used = sems, 0

    def start(self, src, dst):
        copy = pltpu.make_async_copy(src, dst, self.sems.at[self.used])
        self.used += 1
        copy.start()
        return copy

    def pieces(self, steps, refs, target, place):
        return [
            self.start(refs[piece].at[pl.ds(row, count)], target.at[pl.ds(place(m) + within, count)])
            for piece, row, count, m, within in steps
        ]


def wait(copies):
    for c in copies:
        c.wait()


def call(body, info, small, large, raw, outs, big_outs, scratch, copies, us, limit):
    n_small, n_large, n_raw = len(small), len(large), len(raw)
    n_out, n_big = len(outs), len(big_outs)

    def shape_of(array, index):
        return array.shape if index is None else array.shape[1:]

    def kernel(*refs):
        at = 0

        def take(n):
            nonlocal at
            at += n
            return refs[at - n : at]

        (info_ref,), small_refs, large_refs, raw_refs = take(1), take(n_small), take(n_large), take(n_raw)
        out_refs, big_refs = take(n_out), take(n_big)
        buffers, big_buffers, (sems,) = take(n_large), take(n_big), take(1)
        rest = take(len(refs) - at)
        loads = Loads(sems)
        pending = []
        for (array, index), ref, buf in zip(large, large_refs, buffers):
            pending.append(loads.start(ref if index is None else ref.at[index], buf))
        stored = {}

        def get(k):
            if pending[k] is not None:
                pending[k].wait()
                pending[k] = None
            return buffers[k]

        def put(k):
            stored[k] = loads.start(big_buffers[k], big_refs[k])

        body(info_ref, small_refs, get, raw_refs, out_refs, big_buffers, put, rest, loads)
        for k in range(n_large):
            get(k)
        for k in range(n_big):
            if k not in stored:
                put(k)
        wait(stored.values())

    hbm = pl.BlockSpec(memory_space=pltpu.HBM)
    vmem = pl.BlockSpec(memory_space=pltpu.VMEM)
    return pl.pallas_call(
        kernel,
        out_shape=[jax.ShapeDtypeStruct(s, d) for s, d in (*outs, *big_outs)],
        in_specs=[pl.BlockSpec(memory_space=pltpu.SMEM)] + [vmem] * n_small + [hbm] * (n_large + n_raw),
        out_specs=[vmem] * n_out + [hbm] * n_big,
        scratch_shapes=[pltpu.VMEM(shape_of(a, i), a.dtype) for a, i in large]
        + [pltpu.VMEM(s, d) for s, d in big_outs]
        + [pltpu.SemaphoreType.DMA((max(1, n_large + n_big + copies),))]
        + list(scratch),
        compiler_params=pltpu.CompilerParams(vmem_limit_bytes=LIMIT * MIB),
        cost_estimate=pl.CostEstimate(
            flops=0, bytes_accessed=int(us * 1e3), transcendentals=0),
    )(info, *small, *[a for a, _ in large], *raw)


def natural(me, rows):
    return lambda m: pl.multiple_of(jnp.bitwise_xor(me, m) * rows, rows)


def dot_nn(a, b):
    return jnp.dot(a, b, preferred_element_type=f32)


def dot_nt(a, b):
    return lax.dot_general(a, b, (((1,), (1,)), ((), ())), preferred_element_type=f32)


def dot_tn(a, b):
    return lax.dot_general(a, b, (((0,), (0,)), ((), ())), preferred_element_type=f32)


def norm(rows):
    centre = rows - jnp.mean(rows, axis=-1, keepdims=True)
    inverse = lax.rsqrt(jnp.mean(centre * centre, axis=-1, keepdims=True) + epsilon)
    return centre * inverse, inverse


def norm_back(d, unit, inverse, gain):
    q = d * gain
    return inverse * (
        q
        - jnp.mean(q, axis=-1, keepdims=True)
        - unit * jnp.mean(q * unit, axis=-1, keepdims=True)
    )


def down_one(rows, entering):
    at = lax.broadcasted_iota(jnp.int32, rows.shape, 0)
    return jnp.where(at == 0, entering, pltpu.roll(rows, 1, 0))


def up_one(rows, entering):
    at = lax.broadcasted_iota(jnp.int32, rows.shape, 0)
    last = rows.shape[0] - 1
    return jnp.where(at == last, entering, pltpu.roll(rows, last, 0))


def fold(rows):
    total = rows[:8]
    for k in range(8, rows.shape[0], 8):
        total = total + rows[k : k + 8]
    return total


def columns(width, step):
    step = min(step, width)

    def run(body):
        @pl.loop(0, width // step)
        def _(n):
            body(pl.ds(pl.multiple_of(n * step, step), step))

    return run


def row_chunk(b, i, length):
    return pl.ds(pl.multiple_of(b * length + i * ROWS, ROWS), ROWS)


def two_part(mat, value):
    hi = value.astype(bf16)
    lo = (value - hi.astype(f32)).astype(bf16)
    return dot_nn(mat, hi) + dot_nn(mat, lo)


def triangle(length, strictly_before):
    row = lax.broadcasted_iota(jnp.int32, (length, length), 0)
    col = lax.broadcasted_iota(jnp.int32, (length, length), 1)
    keep = (col < row) if strictly_before else (col > row)
    return keep.astype(f32).astype(bf16)


def column_sums(out_ref, sum_ref):
    for k in range(sum_ref.shape[0]):
        out_ref[k : k + 1, :] = jnp.sum(sum_ref[k], axis=0, keepdims=True)


def pack(parts_a, parts_b, vectors, width):
    arrays = [p[0] for p in (*parts_a, *parts_b) if p[0] is not None]
    shard = vectors[0].shape[0]

    def kernel(*refs):
        vec_refs, ins = refs[: len(vectors)], refs[len(vectors) : len(vectors) + len(arrays)]
        outs, (table, sems) = refs[len(vectors) + len(arrays) : -2], refs[-2:]
        copies, n = [], 0
        for out, parts in zip(outs, (parts_a, parts_b)):
            at = 0
            for array, first, count in parts:
                if array is None:
                    spot = (out, at)
                else:
                    copies.append(pltpu.make_async_copy(
                        ins[n].at[pl.ds(first, count)], out.at[pl.ds(at, count)], sems.at[n]))
                    copies[-1].start()
                    n += 1
                at += count
        table[...] = jnp.zeros_like(table)
        for k, ref in enumerate(vec_refs):
            table[k : k + 1, :shard] = ref[...].astype(f32)
        spot[0][spot[1] : spot[1] + 16, :] = table[...].astype(bf16)
        wait(copies)

    return pl.pallas_call(
        kernel,
        out_shape=[jax.ShapeDtypeStruct((sum(p[2] for p in parts), width), bf16)
                   for parts in (parts_a, parts_b)],
        in_specs=[pl.BlockSpec(memory_space=pltpu.VMEM)] * len(vectors)
        + [pl.BlockSpec(memory_space=pltpu.HBM)] * len(arrays),
        out_specs=[pl.BlockSpec(memory_space=pltpu.VMEM)] * 2,
        scratch_shapes=[pltpu.VMEM((16, width), f32), pltpu.SemaphoreType.DMA((len(arrays),))],
        compiler_params=pltpu.CompilerParams(vmem_limit_bytes=LIMIT * MIB),
        cost_estimate=pl.CostEstimate(flops=0, bytes_accessed=1000, transcendentals=0),
    )(*[x.reshape(1, shard) for x in vectors], *arrays)


def pack_wide(key, recept):
    rows, wide = key.shape
    width = recept.shape[1]
    each = recept.shape[0] * width // wide
    half = (rows + each) // 32 * 16

    def kernel(key_ref, recept_ref, top_ref, low_ref, sems):
        copies = [
            pltpu.make_async_copy(key_ref.at[pl.ds(0, half)], top_ref, sems.at[0]),
            pltpu.make_async_copy(
                key_ref.at[pl.ds(half, rows - half)], low_ref.at[pl.ds(0, rows - half)], sems.at[1])]
        for q in range(wide // width):
            copies.append(pltpu.make_async_copy(
                recept_ref.at[pl.ds(q * each, each)],
                low_ref.at[pl.ds(rows - half, each), pl.ds(q * width, width)], sems.at[2 + q]))
        for c in copies:
            c.start()
        wait(copies)

    return pl.pallas_call(
        kernel,
        out_shape=[jax.ShapeDtypeStruct((n, wide), bf16) for n in (half, rows + each - half)],
        in_specs=[pl.BlockSpec(memory_space=pltpu.HBM)] * 2,
        out_specs=[pl.BlockSpec(memory_space=pltpu.VMEM)] * 2,
        scratch_shapes=[pltpu.SemaphoreType.DMA((2 + wide // width,))],
        compiler_params=pltpu.CompilerParams(vmem_limit_bytes=LIMIT * MIB),
        cost_estimate=pl.CostEstimate(flops=0, bytes_accessed=1000, transcendentals=0),
    )(key, recept)


def recept_blocks(loads, steps, raw, w, info, shard, width, wide):
    each = shard * width // wide
    place = natural(info[0], shard)
    return [
        loads.start(raw[piece].at[pl.ds(row, count), pl.ds(q * width, width)],
                    w.at[pl.ds(place(m) + q * each + within, count)])
        for piece, row, count, m, within in steps
        for q in range(wide // width)
    ]


def time_in(info, stream, last, previous, given, pieces, spots, length, shard):
    tokens, width = stream.shape
    batches = tokens // length
    plans = [plan(pieces, spots[k], shard) for k in "kvr"]
    vplan = plan(pieces, spots["vec"], 16)
    order = relative_order()

    def body(info, small, get, raw, outs, big, put, scratch, loads):
        last_ref, prev_ref = small[:2]
        sum_ref, vec_ref, entry_ref = outs
        in_ref = big[0]
        w, vt = scratch
        place = natural(info[0], shard)
        vcopies = loads.pieces(vplan, raw, vt, lambda m: order.index(m) * 16)
        copies = [loads.pieces(plans[k], raw, w.at[k], place) for k in range(3)]
        wait(vcopies)
        if given is not None:
            vec_ref[...] = small[2][...]
        else:
            for at, m in enumerate(order):
                vec_ref[:, pl.ds(place(m), shard)] = vt[at * 16 : at * 16 + 16, :shard].astype(f32)
        unit, _ = norm(last_ref[...].astype(f32))
        edge = unit * vec_ref[G1 : G1 + 1] + vec_ref[B1 : B1 + 1]
        for b in range(batches):
            entry_ref[b : b + 1, :] = jnp.where(info[1] == 1, prev_ref[b], edge[b : b + 1])
        stream_ref = get(0)

        for b in range(batches):
            def step(i, before):
                r = row_chunk(b, i, length)
                na, _ = norm(stream_ref[r, :].astype(f32))
                xa = na * vec_ref[G1 : G1 + 1] + vec_ref[B1 : B1 + 1]
                xs = down_one(xa, before)
                for k, row in enumerate((MK, MV, MR)):
                    mix = vec_ref[row : row + 1]
                    in_ref[k, r, :] = (xa * mix + xs * (1.0 - mix)).astype(bf16)
                return xa[ROWS - 1 :]
            lax.fori_loop(0, length // ROWS, step, entry_ref[b : b + 1])
        put(0)
        def project(k):
            wait(copies[k])
            @columns(width, STEP)
            def _(n):
                big[1 + k][:, n] = dot_nn(in_ref[k], w[k, :, n])
            put(1 + k)
        project(0)
        project(1)
        keys_ref, vals_ref = big[1], big[2]
        for b in range(batches):
            t = slice(b * length, (b + 1) * length)
            @columns(width, LANES)
            def _(n):
                rate = -jnp.exp(vec_ref[DECAY : DECAY + 1, n])
                at = lax.broadcasted_iota(jnp.int32, (length, 1), 0).astype(f32)
                shifted = keys_ref[t, n] - at * rate
                peak = jnp.max(shifted, axis=0, keepdims=True)
                factor = jnp.exp(shifted - peak)
                sum_ref[b : b + 1, n] = jnp.sum(factor * vals_ref[t, n], axis=0, keepdims=True)
                sum_ref[batches + b : batches + b + 1, n] = jnp.sum(factor, axis=0, keepdims=True)
                sum_ref[2 * batches + b : 2 * batches + b + 1, n] = peak + (length - 1.0) * rate
        project(2)

    extra = [] if given is None else [given]
    return call(
        body, info, [last, previous, *extra], [(stream, None)], flat_pieces(pieces),
        [((3 * batches, width), f32), ((16, width), f32), ((batches, width), f32)],
        [((3, tokens, width), bf16)] + [((tokens, width), f32)] * 3,
        [pltpu.VMEM((3, width, width), bf16), pltpu.VMEM((16 * len(order), width), bf16)],
        len(vplan) + sum(map(len, plans)), 9, 40)


def wkv_terms(kvr_ref, ent_ref, vec_ref, b, t, n, batches, length):
    rate = -jnp.exp(vec_ref[DECAY : DECAY + 1, n])
    at = lax.broadcasted_iota(jnp.int32, (length, 1), 0).astype(f32)
    keys = kvr_ref[0][t, n]
    shifted = keys - at * rate
    peak = jnp.max(shifted, axis=0, keepdims=True)
    factor = jnp.exp(shifted - peak)
    near = (at - 1.0) * rate + peak
    opening = at * rate + ent_ref[2 * batches + b : 2 * batches + b + 1, n]
    reward = vec_ref[FIRST : FIRST + 1, n] + keys
    top = jnp.maximum(jnp.maximum(near, opening), reward)
    return at, factor, jnp.exp(near - top), jnp.exp(opening - top), jnp.exp(reward - top)


def time_out(info, kvr, everyone, state, vec, stream, pieces, spots, length, shard):
    tokens, width = stream.shape
    batches = tokens // length
    stretches = len(everyone)
    relative = isinstance(everyone, list)
    if not relative:
        everyone = [everyone]
    steps = plan(pieces, spots["o"], shard)

    def body(info, small, get, raw, outs, big, put, scratch, loads):
        every_ref, (num_ref, den_ref, exp_ref, vec_ref) = small[:-4], small[-4:]
        if not relative:
            every_ref = [every_ref[0].at[z] for z in range(stretches)]
        ent_ref, mean_ref, log_ref, edge_ref = outs
        gated_ref, wkv_ref, rden_ref, mid_ref, xb_ref = big
        (w,) = scratch
        copies = loads.pieces(steps, raw, w, natural(info[0], shard))
        span = -jnp.exp(vec_ref[DECAY : DECAY + 1, :]) * float(length)

        def merge(upto, b):
            upto_f = upto.astype(f32) if upto is not stretches else float(stretches)
            logits = []
            for j in range(stretches):
                row, z = 2 * batches + b, jnp.bitwise_xor(info[2], j) if relative else jnp.int32(j)
                logit = every_ref[j][row : row + 1, :] + (upto_f - 1.0 - z.astype(f32)) * span
                logits.append(logit if upto is stretches else jnp.where(z < upto, logit, -jnp.inf))
            opening = exp_ref[b] + upto_f * span
            top = opening
            for logit in logits:
                top = jnp.maximum(top, logit)
            start = jnp.exp(opening - top)
            num, den = num_ref[b] * start, den_ref[b] * start
            for j, logit in enumerate(logits):
                weight = jnp.exp(logit - top)
                num = num + weight * every_ref[j][b : b + 1, :]
                den = den + weight * every_ref[j][batches + b : batches + b + 1, :]
            return num, den, top

        for b in range(batches):
            for k, part in enumerate(merge(info[2], b)):
                ent_ref[k * batches + b : k * batches + b + 1, :] = part
            num, den, top = merge(stretches, b)
            mean_ref[b] = num / den
            log_ref[b] = top + jnp.log(den)

        lower = triangle(length, True)
        kvr_ref = [get(k) for k in range(3)]
        for b in range(batches):
            t = slice(b * length, (b + 1) * length)
            @columns(width, LANES)
            def _(n):
                _, factor, p, o, e = wkv_terms(kvr_ref, ent_ref, vec_ref, b, t, n, batches, length)
                vals = kvr_ref[1][t, n]
                num = (two_part(lower, factor * vals) * p
                       + ent_ref[b : b + 1, n] * o + vals * e)
                den = (two_part(lower, factor) * p
                       + ent_ref[batches + b : batches + b + 1, n] * o + e)
                rden = 1.0 / den
                wkv = num * rden
                wkv_ref[t, n] = wkv
                rden_ref[t, n] = rden
                gated_ref[t, n] = (jax.nn.sigmoid(kvr_ref[2][t, n]) * wkv).astype(bf16)
        put(0)
        put(1)
        put(2)
        wait(copies)
        stream_ref = get(3)
        @columns(width, STEP)
        def _(n):
            mid_ref[:, n] = stream_ref[:, n].astype(f32) + dot_nn(gated_ref[...], w[:, n])
        put(3)
        @pl.loop(0, tokens // ROWS)
        def _(i):
            r = row_chunk(0, i, 0)
            nb, _ = norm(mid_ref[r, :])
            xb_ref[r, :] = nb * vec_ref[G2 : G2 + 1] + vec_ref[B2 : B2 + 1]
        for b in range(batches):
            last = (b + 1) * length - 1
            edge_ref[b : b + 1, :] = xb_ref[last : last + 1, :]

    one = ((tokens, width), f32)
    return call(
        body, info, [*everyone, *state, vec], [(a, None) for a in (*kvr, stream)], flat_pieces(pieces),
        [((3 * batches, width), f32), ((batches, 1, width), f32), ((batches, 1, width), f32),
         ((batches, width), f32)],
        [((tokens, width), bf16), one, one, one, one],
        [pltpu.VMEM((width, width), bf16)], len(steps), 7, 40)


def key_blocks(loads, steps, raw, w, info, shard, fshard, wanted):
    order = relative_order()
    place = natural(info[0], shard)
    out = {}
    for m in wanted:
        cols = pl.ds(natural(info[0], fshard)(m), fshard)
        out[m] = [
            loads.start(raw[piece].at[pl.ds(row, count), cols],
                        w.at[pl.ds(place(m2) + within, count), pl.ds(order.index(m) * fshard, fshard)])
            for piece, row, count, m2, within in steps
        ]
    return out


def value_blocks(loads, raw, w, fshard, stretches):
    order = relative_order()
    others = [m for m in order if m % 2 == 0 and m]
    each = fshard // stretches
    out = {}
    for at, m in enumerate(order):
        own, gathered = raw[2 * (m % 2)], raw[2 * (m % 2) + 1]
        base = m - m % 2
        if base == 0:
            out[m] = [loads.start(own, w.at[pl.ds(at * fshard, fshard)])]
            continue
        out[m] = [
            loads.start(
                gathered.at[pl.ds((z * len(others) + others.index(base)) * each, each)],
                w.at[pl.ds(at * fshard + z * each, each)])
            for z in range(stretches)
        ]
    return out


def value_copies(stretches):
    count = lax.axis_size("seg")
    return 2 + (count - 2) * stretches


def chan_in(info, xb, edge, previous, vec, pieces_ck, length, shard, fshard):
    tokens, width = xb.shape
    batches = tokens // length
    order = relative_order()
    wide = fshard * len(order)
    steps_k = plan(pieces_ck, 0, shard)
    steps_c = plan(pieces_ck, shard, shard * width // wide)

    def body(info, small, get, raw, outs, big, put, scratch, loads):
        edge_ref, prev_ref, vec_ref = small
        (entry_ref,) = outs
        in_ref, near_ref, far_ref, act_ref, frec_ref = big
        wk, wc = scratch
        half = len(order) // 2
        turn = order[half:] + order[:half]
        blocks = key_blocks(loads, steps_k, raw, wk, info, shard, fshard, turn)
        copies_c = recept_blocks(loads, steps_c, raw, wc, info, shard, width, wide)
        for b in range(batches):
            entry_ref[b : b + 1, :] = jnp.where(info[1] == 1, prev_ref[b], edge_ref[b : b + 1, :])
        xb_ref = get(0)
        for b in range(batches):
            def step(i, before):
                r = row_chunk(b, i, length)
                x = xb_ref[r, :]
                xt = down_one(x, before)
                for k, row in enumerate((CMK, CMR)):
                    mix = vec_ref[row : row + 1]
                    in_ref[k, r, :] = (x * mix + xt * (1.0 - mix)).astype(bf16)
                return x[ROWS - 1 :]
            lax.fori_loop(0, length // ROWS, step, entry_ref[b : b + 1])
        put(0)
        for m in turn:
            wait(blocks[m])
            at = order.index(m)
            hid_ref, lo = (near_ref, at * fshard) if at < half else (far_ref, (at - half) * fshard)
            act = jnp.maximum(dot_nn(in_ref[0], wk[:, at * fshard : (at + 1) * fshard]), 0.0)
            act_ref[:, at * fshard : (at + 1) * fshard] = act.astype(bf16)
            hid_ref[:, lo : lo + fshard] = (act * act).astype(bf16)
            if m == turn[half - 1]:
                put(2)
        put(1)
        put(3)
        wait(copies_c)
        @columns(width, STEP)
        def _(n):
            frec_ref[:, n] = dot_nn(in_ref[1], wc[:, n])

    return call(
        body, info, [edge, previous, vec], [(xb, None)], flat_pieces(pieces_ck),
        [((batches, width), f32)],
        [((2, tokens, width), bf16), ((tokens, wide // 2), bf16), ((tokens, wide // 2), bf16),
         ((tokens, wide), bf16), ((tokens, width), f32)],
        [pltpu.VMEM((width, wide), bf16), pltpu.VMEM((width, width), bf16)],
        len(steps_c) * (wide // width) + len(steps_k) * len(order), 11, 40)


def chan_out(info, near, far, frec, mid, cot, cv, fshard):
    tokens, width = mid.shape
    order = relative_order()
    wide = fshard * len(order)
    stretches = lax.axis_size("stretch")

    def body(info, small, get, raw, outs, big, put, scratch, loads):
        out_ref, df_ref, dr_ref = big
        w, fval = scratch
        blocks = value_blocks(loads, raw, w, fshard, stretches)
        half = len(order) // 2
        for k in range(2):
            hid_ref = get(k)
            for m in order[k * half : (k + 1) * half]:
                wait(blocks[m])
            @columns(width, STEP)
            def _(n):
                part = dot_nn(hid_ref[...], w[k * wide // 2 : (k + 1) * wide // 2, n])
                fval[:, n] = part if k == 0 else fval[:, n] + part
        frec_ref, mid_ref, cot_ref = get(2), get(3), get(4)
        @pl.loop(0, tokens // ROWS)
        def _(i):
            r = row_chunk(0, i, 0)
            sig = jax.nn.sigmoid(frec_ref[r, :])
            cots, value = cot_ref[r, :].astype(f32), fval[r, :]
            df_ref[r, :] = (cots * sig).astype(bf16)
            out_ref[r, :] = (mid_ref[r, :] + sig * value).astype(bf16)
            dr_ref[r, :] = (cots * value * sig * (1.0 - sig)).astype(bf16)

    low = ((tokens, width), bf16)
    return call(
        body, info, [], [(a, None) for a in (near, far, frec, mid, cot)], cv, [], [low, low, low],
        [pltpu.VMEM((wide, width), bf16), pltpu.VMEM((tokens, width), f32)],
        value_copies(stretches), 7, 40)


def hidden_back(info, act, dfval, cv, fshard):
    tokens, width = dfval.shape
    order = relative_order()
    wide = fshard * len(order)
    stretches = lax.axis_size("stretch")

    def body(info, small, get, raw, outs, big, put, scratch, loads):
        (dpre_ref,) = big
        (wv,) = scratch
        values = value_blocks(loads, raw, wv, fshard, stretches)
        dfval_ref, act_ref = get(0), get(1)
        for at, m in enumerate(order):
            wait(values[m])
            block = slice(at * fshard, (at + 1) * fshard)
            d = dot_nt(dfval_ref[...], wv[block, :]) * (2.0 * act_ref[:, block].astype(f32))
            dpre_ref[:, block] = d.astype(bf16)

    return call(
        body, info, [], [(dfval, None), (act, None)], cv, [], [((tokens, wide), bf16)],
        [pltpu.VMEM((wide, width), bf16)], value_copies(stretches), 7, 40)[0]


def chan_back(info, dpre, dfrec, xb, entry, vec, pieces_ck, length, shard, fshard):
    tokens, width = xb.shape
    batches = tokens // length
    order = relative_order()
    wide = fshard * len(order)
    steps_k = plan(pieces_ck, 0, shard)
    steps_c = plan(pieces_ck, shard, shard * width // wide)

    def body(info, small, get, raw, outs, big, put, scratch, loads):
        entry_ref, vec_ref = small
        head_ref, total_ref = outs
        dxt_ref, dxb_ref = big
        wk, wc, df, dr, sum_ref = scratch
        copies_c = recept_blocks(loads, steps_c, raw, wc, info, shard, width, wide)
        keys = key_blocks(loads, steps_k, raw, wk, info, shard, fshard, order)
        dfrec_ref = get(0)
        wait(copies_c)
        @columns(width, STEP)
        def _(n):
            dr[:, n] = dot_nt(dfrec_ref[...], wc[n, :])
        dpre_ref = get(1)
        half = len(order) // 2
        for k in range(2):
            for m in order[k * half : (k + 1) * half]:
                wait(keys[m])
            part_of = slice(k * wide // 2, (k + 1) * wide // 2)
            @columns(width, STEP)
            def _(n):
                part = dot_nt(dpre_ref[:, part_of], wk[n, part_of])
                df[:, n] = part if k == 0 else df[:, n] + part
        sum_ref[...] = jnp.zeros_like(sum_ref)
        xb_ref = get(2)
        for b in range(batches):
            def step(i, before):
                r = row_chunk(b, i, length)
                x = xb_ref[r, :]
                gap = x - down_one(x, before)
                a, c = df[r, :], dr[r, :]
                ck, cr = vec_ref[CMK : CMK + 1], vec_ref[CMR : CMR + 1]
                dxt_ref[r, :] = a * (1.0 - ck) + c * (1.0 - cr)
                dxb_ref[r, :] = a * ck + c * cr
                sum_ref[0] += fold(a * gap)
                sum_ref[1] += fold(c * gap)
                return x[ROWS - 1 :]
            lax.fori_loop(0, length // ROWS, step, entry_ref[b : b + 1])
            head_ref[b : b + 1, :] = dxt_ref[b * length : b * length + 1, :]
        column_sums(total_ref, sum_ref)

    one = ((tokens, width), f32)
    return call(
        body, info, [entry, vec], [(a, None) for a in (dfrec, dpre, xb)], flat_pieces(pieces_ck),
        [((batches, width), f32), ((2, width), f32)], [one, one],
        [pltpu.VMEM((width, wide), bf16), pltpu.VMEM((width, width), bf16),
         pltpu.VMEM((tokens, width), f32), pltpu.VMEM((tokens, width), f32),
         pltpu.VMEM((2, 8, width), f32)],
        len(steps_c) * (wide // width) + len(steps_k) * len(order), 10, 40)


def mid_back(info, dxt, dxb, after, mid, cot, vec, kvr, wkv, rden, ent, pieces, spots, length, shard):
    tokens, width = mid.shape
    batches = tokens // length
    steps = plan(pieces, spots["o"], shard)

    def body(info, small, get, raw, outs, big, put, scratch, loads):
        after_ref, vec_ref, ent_ref = small
        dent_ref, total_ref = outs
        dmid_ref, low_ref, high_ref, rlow_ref, rhigh_ref, gn_ref = big
        w, sum_ref = scratch
        copies = loads.pieces(steps, raw, w, natural(info[0], shard))
        sum_ref[...] = jnp.zeros_like(sum_ref)
        dxt_ref, dxb_ref, mid_ref, cot_ref = get(0), get(1), get(2), get(3)
        for b in range(batches):
            def step(k, after_row):
                r = row_chunk(b, length // ROWS - 1 - k, length)
                nb, inverse = norm(mid_ref[r, :])
                dx = dxt_ref[r, :]
                d = dxb_ref[r, :] + up_one(dx, after_row)
                back = cot_ref[r, :].astype(f32) + norm_back(d, nb, inverse, vec_ref[G2 : G2 + 1])
                dmid_ref[r, :] = back
                low_ref[r, :] = back[:, : width // 2].astype(bf16)
                high_ref[r, :] = back[:, width // 2 :].astype(bf16)
                sum_ref[0] += fold(d * nb)
                sum_ref[1] += fold(d)
                return dx[:1]
            lax.fori_loop(0, length // ROWS, step, after_ref[b : b + 1])
        put(0)
        put(1)
        put(2)
        column_sums(total_ref, sum_ref)
        wait(copies)
        @columns(width, STEP)
        def _(n):
            gn_ref[:, n] = (dot_nt(low_ref[...], w[n, : width // 2])
                            + dot_nt(high_ref[...], w[n, width // 2 :]))
        kvr_ref = [get(4), None, get(5)]
        wkv_ref, rden_ref = get(6), get(7)
        lanes = min(LANES, width // 2)
        for b, half, q in [(b, h, q) for b in range(batches) for h in range(2)
                           for q in range(width // 2 // lanes)]:
            t = slice(b * length, (b + 1) * length)
            n = slice(half * width // 2 + q * lanes, half * width // 2 + (q + 1) * lanes)
            part, at_half = (rlow_ref, rhigh_ref)[half], slice(q * lanes, (q + 1) * lanes)
            if True:
                _, _, _, o, _ = wkv_terms(kvr_ref, ent_ref, vec_ref, b, t, n, batches, length)
                sig = jax.nn.sigmoid(kvr_ref[2][t, n])
                d = gn_ref[t, n] * sig
                wkvs = wkv_ref[t, n]
                part[t, at_half] = (d * wkvs * (1.0 - sig)).astype(bf16)
                gn = d * rden_ref[t, n]
                gn_ref[t, n] = gn
                go = gn * o
                dent_ref[b : b + 1, n] = jnp.sum(go, axis=0, keepdims=True)
                dent_ref[batches + b : batches + b + 1, n] = -jnp.sum(go * wkvs, axis=0, keepdims=True)

    one, half = ((tokens, width), f32), ((tokens, width // 2), bf16)
    return call(
        body, info, [after, vec, ent], [(a, None) for a in (dxt, dxb, mid, cot, kvr[0], kvr[2], wkv, rden)],
        flat_pieces(pieces), [((2 * batches, width), f32), ((2, width), f32)], [one, half, half, half, half, one],
        [pltpu.VMEM((width, width), bf16), pltpu.VMEM((2, 8, width), f32)], len(steps), 9, 40)


def time_back(info, gn, wkv, kvr, ent, back, sums, state, drec, stream, entry, vec, pieces, spots,
              length, shard):
    tokens, width = stream.shape
    batches = tokens // length
    stretches = len(back)
    relative = isinstance(back, list)
    if not relative:
        back = [back]
    plans = [plan(pieces, spots[k], shard) for k in "kvr"]

    def body(info, small, get, raw, outs, big, put, scratch, loads):
        back_ref = small[:-7]
        if not relative:
            back_ref = [back_ref[0].at[z] for z in range(stretches)]
        ent_ref, sums_ref, num_ref, den_ref, exp_ref, entry_ref, vec_ref = small[-7:]
        gnum_ref, gden_ref, gexp_ref, gffn_ref, head_ref, total_ref, extra_ref = outs
        d_ref, dxs_ref, dxa_ref = big
        w, dins, sum_ref, later_ref, loc_ref = scratch
        place = natural(info[0], shard)
        copies = [loads.pieces(plans[k], raw, w.at[k], place) for k in range(3)]
        span = -jnp.exp(vec_ref[DECAY : DECAY + 1, :]) * float(length)
        pos = info[2].astype(f32)
        nums, dens, exps = (slice(k * batches, (k + 1) * batches) for k in range(3))
        zero = jnp.zeros((batches, width), f32)

        def state(ref):
            return jnp.concatenate([ref[b] for b in range(batches)], axis=0)

        later_n = later_d = carry_n = carry_d = grad_n = grad_d = grad_f = zero
        for j in range(stretches):
            there = back_ref[j][exps, :]
            at_z = jnp.bitwise_xor(info[2], j) if relative else jnp.int32(j)
            z = at_z.astype(f32)
            after = at_z > info[2]
            lift = jnp.where(after, jnp.exp(jnp.minimum(
                sums_ref[exps, :] - there + (z - 1.0 - pos) * span, 0.0)), 0.0)
            carry = jnp.where(after, jnp.exp(jnp.minimum(
                ent_ref[exps, :] - there + (z - pos) * span, 0.0)), 0.0)
            raised = jnp.exp(jnp.minimum(state(exp_ref) - there + z * span, 0.0))
            dn, dd = back_ref[j][nums, :], back_ref[j][dens, :]
            grad_f = grad_f + jnp.where(at_z == 0, back_ref[j][3 * batches :, :], 0.0)
            later_n, later_d = later_n + dn * lift, later_d + dd * lift
            carry_n, carry_d = carry_n + dn * carry, carry_d + dd * carry
            grad_n, grad_d = grad_n + dn * raised, grad_d + dd * raised
        later_ref[nums, :], later_ref[dens, :] = later_n, later_d
        grad_e = state(num_ref) * grad_n + state(den_ref) * grad_d
        for b in range(batches):
            gnum_ref[b], gden_ref[b] = grad_n[b : b + 1], grad_d[b : b + 1]
            gexp_ref[b] = grad_e[b : b + 1]
            gffn_ref[b] = grad_f[b : b + 1]
        rate_part = (
            float(length) * (ent_ref[nums, :] * carry_n + ent_ref[dens, :] * carry_d)
            + (length - 1.0) * (later_n * sums_ref[nums, :] + later_d * sums_ref[dens, :]))

        upper = triangle(length, False)
        gn_ref, wkv_ref = get(0), get(1)
        kvr_ref = [get(2), get(3)]
        for b in range(batches):
            t = slice(b * length, (b + 1) * length)
            @columns(width, LANES)
            def _(n):
                at, factor, p, o, e = wkv_terms(kvr_ref, ent_ref, vec_ref, b, t, n, batches, length)
                vals, g = kvr_ref[1][t, n], gn_ref[t, n]
                gd = -g * wkv_ref[t, n]
                direct = e * (g * vals + gd)
                opened = o * (g * ent_ref[b : b + 1, n] + gd * ent_ref[batches + b : batches + b + 1, n])
                rn = two_part(upper, g * p) + later_ref[b : b + 1, n]
                rd = two_part(upper, gd * p) + later_ref[batches + b : batches + b + 1, n]
                chain = factor * (rn * vals + rd)
                d_ref[0, t, n] = (chain + direct).astype(bf16)
                d_ref[1, t, n] = (factor * rn + g * e).astype(bf16)
                loc_ref[b : b + 1, n] = jnp.sum(
                    opened - (at - 1.0) * direct - at * chain, axis=0, keepdims=True)
                loc_ref[batches + b : batches + b + 1, n] = jnp.sum(direct, axis=0, keepdims=True)
        put(0)
        rate_rows = rate_part + loc_ref[:batches, :]
        extra_ref[0:1, :] = jnp.sum(rate_rows, axis=0, keepdims=True) * -jnp.exp(
            vec_ref[DECAY : DECAY + 1, :])
        extra_ref[1:2, :] = jnp.sum(loc_ref[batches:, :], axis=0, keepdims=True)
        for k in range(2):
            wait(copies[k])
            @columns(width, STEP)
            def _(n):
                dins[k, :, n] = dot_nt(d_ref[k], w[k, n, :])
        low_ref, high_ref = get(5), get(6)
        wait(copies[2])
        @columns(width, STEP)
        def _(n):
            dins[2, :, n] = (dot_nt(low_ref[...], w[2, n, : width // 2])
                             + dot_nt(high_ref[...], w[2, n, width // 2 :]))
        sum_ref[...] = jnp.zeros_like(sum_ref)
        stream_ref = get(4)
        for b in range(batches):
            def step(i, before):
                r = row_chunk(b, i, length)
                na, _ = norm(stream_ref[r, :].astype(f32))
                xa = na * vec_ref[G1 : G1 + 1] + vec_ref[B1 : B1 + 1]
                gap = xa - down_one(xa, before)
                dxs = jnp.zeros((ROWS, width), f32)
                dxa = jnp.zeros((ROWS, width), f32)
                for k, row in enumerate((MK, MV, MR)):
                    d, mix = dins[k, r, :], vec_ref[row : row + 1]
                    dxs = dxs + d * (1.0 - mix)
                    dxa = dxa + d * mix
                    sum_ref[k] += fold(d * gap)
                dxs_ref[r, :] = dxs
                dxa_ref[r, :] = dxa
                return xa[ROWS - 1 :]
            lax.fori_loop(0, length // ROWS, step, entry_ref[b : b + 1])
            head_ref[b : b + 1, :] = dxs_ref[b * length : b * length + 1, :]
        column_sums(total_ref, sum_ref)

    one = ((tokens, width), f32)
    return call(
        body, info, [*back, ent, sums, *state, entry, vec],
        [(a, None) for a in (gn, wkv, kvr[0], kvr[1], stream, *drec)], flat_pieces(pieces),
        [((batches, 1, width), f32)] * 4
        + [((batches, width), f32), ((3, width), f32), ((2, width), f32)],
        [((2, tokens, width), bf16), one, one],
        [pltpu.VMEM((3, width, width), bf16), pltpu.VMEM((3, tokens, width), f32),
         pltpu.VMEM((3, 8, width), f32), pltpu.VMEM((2 * batches, width), f32),
         pltpu.VMEM((2 * batches, width), f32)],
        sum(map(len, plans)), 14, 40)


def in_back(info, dxs, dxa, after, dmid, stream, vec, length):
    tokens, width = stream.shape
    batches = tokens // length

    def body(info, small, get, raw, outs, big, put, scratch, loads):
        after_ref, vec_ref = small
        (out_ref,) = big
        (sum_ref,) = scratch
        dxs_ref, dxa_ref, dmid_ref, stream_ref = (get(k) for k in range(4))
        sum_ref[...] = jnp.zeros_like(sum_ref)
        for b in range(batches):
            def step(k, after_row):
                r = row_chunk(b, length // ROWS - 1 - k, length)
                na, inverse = norm(stream_ref[r, :].astype(f32))
                dx = dxs_ref[r, :]
                d = dxa_ref[r, :] + up_one(dx, after_row)
                back = norm_back(d, na, inverse, vec_ref[G1 : G1 + 1])
                out_ref[r, :] = (dmid_ref[r, :] + back).astype(bf16)
                sum_ref[0] += fold(d * na)
                sum_ref[1] += fold(d)
                return dx[:1]
            lax.fori_loop(0, length // ROWS, step, after_ref[b : b + 1])
        column_sums(outs[0], sum_ref)

    return call(
        body, info, [after, vec], [(a, None) for a in (dxs, dxa, dmid, stream)], [],
        [((2, width), f32)], [((tokens, width), bf16)],
        [pltpu.VMEM((2, 8, width), f32)], 0, 6, 40)


def weight_grad(info, arrays, items, layout, us, relative=False, stacked=False, under=()):
    count = lax.axis_size("seg")
    evens = list(range(0, count, 2))
    first = items[0][2]
    lead = first[0] if isinstance(first, list) else first
    tokens, n_wide = arrays[lead[0]].shape[-2:]
    n_wide *= len(first) if isinstance(first, list) else 1
    w = arrays[items[0][0][0]].shape[-1] // {"natural": count, "blocks": len(evens), "joined": len(evens)}[layout]
    pair = 2 if w < 256 else 1
    groups = [evens[1:][k : k + pair] for k in range(0, len(evens) - 1, pair)]
    groups[-1].append(0) if len(groups[-1]) < pair else groups.append([0])
    groups = [g for g in groups if g]
    stretches = lax.axis_size("stretch")
    each_z = w // stretches
    shapes = [(len(evens) * w, n_wide)] if stacked else [(len(items) * w, n_wide)] * len(evens)
    shares = [x.shape[0] // len(evens) for x in under]
    if under:
        shapes = [(len(items) * w + sum(shares), n_wide)] * len(evens)

    def body(info, small, get, raw, outs, big, put, scratch, loads):
        x_all, dy_all = scratch
        copies_under, at = [], len(items) * w
        for n, share in enumerate(shares):
            for k in range(len(evens)):
                copies_under.append(loads.start(
                    raw[len(arrays) + n].at[pl.ds(k * share, share)], big[k].at[pl.ds(at, share)]))
            at += share

        def view(spec):
            which, lead = spec
            return raw[which] if lead is None else raw[which].at[lead]

        def columns_of(ref, m):
            if layout == "natural":
                return ref.at[:, pl.ds(natural(info[0], w)(m), w)]
            return ref.at[:, pl.ds(evens.index(m) * w, w)]

        copies = []
        for k, (x, x_sib, dy, dy_sib) in enumerate(items):
            now = []
            for at, part in ((0, dy), (tokens, dy_sib)):
                if relative:
                    each = n_wide // count
                    for n, m in enumerate(relative_order()):
                        cols = natural(info[0], each)(m if at == 0 else m ^ 1)
                        now.append(loads.start(
                            view(part).at[:, pl.ds(n * each, each)],
                            dy_all.at[k, pl.ds(at, tokens), pl.ds(cols, each)]))
                    continue
                pieces = part if isinstance(part, list) else [part]
                each = n_wide // len(pieces)
                for n, piece in enumerate(pieces):
                    now.append(loads.start(
                        view(piece), dy_all.at[k, pl.ds(at, tokens), pl.ds(n * each, each)]))
            for at, part in ((0, x), (tokens, x_sib)):
                ref, rows = view(part), pl.ds(at, tokens)
                if layout == "joined":
                    for g, ms in enumerate(groups):
                        cols = pl.ds(g * pair * w, len(ms) * w)
                        now.append(loads.start(
                            ref.at[:, cols], x_all.at[k, g, rows, pl.ds(0, len(ms) * w)]))
                    continue
                for g, ms in enumerate(groups):
                    for n, m in enumerate(ms):
                        now.append(loads.start(
                            columns_of(ref, m), x_all.at[k, g, rows, pl.ds(n * w, w)]))
            copies.append(now)
        step = min(512, n_wide)
        for k in range(len(items)):
            wait(copies[k])
        for g, ms in enumerate(groups):
            for k in range(len(items)):
                for q in range(n_wide // step):
                    dst = slice(q * step, (q + 1) * step)
                    block = dot_tn(x_all[k, g, :, : len(ms) * w], dy_all[k, :, dst]).astype(bf16)
                    for n, m in enumerate(ms):
                        if not stacked:
                            big[evens.index(m)][k * w : (k + 1) * w, dst] = block[n * w : (n + 1) * w]
                            continue
                        for z in range(stretches):
                            row = (z * len(evens) + evens.index(m)) * each_z
                            big[0][row : row + each_z, dst] = block[n * w + z * each_z : n * w + (z + 1) * each_z]
            if g == 0:
                wait(copies_under)
            for m in ms if not stacked else []:
                put(evens.index(m))

    return call(
        body, info, [], [], [*arrays, *under], [], [(shape, bf16) for shape in shapes],
        [pltpu.VMEM((len(items), len(groups), 2 * tokens, pair * w), bf16),
         pltpu.VMEM((len(items), 2 * tokens, n_wide), bf16)],
        len(items) * (4 + 2 * len(evens) + 2 * count) + len(under) * len(evens), us, 40)


def grad_send(parts):
    return [hop(part, 2 * k) for k, part in enumerate(parts) if k]


def total(terms):
    out = terms[0].astype(f32)
    for t in terms[1:]:
        out = out + t.astype(f32)
    return out


def grad_finish(info, sets):
    stretches = lax.axis_size("stretch")
    n_wide = sets[0][0].shape[1]
    rows = sum(own.shape[0] for own, _, _ in sets)
    each = sets[0][0].shape[0] // sets[0][2] // stretches
    if each % 16:
        parts = [total([own, *got]).astype(bf16).reshape(items, stretches, each, n_wide)
                 for own, got, items in sets]
        return jnp.swapaxes(jnp.concatenate(parts, axis=0), 0, 1).reshape(rows, n_wide)
    flat = [(a, None) for own, got, _ in sets for a in (own, *got)]

    def body(info, small, get, raw, outs, big, put, scratch, loads):
        at, done = 0, 0
        for own, got, items in sets:
            refs = [get(at + k) for k in range(1 + len(got))]
            at += len(refs)
            for z in range(stretches):
                for k in range(items):
                    src = slice((k * stretches + z) * each, (k * stretches + z + 1) * each)
                    first = z * (rows // stretches) + (done + k) * each
                    big[0][first : first + each, :] = total([r[src, :] for r in refs]).astype(bf16)
            done += items

    return call(body, info, [], flat, [], [], [((rows, n_wide), bf16)], [], 0, 3, 24)[0]


def grad_pieces(info, own, got, items, each, under):
    stretches = lax.axis_size("stretch")
    rows, n_wide = own.shape
    width = each * stretches

    def body(info, small, get, raw, outs, big, put, scratch, loads):
        refs = [get(k) for k in range(1 + len(got))]
        first = items * width + under
        table = total([r[first : first + 16, :] for r in refs])
        half = n_wide // 2
        table = table[:, :half] + table[:, half:]
        hi = table.astype(bf16)
        lo = (table - hi.astype(f32)).astype(bf16)
        for j in list(range(1, stretches)) + [0]:
            z = jnp.bitwise_xor(info[2], j)
            for k in range(items):
                src = pl.ds(pl.multiple_of(k * width + z * each, each), each)
                big[j][k * each : (k + 1) * each, :] = total([r[src, :] for r in refs]).astype(bf16)
            big[j][items * each :, :half] = hi
            big[j][items * each :, half:] = lo
            put(j)
        middle = slice(items * width, first)
        big[stretches][...] = total([r[middle, :] for r in refs])

    return call(
        body, info, [], [(a, None) for a in (own, *got)], [], [],
        [((items * each + 16, n_wide), bf16)] * stretches + [((under, n_wide), f32)], [], 0, 3, 24)


def stretch_part(part):
    return lax.psum_scatter(part, "stretch", scatter_dimension=0, tiled=True)


def stretch_items(out, items):
    own = out.shape[0] // items
    return [out[k * own : (k + 1) * own].astype(f32) for k in range(items)]


def vector_rows(table, width):
    me, count = lax.axis_index("seg"), lax.axis_size("seg")
    own = table.shape[1] // count
    table = jnp.pad(table, ((0, 16 - table.shape[0]), (0, 0)))
    rows = []
    for m in range(0, count, 2):
        pair = lax.dynamic_slice_in_dim(table, (me ^ m) // 2 * (2 * own), 2 * own, 1)
        pair = jnp.pad(pair, ((0, 0), (0, width // 2 - 2 * own)))
        hi = pair.astype(bf16)
        rows.append(jnp.concatenate([hi, (pair - hi.astype(f32)).astype(bf16)], axis=1))
    return jnp.concatenate(rows, axis=0)


def vector_read(rows):
    half = rows.shape[1] // 2
    return rows[:, :half].astype(f32) + rows[:, half:].astype(f32)


def vector_own(pair, own):
    second = (lax.axis_index("seg") & 1) != 0
    lo, hi = pair[:, :own], pair[:, own : 2 * own]
    return jnp.where(second, hi, lo) + hop(jnp.where(second, lo, hi), 1)


def vector_finish(table):
    position, count = lax.axis_index("stretch"), lax.axis_size("stretch")
    bit = count // 2
    while bit:
        lo, hi = jnp.split(table, 2, axis=1)
        upper = (position & bit) != 0
        table = jnp.where(upper, hi, lo) + across(jnp.where(upper, lo, hi), bit)
        bit //= 2
    return table


def own_columns(x, me, w):
    ms = [*range(2, lax.axis_size("seg"), 2), 0]
    return jnp.concatenate([lax.dynamic_slice_in_dim(x, (me ^ m) * w, w, 1) for m in ms], axis=1)


def body(
    stream_in, cotangent, previous_mix, previous_ffn, state_num, state_den, state_exp,
    gain_one, bias_one, gain_two, bias_two, mix_key, mix_value, mix_recept,
    time_decay, time_first, chan_mix_key, chan_mix_recept,
    att_key, att_value, att_recept, att_output, chan_key, chan_value, chan_recept,
):
    mine = lax.axis_index("seg")
    position = lax.axis_index("stretch")
    stretches = lax.axis_size("stretch")
    batches, _, length, width = stream_in.shape
    tokens = batches * length
    shard = att_key.shape[0]
    fshard = chan_value.shape[0]
    wide = chan_key.shape[1]
    aligned = shard % 128 == 0
    count = lax.axis_size("seg")
    info = jnp.stack([mine, (position == 0).astype(jnp.int32), position])

    stream = stream_in.reshape(tokens, width)
    cot = cotangent.reshape(tokens, width)
    state = (state_num, state_den, state_exp)
    vectors = [gain_one, bias_one, gain_two, bias_two, mix_key, mix_value, mix_recept,
               time_decay, time_first, chan_mix_key, chan_mix_recept]

    v = Live()
    evens = list(range(0, count, 2))
    spots = {"k": 0, "v": shard, "vec": 2 * shard, "r": 2 * shard + 16, "o": 3 * shard + 16}
    each = fshard // stretches
    v.own_tm = pack(
        [(att_key, 0, shard), (att_value, 0, shard), (None, 0, 16)],
        [(att_recept, 0, shard), (att_output, 0, shard)], vectors, width)
    v.share = lax.dynamic_slice_in_dim(chan_value, position * each, each, 0)
    v.cv = chan_value
    v.last_in = stream_in[:, 0, length - 1]
    v.sync()
    v.shares = lax.all_gather(v.share, "seg", axis=0, tiled=True)
    v.one_tm = first_stage(v.own_tm)
    v.ck = pack_wide(tie(chan_key, *v.own_tm), chan_recept)
    v.tm0 = sibling({0: v.own_tm})
    v.last_in = along(tie(v.last_in, *v.tm0[1]), 1)
    v.sync()
    v.tm6 = second_stage(v.one_tm, v.one_tm)
    v.tm2 = sibling(v.one_tm)
    v.ck0 = sibling({0: v.ck})
    gathered_cv = lax.all_gather(
        jnp.concatenate([lax.dynamic_slice_in_dim(v.shares, (mine ^ m) * each, each, 0) for m in evens[1:]], axis=0),
        "stretch", axis=0, tiled=True)
    v.sync()
    v.tm6_sib = sibling(v.tm6)
    v.sync()

    v.one_ck = first_stage(v.ck)
    tm = {0: v.own_tm, **v.one_tm, **v.tm6, **v.tm0, **v.tm2, **v.tm6_sib}
    given = None
    if not aligned:
        given = lax.all_gather(jnp.stack(vectors), "seg", axis=1, tiled=True).astype(f32)
        given = jnp.pad(given, ((0, 5), (0, 0)))
    v.sums, v.vec, v.entry, v.kvr_in, *v.kvr = time_in(
        info, stream, v.last_in, previous_mix, given, tm, spots, length, shard)
    v.everyone = lax.all_gather(v.sums, "stretch")
    v.tm = tm
    v.drop("own_tm", "one_tm", "tm6", "tm0", "tm2", "tm6_sib", "share", "shares")
    v.sync()

    v.ck6 = second_stage(v.one_ck, v.one_ck)
    v.ent, v.mean, v.log, v.edge_b, v.gated, v.wkv, v.rden, v.mid, v.xb = time_out(
        info, v.kvr, v.everyone, state, v.vec, stream, v.tm, spots, length, shard)
    first_far = far_bits()[0]
    v.ck2 = sibling({first_far: v.one_ck[first_far]})
    v.edge_b = along(v.edge_b, 1)
    v.drop("everyone")
    v.sync()
    v.ck2 = {**v.ck2, **sibling({m: p for m, p in v.one_ck.items() if m != first_far})}
    v.all_ck = {0: v.ck, **v.one_ck, **v.ck6, **v.ck0, **v.ck2, **sibling(v.ck6)}
    v.gathered_cv = gathered_cv
    v.drop("ck", "one_ck", "ck6", "ck0", "ck2")
    v.sync()

    v.entry_b, v.f_in, v.near, v.far, v.act, v.frec = chan_in(
        info, v.xb, v.edge_b, previous_ffn, v.vec, v.all_ck, length, shard, fshard)
    v.all_cv = [v.cv, v.gathered_cv, hop(v.cv, 1), hop(v.gathered_cv, 1)]
    v.drop("cv", "gathered_cv")
    v.sync()
    v.block_out, v.d_fval, v.d_frec = chan_out(
        info, v.near, v.far, v.frec, v.mid, cot, v.all_cv, fshard)
    v.far_sib = hop(v.far, 1)
    v.f_sib = hop(v.f_in, 1)
    v.g_sib = hop(v.gated, 1)
    v.kvr_sib = hop(v.kvr_in, 1)
    v.drop("frec", "far")
    v.sync()

    def pairs(*arrays):
        if aligned:
            return [a for pair in arrays for a in pair]
        return [own_columns(a, mine, shard) for pair in arrays for a in pair]

    layout = "natural" if aligned else "joined"
    flat = tuple((j, None) for j in range(4))
    arrays = [v.near, v.far_sib, v.d_fval, hop(v.d_fval, 1)]
    v.stack_cv = weight_grad(info, arrays, [flat], "blocks", 6, stacked=True)[0]
    v.dfrec_sib = hop(v.d_frec, 1)
    v.drop("near", "far_sib")
    v.sync()

    z_cv = stretch_part(v.stack_cv)
    v.dpre = hidden_back(info, v.act, v.d_fval, v.all_cv, fshard)
    dpre_sib = hop(v.dpre, 1)
    v.head_b, v.sums_c, v.dxt, v.dxb = chan_back(
        info, v.dpre, v.d_frec, v.xb, v.entry_b, v.vec, v.all_ck, length, shard, fshard)
    v.next_b = along(v.head_b, -1)
    dpre = tie(v.dpre, v.dxt)
    if aligned:
        v.parts_ck = weight_grad(
            info, [v.f_in, v.f_sib, dpre, dpre_sib], [((0, 0), (1, 0), (2, None), (3, None))], layout, 7, True)
    else:
        v.parts_ck = weight_grad(
            info, [*pairs((v.f_in[0], v.f_sib[0])), dpre, dpre_sib], [flat], layout, 7, True)
    v.drop("all_ck", "all_cv", "xb", "entry_b", "act", "d_fval", "dpre", "stack_cv")
    v.sync()

    v.got_ck = grad_send(v.parts_ck)
    dent, v.sums_m, v.dmid, *lows, gn = mid_back(
        info, v.dxt, v.dxb, v.next_b, v.mid, cot, v.vec, v.kvr, v.wkv, v.rden, v.ent, v.tm, spots,
        length, shard)
    v.dbr, v.drec = lows[:2], lows[2:]
    back = lax.all_gather(jnp.concatenate([dent, v.ent[2 * batches :], v.head_b], axis=0), "stretch")
    *v.grads, v.head_a, v.sums_t, v.extra, v.d_kv, v.dxs, v.dxa = time_back(
        info, gn, v.wkv, v.kvr, v.ent, back, v.sums, state, v.drec, stream, v.entry, v.vec,
        v.tm, spots, length, shard)
    v.dbr_sib = [hop(a, 1) for a in v.dbr]
    v.drec_sib = [hop(a, 1) for a in v.drec]
    dys = [([(at, None), (at + 1, None)], [(at + 2, None), (at + 3, None)]) for at in (0, 4)]
    lows = [*v.dbr, *v.dbr_sib, *v.drec, *v.drec_sib, v.d_frec, v.dfrec_sib]
    last = ((8, None), (9, None))
    if aligned:
        v.parts_ocr = weight_grad(
            info, [*lows, tie(v.gated, v.d_kv), v.g_sib, v.f_in, v.f_sib, v.kvr_in, v.kvr_sib],
            [((10, None), (11, None), *dys[0]), ((12, 1), (13, 1), *last), ((14, 2), (15, 2), *dys[1])],
            layout, 6)
    else:
        xs = pairs((tie(v.gated, v.d_kv), v.g_sib), (v.f_in[1], v.f_sib[1]), (v.kvr_in[2], v.kvr_sib[2]))
        v.parts_ocr = weight_grad(
            info, [*lows, *xs],
            [((10, None), (11, None), *dys[0]), ((12, None), (13, None), *last),
             ((14, None), (15, None), *dys[1])], layout, 6)
    v.drop("wkv", "kvr", "ent", "sums", "entry", "tm", "dxt", "dxb", "mid", "rden", "next_b", "head_b")
    v.sync()
    v.dkv_sib = hop(v.d_kv, 1)
    v.next_a = along(v.head_a, -1)
    v.part_ck = grad_finish(info, [(v.parts_ck[0], v.got_ck, 1)])
    v.drop("gated", "g_sib", "dbr", "dbr_sib", "drec", "drec_sib", "f_in", "f_sib", "d_frec", "dfrec_sib",
           "parts_ck", "got_ck")
    v.z_cv = z_cv
    v.sync()

    v.got_ocr = grad_send(v.parts_ocr)
    z_ck = stretch_part(v.part_ck)
    sums_i, v.grad_stream = in_back(info, v.dxs, v.dxa, v.next_a, v.dmid, stream, v.vec, length)
    table = jnp.concatenate([sums_i, v.sums_m, v.sums_t, v.extra, v.sums_c], axis=0)
    under = [v.z_cv, vector_rows(table, width)]
    if aligned:
        v.parts_kv = weight_grad(
            info, [v.kvr_in, v.kvr_sib, v.d_kv, v.dkv_sib],
            [tuple((j, k) for j in range(4)) for k in range(2)], layout, 7, under=under)
    else:
        xs = pairs(*[(v.kvr_in[k], v.kvr_sib[k]) for k in range(2)])
        v.parts_kv = weight_grad(
            info, [*xs, v.d_kv, v.dkv_sib],
            [((2 * k, None), (2 * k + 1, None), (4, k), (5, k)) for k in range(2)], layout, 7, under=under)
    v.heads = lax.all_gather(v.head_a, "stretch")[0]
    v.drop("kvr_in", "kvr_sib", "d_kv", "dkv_sib", "dxs", "dxa", "dmid", "next_a", "part_ck",
           "sums_m", "sums_t", "extra", "sums_c", "z_cv")
    v.sync()

    v.got_kv = grad_send(v.parts_kv)
    z_ocr = stretch_part(grad_finish(info, [(v.parts_ocr[0], v.got_ocr, 3)]))
    v.z_ck = z_ck
    v.drop("parts_ocr", "got_ocr")
    v.sync()
    rows = shard // stretches
    by_hops = stretches == 4 and rows % 16 == 0
    if by_hops:
        *v.pieces, v.out_cv = grad_pieces(info, v.parts_kv[0], v.got_kv, 2, rows, each)
    else:
        whole = total([v.parts_kv[0], *v.got_kv])
        first = 2 * shard
        v.out_cv, v.table = whole[first : first + each], vector_read(whole[first + each :])
        v.part_kv = grad_finish(info, [(v.parts_kv[0][:first], [g[:first] for g in v.got_kv], 2)])
    v.z_ocr = z_ocr
    v.drop("parts_kv", "got_kv")
    v.sync()
    if by_hops:
        pieces = [v.pieces[0], *[across(v.pieces[j], j) for j in range(1, stretches)]]
        z_kv = total([p[: 2 * rows] for p in pieces])
        small = sum(vector_read(p[2 * rows : 2 * rows + 11]) for p in pieces)
        small = lax.dynamic_slice_in_dim(vector_own(small, shard), position * rows, rows, 1)
    else:
        z_kv = stretch_part(v.part_kv)
        small = vector_finish(vector_own(v.table[:11], shard))
    out_cv, out_ck = [v.out_cv], stretch_items(v.z_ck, 1)
    out_o, out_c, out_r = stretch_items(v.z_ocr, 3)
    out_k, out_v = stretch_items(z_kv, 2)
    grad_previous_mix = v.heads
    block_out, grad_stream = v.block_out, v.grad_stream

    shape = stream_in.shape
    return (
        block_out.reshape(shape), grad_stream.reshape(shape), *[small[i] for i in range(11)],
        out_k, out_v, out_r, out_o, *out_ck, *out_cv, out_c,
        *v.grads[:3], grad_previous_mix[:, None], v.grads[3], v.mean, v.log,
    )


def solution(mesh):
    rows = P(None, "seg", "stretch", None)
    state = P(None, "seg", None)
    both = P(("seg", "stretch"))
    table = P(("seg", "stretch"), None)
    return jax.shard_map(
        body,
        mesh=mesh,
        in_specs=(rows,) * 2 + (state,) * 5 + (P("seg"),) * 11 + (P("seg", None),) * 7,
        out_specs=(rows,) * 2 + (both,) * 11 + (table,) * 7 + (state,) * 7,
        check_vma=False,
    )
```

```python
import jax
import jax.numpy as jnp
from jax import lax
from jax.experimental import pallas as pl
from jax.experimental.pallas import tpu as pltpu
from jax.sharding import PartitionSpec as P

epsilon = 1e-05
bf16 = jnp.bfloat16
f32 = jnp.float32
ROWS = 64
STEP = 512
LANES = 512
LIMIT = 63
MIB = 2**20
G1, B1, G2, B2, MK, MV, MR, DECAY, FIRST, CMK, CMR = range(11)


def hop(value, bit):
    count = lax.axis_size("seg")
    return lax.ppermute(value, "seg", [(i, i ^ bit) for i in range(count)])


def along(value, steps):
    count = lax.axis_size("stretch")
    first, last = (max(0, -steps), min(count, count - steps))
    return lax.ppermute(value, "stretch", [(i, i + steps) for i in range(first, last)])


def across(value, j):
    count = lax.axis_size("stretch")
    return lax.ppermute(value, "stretch", [(i, i ^ j) for i in range(count)])


def exchange(value):
    count = lax.axis_size("stretch")
    if count == 4:
        near, far = across(value, 1), across(value, 2)
        return [value, near, far, across(near, 2)]
    return lax.all_gather(value, "stretch")


def tie(value, *others):
    return lax.optimization_barrier((value, *others))[0]


def exchange_two(value):
    if lax.axis_size("stretch") != 4:
        return lax.all_gather(value, "stretch")
    near = across(value, 1)
    return [value, near, across(jnp.concatenate([value, near], axis=0), 2)]


class Live:
    def __init__(self):
        self.__dict__["held"] = {}

    def __getattr__(self, name):
        return self.held[name]

    def __setattr__(self, name, value):
        self.held[name] = value

    def drop(self, *names):
        for name in names:
            del self.held[name]

    def sync(self):
        self.__dict__["held"] = lax.optimization_barrier(self.held)


def far_bits():
    bits, b = [], 2
    while b < lax.axis_size("seg"):
        bits.append(b)
        b *= 2
    return bits


def relative_order():
    count = lax.axis_size("seg")
    return list(range(0, count, 2)) + list(range(1, count, 2))


def first_stage(own):
    return {b: [hop(part, b) for part in own] for b in far_bits()}


def second_stage(direct, held):
    rest = far_bits()
    held = dict(held)
    for m in sorted(range(0, lax.axis_size("seg"), 2), key=lambda m: (bin(m).count("1"), m)):
        if m == 0 or m in held:
            continue
        bits = [b for b in rest if m & b]
        held[m] = [hop(held[m ^ bits[-1]][0], bits[-1]), hop(held[m ^ bits[0]][1], bits[0])]
    return {m: held[m] for m in held if m not in direct}


def sibling(pieces):
    return {m ^ 1: [hop(p, 1) for p in parts] for m, parts in pieces.items()}


def plan(pieces, first, rows):
    steps, at = [], 0
    for m in relative_order():
        base = 0
        for part in pieces[m]:
            lo, hi = max(first, base), min(first + rows, base + part.shape[0])
            if lo < hi:
                steps.append((at, lo - base, hi - lo, m, lo - first))
            base += part.shape[0]
            at += 1
    return steps


def flat_pieces(pieces):
    return [part for m in relative_order() for part in pieces[m]]


class Loads:
    def __init__(self, sems):
        self.sems, self.used = sems, 0

    def start(self, src, dst):
        copy = pltpu.make_async_copy(src, dst, self.sems.at[self.used])
        self.used += 1
        copy.start()
        return copy

    def pieces(self, steps, refs, target, place):
        return [
            self.start(refs[piece].at[pl.ds(row, count)], target.at[pl.ds(place(m) + within, count)])
            for piece, row, count, m, within in steps
        ]


def wait(copies):
    for c in copies:
        c.wait()


def call(body, info, small, large, raw, outs, big_outs, scratch, copies, us, limit):
    n_small, n_large, n_raw = len(small), len(large), len(raw)
    n_out, n_big = len(outs), len(big_outs)

    def shape_of(array, index):
        return array.shape if index is None else array.shape[1:]

    def kernel(*refs):
        at = 0

        def take(n):
            nonlocal at
            at += n
            return refs[at - n : at]

        (info_ref,), small_refs, large_refs, raw_refs = take(1), take(n_small), take(n_large), take(n_raw)
        out_refs, big_refs = take(n_out), take(n_big)
        buffers, big_buffers, (sems,) = take(n_large), take(n_big), take(1)
        rest = take(len(refs) - at)
        loads = Loads(sems)
        pending = []
        for (array, index), ref, buf in zip(large, large_refs, buffers):
            pending.append(loads.start(ref if index is None else ref.at[index], buf))
        stored = {}

        def get(k):
            if pending[k] is not None:
                pending[k].wait()
                pending[k] = None
            return buffers[k]

        def put(k):
            stored[k] = loads.start(big_buffers[k], big_refs[k])

        body(info_ref, small_refs, get, raw_refs, out_refs, big_buffers, put, rest, loads)
        for k in range(n_large):
            get(k)
        for k in range(n_big):
            if k not in stored:
                put(k)
        wait(stored.values())

    hbm = pl.BlockSpec(memory_space=pltpu.HBM)
    vmem = pl.BlockSpec(memory_space=pltpu.VMEM)
    return pl.pallas_call(
        kernel,
        out_shape=[jax.ShapeDtypeStruct(s, d) for s, d in (*outs, *big_outs)],
        in_specs=[pl.BlockSpec(memory_space=pltpu.SMEM)] + [vmem] * n_small + [hbm] * (n_large + n_raw),
        out_specs=[vmem] * n_out + [hbm] * n_big,
        scratch_shapes=[pltpu.VMEM(shape_of(a, i), a.dtype) for a, i in large]
        + [pltpu.VMEM(s, d) for s, d in big_outs]
        + [pltpu.SemaphoreType.DMA((max(1, n_large + n_big + copies),))]
        + list(scratch),
        compiler_params=pltpu.CompilerParams(vmem_limit_bytes=LIMIT * MIB),
        cost_estimate=pl.CostEstimate(
            flops=0, bytes_accessed=int(us * 1e3), transcendentals=0),
    )(info, *small, *[a for a, _ in large], *raw)


def natural(me, rows):
    return lambda m: pl.multiple_of(jnp.bitwise_xor(me, m) * rows, rows)


def dot_nn(a, b):
    return jnp.dot(a, b, preferred_element_type=f32)


def dot_nt(a, b):
    return lax.dot_general(a, b, (((1,), (1,)), ((), ())), preferred_element_type=f32)


def dot_tn(a, b):
    return lax.dot_general(a, b, (((0,), (0,)), ((), ())), preferred_element_type=f32)


def norm(rows):
    centre = rows - jnp.mean(rows, axis=-1, keepdims=True)
    inverse = lax.rsqrt(jnp.mean(centre * centre, axis=-1, keepdims=True) + epsilon)
    return centre * inverse, inverse


def norm_back(d, unit, inverse, gain):
    q = d * gain
    return inverse * (
        q
        - jnp.mean(q, axis=-1, keepdims=True)
        - unit * jnp.mean(q * unit, axis=-1, keepdims=True)
    )


def down_one(rows, entering):
    at = lax.broadcasted_iota(jnp.int32, rows.shape, 0)
    return jnp.where(at == 0, entering, pltpu.roll(rows, 1, 0))


def up_one(rows, entering):
    at = lax.broadcasted_iota(jnp.int32, rows.shape, 0)
    last = rows.shape[0] - 1
    return jnp.where(at == last, entering, pltpu.roll(rows, last, 0))


def fold(rows):
    total = rows[:8]
    for k in range(8, rows.shape[0], 8):
        total = total + rows[k : k + 8]
    return total


def columns(width, step):
    step = min(step, width)

    def run(body):
        @pl.loop(0, width // step)
        def _(n):
            body(pl.ds(pl.multiple_of(n * step, step), step))

    return run


def row_chunk(b, i, length):
    return pl.ds(pl.multiple_of(b * length + i * ROWS, ROWS), ROWS)


def two_part(mat, value):
    hi = value.astype(bf16)
    lo = (value - hi.astype(f32)).astype(bf16)
    return dot_nn(mat, hi) + dot_nn(mat, lo)


def triangle(length, strictly_before):
    row = lax.broadcasted_iota(jnp.int32, (length, length), 0)
    col = lax.broadcasted_iota(jnp.int32, (length, length), 1)
    keep = (col < row) if strictly_before else (col > row)
    return keep.astype(f32).astype(bf16)


def column_sums(out_ref, sum_ref):
    for k in range(sum_ref.shape[0]):
        out_ref[k : k + 1, :] = jnp.sum(sum_ref[k], axis=0, keepdims=True)


def pack(parts_a, parts_b, vectors, width):
    arrays = [p[0] for p in (*parts_a, *parts_b) if p[0] is not None]
    shard = vectors[0].shape[0]

    def kernel(*refs):
        vec_refs, ins = refs[: len(vectors)], refs[len(vectors) : len(vectors) + len(arrays)]
        outs, (table, sems) = refs[len(vectors) + len(arrays) : -2], refs[-2:]
        copies, n = [], 0
        for out, parts in zip(outs, (parts_a, parts_b)):
            at = 0
            for array, first, count in parts:
                if array is None:
                    spot = (out, at)
                else:
                    copies.append(pltpu.make_async_copy(
                        ins[n].at[pl.ds(first, count)], out.at[pl.ds(at, count)], sems.at[n]))
                    copies[-1].start()
                    n += 1
                at += count
        table[...] = jnp.zeros_like(table)
        for k, ref in enumerate(vec_refs):
            table[k : k + 1, :shard] = ref[...].astype(f32)
        spot[0][spot[1] : spot[1] + 16, :] = table[...].astype(bf16)
        wait(copies)

    return pl.pallas_call(
        kernel,
        out_shape=[jax.ShapeDtypeStruct((sum(p[2] for p in parts), width), bf16)
                   for parts in (parts_a, parts_b)],
        in_specs=[pl.BlockSpec(memory_space=pltpu.VMEM)] * len(vectors)
        + [pl.BlockSpec(memory_space=pltpu.HBM)] * len(arrays),
        out_specs=[pl.BlockSpec(memory_space=pltpu.VMEM)] * 2,
        scratch_shapes=[pltpu.VMEM((16, width), f32), pltpu.SemaphoreType.DMA((len(arrays),))],
        compiler_params=pltpu.CompilerParams(vmem_limit_bytes=LIMIT * MIB),
        cost_estimate=pl.CostEstimate(flops=0, bytes_accessed=1000, transcendentals=0),
    )(*[x.reshape(1, shard) for x in vectors], *arrays)


def pack_wide(key, recept):
    rows, wide = key.shape
    width = recept.shape[1]
    each = recept.shape[0] * width // wide
    half = (rows + each) // 32 * 16

    def kernel(key_ref, recept_ref, top_ref, low_ref, sems):
        copies = [
            pltpu.make_async_copy(key_ref.at[pl.ds(0, half)], top_ref, sems.at[0]),
            pltpu.make_async_copy(
                key_ref.at[pl.ds(half, rows - half)], low_ref.at[pl.ds(0, rows - half)], sems.at[1])]
        for q in range(wide // width):
            copies.append(pltpu.make_async_copy(
                recept_ref.at[pl.ds(q * each, each)],
                low_ref.at[pl.ds(rows - half, each), pl.ds(q * width, width)], sems.at[2 + q]))
        for c in copies:
            c.start()
        wait(copies)

    return pl.pallas_call(
        kernel,
        out_shape=[jax.ShapeDtypeStruct((n, wide), bf16) for n in (half, rows + each - half)],
        in_specs=[pl.BlockSpec(memory_space=pltpu.HBM)] * 2,
        out_specs=[pl.BlockSpec(memory_space=pltpu.VMEM)] * 2,
        scratch_shapes=[pltpu.SemaphoreType.DMA((2 + wide // width,))],
        compiler_params=pltpu.CompilerParams(vmem_limit_bytes=LIMIT * MIB),
        cost_estimate=pl.CostEstimate(flops=0, bytes_accessed=1000, transcendentals=0),
    )(key, recept)


def recept_blocks(loads, steps, raw, w, info, shard, width, wide):
    each = shard * width // wide
    place = natural(info[0], shard)
    return [
        loads.start(raw[piece].at[pl.ds(row, count), pl.ds(q * width, width)],
                    w.at[pl.ds(place(m) + q * each + within, count)])
        for piece, row, count, m, within in steps
        for q in range(wide // width)
    ]


def time_in(info, stream, last, previous, given, pieces, spots, length, shard):
    tokens, width = stream.shape
    batches = tokens // length
    plans = [plan(pieces, spots[k], shard) for k in "kvr"]
    vplan = plan(pieces, spots["vec"], 16)
    order = relative_order()

    def body(info, small, get, raw, outs, big, put, scratch, loads):
        last_ref, prev_ref = small[:2]
        sum_ref, vec_ref, entry_ref = outs
        in_ref = big[0]
        w, vt = scratch
        place = natural(info[0], shard)
        vcopies = loads.pieces(vplan, raw, vt, lambda m: order.index(m) * 16)
        copies = [loads.pieces(plans[k], raw, w.at[k], place) for k in range(3)]
        wait(vcopies)
        if given is not None:
            vec_ref[...] = small[2][...]
        else:
            for at, m in enumerate(order):
                vec_ref[:, pl.ds(place(m), shard)] = vt[at * 16 : at * 16 + 16, :shard].astype(f32)
        unit, _ = norm(last_ref[...].astype(f32))
        edge = unit * vec_ref[G1 : G1 + 1] + vec_ref[B1 : B1 + 1]
        for b in range(batches):
            entry_ref[b : b + 1, :] = jnp.where(info[1] == 1, prev_ref[b], edge[b : b + 1])
        stream_ref = get(0)

        for b in range(batches):
            def step(i, before):
                r = row_chunk(b, i, length)
                na, _ = norm(stream_ref[r, :].astype(f32))
                xa = na * vec_ref[G1 : G1 + 1] + vec_ref[B1 : B1 + 1]
                xs = down_one(xa, before)
                for k, row in enumerate((MK, MV, MR)):
                    mix = vec_ref[row : row + 1]
                    in_ref[k, r, :] = (xa * mix + xs * (1.0 - mix)).astype(bf16)
                return xa[ROWS - 1 :]
            lax.fori_loop(0, length // ROWS, step, entry_ref[b : b + 1])
        put(0)
        def project(k):
            wait(copies[k])
            @columns(width, STEP)
            def _(n):
                big[1 + k][:, n] = dot_nn(in_ref[k], w[k, :, n])
            put(1 + k)
        project(0)
        project(1)
        keys_ref, vals_ref = big[1], big[2]
        for b in range(batches):
            t = slice(b * length, (b + 1) * length)
            @columns(width, LANES)
            def _(n):
                rate = -jnp.exp(vec_ref[DECAY : DECAY + 1, n])
                at = lax.broadcasted_iota(jnp.int32, (length, 1), 0).astype(f32)
                shifted = keys_ref[t, n] - at * rate
                peak = jnp.max(shifted, axis=0, keepdims=True)
                factor = jnp.exp(shifted - peak)
                sum_ref[b : b + 1, n] = jnp.sum(factor * vals_ref[t, n], axis=0, keepdims=True)
                sum_ref[batches + b : batches + b + 1, n] = jnp.sum(factor, axis=0, keepdims=True)
                sum_ref[2 * batches + b : 2 * batches + b + 1, n] = peak + (length - 1.0) * rate
        project(2)

    extra = [] if given is None else [given]
    return call(
        body, info, [last, previous, *extra], [(stream, None)], flat_pieces(pieces),
        [((3 * batches, width), f32), ((16, width), f32), ((batches, width), f32)],
        [((3, tokens, width), bf16)] + [((tokens, width), f32)] * 3,
        [pltpu.VMEM((3, width, width), bf16), pltpu.VMEM((16 * len(order), width), bf16)],
        len(vplan) + sum(map(len, plans)), 9, 40)


def wkv_terms(kvr_ref, ent_ref, vec_ref, b, t, n, batches, length):
    rate = -jnp.exp(vec_ref[DECAY : DECAY + 1, n])
    at = lax.broadcasted_iota(jnp.int32, (length, 1), 0).astype(f32)
    keys = kvr_ref[0][t, n]
    shifted = keys - at * rate
    peak = jnp.max(shifted, axis=0, keepdims=True)
    factor = jnp.exp(shifted - peak)
    near = (at - 1.0) * rate + peak
    opening = at * rate + ent_ref[2 * batches + b : 2 * batches + b + 1, n]
    reward = vec_ref[FIRST : FIRST + 1, n] + keys
    top = jnp.maximum(jnp.maximum(near, opening), reward)
    return at, factor, jnp.exp(near - top), jnp.exp(opening - top), jnp.exp(reward - top)


def time_out(info, kvr, everyone, state, vec, stream, pieces, spots, length, shard):
    tokens, width = stream.shape
    batches = tokens // length
    stretches = len(everyone)
    relative = isinstance(everyone, list)
    if not relative:
        everyone = [everyone]
    steps = plan(pieces, spots["o"], shard)

    def body(info, small, get, raw, outs, big, put, scratch, loads):
        every_ref, (num_ref, den_ref, exp_ref, vec_ref) = small[:-4], small[-4:]
        if not relative:
            every_ref = [every_ref[0].at[z] for z in range(stretches)]
        ent_ref, mean_ref, log_ref, edge_ref = outs
        gated_ref, wkv_ref, rden_ref, mid_ref, xb_ref = big
        (w,) = scratch
        copies = loads.pieces(steps, raw, w, natural(info[0], shard))
        span = -jnp.exp(vec_ref[DECAY : DECAY + 1, :]) * float(length)

        def merge(upto, b):
            upto_f = upto.astype(f32) if upto is not stretches else float(stretches)
            logits = []
            for j in range(stretches):
                row, z = 2 * batches + b, jnp.bitwise_xor(info[2], j) if relative else jnp.int32(j)
                logit = every_ref[j][row : row + 1, :] + (upto_f - 1.0 - z.astype(f32)) * span
                logits.append(logit if upto is stretches else jnp.where(z < upto, logit, -jnp.inf))
            opening = exp_ref[b] + upto_f * span
            top = opening
            for logit in logits:
                top = jnp.maximum(top, logit)
            start = jnp.exp(opening - top)
            num, den = num_ref[b] * start, den_ref[b] * start
            for j, logit in enumerate(logits):
                weight = jnp.exp(logit - top)
                num = num + weight * every_ref[j][b : b + 1, :]
                den = den + weight * every_ref[j][batches + b : batches + b + 1, :]
            return num, den, top

        for b in range(batches):
            for k, part in enumerate(merge(info[2], b)):
                ent_ref[k * batches + b : k * batches + b + 1, :] = part
            num, den, top = merge(stretches, b)
            mean_ref[b] = num / den
            log_ref[b] = top + jnp.log(den)

        lower = triangle(length, True)
        kvr_ref = [get(k) for k in range(3)]
        for b in range(batches):
            t = slice(b * length, (b + 1) * length)
            @columns(width, LANES)
            def _(n):
                _, factor, p, o, e = wkv_terms(kvr_ref, ent_ref, vec_ref, b, t, n, batches, length)
                vals = kvr_ref[1][t, n]
                num = (two_part(lower, factor * vals) * p
                       + ent_ref[b : b + 1, n] * o + vals * e)
                den = (two_part(lower, factor) * p
                       + ent_ref[batches + b : batches + b + 1, n] * o + e)
                rden = 1.0 / den
                wkv = num * rden
                wkv_ref[t, n] = wkv
                rden_ref[t, n] = rden
                gated_ref[t, n] = (jax.nn.sigmoid(kvr_ref[2][t, n]) * wkv).astype(bf16)
        put(0)
        put(1)
        put(2)
        wait(copies)
        stream_ref = get(3)
        @columns(width, STEP)
        def _(n):
            mid_ref[:, n] = stream_ref[:, n].astype(f32) + dot_nn(gated_ref[...], w[:, n])
        put(3)
        @pl.loop(0, tokens // ROWS)
        def _(i):
            r = row_chunk(0, i, 0)
            nb, _ = norm(mid_ref[r, :])
            xb_ref[r, :] = nb * vec_ref[G2 : G2 + 1] + vec_ref[B2 : B2 + 1]
        for b in range(batches):
            last = (b + 1) * length - 1
            edge_ref[b : b + 1, :] = xb_ref[last : last + 1, :]

    one = ((tokens, width), f32)
    return call(
        body, info, [*everyone, *state, vec], [(a, None) for a in (*kvr, stream)], flat_pieces(pieces),
        [((3 * batches, width), f32), ((batches, 1, width), f32), ((batches, 1, width), f32),
         ((batches, width), f32)],
        [((tokens, width), bf16), one, one, one, one],
        [pltpu.VMEM((width, width), bf16)], len(steps), 7, 40)


def key_blocks(loads, steps, raw, w, info, shard, fshard, wanted):
    order = relative_order()
    place = natural(info[0], shard)
    out = {}
    for m in wanted:
        cols = pl.ds(natural(info[0], fshard)(m), fshard)
        out[m] = [
            loads.start(raw[piece].at[pl.ds(row, count), cols],
                        w.at[pl.ds(place(m2) + within, count), pl.ds(order.index(m) * fshard, fshard)])
            for piece, row, count, m2, within in steps
        ]
    return out


def value_blocks(loads, raw, w, fshard, stretches):
    order = relative_order()
    others = [m for m in order if m % 2 == 0 and m]
    each = fshard // stretches
    out = {}
    for at, m in enumerate(order):
        own, gathered = raw[2 * (m % 2)], raw[2 * (m % 2) + 1]
        base = m - m % 2
        if base == 0:
            out[m] = [loads.start(own, w.at[pl.ds(at * fshard, fshard)])]
            continue
        out[m] = [
            loads.start(
                gathered.at[pl.ds((z * len(others) + others.index(base)) * each, each)],
                w.at[pl.ds(at * fshard + z * each, each)])
            for z in range(stretches)
        ]
    return out


def value_copies(stretches):
    count = lax.axis_size("seg")
    return 2 + (count - 2) * stretches


def chan_in(info, xb, edge, previous, vec, pieces_ck, length, shard, fshard):
    tokens, width = xb.shape
    batches = tokens // length
    order = relative_order()
    wide = fshard * len(order)
    steps_k = plan(pieces_ck, 0, shard)
    steps_c = plan(pieces_ck, shard, shard * width // wide)

    def body(info, small, get, raw, outs, big, put, scratch, loads):
        edge_ref, prev_ref, vec_ref = small
        (entry_ref,) = outs
        in_ref, near_ref, far_ref, act_ref, frec_ref = big
        wk, wc = scratch
        half = len(order) // 2
        turn = order[half:] + order[:half]
        blocks = key_blocks(loads, steps_k, raw, wk, info, shard, fshard, turn)
        copies_c = recept_blocks(loads, steps_c, raw, wc, info, shard, width, wide)
        for b in range(batches):
            entry_ref[b : b + 1, :] = jnp.where(info[1] == 1, prev_ref[b], edge_ref[b : b + 1, :])
        xb_ref = get(0)
        for b in range(batches):
            def step(i, before):
                r = row_chunk(b, i, length)
                x = xb_ref[r, :]
                xt = down_one(x, before)
                for k, row in enumerate((CMK, CMR)):
                    mix = vec_ref[row : row + 1]
                    in_ref[k, r, :] = (x * mix + xt * (1.0 - mix)).astype(bf16)
                return x[ROWS - 1 :]
            lax.fori_loop(0, length // ROWS, step, entry_ref[b : b + 1])
        put(0)
        for m in turn:
            wait(blocks[m])
            at = order.index(m)
            hid_ref, lo = (near_ref, at * fshard) if at < half else (far_ref, (at - half) * fshard)
            act = jnp.maximum(dot_nn(in_ref[0], wk[:, at * fshard : (at + 1) * fshard]), 0.0)
            act_ref[:, at * fshard : (at + 1) * fshard] = act.astype(bf16)
            hid_ref[:, lo : lo + fshard] = (act * act).astype(bf16)
            if m == turn[half - 1]:
                put(2)
        put(1)
        put(3)
        wait(copies_c)
        @columns(width, STEP)
        def _(n):
            frec_ref[:, n] = dot_nn(in_ref[1], wc[:, n])

    return call(
        body, info, [edge, previous, vec], [(xb, None)], flat_pieces(pieces_ck),
        [((batches, width), f32)],
        [((2, tokens, width), bf16), ((tokens, wide // 2), bf16), ((tokens, wide // 2), bf16),
         ((tokens, wide), bf16), ((tokens, width), f32)],
        [pltpu.VMEM((width, wide), bf16), pltpu.VMEM((width, width), bf16)],
        len(steps_c) * (wide // width) + len(steps_k) * len(order), 11, 40)


def chan_out(info, near, far, frec, mid, cot, cv, fshard):
    tokens, width = mid.shape
    order = relative_order()
    wide = fshard * len(order)
    stretches = lax.axis_size("stretch")

    def body(info, small, get, raw, outs, big, put, scratch, loads):
        out_ref, df_ref, dr_ref = big
        w, fval = scratch
        blocks = value_blocks(loads, raw, w, fshard, stretches)
        half = len(order) // 2
        for k in range(2):
            hid_ref = get(k)
            for m in order[k * half : (k + 1) * half]:
                wait(blocks[m])
            @columns(width, STEP)
            def _(n):
                part = dot_nn(hid_ref[...], w[k * wide // 2 : (k + 1) * wide // 2, n])
                fval[:, n] = part if k == 0 else fval[:, n] + part
        frec_ref, mid_ref, cot_ref = get(2), get(3), get(4)
        @pl.loop(0, tokens // ROWS)
        def _(i):
            r = row_chunk(0, i, 0)
            sig = jax.nn.sigmoid(frec_ref[r, :])
            cots, value = cot_ref[r, :].astype(f32), fval[r, :]
            df_ref[r, :] = (cots * sig).astype(bf16)
            out_ref[r, :] = (mid_ref[r, :] + sig * value).astype(bf16)
            dr_ref[r, :] = (cots * value * sig * (1.0 - sig)).astype(bf16)

    low = ((tokens, width), bf16)
    return call(
        body, info, [], [(a, None) for a in (near, far, frec, mid, cot)], cv, [], [low, low, low],
        [pltpu.VMEM((wide, width), bf16), pltpu.VMEM((tokens, width), f32)],
        value_copies(stretches), 7, 40)


def hidden_back(info, act, dfval, cv, fshard):
    tokens, width = dfval.shape
    order = relative_order()
    wide = fshard * len(order)
    stretches = lax.axis_size("stretch")

    def body(info, small, get, raw, outs, big, put, scratch, loads):
        (dpre_ref,) = big
        (wv,) = scratch
        values = value_blocks(loads, raw, wv, fshard, stretches)
        dfval_ref, act_ref = get(0), get(1)
        for at, m in enumerate(order):
            wait(values[m])
            block = slice(at * fshard, (at + 1) * fshard)
            d = dot_nt(dfval_ref[...], wv[block, :]) * (2.0 * act_ref[:, block].astype(f32))
            dpre_ref[:, block] = d.astype(bf16)

    return call(
        body, info, [], [(dfval, None), (act, None)], cv, [], [((tokens, wide), bf16)],
        [pltpu.VMEM((wide, width), bf16)], value_copies(stretches), 7, 40)[0]


def chan_back(info, dpre, dfrec, xb, entry, vec, pieces_ck, length, shard, fshard):
    tokens, width = xb.shape
    batches = tokens // length
    order = relative_order()
    wide = fshard * len(order)
    steps_k = plan(pieces_ck, 0, shard)
    steps_c = plan(pieces_ck, shard, shard * width // wide)

    def body(info, small, get, raw, outs, big, put, scratch, loads):
        entry_ref, vec_ref = small
        head_ref, total_ref = outs
        dxt_ref, dxb_ref = big
        wk, wc, df, dr, sum_ref = scratch
        copies_c = recept_blocks(loads, steps_c, raw, wc, info, shard, width, wide)
        keys = key_blocks(loads, steps_k, raw, wk, info, shard, fshard, order)
        dfrec_ref = get(0)
        wait(copies_c)
        @columns(width, STEP)
        def _(n):
            dr[:, n] = dot_nt(dfrec_ref[...], wc[n, :])
        dpre_ref = get(1)
        half = len(order) // 2
        for k in range(2):
            for m in order[k * half : (k + 1) * half]:
                wait(keys[m])
            part_of = slice(k * wide // 2, (k + 1) * wide // 2)
            @columns(width, STEP)
            def _(n):
                part = dot_nt(dpre_ref[:, part_of], wk[n, part_of])
                df[:, n] = part if k == 0 else df[:, n] + part
        sum_ref[...] = jnp.zeros_like(sum_ref)
        xb_ref = get(2)
        for b in range(batches):
            def step(i, before):
                r = row_chunk(b, i, length)
                x = xb_ref[r, :]
                gap = x - down_one(x, before)
                a, c = df[r, :], dr[r, :]
                ck, cr = vec_ref[CMK : CMK + 1], vec_ref[CMR : CMR + 1]
                dxt_ref[r, :] = a * (1.0 - ck) + c * (1.0 - cr)
                dxb_ref[r, :] = a * ck + c * cr
                sum_ref[0] += fold(a * gap)
                sum_ref[1] += fold(c * gap)
                return x[ROWS - 1 :]
            lax.fori_loop(0, length // ROWS, step, entry_ref[b : b + 1])
            head_ref[b : b + 1, :] = dxt_ref[b * length : b * length + 1, :]
        column_sums(total_ref, sum_ref)

    one = ((tokens, width), f32)
    return call(
        body, info, [entry, vec], [(a, None) for a in (dfrec, dpre, xb)], flat_pieces(pieces_ck),
        [((batches, width), f32), ((2, width), f32)], [one, one],
        [pltpu.VMEM((width, wide), bf16), pltpu.VMEM((width, width), bf16),
         pltpu.VMEM((tokens, width), f32), pltpu.VMEM((tokens, width), f32),
         pltpu.VMEM((2, 8, width), f32)],
        len(steps_c) * (wide // width) + len(steps_k) * len(order), 10, 40)


def mid_back(info, dxt, dxb, after, head, mid, cot, vec, kvr, wkv, rden, ent, pieces, spots, length, shard):
    tokens, width = mid.shape
    batches = tokens // length
    steps = plan(pieces, spots["o"], shard)

    def body(info, small, get, raw, outs, big, put, scratch, loads):
        after_ref, head_ref, vec_ref, ent_ref = small
        dent_ref, total_ref = outs
        dent_ref[2 * batches : 3 * batches, :] = ent_ref[2 * batches :, :]
        dent_ref[3 * batches :, :] = head_ref[...]
        dmid_ref, low_ref, high_ref, rlow_ref, rhigh_ref, gn_ref = big
        w, sum_ref = scratch
        copies = loads.pieces(steps, raw, w, natural(info[0], shard))
        sum_ref[...] = jnp.zeros_like(sum_ref)
        dxt_ref, dxb_ref, mid_ref, cot_ref = get(0), get(1), get(2), get(3)
        for b in range(batches):
            def step(k, after_row):
                r = row_chunk(b, length // ROWS - 1 - k, length)
                nb, inverse = norm(mid_ref[r, :])
                dx = dxt_ref[r, :]
                d = dxb_ref[r, :] + up_one(dx, after_row)
                back = cot_ref[r, :].astype(f32) + norm_back(d, nb, inverse, vec_ref[G2 : G2 + 1])
                dmid_ref[r, :] = back
                low_ref[r, :] = back[:, : width // 2].astype(bf16)
                high_ref[r, :] = back[:, width // 2 :].astype(bf16)
                sum_ref[0] += fold(d * nb)
                sum_ref[1] += fold(d)
                return dx[:1]
            lax.fori_loop(0, length // ROWS, step, after_ref[b : b + 1])
        put(0)
        put(1)
        put(2)
        column_sums(total_ref, sum_ref)
        wait(copies)
        @columns(width, STEP)
        def _(n):
            gn_ref[:, n] = (dot_nt(low_ref[...], w[n, : width // 2])
                            + dot_nt(high_ref[...], w[n, width // 2 :]))
        kvr_ref = [get(4), None, get(5)]
        wkv_ref, rden_ref = get(6), get(7)
        lanes = min(LANES, width // 2)
        for b, half, q in [(b, h, q) for b in range(batches) for h in range(2)
                           for q in range(width // 2 // lanes)]:
            t = slice(b * length, (b + 1) * length)
            n = slice(half * width // 2 + q * lanes, half * width // 2 + (q + 1) * lanes)
            part, at_half = (rlow_ref, rhigh_ref)[half], slice(q * lanes, (q + 1) * lanes)
            if True:
                _, _, _, o, _ = wkv_terms(kvr_ref, ent_ref, vec_ref, b, t, n, batches, length)
                sig = jax.nn.sigmoid(kvr_ref[2][t, n])
                d = gn_ref[t, n] * sig
                wkvs = wkv_ref[t, n]
                part[t, at_half] = (d * wkvs * (1.0 - sig)).astype(bf16)
                gn = d * rden_ref[t, n]
                gn_ref[t, n] = gn
                go = gn * o
                dent_ref[b : b + 1, n] = jnp.sum(go, axis=0, keepdims=True)
                dent_ref[batches + b : batches + b + 1, n] = -jnp.sum(go * wkvs, axis=0, keepdims=True)

    one, half = ((tokens, width), f32), ((tokens, width // 2), bf16)
    return call(
        body, info, [after, head, vec, ent], [(a, None) for a in (dxt, dxb, mid, cot, kvr[0], kvr[2], wkv, rden)],
        flat_pieces(pieces), [((4 * batches, width), f32), ((2, width), f32)], [one, half, half, half, half, one],
        [pltpu.VMEM((width, width), bf16), pltpu.VMEM((2, 8, width), f32)], len(steps), 9, 40)


def time_back(info, gn, wkv, kvr, ent, back, sums, state, drec, stream, entry, vec, pieces, spots,
              length, shard):
    tokens, width = stream.shape
    batches = tokens // length
    relative = isinstance(back, list)
    stretches = 4 if relative else len(back)
    if not relative:
        back = [back]
    plans = [plan(pieces, spots[k], shard) for k in "kvr"]

    def body(info, small, get, raw, outs, big, put, scratch, loads):
        back_ref = small[:-7]
        if not relative:
            back_ref = [back_ref[0].at[z] for z in range(stretches)]
        else:
            rows = 4 * batches
            back_ref = [*back_ref[:2], *[back_ref[2].at[pl.ds(k * rows, rows)] for k in range(2)]]
        ent_ref, sums_ref, num_ref, den_ref, exp_ref, entry_ref, vec_ref = small[-7:]
        gnum_ref, gden_ref, gexp_ref, gffn_ref, head_ref, total_ref, extra_ref = outs
        d_ref, dxs_ref, dxa_ref = big
        w, dins, sum_ref, later_ref, loc_ref = scratch
        place = natural(info[0], shard)
        copies = [loads.pieces(plans[k], raw, w.at[k], place) for k in range(3)]
        span = -jnp.exp(vec_ref[DECAY : DECAY + 1, :]) * float(length)
        pos = info[2].astype(f32)
        nums, dens, exps = (slice(k * batches, (k + 1) * batches) for k in range(3))
        zero = jnp.zeros((batches, width), f32)

        def state(ref):
            return jnp.concatenate([ref[b] for b in range(batches)], axis=0)

        later_n = later_d = carry_n = carry_d = grad_n = grad_d = grad_f = zero
        for j in range(stretches):
            there = back_ref[j][exps, :]
            at_z = jnp.bitwise_xor(info[2], j) if relative else jnp.int32(j)
            z = at_z.astype(f32)
            after = at_z > info[2]
            lift = jnp.where(after, jnp.exp(jnp.minimum(
                sums_ref[exps, :] - there + (z - 1.0 - pos) * span, 0.0)), 0.0)
            carry = jnp.where(after, jnp.exp(jnp.minimum(
                ent_ref[exps, :] - there + (z - pos) * span, 0.0)), 0.0)
            raised = jnp.exp(jnp.minimum(state(exp_ref) - there + z * span, 0.0))
            dn, dd = back_ref[j][nums, :], back_ref[j][dens, :]
            grad_f = grad_f + jnp.where(at_z == 0, back_ref[j][3 * batches :, :], 0.0)
            later_n, later_d = later_n + dn * lift, later_d + dd * lift
            carry_n, carry_d = carry_n + dn * carry, carry_d + dd * carry
            grad_n, grad_d = grad_n + dn * raised, grad_d + dd * raised
        later_ref[nums, :], later_ref[dens, :] = later_n, later_d
        grad_e = state(num_ref) * grad_n + state(den_ref) * grad_d
        for b in range(batches):
            gnum_ref[b], gden_ref[b] = grad_n[b : b + 1], grad_d[b : b + 1]
            gexp_ref[b] = grad_e[b : b + 1]
            gffn_ref[b] = grad_f[b : b + 1]
        rate_part = (
            float(length) * (ent_ref[nums, :] * carry_n + ent_ref[dens, :] * carry_d)
            + (length - 1.0) * (later_n * sums_ref[nums, :] + later_d * sums_ref[dens, :]))

        upper = triangle(length, False)
        gn_ref, wkv_ref = get(0), get(1)
        kvr_ref = [get(2), get(3)]
        for b in range(batches):
            t = slice(b * length, (b + 1) * length)
            @columns(width, LANES)
            def _(n):
                at, factor, p, o, e = wkv_terms(kvr_ref, ent_ref, vec_ref, b, t, n, batches, length)
                vals, g = kvr_ref[1][t, n], gn_ref[t, n]
                gd = -g * wkv_ref[t, n]
                direct = e * (g * vals + gd)
                opened = o * (g * ent_ref[b : b + 1, n] + gd * ent_ref[batches + b : batches + b + 1, n])
                rn = two_part(upper, g * p) + later_ref[b : b + 1, n]
                rd = two_part(upper, gd * p) + later_ref[batches + b : batches + b + 1, n]
                chain = factor * (rn * vals + rd)
                d_ref[0, t, n] = (chain + direct).astype(bf16)
                d_ref[1, t, n] = (factor * rn + g * e).astype(bf16)
                loc_ref[b : b + 1, n] = jnp.sum(
                    opened - (at - 1.0) * direct - at * chain, axis=0, keepdims=True)
                loc_ref[batches + b : batches + b + 1, n] = jnp.sum(direct, axis=0, keepdims=True)
        put(0)
        rate_rows = rate_part + loc_ref[:batches, :]
        extra_ref[0:1, :] = jnp.sum(rate_rows, axis=0, keepdims=True) * -jnp.exp(
            vec_ref[DECAY : DECAY + 1, :])
        extra_ref[1:2, :] = jnp.sum(loc_ref[batches:, :], axis=0, keepdims=True)
        for k in range(2):
            wait(copies[k])
            @columns(width, STEP)
            def _(n):
                dins[k, :, n] = dot_nt(d_ref[k], w[k, n, :])
        low_ref, high_ref = get(5), get(6)
        wait(copies[2])
        @columns(width, STEP)
        def _(n):
            dins[2, :, n] = (dot_nt(low_ref[...], w[2, n, : width // 2])
                             + dot_nt(high_ref[...], w[2, n, width // 2 :]))
        sum_ref[...] = jnp.zeros_like(sum_ref)
        stream_ref = get(4)
        for b in range(batches):
            def step(i, before):
                r = row_chunk(b, i, length)
                na, _ = norm(stream_ref[r, :].astype(f32))
                xa = na * vec_ref[G1 : G1 + 1] + vec_ref[B1 : B1 + 1]
                gap = xa - down_one(xa, before)
                dxs = jnp.zeros((ROWS, width), f32)
                dxa = jnp.zeros((ROWS, width), f32)
                for k, row in enumerate((MK, MV, MR)):
                    d, mix = dins[k, r, :], vec_ref[row : row + 1]
                    dxs = dxs + d * (1.0 - mix)
                    dxa = dxa + d * mix
                    sum_ref[k] += fold(d * gap)
                dxs_ref[r, :] = dxs
                dxa_ref[r, :] = dxa
                return xa[ROWS - 1 :]
            lax.fori_loop(0, length // ROWS, step, entry_ref[b : b + 1])
            head_ref[b : b + 1, :] = dxs_ref[b * length : b * length + 1, :]
        column_sums(total_ref, sum_ref)

    one = ((tokens, width), f32)
    return call(
        body, info, [*back, ent, sums, *state, entry, vec],
        [(a, None) for a in (gn, wkv, kvr[0], kvr[1], stream, *drec)], flat_pieces(pieces),
        [((batches, 1, width), f32)] * 4
        + [((batches, width), f32), ((3, width), f32), ((2, width), f32)],
        [((2, tokens, width), bf16), one, one],
        [pltpu.VMEM((3, width, width), bf16), pltpu.VMEM((3, tokens, width), f32),
         pltpu.VMEM((3, 8, width), f32), pltpu.VMEM((2 * batches, width), f32),
         pltpu.VMEM((2 * batches, width), f32)],
        sum(map(len, plans)), 14, 40)


def in_back(info, dxs, dxa, after, dmid, stream, vec, length):
    tokens, width = stream.shape
    batches = tokens // length

    def body(info, small, get, raw, outs, big, put, scratch, loads):
        after_ref, vec_ref = small
        (out_ref,) = big
        (sum_ref,) = scratch
        dxs_ref, dxa_ref, dmid_ref, stream_ref = (get(k) for k in range(4))
        sum_ref[...] = jnp.zeros_like(sum_ref)
        for b in range(batches):
            def step(k, after_row):
                r = row_chunk(b, length // ROWS - 1 - k, length)
                na, inverse = norm(stream_ref[r, :].astype(f32))
                dx = dxs_ref[r, :]
                d = dxa_ref[r, :] + up_one(dx, after_row)
                back = norm_back(d, na, inverse, vec_ref[G1 : G1 + 1])
                out_ref[r, :] = (dmid_ref[r, :] + back).astype(bf16)
                sum_ref[0] += fold(d * na)
                sum_ref[1] += fold(d)
                return dx[:1]
            lax.fori_loop(0, length // ROWS, step, after_ref[b : b + 1])
        column_sums(outs[0], sum_ref)

    return call(
        body, info, [after, vec], [(a, None) for a in (dxs, dxa, dmid, stream)], [],
        [((2, width), f32)], [((tokens, width), bf16)],
        [pltpu.VMEM((2, 8, width), f32)], 0, 6, 40)


def weight_grad(info, arrays, items, layout, us, relative=False, stacked=False, under=()):
    count = lax.axis_size("seg")
    evens = list(range(0, count, 2))
    first = items[0][2]
    lead = first[0] if isinstance(first, list) else first
    tokens, n_wide = arrays[lead[0]].shape[-2:]
    n_wide *= len(first) if isinstance(first, list) else 1
    w = arrays[items[0][0][0]].shape[-1] // {"natural": count, "blocks": len(evens), "joined": len(evens)}[layout]
    pair = 2 if w < 256 else 1
    groups = [evens[1:][k : k + pair] for k in range(0, len(evens) - 1, pair)]
    groups[-1].append(0) if len(groups[-1]) < pair else groups.append([0])
    groups = [g for g in groups if g]
    stretches = lax.axis_size("stretch")
    each_z = w // stretches
    shapes = [(len(evens) * len(items) * w, n_wide)] if stacked else [(len(items) * w, n_wide)] * len(evens)
    shares = [x.shape[0] // len(evens) for x in under]
    if under:
        shapes = [(len(items) * w + sum(shares), n_wide)] * len(evens)

    def body(info, small, get, raw, outs, big, put, scratch, loads):
        x_all, dy_all = scratch
        copies_under, at = [], len(items) * w
        for n, share in enumerate(shares):
            for k in range(len(evens)):
                copies_under.append(loads.start(
                    raw[len(arrays) + n].at[pl.ds(k * share, share)], big[k].at[pl.ds(at, share)]))
            at += share

        def view(spec):
            which, lead = spec
            return raw[which] if lead is None else raw[which].at[lead]

        def columns_of(ref, m):
            if layout == "natural":
                return ref.at[:, pl.ds(natural(info[0], w)(m), w)]
            return ref.at[:, pl.ds(evens.index(m) * w, w)]

        copies = []
        for k, (x, x_sib, dy, dy_sib) in enumerate(items):
            now = []
            for at, part in ((0, dy), (tokens, dy_sib)):
                if relative:
                    each = n_wide // count
                    for n, m in enumerate(relative_order()):
                        cols = natural(info[0], each)(m if at == 0 else m ^ 1)
                        now.append(loads.start(
                            view(part).at[:, pl.ds(n * each, each)],
                            dy_all.at[k, pl.ds(at, tokens), pl.ds(cols, each)]))
                    continue
                pieces = part if isinstance(part, list) else [part]
                each = n_wide // len(pieces)
                for n, piece in enumerate(pieces):
                    now.append(loads.start(
                        view(piece), dy_all.at[k, pl.ds(at, tokens), pl.ds(n * each, each)]))
            for at, part in ((0, x), (tokens, x_sib)):
                ref, rows = view(part), pl.ds(at, tokens)
                if layout == "joined":
                    for g, ms in enumerate(groups):
                        cols = pl.ds(g * pair * w, len(ms) * w)
                        now.append(loads.start(
                            ref.at[:, cols], x_all.at[k, g, rows, pl.ds(0, len(ms) * w)]))
                    continue
                for g, ms in enumerate(groups):
                    for n, m in enumerate(ms):
                        now.append(loads.start(
                            columns_of(ref, m), x_all.at[k, g, rows, pl.ds(n * w, w)]))
            copies.append(now)
        step = min(512, n_wide)
        for k in range(len(items)):
            wait(copies[k])
        for g, ms in enumerate(groups):
            for k in range(len(items)):
                for q in range(n_wide // step):
                    dst = slice(q * step, (q + 1) * step)
                    block = dot_tn(x_all[k, g, :, : len(ms) * w], dy_all[k, :, dst]).astype(bf16)
                    for n, m in enumerate(ms):
                        if not stacked:
                            big[evens.index(m)][k * w : (k + 1) * w, dst] = block[n * w : (n + 1) * w]
                            continue
                        for z in range(stretches):
                            row = ((z * len(evens) + evens.index(m)) * len(items) + k) * each_z
                            big[0][row : row + each_z, dst] = block[n * w + z * each_z : n * w + (z + 1) * each_z]
            if g == 0:
                wait(copies_under)
            for m in ms if not stacked else []:
                put(evens.index(m))

    return call(
        body, info, [], [], [*arrays, *under], [], [(shape, bf16) for shape in shapes],
        [pltpu.VMEM((len(items), len(groups), 2 * tokens, pair * w), bf16),
         pltpu.VMEM((len(items), 2 * tokens, n_wide), bf16)],
        len(items) * (4 + 2 * len(evens) + 2 * count) + len(under) * len(evens), us, 40)


def grad_send(parts):
    return [hop(part, 2 * k) for k, part in enumerate(parts) if k]


def total(terms):
    out = terms[0].astype(f32)
    for t in terms[1:]:
        out = out + t.astype(f32)
    return out


def grad_stack(info, key, recept):
    stretches = lax.axis_size("stretch")
    own, width = recept[0].shape
    each, blocks = own // stretches, key[0].shape[1] // width
    rows = (blocks + 1) * each
    if each % 16:
        wide = total(key).astype(bf16).reshape(stretches, each, blocks, width)
        wide = jnp.swapaxes(wide, 1, 2).reshape(stretches, blocks * each, width)
        narrow = total(recept).astype(bf16).reshape(stretches, each, width)
        return jnp.concatenate([wide, narrow], axis=1).reshape(stretches * rows, width)
    terms = len(key)

    def body(info, small, get, raw, outs, big, put, scratch, loads):
        keys, recepts = scratch
        copies = []
        for z in range(stretches):
            src = pl.ds(z * each, each)
            now = [loads.start(raw[j].at[src], keys.at[j, z]) for j in range(terms)]
            copies.append(now + [loads.start(raw[terms + j].at[src], recepts.at[j, z]) for j in range(terms)])
        for z in range(stretches):
            wait(copies[z])
            for q in range(blocks):
                at = z * rows + q * each
                big[0][at : at + each, :] = total(
                    [keys[j, z, :, q * width : (q + 1) * width] for j in range(terms)]).astype(bf16)
            at = z * rows + blocks * each
            big[0][at : at + each, :] = total([recepts[j, z] for j in range(terms)]).astype(bf16)

    return call(
        body, info, [], [], [*key, *recept], [], [((stretches * rows, width), bf16)],
        [pltpu.VMEM((terms, stretches, each, blocks * width), bf16),
         pltpu.VMEM((terms, stretches, each, width), bf16)],
        stretches * 2 * terms, 4, 24)[0]


def grad_pieces(info, own, got, items, each):
    stretches = lax.axis_size("stretch")
    rows, n_wide = own.shape
    width = each * stretches

    def body(info, small, get, raw, outs, big, put, scratch, loads):
        refs = [get(k) for k in range(1 + len(got))]
        first = items * width
        table = total([r[first : first + 16, :] for r in refs])
        half = n_wide // 2
        table = table[:, :half] + table[:, half:]
        hi = table.astype(bf16)
        lo = (table - hi.astype(f32)).astype(bf16)
        for j in list(range(1, stretches)) + [0]:
            z = jnp.bitwise_xor(info[2], j)
            for k in range(items):
                src = pl.ds(pl.multiple_of(k * width + z * each, each), each)
                big[j][k * each : (k + 1) * each, :] = total([r[src, :] for r in refs]).astype(bf16)
            big[j][items * each :, :half] = hi
            big[j][items * each :, half:] = lo
            put(j)

    return call(
        body, info, [], [(a, None) for a in (own, *got)], [], [],
        [((items * each + 16, n_wide), bf16)] * stretches, [], 0, 3, 24)


def stretch_part(part):
    return lax.psum_scatter(part, "stretch", scatter_dimension=0, tiled=True)


def stretch_items(out, items):
    own = out.shape[0] // items
    return [out[k * own : (k + 1) * own].astype(f32) for k in range(items)]


def vector_rows(table, width):
    me, count = lax.axis_index("seg"), lax.axis_size("seg")
    own = table.shape[1] // count
    table = jnp.pad(table, ((0, 16 - table.shape[0]), (0, 0)))
    rows = []
    for m in range(0, count, 2):
        pair = lax.dynamic_slice_in_dim(table, (me ^ m) // 2 * (2 * own), 2 * own, 1)
        pair = jnp.pad(pair, ((0, 0), (0, width // 2 - 2 * own)))
        hi = pair.astype(bf16)
        rows.append(jnp.concatenate([hi, (pair - hi.astype(f32)).astype(bf16)], axis=1))
    return jnp.concatenate(rows, axis=0)


def vector_read(rows):
    half = rows.shape[1] // 2
    return rows[:, :half].astype(f32) + rows[:, half:].astype(f32)


def vector_own(pair, own):
    second = (lax.axis_index("seg") & 1) != 0
    lo, hi = pair[:, :own], pair[:, own : 2 * own]
    return jnp.where(second, hi, lo) + hop(jnp.where(second, lo, hi), 1)


def vector_finish(table):
    position, count = lax.axis_index("stretch"), lax.axis_size("stretch")
    bit = count // 2
    while bit:
        lo, hi = jnp.split(table, 2, axis=1)
        upper = (position & bit) != 0
        table = jnp.where(upper, hi, lo) + across(jnp.where(upper, lo, hi), bit)
        bit //= 2
    return table


def own_columns(x, me, w):
    ms = [*range(2, lax.axis_size("seg"), 2), 0]
    return jnp.concatenate([lax.dynamic_slice_in_dim(x, (me ^ m) * w, w, 1) for m in ms], axis=1)


def body(
    stream_in, cotangent, previous_mix, previous_ffn, state_num, state_den, state_exp,
    gain_one, bias_one, gain_two, bias_two, mix_key, mix_value, mix_recept,
    time_decay, time_first, chan_mix_key, chan_mix_recept,
    att_key, att_value, att_recept, att_output, chan_key, chan_value, chan_recept,
):
    mine = lax.axis_index("seg")
    position = lax.axis_index("stretch")
    stretches = lax.axis_size("stretch")
    batches, _, length, width = stream_in.shape
    tokens = batches * length
    shard = att_key.shape[0]
    fshard = chan_value.shape[0]
    wide = chan_key.shape[1]
    aligned = shard % 128 == 0
    count = lax.axis_size("seg")
    info = jnp.stack([mine, (position == 0).astype(jnp.int32), position])

    stream = stream_in.reshape(tokens, width)
    cot = cotangent.reshape(tokens, width)
    state = (state_num, state_den, state_exp)
    vectors = [gain_one, bias_one, gain_two, bias_two, mix_key, mix_value, mix_recept,
               time_decay, time_first, chan_mix_key, chan_mix_recept]

    v = Live()
    evens = list(range(0, count, 2))
    spots = {"k": 0, "v": shard, "vec": 2 * shard, "r": 2 * shard + 16, "o": 3 * shard + 16}
    each = fshard // stretches
    v.own_tm = pack(
        [(att_key, 0, shard), (att_value, 0, shard), (None, 0, 16)],
        [(att_recept, 0, shard), (att_output, 0, shard)], vectors, width)
    v.share = lax.dynamic_slice_in_dim(chan_value, position * each, each, 0)
    v.cv = chan_value
    v.last_in = stream_in[:, 0, length - 1]
    v.sync()
    v.shares = lax.all_gather(v.share, "seg", axis=0, tiled=True)
    v.one_tm = first_stage(v.own_tm)
    v.ck = pack_wide(tie(chan_key, *v.own_tm), chan_recept)
    v.tm0 = sibling({0: v.own_tm})
    v.last_in = along(tie(v.last_in, *v.tm0[1]), 1)
    v.sync()
    v.tm6 = second_stage(v.one_tm, v.one_tm)
    v.tm2 = sibling(v.one_tm)
    v.ck0 = sibling({0: v.ck})
    gathered_cv = lax.all_gather(
        jnp.concatenate([lax.dynamic_slice_in_dim(v.shares, (mine ^ m) * each, each, 0) for m in evens[1:]], axis=0),
        "stretch", axis=0, tiled=True)
    v.sync()
    v.tm6_sib = sibling(v.tm6)
    v.sync()

    v.one_ck = first_stage(v.ck)
    tm = {0: v.own_tm, **v.one_tm, **v.tm6, **v.tm0, **v.tm2, **v.tm6_sib}
    given = None
    if not aligned:
        given = lax.all_gather(jnp.stack(vectors), "seg", axis=1, tiled=True).astype(f32)
        given = jnp.pad(given, ((0, 5), (0, 0)))
    v.sums, v.vec, v.entry, v.kvr_in, *v.kvr = time_in(
        info, stream, v.last_in, previous_mix, given, tm, spots, length, shard)
    v.everyone = lax.all_gather(v.sums, "stretch")
    v.tm = tm
    v.drop("own_tm", "one_tm", "tm6", "tm0", "tm2", "tm6_sib", "share", "shares")
    v.sync()

    v.ck6 = second_stage(v.one_ck, v.one_ck)
    v.ent, v.mean, v.log, v.edge_b, v.gated, v.wkv, v.rden, v.mid, v.xb = time_out(
        info, v.kvr, v.everyone, state, v.vec, stream, v.tm, spots, length, shard)
    first_far = far_bits()[0]
    v.ck2 = sibling({first_far: v.one_ck[first_far]})
    v.edge_b = along(v.edge_b, 1)
    v.drop("everyone")
    v.sync()
    v.ck2 = {**v.ck2, **sibling({m: p for m, p in v.one_ck.items() if m != first_far})}
    v.all_ck = {0: v.ck, **v.one_ck, **v.ck6, **v.ck0, **v.ck2, **sibling(v.ck6)}
    v.gathered_cv = gathered_cv
    v.drop("ck", "one_ck", "ck6", "ck0", "ck2")
    v.sync()

    v.entry_b, v.f_in, v.near, v.far, v.act, v.frec = chan_in(
        info, v.xb, v.edge_b, previous_ffn, v.vec, v.all_ck, length, shard, fshard)
    v.all_cv = [v.cv, v.gathered_cv, hop(v.cv, 1), hop(v.gathered_cv, 1)]
    v.drop("cv", "gathered_cv")
    v.sync()
    v.block_out, v.d_fval, v.d_frec = chan_out(
        info, v.near, v.far, v.frec, v.mid, cot, v.all_cv, fshard)
    v.far_sib = hop(v.far, 1)
    v.f_sib = hop(v.f_in, 1)
    v.g_sib = hop(v.gated, 1)
    v.kvr_sib = hop(v.kvr_in, 1)
    v.drop("frec", "far")
    v.sync()

    def pairs(*arrays):
        if aligned:
            return [a for pair in arrays for a in pair]
        return [own_columns(a, mine, shard) for pair in arrays for a in pair]

    layout = "natural" if aligned else "joined"
    flat = tuple((j, None) for j in range(4))
    arrays = [v.near, v.far_sib, v.d_fval, hop(v.d_fval, 1)]
    v.stack_cv = weight_grad(info, arrays, [flat], "blocks", 6, stacked=True)[0]
    dfrec_sib = hop(v.d_frec, 1)
    if aligned:
        v.parts_c = weight_grad(
            info, [v.f_in, v.f_sib, v.d_frec, dfrec_sib], [((0, 1), (1, 1), (2, None), (3, None))], layout, 3)
    else:
        v.parts_c = weight_grad(
            info, [*pairs((v.f_in[1], v.f_sib[1])), v.d_frec, dfrec_sib], [flat], layout, 3)
    v.drop("near", "far_sib")
    v.sync()

    z_cv = stretch_part(v.stack_cv)
    v.got_c = grad_send(v.parts_c)
    v.dpre = hidden_back(info, v.act, v.d_fval, v.all_cv, fshard)
    dpre_sib = hop(v.dpre, 1)
    v.head_b, v.sums_c, v.dxt, v.dxb = chan_back(
        info, v.dpre, v.d_frec, v.xb, v.entry_b, v.vec, v.all_ck, length, shard, fshard)
    v.next_b = along(v.head_b, -1)
    dpre = tie(v.dpre, v.dxt)
    if aligned:
        v.parts_ck = weight_grad(
            info, [v.f_in, v.f_sib, dpre, dpre_sib], [((0, 0), (1, 0), (2, None), (3, None))], layout, 7, True)
    else:
        v.parts_ck = weight_grad(
            info, [*pairs((v.f_in[0], v.f_sib[0])), dpre, dpre_sib], [flat], layout, 7, True)
    v.drop("all_ck", "all_cv", "xb", "entry_b", "act", "d_fval", "dpre", "stack_cv")
    v.sync()

    v.got_ck = grad_send(v.parts_ck)
    backs, v.sums_m, v.dmid, *lows, gn = mid_back(
        info, v.dxt, v.dxb, v.next_b, v.head_b, v.mid, cot, v.vec, v.kvr, v.wkv, v.rden, v.ent, v.tm, spots,
        length, shard)
    v.dbr, v.drec = lows[:2], lows[2:]
    back = exchange_two(backs)
    *v.grads, v.head_a, v.sums_t, v.extra, v.d_kv, v.dxs, v.dxa = time_back(
        info, gn, v.wkv, v.kvr, v.ent, back, v.sums, state, v.drec, stream, v.entry, v.vec,
        v.tm, spots, length, shard)
    v.dbr_sib = [hop(a, 1) for a in v.dbr]
    v.drec_sib = [hop(a, 1) for a in v.drec]
    dys = [([(at, None), (at + 1, None)], [(at + 2, None), (at + 3, None)]) for at in (0, 4)]
    lows = [*v.dbr, *v.dbr_sib, *v.drec, *v.drec_sib]
    gated = tie(v.gated, v.d_kv)
    if aligned:
        v.parts_or = weight_grad(
            info, [*lows, gated, v.g_sib, v.kvr_in, v.kvr_sib],
            [((8, None), (9, None), *dys[0]), ((10, 2), (11, 2), *dys[1])], layout, 6, stacked=True)
    else:
        xs = pairs((gated, v.g_sib), (v.kvr_in[2], v.kvr_sib[2]))
        v.parts_or = weight_grad(
            info, [*lows, *xs], [((8, None), (9, None), *dys[0]), ((10, None), (11, None), *dys[1])], layout, 6,
            stacked=True)
    v.drop("wkv", "kvr", "ent", "sums", "entry", "tm", "dxt", "dxb", "mid", "rden", "next_b", "head_b")
    v.sync()
    v.dkv_sib = hop(v.d_kv, 1)
    v.next_a = along(v.head_a, -1)
    z_or = stretch_part(v.parts_or[0])
    v.stack = grad_stack(info, [v.parts_ck[0], *v.got_ck], [v.parts_c[0], *v.got_c])
    v.drop("gated", "g_sib", "dbr", "dbr_sib", "drec", "drec_sib", "f_in", "f_sib", "d_frec",
           "parts_ck", "got_ck", "parts_c", "got_c", "parts_or")
    v.z_cv = z_cv
    v.sync()

    v.parts_cv = [v.z_cv[k * each : (k + 1) * each] for k in range(len(evens))]
    z_rest = stretch_part(v.stack)
    v.got_cv = grad_send(v.parts_cv)
    sums_i, v.grad_stream = in_back(info, v.dxs, v.dxa, v.next_a, v.dmid, stream, v.vec, length)
    table = jnp.concatenate([sums_i, v.sums_m, v.sums_t, v.extra, v.sums_c], axis=0)
    under = [vector_rows(table, width)]
    if aligned:
        v.parts_kv = weight_grad(
            info, [v.kvr_in, v.kvr_sib, v.d_kv, v.dkv_sib],
            [tuple((j, k) for j in range(4)) for k in range(2)], layout, 7, under=under)
    else:
        xs = pairs(*[(v.kvr_in[k], v.kvr_sib[k]) for k in range(2)])
        v.parts_kv = weight_grad(
            info, [*xs, v.d_kv, v.dkv_sib],
            [((2 * k, None), (2 * k + 1, None), (4, k), (5, k)) for k in range(2)], layout, 7, under=under)
    v.drop("kvr_in", "kvr_sib", "d_kv", "dkv_sib", "dxs", "dxa", "dmid", "next_a", "stack",
           "sums_m", "sums_t", "extra", "sums_c", "z_cv")
    v.sync()

    v.got_kv = grad_send(v.parts_kv)
    v.heads = lax.all_gather(v.head_a, "stretch")[0]
    v.out_cv = total([v.parts_cv[0], *v.got_cv])
    v.drop("parts_cv", "got_cv")
    v.z_or = z_or
    v.sync()
    rows = shard // stretches
    by_hops = stretches == 4 and rows % 16 == 0
    if by_hops:
        v.pieces = grad_pieces(info, v.parts_kv[0], v.got_kv, 2, rows)
    else:
        whole = total([v.parts_kv[0], *v.got_kv])
        first = 2 * shard
        v.table = vector_read(whole[first:])
        v.part_kv = whole[:first].astype(bf16).reshape(2, stretches, rows, width)
        v.part_kv = jnp.swapaxes(v.part_kv, 0, 1).reshape(first, width)
    parts = [v.z_or[2 * k * rows : 2 * (k + 1) * rows] for k in range(len(evens))]
    v.parts_or = [parts[0], *grad_send(parts)]
    v.drop("parts_kv", "got_kv", "z_or")
    v.sync()
    blocks = wide // width
    out_ck = jnp.concatenate([z_rest[q * rows : (q + 1) * rows] for q in range(blocks)], axis=1).astype(f32)
    out_c = z_rest[blocks * rows : (blocks + 1) * rows].astype(f32)
    if by_hops:
        pieces = [v.pieces[0], *[across(v.pieces[j], j) for j in range(1, stretches)]]
        z_kv = total([p[: 2 * rows] for p in pieces])
        small = sum(vector_read(p[2 * rows : 2 * rows + 11]) for p in pieces)
        small = lax.dynamic_slice_in_dim(vector_own(small, shard), position * rows, rows, 1)
    else:
        z_kv = stretch_part(v.part_kv)
        small = vector_finish(vector_own(v.table[:11], shard))
    out_k, out_v = stretch_items(z_kv, 2)
    out_o, out_r = stretch_items(total(v.parts_or), 2)
    out_cv = v.out_cv
    grad_previous_mix = v.heads
    block_out, grad_stream = v.block_out, v.grad_stream

    shape = stream_in.shape
    return (
        block_out.reshape(shape), grad_stream.reshape(shape), *[small[i] for i in range(11)],
        out_k, out_v, out_r, out_o, out_ck, out_cv, out_c,
        *v.grads[:3], grad_previous_mix[:, None], v.grads[3], v.mean, v.log,
    )


def solution(mesh):
    rows = P(None, "seg", "stretch", None)
    state = P(None, "seg", None)
    both = P(("seg", "stretch"))
    table = P(("seg", "stretch"), None)
    return jax.shard_map(
        body,
        mesh=mesh,
        in_specs=(rows,) * 2 + (state,) * 5 + (P("seg"),) * 11 + (P("seg", None),) * 7,
        out_specs=(rows,) * 2 + (both,) * 11 + (table,) * 7 + (state,) * 7,
        check_vma=False,
    )
```

```python
import jax
import jax.numpy as jnp
from jax import lax
from jax.experimental import pallas as pl
from jax.experimental.pallas import tpu as pltpu
from jax.sharding import PartitionSpec as P

epsilon = 1e-05
bf16 = jnp.bfloat16
f32 = jnp.float32
ROWS = 64
STEP = 512
LANES = 512
LIMIT = 63
MIB = 2**20
G1, B1, G2, B2, MK, MV, MR, DECAY, FIRST, CMK, CMR = range(11)


def hop(value, bit):
    count = lax.axis_size("seg")
    return lax.ppermute(value, "seg", [(i, i ^ bit) for i in range(count)])


def along(value, steps):
    count = lax.axis_size("stretch")
    first, last = (max(0, -steps), min(count, count - steps))
    return lax.ppermute(value, "stretch", [(i, i + steps) for i in range(first, last)])


def across(value, j):
    count = lax.axis_size("stretch")
    return lax.ppermute(value, "stretch", [(i, i ^ j) for i in range(count)])


def exchange(value):
    count = lax.axis_size("stretch")
    if count == 4:
        near, far = across(value, 1), across(value, 2)
        return [value, near, far, across(near, 2)]
    return lax.all_gather(value, "stretch")


def tie(value, *others):
    return lax.optimization_barrier((value, *others))[0]


def exchange_two(value):
    if lax.axis_size("stretch") != 4:
        return lax.all_gather(value, "stretch")
    near = across(value, 1)
    return [value, near, across(jnp.concatenate([value, near], axis=0), 2)]


class Live:
    def __init__(self):
        self.__dict__["held"] = {}

    def __getattr__(self, name):
        return self.held[name]

    def __setattr__(self, name, value):
        self.held[name] = value

    def drop(self, *names):
        for name in names:
            del self.held[name]

    def sync(self):
        self.__dict__["held"] = lax.optimization_barrier(self.held)


def far_bits():
    bits, b = [], 2
    while b < lax.axis_size("seg"):
        bits.append(b)
        b *= 2
    return bits


def relative_order():
    count = lax.axis_size("seg")
    return list(range(0, count, 2)) + list(range(1, count, 2))


def first_stage(own):
    return {b: [hop(part, b) for part in own] for b in far_bits()}


def second_stage(direct, held):
    rest = far_bits()
    held = dict(held)
    for m in sorted(range(0, lax.axis_size("seg"), 2), key=lambda m: (bin(m).count("1"), m)):
        if m == 0 or m in held:
            continue
        bits = [b for b in rest if m & b]
        held[m] = [hop(held[m ^ bits[-1]][0], bits[-1]), hop(held[m ^ bits[0]][1], bits[0])]
    return {m: held[m] for m in held if m not in direct}


def sibling(pieces):
    return {m ^ 1: [hop(p, 1) for p in parts] for m, parts in pieces.items()}


def plan(pieces, first, rows):
    steps, at = [], 0
    for m in relative_order():
        base = 0
        for part in pieces[m]:
            lo, hi = max(first, base), min(first + rows, base + part.shape[0])
            if lo < hi:
                steps.append((at, lo - base, hi - lo, m, lo - first))
            base += part.shape[0]
            at += 1
    return steps


def flat_pieces(pieces):
    return [part for m in relative_order() for part in pieces[m]]


class Loads:
    def __init__(self, sems):
        self.sems, self.used = sems, 0

    def start(self, src, dst):
        copy = pltpu.make_async_copy(src, dst, self.sems.at[self.used])
        self.used += 1
        copy.start()
        return copy

    def pieces(self, steps, refs, target, place):
        return [
            self.start(refs[piece].at[pl.ds(row, count)], target.at[pl.ds(place(m) + within, count)])
            for piece, row, count, m, within in steps
        ]


def wait(copies):
    for c in copies:
        c.wait()


def call(body, info, small, large, raw, outs, big_outs, scratch, copies, us, limit):
    n_small, n_large, n_raw = len(small), len(large), len(raw)
    n_out, n_big = len(outs), len(big_outs)

    def shape_of(array, index):
        return array.shape if index is None else array.shape[1:]

    def kernel(*refs):
        at = 0

        def take(n):
            nonlocal at
            at += n
            return refs[at - n : at]

        (info_ref,), small_refs, large_refs, raw_refs = take(1), take(n_small), take(n_large), take(n_raw)
        out_refs, big_refs = take(n_out), take(n_big)
        buffers, big_buffers, (sems,) = take(n_large), take(n_big), take(1)
        rest = take(len(refs) - at)
        loads = Loads(sems)
        pending = []
        for (array, index), ref, buf in zip(large, large_refs, buffers):
            pending.append(loads.start(ref if index is None else ref.at[index], buf))
        stored = {}

        def get(k):
            if pending[k] is not None:
                pending[k].wait()
                pending[k] = None
            return buffers[k]

        def put(k, part=None):
            src, dst = big_buffers[k], big_refs[k]
            if part is not None:
                src, dst = src.at[part], dst.at[part]
            stored.setdefault(k, []).append(loads.start(src, dst))

        body(info_ref, small_refs, get, raw_refs, out_refs, big_buffers, put, rest, loads)
        for k in range(n_large):
            get(k)
        for k in range(n_big):
            if k not in stored:
                put(k)
        wait([c for copies in stored.values() for c in copies])

    hbm = pl.BlockSpec(memory_space=pltpu.HBM)
    vmem = pl.BlockSpec(memory_space=pltpu.VMEM)
    return pl.pallas_call(
        kernel,
        out_shape=[jax.ShapeDtypeStruct(s, d) for s, d in (*outs, *big_outs)],
        in_specs=[pl.BlockSpec(memory_space=pltpu.SMEM)] + [vmem] * n_small + [hbm] * (n_large + n_raw),
        out_specs=[vmem] * n_out + [hbm] * n_big,
        scratch_shapes=[pltpu.VMEM(shape_of(a, i), a.dtype) for a, i in large]
        + [pltpu.VMEM(s, d) for s, d in big_outs]
        + [pltpu.SemaphoreType.DMA((max(1, n_large + n_big + copies),))]
        + list(scratch),
        compiler_params=pltpu.CompilerParams(vmem_limit_bytes=LIMIT * MIB),
        cost_estimate=pl.CostEstimate(
            flops=0, bytes_accessed=int(us * 1e3), transcendentals=0),
    )(info, *small, *[a for a, _ in large], *raw)


def natural(me, rows):
    return lambda m: pl.multiple_of(jnp.bitwise_xor(me, m) * rows, rows)


def dot_nn(a, b):
    return jnp.dot(a, b, preferred_element_type=f32)


def dot_nt(a, b):
    return lax.dot_general(a, b, (((1,), (1,)), ((), ())), preferred_element_type=f32)


def dot_tn(a, b):
    return lax.dot_general(a, b, (((0,), (0,)), ((), ())), preferred_element_type=f32)


def norm(rows):
    centre = rows - jnp.mean(rows, axis=-1, keepdims=True)
    inverse = lax.rsqrt(jnp.mean(centre * centre, axis=-1, keepdims=True) + epsilon)
    return centre * inverse, inverse


def norm_back(d, unit, inverse, gain):
    q = d * gain
    return inverse * (
        q
        - jnp.mean(q, axis=-1, keepdims=True)
        - unit * jnp.mean(q * unit, axis=-1, keepdims=True)
    )


def down_one(rows, entering):
    at = lax.broadcasted_iota(jnp.int32, rows.shape, 0)
    return jnp.where(at == 0, entering, pltpu.roll(rows, 1, 0))


def up_one(rows, entering):
    at = lax.broadcasted_iota(jnp.int32, rows.shape, 0)
    last = rows.shape[0] - 1
    return jnp.where(at == last, entering, pltpu.roll(rows, last, 0))


def fold(rows):
    total = rows[:8]
    for k in range(8, rows.shape[0], 8):
        total = total + rows[k : k + 8]
    return total


def columns(width, step):
    step = min(step, width)

    def run(body):
        @pl.loop(0, width // step)
        def _(n):
            body(pl.ds(pl.multiple_of(n * step, step), step))

    return run


def row_chunk(b, i, length):
    return pl.ds(pl.multiple_of(b * length + i * ROWS, ROWS), ROWS)


def two_part(mat, value):
    hi = value.astype(bf16)
    lo = (value - hi.astype(f32)).astype(bf16)
    return dot_nn(mat, hi) + dot_nn(mat, lo)


def triangle(length, strictly_before):
    row = lax.broadcasted_iota(jnp.int32, (length, length), 0)
    col = lax.broadcasted_iota(jnp.int32, (length, length), 1)
    keep = (col < row) if strictly_before else (col > row)
    return keep.astype(f32).astype(bf16)


def column_sums(out_ref, sum_ref):
    for k in range(sum_ref.shape[0]):
        out_ref[k : k + 1, :] = jnp.sum(sum_ref[k], axis=0, keepdims=True)


def pack(parts_a, parts_b, vectors, width):
    arrays = [p[0] for p in (*parts_a, *parts_b) if p[0] is not None]
    shard = vectors[0].shape[0]

    def kernel(*refs):
        vec_refs, ins = refs[: len(vectors)], refs[len(vectors) : len(vectors) + len(arrays)]
        outs, (table, sems) = refs[len(vectors) + len(arrays) : -2], refs[-2:]
        copies, n = [], 0
        for out, parts in zip(outs, (parts_a, parts_b)):
            at = 0
            for array, first, count in parts:
                if array is None:
                    spot = (out, at)
                else:
                    copies.append(pltpu.make_async_copy(
                        ins[n].at[pl.ds(first, count)], out.at[pl.ds(at, count)], sems.at[n]))
                    copies[-1].start()
                    n += 1
                at += count
        table[...] = jnp.zeros_like(table)
        for k, ref in enumerate(vec_refs):
            table[k : k + 1, :shard] = ref[...].astype(f32)
        spot[0][spot[1] : spot[1] + 16, :] = table[...].astype(bf16)
        wait(copies)

    return pl.pallas_call(
        kernel,
        out_shape=[jax.ShapeDtypeStruct((sum(p[2] for p in parts), width), bf16)
                   for parts in (parts_a, parts_b)],
        in_specs=[pl.BlockSpec(memory_space=pltpu.VMEM)] * len(vectors)
        + [pl.BlockSpec(memory_space=pltpu.HBM)] * len(arrays),
        out_specs=[pl.BlockSpec(memory_space=pltpu.VMEM)] * 2,
        scratch_shapes=[pltpu.VMEM((16, width), f32), pltpu.SemaphoreType.DMA((len(arrays),))],
        compiler_params=pltpu.CompilerParams(vmem_limit_bytes=LIMIT * MIB),
        cost_estimate=pl.CostEstimate(flops=0, bytes_accessed=1000, transcendentals=0),
    )(*[x.reshape(1, shard) for x in vectors], *arrays)


def pack_wide(key, recept):
    rows, wide = key.shape
    width = recept.shape[1]
    each = recept.shape[0] * width // wide
    half = (rows + each) // 32 * 16

    def kernel(key_ref, recept_ref, top_ref, low_ref, sems):
        copies = [
            pltpu.make_async_copy(key_ref.at[pl.ds(0, half)], top_ref, sems.at[0]),
            pltpu.make_async_copy(
                key_ref.at[pl.ds(half, rows - half)], low_ref.at[pl.ds(0, rows - half)], sems.at[1])]
        for q in range(wide // width):
            copies.append(pltpu.make_async_copy(
                recept_ref.at[pl.ds(q * each, each)],
                low_ref.at[pl.ds(rows - half, each), pl.ds(q * width, width)], sems.at[2 + q]))
        for c in copies:
            c.start()
        wait(copies)

    return pl.pallas_call(
        kernel,
        out_shape=[jax.ShapeDtypeStruct((n, wide), bf16) for n in (half, rows + each - half)],
        in_specs=[pl.BlockSpec(memory_space=pltpu.HBM)] * 2,
        out_specs=[pl.BlockSpec(memory_space=pltpu.VMEM)] * 2,
        scratch_shapes=[pltpu.SemaphoreType.DMA((2 + wide // width,))],
        compiler_params=pltpu.CompilerParams(vmem_limit_bytes=LIMIT * MIB),
        cost_estimate=pl.CostEstimate(flops=0, bytes_accessed=1000, transcendentals=0),
    )(key, recept)


def recept_blocks(loads, steps, raw, w, info, shard, width, wide):
    each = shard * width // wide
    place = natural(info[0], shard)
    return [
        loads.start(raw[piece].at[pl.ds(row, count), pl.ds(q * width, width)],
                    w.at[pl.ds(place(m) + q * each + within, count)])
        for piece, row, count, m, within in steps
        for q in range(wide // width)
    ]


def time_in(info, stream, last, previous, given, pieces, spots, length, shard):
    tokens, width = stream.shape
    batches = tokens // length
    plans = [plan(pieces, spots[k], shard) for k in "kvr"]
    vplan = plan(pieces, spots["vec"], 16)
    order = relative_order()

    def body(info, small, get, raw, outs, big, put, scratch, loads):
        last_ref, prev_ref = small[:2]
        sum_ref, vec_ref, entry_ref = outs
        in_ref = big[0]
        w, vt = scratch
        place = natural(info[0], shard)
        vcopies = loads.pieces(vplan, raw, vt, lambda m: order.index(m) * 16)
        copies = [loads.pieces(plans[k], raw, w.at[k], place) for k in range(3)]
        wait(vcopies)
        if given is not None:
            vec_ref[...] = small[2][...]
        else:
            for at, m in enumerate(order):
                vec_ref[:, pl.ds(place(m), shard)] = vt[at * 16 : at * 16 + 16, :shard].astype(f32)
        unit, _ = norm(last_ref[...].astype(f32))
        edge = unit * vec_ref[G1 : G1 + 1] + vec_ref[B1 : B1 + 1]
        for b in range(batches):
            entry_ref[b : b + 1, :] = jnp.where(info[1] == 1, prev_ref[b], edge[b : b + 1])
        stream_ref = get(0)

        for b in range(batches):
            def step(i, before):
                r = row_chunk(b, i, length)
                na, _ = norm(stream_ref[r, :].astype(f32))
                xa = na * vec_ref[G1 : G1 + 1] + vec_ref[B1 : B1 + 1]
                xs = down_one(xa, before)
                for k, row in enumerate((MK, MV, MR)):
                    mix = vec_ref[row : row + 1]
                    in_ref[k, r, :] = (xa * mix + xs * (1.0 - mix)).astype(bf16)
                return xa[ROWS - 1 :]
            lax.fori_loop(0, length // ROWS, step, entry_ref[b : b + 1])
        put(0)
        def project(k):
            wait(copies[k])
            @columns(width, STEP)
            def _(n):
                big[1 + k][:, n] = dot_nn(in_ref[k], w[k, :, n]).astype(big[1 + k].dtype)
            put(1 + k)
        project(0)
        project(1)
        keys_ref, vals_ref = big[1], big[2]
        for b in range(batches):
            t = slice(b * length, (b + 1) * length)
            @columns(width, LANES)
            def _(n):
                rate = -jnp.exp(vec_ref[DECAY : DECAY + 1, n])
                at = lax.broadcasted_iota(jnp.int32, (length, 1), 0).astype(f32)
                shifted = keys_ref[t, n] - at * rate
                peak = jnp.max(shifted, axis=0, keepdims=True)
                factor = jnp.exp(shifted - peak)
                sum_ref[b : b + 1, n] = jnp.sum(
                    factor * vals_ref[t, n].astype(f32), axis=0, keepdims=True)
                sum_ref[batches + b : batches + b + 1, n] = jnp.sum(factor, axis=0, keepdims=True)
                sum_ref[2 * batches + b : 2 * batches + b + 1, n] = peak + (length - 1.0) * rate
        project(2)

    extra = [] if given is None else [given]
    return call(
        body, info, [last, previous, *extra], [(stream, None)], flat_pieces(pieces),
        [((3 * batches, width), f32), ((16, width), f32), ((batches, width), f32)],
        [((3, tokens, width), bf16), ((tokens, width), f32)] + [((tokens, width), bf16)] * 2,
        [pltpu.VMEM((3, width, width), bf16), pltpu.VMEM((16 * len(order), width), bf16)],
        len(vplan) + sum(map(len, plans)), 9, 40)


def wkv_terms(kvr_ref, ent_ref, vec_ref, b, t, n, batches, length):
    rate = -jnp.exp(vec_ref[DECAY : DECAY + 1, n])
    at = lax.broadcasted_iota(jnp.int32, (length, 1), 0).astype(f32)
    keys = kvr_ref[0][t, n]
    shifted = keys - at * rate
    peak = jnp.max(shifted, axis=0, keepdims=True)
    factor = jnp.exp(shifted - peak)
    near = (at - 1.0) * rate + peak
    opening = at * rate + ent_ref[2 * batches + b : 2 * batches + b + 1, n]
    reward = vec_ref[FIRST : FIRST + 1, n] + keys
    top = jnp.maximum(jnp.maximum(near, opening), reward)
    return at, factor, jnp.exp(near - top), jnp.exp(opening - top), jnp.exp(reward - top)


def time_out(info, kvr, everyone, state, vec, stream, pieces, spots, length, shard):
    tokens, width = stream.shape
    batches = tokens // length
    stretches = len(everyone)
    relative = isinstance(everyone, list)
    if not relative:
        everyone = [everyone]
    steps = plan(pieces, spots["o"], shard)

    def body(info, small, get, raw, outs, big, put, scratch, loads):
        every_ref, (num_ref, den_ref, exp_ref, vec_ref) = small[:-4], small[-4:]
        if not relative:
            every_ref = [every_ref[0].at[z] for z in range(stretches)]
        ent_ref, mean_ref, log_ref, edge_ref = outs
        gated_ref, wkv_ref, rden_ref, mid_ref, xb_ref = big
        (w,) = scratch
        copies = loads.pieces(steps, raw, w, natural(info[0], shard))
        span = -jnp.exp(vec_ref[DECAY : DECAY + 1, :]) * float(length)

        def merge(upto, b):
            upto_f = upto.astype(f32) if upto is not stretches else float(stretches)
            logits = []
            for j in range(stretches):
                row, z = 2 * batches + b, jnp.bitwise_xor(info[2], j) if relative else jnp.int32(j)
                logit = every_ref[j][row : row + 1, :] + (upto_f - 1.0 - z.astype(f32)) * span
                logits.append(logit if upto is stretches else jnp.where(z < upto, logit, -jnp.inf))
            opening = exp_ref[b] + upto_f * span
            top = opening
            for logit in logits:
                top = jnp.maximum(top, logit)
            start = jnp.exp(opening - top)
            num, den = num_ref[b] * start, den_ref[b] * start
            for j, logit in enumerate(logits):
                weight = jnp.exp(logit - top)
                num = num + weight * every_ref[j][b : b + 1, :]
                den = den + weight * every_ref[j][batches + b : batches + b + 1, :]
            return num, den, top

        for b in range(batches):
            for k, part in enumerate(merge(info[2], b)):
                ent_ref[k * batches + b : k * batches + b + 1, :] = part
            num, den, top = merge(stretches, b)
            mean_ref[b] = num / den
            log_ref[b] = top + jnp.log(den)

        lower = triangle(length, True)
        kvr_ref = [get(k) for k in range(3)]
        for b in range(batches):
            t = slice(b * length, (b + 1) * length)
            @columns(width, LANES)
            def _(n):
                _, factor, p, o, e = wkv_terms(kvr_ref, ent_ref, vec_ref, b, t, n, batches, length)
                vals = kvr_ref[1][t, n].astype(f32)
                num = (two_part(lower, factor * vals) * p
                       + ent_ref[b : b + 1, n] * o + vals * e)
                den = (two_part(lower, factor) * p
                       + ent_ref[batches + b : batches + b + 1, n] * o + e)
                rden = 1.0 / den
                wkv = num * rden
                wkv_ref[t, n] = wkv.astype(bf16)
                rden_ref[t, n] = rden.astype(bf16)
                gated_ref[t, n] = (jax.nn.sigmoid(kvr_ref[2][t, n].astype(f32)) * wkv).astype(bf16)
        put(0)
        put(1)
        put(2)
        wait(copies)
        stream_ref = get(3)
        @columns(width, STEP)
        def _(n):
            mid_ref[:, n] = stream_ref[:, n].astype(f32) + dot_nn(gated_ref[...], w[:, n])
        put(3)
        @pl.loop(0, tokens // ROWS)
        def _(i):
            r = row_chunk(0, i, 0)
            nb, _ = norm(mid_ref[r, :])
            xb_ref[r, :] = (nb * vec_ref[G2 : G2 + 1] + vec_ref[B2 : B2 + 1]).astype(bf16)
        for b in range(batches):
            last = (b + 1) * length
            edge_ref[b : b + 1, :] = xb_ref[last - 16 : last, :].astype(f32)[15:]

    one, low = ((tokens, width), f32), ((tokens, width), bf16)
    return call(
        body, info, [*everyone, *state, vec], [(a, None) for a in (*kvr, stream)], flat_pieces(pieces),
        [((3 * batches, width), f32), ((batches, 1, width), f32), ((batches, 1, width), f32),
         ((batches, width), f32)],
        [low, low, low, one, low],
        [pltpu.VMEM((width, width), bf16)], len(steps), 7, 40)


def key_blocks(loads, steps, raw, w, info, shard, fshard, wanted):
    order = relative_order()
    place = natural(info[0], shard)
    out = {}
    for m in wanted:
        cols = pl.ds(natural(info[0], fshard)(m), fshard)
        out[m] = [
            loads.start(raw[piece].at[pl.ds(row, count), cols],
                        w.at[pl.ds(place(m2) + within, count), pl.ds(order.index(m) * fshard, fshard)])
            for piece, row, count, m2, within in steps
        ]
    return out


def value_blocks(loads, raw, w, fshard, stretches):
    order = relative_order()
    others = [m for m in order if m % 2 == 0 and m]
    each = fshard // stretches
    out = {}
    for at, m in enumerate(order):
        own, gathered = raw[2 * (m % 2)], raw[2 * (m % 2) + 1]
        base = m - m % 2
        if base == 0:
            out[m] = [loads.start(own, w.at[pl.ds(at * fshard, fshard)])]
            continue
        out[m] = [
            loads.start(
                gathered.at[pl.ds((z * len(others) + others.index(base)) * each, each)],
                w.at[pl.ds(at * fshard + z * each, each)])
            for z in range(stretches)
        ]
    return out


def value_copies(stretches):
    count = lax.axis_size("seg")
    return 2 + (count - 2) * stretches


def chan_in(info, xb, edge, previous, vec, pieces_ck, length, shard, fshard):
    tokens, width = xb.shape
    batches = tokens // length
    order = relative_order()
    wide = fshard * len(order)
    steps_k = plan(pieces_ck, 0, shard)
    steps_c = plan(pieces_ck, shard, shard * width // wide)

    def body(info, small, get, raw, outs, big, put, scratch, loads):
        edge_ref, prev_ref, vec_ref = small
        (entry_ref,) = outs
        in_ref, near_ref, far_ref, act_ref, frec_ref = big
        wk, wc = scratch
        half = len(order) // 2
        turn = order[half:] + order[:half]
        blocks = key_blocks(loads, steps_k, raw, wk, info, shard, fshard, turn)
        copies_c = recept_blocks(loads, steps_c, raw, wc, info, shard, width, wide)
        for b in range(batches):
            entry_ref[b : b + 1, :] = jnp.where(info[1] == 1, prev_ref[b], edge_ref[b : b + 1, :])
        xb_ref = get(0)
        for b in range(batches):
            def step(i, before):
                r = row_chunk(b, i, length)
                x = xb_ref[r, :].astype(f32)
                xt = down_one(x, before)
                for k, row in enumerate((CMK, CMR)):
                    mix = vec_ref[row : row + 1]
                    in_ref[k, r, :] = (x * mix + xt * (1.0 - mix)).astype(bf16)
                return x[ROWS - 1 :]
            lax.fori_loop(0, length // ROWS, step, entry_ref[b : b + 1])
        put(0)
        for m in turn:
            wait(blocks[m])
            at = order.index(m)
            hid_ref, lo = (near_ref, at * fshard) if at < half else (far_ref, (at - half) * fshard)
            act = jnp.maximum(dot_nn(in_ref[0], wk[:, at * fshard : (at + 1) * fshard]), 0.0)
            act_ref[:, at * fshard : (at + 1) * fshard] = act.astype(bf16)
            hid_ref[:, lo : lo + fshard] = (act * act).astype(bf16)
            if m == turn[half - 1]:
                put(2)
        put(1)
        put(3)
        wait(copies_c)
        @columns(width, STEP)
        def _(n):
            frec_ref[:, n] = dot_nn(in_ref[1], wc[:, n]).astype(bf16)

    return call(
        body, info, [edge, previous, vec], [(xb, None)], flat_pieces(pieces_ck),
        [((batches, width), f32)],
        [((2, tokens, width), bf16), ((tokens, wide // 2), bf16), ((tokens, wide // 2), bf16),
         ((tokens, wide), bf16), ((tokens, width), bf16)],
        [pltpu.VMEM((width, wide), bf16), pltpu.VMEM((width, width), bf16)],
        len(steps_c) * (wide // width) + len(steps_k) * len(order), 11, 40)


def chan_out(info, near, far, frec, mid, cot, cv, fshard):
    tokens, width = mid.shape
    order = relative_order()
    wide = fshard * len(order)
    stretches = lax.axis_size("stretch")

    def body(info, small, get, raw, outs, big, put, scratch, loads):
        out_ref, df_ref, dr_ref = big
        w, fval = scratch
        blocks = value_blocks(loads, raw, w, fshard, stretches)
        half = len(order) // 2
        for k in range(2):
            hid_ref = get(k)
            for m in order[k * half : (k + 1) * half]:
                wait(blocks[m])
            @columns(width, STEP)
            def _(n):
                part = dot_nn(hid_ref[...], w[k * wide // 2 : (k + 1) * wide // 2, n])
                fval[:, n] = part if k == 0 else fval[:, n] + part
        frec_ref, mid_ref, cot_ref = get(2), get(3), get(4)
        @pl.loop(0, tokens // ROWS)
        def _(i):
            r = row_chunk(0, i, 0)
            sig = jax.nn.sigmoid(frec_ref[r, :].astype(f32))
            cots, value = cot_ref[r, :].astype(f32), fval[r, :]
            df_ref[r, :] = (cots * sig).astype(bf16)
            out_ref[r, :] = (mid_ref[r, :] + sig * value).astype(bf16)
            dr_ref[r, :] = (cots * value * sig * (1.0 - sig)).astype(bf16)

    low = ((tokens, width), bf16)
    return call(
        body, info, [], [(a, None) for a in (near, far, frec, mid, cot)], cv, [], [low, low, low],
        [pltpu.VMEM((wide, width), bf16), pltpu.VMEM((tokens, width), f32)],
        value_copies(stretches), 7, 40)


def hidden_back(info, act, dfval, cv, fshard):
    tokens, width = dfval.shape
    order = relative_order()
    wide = fshard * len(order)
    stretches = lax.axis_size("stretch")

    def body(info, small, get, raw, outs, big, put, scratch, loads):
        (dpre_ref,) = big
        (wv,) = scratch
        values = value_blocks(loads, raw, wv, fshard, stretches)
        dfval_ref, act_ref = get(0), get(1)
        for at, m in enumerate(order):
            wait(values[m])
            block = slice(at * fshard, (at + 1) * fshard)
            d = dot_nt(dfval_ref[...], wv[block, :]) * (2.0 * act_ref[:, block].astype(f32))
            dpre_ref[:, block] = d.astype(bf16)
            put(0, (slice(None), pl.ds(at * fshard, fshard)))

    return call(
        body, info, [], [(dfval, None), (act, None)], cv, [], [((tokens, wide), bf16)],
        [pltpu.VMEM((wide, width), bf16)], value_copies(stretches) + len(order), 7, 40)[0]


def chan_back(info, dpre, dfrec, xb, entry, vec, pieces_ck, length, shard, fshard):
    tokens, width = xb.shape
    batches = tokens // length
    order = relative_order()
    wide = fshard * len(order)
    steps_k = plan(pieces_ck, 0, shard)
    steps_c = plan(pieces_ck, shard, shard * width // wide)

    def body(info, small, get, raw, outs, big, put, scratch, loads):
        entry_ref, vec_ref = small
        head_ref, total_ref = outs
        dxt_ref, dxb_ref = big
        wk, wc, df, dr, sum_ref = scratch
        copies_c = recept_blocks(loads, steps_c, raw, wc, info, shard, width, wide)
        keys = key_blocks(loads, steps_k, raw, wk, info, shard, fshard, order)
        dfrec_ref = get(0)
        wait(copies_c)
        @columns(width, STEP)
        def _(n):
            dr[:, n] = dot_nt(dfrec_ref[...], wc[n, :])
        dpre_ref = get(1)
        half = len(order) // 2
        for k in range(2):
            for m in order[k * half : (k + 1) * half]:
                wait(keys[m])
            part_of = slice(k * wide // 2, (k + 1) * wide // 2)
            @columns(width, STEP)
            def _(n):
                part = dot_nt(dpre_ref[:, part_of], wk[n, part_of])
                df[:, n] = part if k == 0 else df[:, n] + part
        sum_ref[...] = jnp.zeros_like(sum_ref)
        xb_ref = get(2)
        for b in range(batches):
            def step(i, before):
                r = row_chunk(b, i, length)
                x = xb_ref[r, :].astype(f32)
                gap = x - down_one(x, before)
                a, c = df[r, :], dr[r, :]
                ck, cr = vec_ref[CMK : CMK + 1], vec_ref[CMR : CMR + 1]
                dxt_ref[r, :] = (a * (1.0 - ck) + c * (1.0 - cr)).astype(bf16)
                dxb_ref[r, :] = (a * ck + c * cr).astype(bf16)
                sum_ref[0] += fold(a * gap)
                sum_ref[1] += fold(c * gap)
                return x[ROWS - 1 :]
            lax.fori_loop(0, length // ROWS, step, entry_ref[b : b + 1])
            head_ref[b : b + 1, :] = dxt_ref[b * length : b * length + 16, :].astype(f32)[:1]
        column_sums(total_ref, sum_ref)

    low = ((tokens, width), bf16)
    return call(
        body, info, [entry, vec], [(a, None) for a in (dfrec, dpre, xb)], flat_pieces(pieces_ck),
        [((batches, width), f32), ((2, width), f32)], [low, low],
        [pltpu.VMEM((width, wide), bf16), pltpu.VMEM((width, width), bf16),
         pltpu.VMEM((tokens, width), f32), pltpu.VMEM((tokens, width), f32),
         pltpu.VMEM((2, 8, width), f32)],
        len(steps_c) * (wide // width) + len(steps_k) * len(order), 10, 40)


def mid_back(info, dxt, dxb, after, head, mid, cot, vec, kvr, wkv, rden, ent, pieces, spots, length, shard):
    tokens, width = mid.shape
    batches = tokens // length
    steps = plan(pieces, spots["o"], shard)

    def body(info, small, get, raw, outs, big, put, scratch, loads):
        after_ref, head_ref, vec_ref, ent_ref = small
        dent_ref, total_ref = outs
        dent_ref[2 * batches : 3 * batches, :] = ent_ref[2 * batches :, :]
        dent_ref[3 * batches :, :] = head_ref[...]
        dmid_ref, low_ref, high_ref, rlow_ref, rhigh_ref, gn_ref = big
        w, sum_ref, dgate = scratch
        copies = loads.pieces(steps, raw, w, natural(info[0], shard))
        sum_ref[...] = jnp.zeros_like(sum_ref)
        dxt_ref, dxb_ref, mid_ref, cot_ref = get(0), get(1), get(2), get(3)
        for b in range(batches):
            def step(k, after_row):
                r = row_chunk(b, length // ROWS - 1 - k, length)
                nb, inverse = norm(mid_ref[r, :])
                dx = dxt_ref[r, :].astype(f32)
                d = dxb_ref[r, :].astype(f32) + up_one(dx, after_row)
                back = cot_ref[r, :].astype(f32) + norm_back(d, nb, inverse, vec_ref[G2 : G2 + 1])
                dmid_ref[r, :] = back.astype(bf16)
                low_ref[r, :] = back[:, : width // 2].astype(bf16)
                high_ref[r, :] = back[:, width // 2 :].astype(bf16)
                sum_ref[0] += fold(d * nb)
                sum_ref[1] += fold(d)
                return dx[:1]
            lax.fori_loop(0, length // ROWS, step, after_ref[b : b + 1])
        put(0)
        put(1)
        put(2)
        column_sums(total_ref, sum_ref)
        wait(copies)
        @columns(width, STEP)
        def _(n):
            dgate[:, n] = (dot_nt(low_ref[...], w[n, : width // 2])
                           + dot_nt(high_ref[...], w[n, width // 2 :]))
        kvr_ref = [get(4), None, get(5)]
        wkv_ref, rden_ref = get(6), get(7)
        lanes = min(LANES, width // 2)
        for b, half, q in [(b, h, q) for b in range(batches) for h in range(2)
                           for q in range(width // 2 // lanes)]:
            t = slice(b * length, (b + 1) * length)
            n = slice(half * width // 2 + q * lanes, half * width // 2 + (q + 1) * lanes)
            part, at_half = (rlow_ref, rhigh_ref)[half], slice(q * lanes, (q + 1) * lanes)
            if True:
                _, _, _, o, _ = wkv_terms(kvr_ref, ent_ref, vec_ref, b, t, n, batches, length)
                sig = jax.nn.sigmoid(kvr_ref[2][t, n].astype(f32))
                d = dgate[t, n] * sig
                wkvs = wkv_ref[t, n].astype(f32)
                part[t, at_half] = (d * wkvs * (1.0 - sig)).astype(bf16)
                gn = d * rden_ref[t, n].astype(f32)
                gn_ref[t, n] = gn.astype(bf16)
                go = gn * o
                dent_ref[b : b + 1, n] = jnp.sum(go, axis=0, keepdims=True)
                dent_ref[batches + b : batches + b + 1, n] = -jnp.sum(go * wkvs, axis=0, keepdims=True)

    low, half = ((tokens, width), bf16), ((tokens, width // 2), bf16)
    return call(
        body, info, [after, head, vec, ent], [(a, None) for a in (dxt, dxb, mid, cot, kvr[0], kvr[2], wkv, rden)],
        flat_pieces(pieces), [((4 * batches, width), f32), ((2, width), f32)], [low, half, half, half, half, low],
        [pltpu.VMEM((width, width), bf16), pltpu.VMEM((2, 8, width), f32), pltpu.VMEM((tokens, width), f32)],
        len(steps), 9, 40)


def time_back(info, gn, wkv, kvr, ent, back, sums, state, drec, stream, entry, vec, pieces, spots,
              length, shard):
    tokens, width = stream.shape
    batches = tokens // length
    relative = isinstance(back, list)
    stretches = 4 if relative else len(back)
    if not relative:
        back = [back]
    plans = [plan(pieces, spots[k], shard) for k in "kvr"]

    def body(info, small, get, raw, outs, big, put, scratch, loads):
        back_ref = small[:-7]
        if not relative:
            back_ref = [back_ref[0].at[z] for z in range(stretches)]
        else:
            rows = 4 * batches
            back_ref = [*back_ref[:2], *[back_ref[2].at[pl.ds(k * rows, rows)] for k in range(2)]]
        ent_ref, sums_ref, num_ref, den_ref, exp_ref, entry_ref, vec_ref = small[-7:]
        gnum_ref, gden_ref, gexp_ref, gffn_ref, head_ref, total_ref, extra_ref = outs
        d_ref, dxs_ref, dxa_ref = big
        w, dins, sum_ref, later_ref, loc_ref = scratch
        place = natural(info[0], shard)
        copies = [loads.pieces(plans[k], raw, w.at[k], place) for k in range(3)]
        span = -jnp.exp(vec_ref[DECAY : DECAY + 1, :]) * float(length)
        pos = info[2].astype(f32)
        nums, dens, exps = (slice(k * batches, (k + 1) * batches) for k in range(3))
        zero = jnp.zeros((batches, width), f32)

        def state(ref):
            return jnp.concatenate([ref[b] for b in range(batches)], axis=0)

        later_n = later_d = carry_n = carry_d = grad_n = grad_d = grad_f = zero
        for j in range(stretches):
            there = back_ref[j][exps, :]
            at_z = jnp.bitwise_xor(info[2], j) if relative else jnp.int32(j)
            z = at_z.astype(f32)
            after = at_z > info[2]
            lift = jnp.where(after, jnp.exp(jnp.minimum(
                sums_ref[exps, :] - there + (z - 1.0 - pos) * span, 0.0)), 0.0)
            carry = jnp.where(after, jnp.exp(jnp.minimum(
                ent_ref[exps, :] - there + (z - pos) * span, 0.0)), 0.0)
            raised = jnp.exp(jnp.minimum(state(exp_ref) - there + z * span, 0.0))
            dn, dd = back_ref[j][nums, :], back_ref[j][dens, :]
            grad_f = grad_f + jnp.where(at_z == 0, back_ref[j][3 * batches :, :], 0.0)
            later_n, later_d = later_n + dn * lift, later_d + dd * lift
            carry_n, carry_d = carry_n + dn * carry, carry_d + dd * carry
            grad_n, grad_d = grad_n + dn * raised, grad_d + dd * raised
        later_ref[nums, :], later_ref[dens, :] = later_n, later_d
        grad_e = state(num_ref) * grad_n + state(den_ref) * grad_d
        for b in range(batches):
            gnum_ref[b], gden_ref[b] = grad_n[b : b + 1], grad_d[b : b + 1]
            gexp_ref[b] = grad_e[b : b + 1]
            gffn_ref[b] = grad_f[b : b + 1]
        rate_part = (
            float(length) * (ent_ref[nums, :] * carry_n + ent_ref[dens, :] * carry_d)
            + (length - 1.0) * (later_n * sums_ref[nums, :] + later_d * sums_ref[dens, :]))

        upper = triangle(length, False)
        gn_ref, wkv_ref = get(0), get(1)
        kvr_ref = [get(2), get(3)]
        for b in range(batches):
            t = slice(b * length, (b + 1) * length)
            @columns(width, LANES)
            def _(n):
                at, factor, p, o, e = wkv_terms(kvr_ref, ent_ref, vec_ref, b, t, n, batches, length)
                vals, g = kvr_ref[1][t, n].astype(f32), gn_ref[t, n].astype(f32)
                gd = -g * wkv_ref[t, n].astype(f32)
                direct = e * (g * vals + gd)
                opened = o * (g * ent_ref[b : b + 1, n] + gd * ent_ref[batches + b : batches + b + 1, n])
                rn = two_part(upper, g * p) + later_ref[b : b + 1, n]
                rd = two_part(upper, gd * p) + later_ref[batches + b : batches + b + 1, n]
                chain = factor * (rn * vals + rd)
                d_ref[0, t, n] = (chain + direct).astype(bf16)
                d_ref[1, t, n] = (factor * rn + g * e).astype(bf16)
                loc_ref[b : b + 1, n] = jnp.sum(
                    opened - (at - 1.0) * direct - at * chain, axis=0, keepdims=True)
                loc_ref[batches + b : batches + b + 1, n] = jnp.sum(direct, axis=0, keepdims=True)
        put(0)
        rate_rows = rate_part + loc_ref[:batches, :]
        extra_ref[0:1, :] = jnp.sum(rate_rows, axis=0, keepdims=True) * -jnp.exp(
            vec_ref[DECAY : DECAY + 1, :])
        extra_ref[1:2, :] = jnp.sum(loc_ref[batches:, :], axis=0, keepdims=True)
        for k in range(2):
            wait(copies[k])
            @columns(width, STEP)
            def _(n):
                dins[k, :, n] = dot_nt(d_ref[k], w[k, n, :])
        low_ref, high_ref = get(5), get(6)
        wait(copies[2])
        @columns(width, STEP)
        def _(n):
            dins[2, :, n] = (dot_nt(low_ref[...], w[2, n, : width // 2])
                             + dot_nt(high_ref[...], w[2, n, width // 2 :]))
        sum_ref[...] = jnp.zeros_like(sum_ref)
        stream_ref = get(4)
        for b in range(batches):
            def step(i, before):
                r = row_chunk(b, i, length)
                na, _ = norm(stream_ref[r, :].astype(f32))
                xa = na * vec_ref[G1 : G1 + 1] + vec_ref[B1 : B1 + 1]
                gap = xa - down_one(xa, before)
                dxs = jnp.zeros((ROWS, width), f32)
                dxa = jnp.zeros((ROWS, width), f32)
                for k, row in enumerate((MK, MV, MR)):
                    d, mix = dins[k, r, :], vec_ref[row : row + 1]
                    dxs = dxs + d * (1.0 - mix)
                    dxa = dxa + d * mix
                    sum_ref[k] += fold(d * gap)
                dxs_ref[r, :] = dxs.astype(bf16)
                dxa_ref[r, :] = dxa.astype(bf16)
                return xa[ROWS - 1 :]
            lax.fori_loop(0, length // ROWS, step, entry_ref[b : b + 1])
            head_ref[b : b + 1, :] = dxs_ref[b * length : b * length + 16, :].astype(f32)[:1]
        column_sums(total_ref, sum_ref)

    low = ((tokens, width), bf16)
    return call(
        body, info, [*back, ent, sums, *state, entry, vec],
        [(a, None) for a in (gn, wkv, kvr[0], kvr[1], stream, *drec)], flat_pieces(pieces),
        [((batches, 1, width), f32)] * 4
        + [((batches, width), f32), ((3, width), f32), ((2, width), f32)],
        [((2, tokens, width), bf16), low, low],
        [pltpu.VMEM((3, width, width), bf16), pltpu.VMEM((3, tokens, width), f32),
         pltpu.VMEM((3, 8, width), f32), pltpu.VMEM((2 * batches, width), f32),
         pltpu.VMEM((2 * batches, width), f32)],
        sum(map(len, plans)), 14, 40)


def in_back(info, dxs, dxa, after, dmid, stream, vec, length):
    tokens, width = stream.shape
    batches = tokens // length

    def body(info, small, get, raw, outs, big, put, scratch, loads):
        after_ref, vec_ref = small
        (out_ref,) = big
        (sum_ref,) = scratch
        dxs_ref, dxa_ref, dmid_ref, stream_ref = (get(k) for k in range(4))
        sum_ref[...] = jnp.zeros_like(sum_ref)
        for b in range(batches):
            def step(k, after_row):
                r = row_chunk(b, length // ROWS - 1 - k, length)
                na, inverse = norm(stream_ref[r, :].astype(f32))
                dx = dxs_ref[r, :].astype(f32)
                d = dxa_ref[r, :].astype(f32) + up_one(dx, after_row)
                back = norm_back(d, na, inverse, vec_ref[G1 : G1 + 1])
                out_ref[r, :] = (dmid_ref[r, :].astype(f32) + back).astype(bf16)
                sum_ref[0] += fold(d * na)
                sum_ref[1] += fold(d)
                return dx[:1]
            lax.fori_loop(0, length // ROWS, step, after_ref[b : b + 1])
        column_sums(outs[0], sum_ref)

    return call(
        body, info, [after, vec], [(a, None) for a in (dxs, dxa, dmid, stream)], [],
        [((2, width), f32)], [((tokens, width), bf16)],
        [pltpu.VMEM((2, 8, width), f32)], 0, 6, 40)


def weight_grad(info, arrays, items, layout, us, relative=False, stacked=False, under=()):
    count = lax.axis_size("seg")
    evens = list(range(0, count, 2))
    first = items[0][2]
    lead = first[0] if isinstance(first, list) else first
    tokens, n_wide = arrays[lead[0]].shape[-2:]
    n_wide *= len(first) if isinstance(first, list) else 1
    w = arrays[items[0][0][0]].shape[-1] // {"natural": count, "blocks": len(evens), "joined": len(evens)}[layout]
    pair = 2 if w < 256 else 1
    groups = [evens[1:][k : k + pair] for k in range(0, len(evens) - 1, pair)]
    groups[-1].append(0) if len(groups[-1]) < pair else groups.append([0])
    groups = [g for g in groups if g]
    stretches = lax.axis_size("stretch")
    each_z = w // stretches
    shapes = [(len(evens) * len(items) * w, n_wide)] if stacked else [(len(items) * w, n_wide)] * len(evens)
    shares = [x.shape[0] // len(evens) for x in under]
    if under:
        shapes = [(len(items) * w + sum(shares), n_wide)] * len(evens)

    def body(info, small, get, raw, outs, big, put, scratch, loads):
        x_all, dy_all = scratch
        copies_under, at = [], len(items) * w
        for n, share in enumerate(shares):
            for k in range(len(evens)):
                copies_under.append(loads.start(
                    raw[len(arrays) + n].at[pl.ds(k * share, share)], big[k].at[pl.ds(at, share)]))
            at += share

        def view(spec):
            which, lead = spec
            return raw[which] if lead is None else raw[which].at[lead]

        def columns_of(ref, m):
            if layout == "natural":
                return ref.at[:, pl.ds(natural(info[0], w)(m), w)]
            return ref.at[:, pl.ds(evens.index(m) * w, w)]

        x_loads, dy_loads = {}, {}
        for k, (x, x_sib, dy, dy_sib) in enumerate(items):
            for at, part in ((0, dy), (tokens, dy_sib)):
                if relative:
                    each = n_wide // count
                    for n, m in enumerate(relative_order()):
                        cols = natural(info[0], each)(m if at == 0 else m ^ 1)
                        dy_loads.setdefault(k, []).append(loads.start(
                            view(part).at[:, pl.ds(n * each, each)],
                            dy_all.at[k, pl.ds(at, tokens), pl.ds(cols, each)]))
                    continue
                pieces = part if isinstance(part, list) else [part]
                each = n_wide // len(pieces)
                for n, piece in enumerate(pieces):
                    dy_loads.setdefault(k, []).append(loads.start(
                        view(piece), dy_all.at[k, pl.ds(at, tokens), pl.ds(n * each, each)]))
            for g, ms in enumerate(groups):
                for at, part in ((0, x), (tokens, x_sib)):
                    ref, rows = view(part), pl.ds(at, tokens)
                    if layout == "joined":
                        cols = pl.ds(g * pair * w, len(ms) * w)
                        x_loads.setdefault((k, g), []).append(loads.start(
                            ref.at[:, cols], x_all.at[k, g, rows, pl.ds(0, len(ms) * w)]))
                        continue
                    for n, m in enumerate(ms):
                        x_loads.setdefault((k, g), []).append(loads.start(
                            columns_of(ref, m), x_all.at[k, g, rows, pl.ds(n * w, w)]))

        def need(table, key):
            wait(table.pop(key, ()))

        step = min(512, n_wide)
        for g, ms in enumerate(groups):
            for k in range(len(items)):
                need(x_loads, (k, g))
                for q in range(n_wide // step):
                    need(dy_loads, k)
                    dst = slice(q * step, (q + 1) * step)
                    block = dot_tn(x_all[k, g, :, : len(ms) * w], dy_all[k, :, dst]).astype(bf16)
                    for n, m in enumerate(ms):
                        if not stacked:
                            big[evens.index(m)][k * w : (k + 1) * w, dst] = block[n * w : (n + 1) * w]
                            continue
                        for z in range(stretches):
                            row = ((z * len(evens) + evens.index(m)) * len(items) + k) * each_z
                            big[0][row : row + each_z, dst] = block[n * w + z * each_z : n * w + (z + 1) * each_z]
            if g == 0:
                wait(copies_under)
            for m in ms:
                if not stacked:
                    put(evens.index(m))
                    continue
                rows = len(items) * each_z
                if rows % 16 == 0:
                    for z in range(stretches):
                        put(0, pl.ds((z * len(evens) + evens.index(m)) * rows, rows))

    return call(
        body, info, [], [], [*arrays, *under], [], [(shape, bf16) for shape in shapes],
        [pltpu.VMEM((len(items), len(groups), 2 * tokens, pair * w), bf16),
         pltpu.VMEM((len(items), 2 * tokens, n_wide), bf16)],
        len(items) * (4 + 2 * len(evens) + 2 * count) + len(evens) * (len(under) + stretches), us, 40)


def grad_send(parts):
    return [hop(part, 2 * k) for k, part in enumerate(parts) if k]


def total(terms):
    out = terms[0].astype(f32)
    for t in terms[1:]:
        out = out + t.astype(f32)
    return out


def grad_stack(info, key, recept):
    stretches = lax.axis_size("stretch")
    own, width = recept[0].shape
    each, blocks = own // stretches, key[0].shape[1] // width
    rows = (blocks + 1) * each
    if each % 16:
        wide = total(key).astype(bf16).reshape(stretches, each, blocks, width)
        wide = jnp.swapaxes(wide, 1, 2).reshape(stretches, blocks * each, width)
        narrow = total(recept).astype(bf16).reshape(stretches, each, width)
        return jnp.concatenate([wide, narrow], axis=1).reshape(stretches * rows, width)
    terms = len(key)

    def body(info, small, get, raw, outs, big, put, scratch, loads):
        keys, recepts = scratch
        copies = []
        for z in range(stretches):
            src = pl.ds(z * each, each)
            now = [loads.start(raw[j].at[src], keys.at[j, z]) for j in range(terms)]
            copies.append(now + [loads.start(raw[terms + j].at[src], recepts.at[j, z]) for j in range(terms)])
        for z in range(stretches):
            wait(copies[z])
            for q in range(blocks):
                at = z * rows + q * each
                big[0][at : at + each, :] = total(
                    [keys[j, z, :, q * width : (q + 1) * width] for j in range(terms)]).astype(bf16)
            at = z * rows + blocks * each
            big[0][at : at + each, :] = total([recepts[j, z] for j in range(terms)]).astype(bf16)

    return call(
        body, info, [], [], [*key, *recept], [], [((stretches * rows, width), bf16)],
        [pltpu.VMEM((terms, stretches, each, blocks * width), bf16),
         pltpu.VMEM((terms, stretches, each, width), bf16)],
        stretches * 2 * terms, 4, 24)[0]


def grad_pieces(info, own, got, items, each):
    stretches = lax.axis_size("stretch")
    rows, n_wide = own.shape
    width = each * stretches

    def body(info, small, get, raw, outs, big, put, scratch, loads):
        refs = [get(k) for k in range(1 + len(got))]
        first = items * width
        table = total([r[first : first + 16, :] for r in refs])
        half = n_wide // 2
        table = table[:, :half] + table[:, half:]
        hi = table.astype(bf16)
        lo = (table - hi.astype(f32)).astype(bf16)
        for j in list(range(1, stretches)) + [0]:
            z = jnp.bitwise_xor(info[2], j)
            for k in range(items):
                src = pl.ds(pl.multiple_of(k * width + z * each, each), each)
                big[j][k * each : (k + 1) * each, :] = total([r[src, :] for r in refs]).astype(bf16)
            big[j][items * each :, :half] = hi
            big[j][items * each :, half:] = lo
            put(j)

    return call(
        body, info, [], [(a, None) for a in (own, *got)], [], [],
        [((items * each + 16, n_wide), bf16)] * stretches, [], 0, 3, 24)


def stretch_part(part):
    return lax.psum_scatter(part, "stretch", scatter_dimension=0, tiled=True)


def stretch_items(out, items):
    own = out.shape[0] // items
    return [out[k * own : (k + 1) * own].astype(f32) for k in range(items)]


def vector_rows(table, width):
    me, count = lax.axis_index("seg"), lax.axis_size("seg")
    own = table.shape[1] // count
    table = jnp.pad(table, ((0, 16 - table.shape[0]), (0, 0)))
    rows = []
    for m in range(0, count, 2):
        pair = lax.dynamic_slice_in_dim(table, (me ^ m) // 2 * (2 * own), 2 * own, 1)
        pair = jnp.pad(pair, ((0, 0), (0, width // 2 - 2 * own)))
        hi = pair.astype(bf16)
        rows.append(jnp.concatenate([hi, (pair - hi.astype(f32)).astype(bf16)], axis=1))
    return jnp.concatenate(rows, axis=0)


def vector_read(rows):
    half = rows.shape[1] // 2
    return rows[:, :half].astype(f32) + rows[:, half:].astype(f32)


def vector_own(pair, own):
    second = (lax.axis_index("seg") & 1) != 0
    lo, hi = pair[:, :own], pair[:, own : 2 * own]
    return jnp.where(second, hi, lo) + hop(jnp.where(second, lo, hi), 1)


def vector_finish(table):
    position, count = lax.axis_index("stretch"), lax.axis_size("stretch")
    bit = count // 2
    while bit:
        lo, hi = jnp.split(table, 2, axis=1)
        upper = (position & bit) != 0
        table = jnp.where(upper, hi, lo) + across(jnp.where(upper, lo, hi), bit)
        bit //= 2
    return table


def own_columns(x, me, w):
    ms = [*range(2, lax.axis_size("seg"), 2), 0]
    return jnp.concatenate([lax.dynamic_slice_in_dim(x, (me ^ m) * w, w, 1) for m in ms], axis=1)


def body(
    stream_in, cotangent, previous_mix, previous_ffn, state_num, state_den, state_exp,
    gain_one, bias_one, gain_two, bias_two, mix_key, mix_value, mix_recept,
    time_decay, time_first, chan_mix_key, chan_mix_recept,
    att_key, att_value, att_recept, att_output, chan_key, chan_value, chan_recept,
):
    mine = lax.axis_index("seg")
    position = lax.axis_index("stretch")
    stretches = lax.axis_size("stretch")
    batches, _, length, width = stream_in.shape
    tokens = batches * length
    shard = att_key.shape[0]
    fshard = chan_value.shape[0]
    wide = chan_key.shape[1]
    aligned = shard % 128 == 0
    count = lax.axis_size("seg")
    info = jnp.stack([mine, (position == 0).astype(jnp.int32), position])

    stream = stream_in.reshape(tokens, width)
    cot = cotangent.reshape(tokens, width)
    state = (state_num, state_den, state_exp)
    vectors = [gain_one, bias_one, gain_two, bias_two, mix_key, mix_value, mix_recept,
               time_decay, time_first, chan_mix_key, chan_mix_recept]

    v = Live()
    evens = list(range(0, count, 2))
    spots = {"k": 0, "v": shard, "vec": 2 * shard, "r": 2 * shard + 16, "o": 3 * shard + 16}
    each = fshard // stretches
    v.own_tm = pack(
        [(att_key, 0, shard), (att_value, 0, shard), (None, 0, 16)],
        [(att_recept, 0, shard), (att_output, 0, shard)], vectors, width)
    v.share = lax.dynamic_slice_in_dim(chan_value, position * each, each, 0)
    v.cv = chan_value
    v.last_in = stream_in[:, 0, length - 1]
    v.sync()
    v.shares = lax.all_gather(v.share, "seg", axis=0, tiled=True)
    v.one_tm = first_stage(v.own_tm)
    v.ck = pack_wide(tie(chan_key, *v.own_tm), chan_recept)
    v.tm0 = sibling({0: v.own_tm})
    v.last_in = along(tie(v.last_in, *v.tm0[1]), 1)
    v.sync()
    v.tm6 = second_stage(v.one_tm, v.one_tm)
    v.tm2 = sibling(v.one_tm)
    v.ck0 = sibling({0: v.ck})
    gathered_cv = lax.all_gather(
        jnp.concatenate([lax.dynamic_slice_in_dim(v.shares, (mine ^ m) * each, each, 0) for m in evens[1:]], axis=0),
        "stretch", axis=0, tiled=True)
    v.sync()
    v.tm6_sib = sibling(v.tm6)
    v.sync()

    v.one_ck = first_stage(v.ck)
    tm = {0: v.own_tm, **v.one_tm, **v.tm6, **v.tm0, **v.tm2, **v.tm6_sib}
    given = None
    if not aligned:
        given = lax.all_gather(jnp.stack(vectors), "seg", axis=1, tiled=True).astype(f32)
        given = jnp.pad(given, ((0, 5), (0, 0)))
    v.sums, v.vec, v.entry, v.kvr_in, *v.kvr = time_in(
        info, stream, v.last_in, previous_mix, given, tm, spots, length, shard)
    v.everyone = lax.all_gather(v.sums, "stretch")
    v.tm = tm
    v.drop("own_tm", "one_tm", "tm6", "tm0", "tm2", "tm6_sib", "share", "shares")
    v.sync()

    v.ck6 = second_stage(v.one_ck, v.one_ck)
    v.ent, v.mean, v.log, v.edge_b, v.gated, v.wkv, v.rden, v.mid, v.xb = time_out(
        info, v.kvr, v.everyone, state, v.vec, stream, v.tm, spots, length, shard)
    first_far = far_bits()[0]
    v.ck2 = sibling({first_far: v.one_ck[first_far]})
    v.edge_b = along(v.edge_b, 1)
    v.drop("everyone")
    v.sync()
    v.ck2 = {**v.ck2, **sibling({m: p for m, p in v.one_ck.items() if m != first_far})}
    v.all_ck = {0: v.ck, **v.one_ck, **v.ck6, **v.ck0, **v.ck2, **sibling(v.ck6)}
    v.gathered_cv = gathered_cv
    v.drop("ck", "one_ck", "ck6", "ck0", "ck2")
    v.sync()

    v.entry_b, v.f_in, v.near, v.far, v.act, v.frec = chan_in(
        info, v.xb, v.edge_b, previous_ffn, v.vec, v.all_ck, length, shard, fshard)
    v.all_cv = [v.cv, v.gathered_cv, hop(v.cv, 1), hop(v.gathered_cv, 1)]
    v.drop("cv", "gathered_cv")
    v.sync()
    v.block_out, v.d_fval, v.d_frec = chan_out(
        info, v.near, v.far, v.frec, v.mid, cot, v.all_cv, fshard)
    v.far_sib = hop(v.far, 1)
    v.f_sib = hop(v.f_in, 1)
    v.g_sib = hop(v.gated, 1)
    v.kvr_sib = hop(v.kvr_in, 1)
    v.drop("frec", "far")
    v.sync()

    def pairs(*arrays):
        if aligned:
            return [a for pair in arrays for a in pair]
        return [own_columns(a, mine, shard) for pair in arrays for a in pair]

    layout = "natural" if aligned else "joined"
    flat = tuple((j, None) for j in range(4))
    arrays = [v.near, v.far_sib, v.d_fval, hop(v.d_fval, 1)]
    v.stack_cv = weight_grad(info, arrays, [flat], "blocks", 6, stacked=True)[0]
    v.dfrec_sib = hop(v.d_frec, 1)
    v.drop("near", "far_sib")
    v.sync()

    z_cv = stretch_part(v.stack_cv)
    v.dpre = hidden_back(info, v.act, v.d_fval, v.all_cv, fshard)
    d_frec = tie(v.d_frec, v.dpre)
    if aligned:
        v.parts_c = weight_grad(
            info, [v.f_in, v.f_sib, d_frec, v.dfrec_sib], [((0, 1), (1, 1), (2, None), (3, None))], layout, 3)
    else:
        v.parts_c = weight_grad(
            info, [*pairs((v.f_in[1], v.f_sib[1])), d_frec, v.dfrec_sib], [flat], layout, 3)
    v.got_c = grad_send(v.parts_c)
    dpre_sib = hop(v.dpre, 1)
    v.head_b, v.sums_c, v.dxt, v.dxb = chan_back(
        info, v.dpre, v.d_frec, v.xb, v.entry_b, v.vec, v.all_ck, length, shard, fshard)
    v.next_b = along(v.head_b, -1)
    dpre = tie(v.dpre, v.dxt)
    if aligned:
        v.parts_ck = weight_grad(
            info, [v.f_in, v.f_sib, dpre, dpre_sib], [((0, 0), (1, 0), (2, None), (3, None))], layout, 7, True)
    else:
        v.parts_ck = weight_grad(
            info, [*pairs((v.f_in[0], v.f_sib[0])), dpre, dpre_sib], [flat], layout, 7, True)
    v.drop("all_ck", "all_cv", "xb", "entry_b", "act", "d_fval", "dpre", "stack_cv")
    v.sync()

    v.got_ck = grad_send(v.parts_ck)
    backs, v.sums_m, v.dmid, *lows, gn = mid_back(
        info, v.dxt, v.dxb, v.next_b, v.head_b, v.mid, cot, v.vec, v.kvr, v.wkv, v.rden, v.ent, v.tm, spots,
        length, shard)
    v.dbr, v.drec = lows[:2], lows[2:]
    back = exchange_two(backs)
    *v.grads, v.head_a, v.sums_t, v.extra, v.d_kv, v.dxs, v.dxa = time_back(
        info, gn, v.wkv, v.kvr, v.ent, back, v.sums, state, v.drec, stream, v.entry, v.vec,
        v.tm, spots, length, shard)
    v.dbr_sib = [hop(a, 1) for a in v.dbr]
    v.drec_sib = [hop(a, 1) for a in v.drec]
    dys = [([(at, None), (at + 1, None)], [(at + 2, None), (at + 3, None)]) for at in (0, 4)]
    lows = [*v.dbr, *v.dbr_sib, *v.drec, *v.drec_sib]
    gated = tie(v.gated, v.d_kv)
    if aligned:
        v.parts_or = weight_grad(
            info, [*lows, gated, v.g_sib, v.kvr_in, v.kvr_sib],
            [((8, None), (9, None), *dys[0]), ((10, 2), (11, 2), *dys[1])], layout, 6, stacked=True)
    else:
        xs = pairs((gated, v.g_sib), (v.kvr_in[2], v.kvr_sib[2]))
        v.parts_or = weight_grad(
            info, [*lows, *xs], [((8, None), (9, None), *dys[0]), ((10, None), (11, None), *dys[1])], layout, 6,
            stacked=True)
    v.drop("wkv", "kvr", "ent", "sums", "entry", "tm", "dxt", "dxb", "mid", "rden", "next_b", "head_b")
    v.sync()
    v.dkv_sib = hop(v.d_kv, 1)
    v.next_a = along(v.head_a, -1)
    z_or = stretch_part(v.parts_or[0])
    v.stack = grad_stack(info, [v.parts_ck[0], *v.got_ck], [v.parts_c[0], *v.got_c])
    v.drop("gated", "g_sib", "dbr", "dbr_sib", "drec", "drec_sib", "f_in", "f_sib", "d_frec",
           "parts_ck", "got_ck", "parts_c", "got_c", "parts_or")
    v.z_cv = z_cv
    v.sync()

    v.parts_cv = [v.z_cv[k * each : (k + 1) * each] for k in range(len(evens))]
    z_rest = stretch_part(v.stack)
    v.got_cv = grad_send(v.parts_cv)
    sums_i, v.grad_stream = in_back(info, v.dxs, v.dxa, v.next_a, v.dmid, stream, v.vec, length)
    table = jnp.concatenate([sums_i, v.sums_m, v.sums_t, v.extra, v.sums_c], axis=0)
    under = [vector_rows(table, width)]
    if aligned:
        v.parts_kv = weight_grad(
            info, [v.kvr_in, v.kvr_sib, v.d_kv, v.dkv_sib],
            [tuple((j, k) for j in range(4)) for k in range(2)], layout, 7, under=under)
    else:
        xs = pairs(*[(v.kvr_in[k], v.kvr_sib[k]) for k in range(2)])
        v.parts_kv = weight_grad(
            info, [*xs, v.d_kv, v.dkv_sib],
            [((2 * k, None), (2 * k + 1, None), (4, k), (5, k)) for k in range(2)], layout, 7, under=under)
    v.drop("kvr_in", "kvr_sib", "d_kv", "dkv_sib", "dxs", "dxa", "dmid", "next_a", "stack",
           "sums_m", "sums_t", "extra", "sums_c", "z_cv")
    v.sync()

    v.got_kv = grad_send(v.parts_kv)
    v.heads = lax.all_gather(v.head_a, "stretch")[0]
    v.out_cv = total([v.parts_cv[0], *v.got_cv])
    v.drop("parts_cv", "got_cv")
    v.z_or = z_or
    v.sync()
    rows = shard // stretches
    by_hops = stretches == 4 and rows % 16 == 0
    if by_hops:
        v.pieces = grad_pieces(info, v.parts_kv[0], v.got_kv, 2, rows)
    else:
        whole = total([v.parts_kv[0], *v.got_kv])
        first = 2 * shard
        v.table = vector_read(whole[first:])
        v.part_kv = whole[:first].astype(bf16).reshape(2, stretches, rows, width)
        v.part_kv = jnp.swapaxes(v.part_kv, 0, 1).reshape(first, width)
    parts = [v.z_or[2 * k * rows : 2 * (k + 1) * rows] for k in range(len(evens))]
    v.parts_or = [parts[0], *grad_send(parts)]
    v.drop("parts_kv", "got_kv", "z_or")
    v.sync()
    blocks = wide // width
    out_ck = jnp.concatenate([z_rest[q * rows : (q + 1) * rows] for q in range(blocks)], axis=1).astype(f32)
    out_c = z_rest[blocks * rows : (blocks + 1) * rows].astype(f32)
    if by_hops:
        pieces = [v.pieces[0], *[across(v.pieces[j], j) for j in range(1, stretches)]]
        z_kv = total([p[: 2 * rows] for p in pieces])
        small = sum(vector_read(p[2 * rows : 2 * rows + 11]) for p in pieces)
        small = lax.dynamic_slice_in_dim(vector_own(small, shard), position * rows, rows, 1)
    else:
        z_kv = stretch_part(v.part_kv)
        small = vector_finish(vector_own(v.table[:11], shard))
    out_k, out_v = stretch_items(z_kv, 2)
    out_o, out_r = stretch_items(total(v.parts_or), 2)
    out_cv = v.out_cv
    grad_previous_mix = v.heads
    block_out, grad_stream = v.block_out, v.grad_stream

    shape = stream_in.shape
    return (
        block_out.reshape(shape), grad_stream.reshape(shape), *[small[i] for i in range(11)],
        out_k, out_v, out_r, out_o, out_ck, out_cv, out_c,
        *v.grads[:3], grad_previous_mix[:, None], v.grads[3], v.mean, v.log,
    )


def solution(mesh):
    rows = P(None, "seg", "stretch", None)
    state = P(None, "seg", None)
    both = P(("seg", "stretch"))
    table = P(("seg", "stretch"), None)
    return jax.shard_map(
        body,
        mesh=mesh,
        in_specs=(rows,) * 2 + (state,) * 5 + (P("seg"),) * 11 + (P("seg", None),) * 7,
        out_specs=(rows,) * 2 + (both,) * 11 + (table,) * 7 + (state,) * 7,
        check_vma=False,
    )
```

```python
import jax
import jax.numpy as jnp
from jax import lax
from jax.experimental import pallas as pl
from jax.experimental.pallas import tpu as pltpu
from jax.sharding import PartitionSpec as P

epsilon = 1e-05
bf16 = jnp.bfloat16
f32 = jnp.float32
ROWS = 64
STEP = 512
LANES = 512
LIMIT = 63
MIB = 2**20
G1, B1, G2, B2, MK, MV, MR, DECAY, FIRST, CMK, CMR = range(11)


def hop(value, bit):
    count = lax.axis_size("seg")
    return lax.ppermute(value, "seg", [(i, i ^ bit) for i in range(count)])


def along(value, steps):
    count = lax.axis_size("stretch")
    first, last = (max(0, -steps), min(count, count - steps))
    return lax.ppermute(value, "stretch", [(i, i + steps) for i in range(first, last)])


def across(value, j):
    count = lax.axis_size("stretch")
    return lax.ppermute(value, "stretch", [(i, i ^ j) for i in range(count)])


def exchange(value):
    count = lax.axis_size("stretch")
    if count == 4:
        near, far = across(value, 1), across(value, 2)
        return [value, near, far, across(near, 2)]
    return lax.all_gather(value, "stretch")


def tie(value, *others):
    return lax.optimization_barrier((value, *others))[0]


def exchange_two(value):
    if lax.axis_size("stretch") != 4:
        return lax.all_gather(value, "stretch")
    near = across(value, 1)
    return [value, near, across(jnp.concatenate([value, near], axis=0), 2)]


class Live:
    def __init__(self):
        self.__dict__["held"] = {}

    def __getattr__(self, name):
        return self.held[name]

    def __setattr__(self, name, value):
        self.held[name] = value

    def drop(self, *names):
        for name in names:
            del self.held[name]

    def sync(self):
        self.__dict__["held"] = lax.optimization_barrier(self.held)


def far_bits():
    bits, b = [], 2
    while b < lax.axis_size("seg"):
        bits.append(b)
        b *= 2
    return bits


def relative_order():
    count = lax.axis_size("seg")
    return list(range(0, count, 2)) + list(range(1, count, 2))


def first_stage(own):
    return {b: [hop(part, b) for part in own] for b in far_bits()}


def second_stage(direct, held):
    rest = far_bits()
    held = dict(held)
    for m in sorted(range(0, lax.axis_size("seg"), 2), key=lambda m: (bin(m).count("1"), m)):
        if m == 0 or m in held:
            continue
        bits = [b for b in rest if m & b]
        held[m] = [hop(held[m ^ bits[-1]][0], bits[-1]), hop(held[m ^ bits[0]][1], bits[0])]
    return {m: held[m] for m in held if m not in direct}


def sibling(pieces):
    return {m ^ 1: [hop(p, 1) for p in parts] for m, parts in pieces.items()}


def plan(pieces, first, rows):
    steps, at = [], 0
    for m in relative_order():
        base = 0
        for part in pieces[m]:
            lo, hi = max(first, base), min(first + rows, base + part.shape[0])
            if lo < hi:
                steps.append((at, lo - base, hi - lo, m, lo - first))
            base += part.shape[0]
            at += 1
    return steps


def flat_pieces(pieces):
    return [part for m in relative_order() for part in pieces[m]]


class Loads:
    def __init__(self, sems):
        self.sems, self.used = sems, 0

    def start(self, src, dst):
        copy = pltpu.make_async_copy(src, dst, self.sems.at[self.used])
        self.used += 1
        copy.start()
        return copy

    def pieces(self, steps, refs, target, place):
        return [
            self.start(refs[piece].at[pl.ds(row, count)], target.at[pl.ds(place(m) + within, count)])
            for piece, row, count, m, within in steps
        ]


def wait(copies):
    for c in copies:
        c.wait()


def call(body, info, small, large, raw, outs, big_outs, scratch, copies, us, limit):
    n_small, n_large, n_raw = len(small), len(large), len(raw)
    n_out, n_big = len(outs), len(big_outs)

    def shape_of(array, index):
        return array.shape if index is None else array.shape[1:]

    def kernel(*refs):
        at = 0

        def take(n):
            nonlocal at
            at += n
            return refs[at - n : at]

        (info_ref,), small_refs, large_refs, raw_refs = take(1), take(n_small), take(n_large), take(n_raw)
        out_refs, big_refs = take(n_out), take(n_big)
        buffers, big_buffers, (sems,) = take(n_large), take(n_big), take(1)
        rest = take(len(refs) - at)
        loads = Loads(sems)
        pending = []
        for (array, index), ref, buf in zip(large, large_refs, buffers):
            pending.append(loads.start(ref if index is None else ref.at[index], buf))
        stored = {}

        def get(k):
            if pending[k] is not None:
                pending[k].wait()
                pending[k] = None
            return buffers[k]

        def put(k, part=None):
            src, dst = big_buffers[k], big_refs[k]
            if part is not None:
                src, dst = src.at[part], dst.at[part]
            stored.setdefault(k, []).append(loads.start(src, dst))

        body(info_ref, small_refs, get, raw_refs, out_refs, big_buffers, put, rest, loads)
        for k in range(n_large):
            get(k)
        for k in range(n_big):
            if k not in stored:
                put(k)
        wait([c for copies in stored.values() for c in copies])

    hbm = pl.BlockSpec(memory_space=pltpu.HBM)
    vmem = pl.BlockSpec(memory_space=pltpu.VMEM)
    return pl.pallas_call(
        kernel,
        out_shape=[jax.ShapeDtypeStruct(s, d) for s, d in (*outs, *big_outs)],
        in_specs=[pl.BlockSpec(memory_space=pltpu.SMEM)] + [vmem] * n_small + [hbm] * (n_large + n_raw),
        out_specs=[vmem] * n_out + [hbm] * n_big,
        scratch_shapes=[pltpu.VMEM(shape_of(a, i), a.dtype) for a, i in large]
        + [pltpu.VMEM(s, d) for s, d in big_outs]
        + [pltpu.SemaphoreType.DMA((max(1, n_large + n_big + copies),))]
        + list(scratch),
        compiler_params=pltpu.CompilerParams(vmem_limit_bytes=LIMIT * MIB),
        cost_estimate=pl.CostEstimate(
            flops=0, bytes_accessed=int(us * 1e3), transcendentals=0),
    )(info, *small, *[a for a, _ in large], *raw)


def natural(me, rows):
    return lambda m: pl.multiple_of(jnp.bitwise_xor(me, m) * rows, rows)


def dot_nn(a, b):
    return jnp.dot(a, b, preferred_element_type=f32)


def dot_nt(a, b):
    return lax.dot_general(a, b, (((1,), (1,)), ((), ())), preferred_element_type=f32)


def dot_tn(a, b):
    return lax.dot_general(a, b, (((0,), (0,)), ((), ())), preferred_element_type=f32)


def norm(rows):
    centre = rows - jnp.mean(rows, axis=-1, keepdims=True)
    inverse = lax.rsqrt(jnp.mean(centre * centre, axis=-1, keepdims=True) + epsilon)
    return centre * inverse, inverse


def norm_back(d, unit, inverse, gain):
    q = d * gain
    return inverse * (
        q
        - jnp.mean(q, axis=-1, keepdims=True)
        - unit * jnp.mean(q * unit, axis=-1, keepdims=True)
    )


def down_one(rows, entering):
    at = lax.broadcasted_iota(jnp.int32, rows.shape, 0)
    return jnp.where(at == 0, entering, pltpu.roll(rows, 1, 0))


def up_one(rows, entering):
    at = lax.broadcasted_iota(jnp.int32, rows.shape, 0)
    last = rows.shape[0] - 1
    return jnp.where(at == last, entering, pltpu.roll(rows, last, 0))


def fold(rows):
    total = rows[:8]
    for k in range(8, rows.shape[0], 8):
        total = total + rows[k : k + 8]
    return total


def columns(width, step):
    step = min(step, width)

    def run(body):
        @pl.loop(0, width // step)
        def _(n):
            body(pl.ds(pl.multiple_of(n * step, step), step))

    return run


def row_chunk(b, i, length):
    return pl.ds(pl.multiple_of(b * length + i * ROWS, ROWS), ROWS)


def two_part(mat, value):
    hi = value.astype(bf16)
    lo = (value - hi.astype(f32)).astype(bf16)
    return dot_nn(mat, hi) + dot_nn(mat, lo)


def triangle(length, strictly_before):
    row = lax.broadcasted_iota(jnp.int32, (length, length), 0)
    col = lax.broadcasted_iota(jnp.int32, (length, length), 1)
    keep = (col < row) if strictly_before else (col > row)
    return keep.astype(f32).astype(bf16)


def column_sums(out_ref, sum_ref):
    for k in range(sum_ref.shape[0]):
        out_ref[k : k + 1, :] = jnp.sum(sum_ref[k], axis=0, keepdims=True)


def pack(parts_a, parts_b, vectors, width):
    arrays = [p[0] for p in (*parts_a, *parts_b) if p[0] is not None]
    shard = vectors[0].shape[0]

    def kernel(*refs):
        vec_refs, ins = refs[: len(vectors)], refs[len(vectors) : len(vectors) + len(arrays)]
        outs, (table, sems) = refs[len(vectors) + len(arrays) : -2], refs[-2:]
        copies, n = [], 0
        for out, parts in zip(outs, (parts_a, parts_b)):
            at = 0
            for array, first, count in parts:
                if array is None:
                    spot = (out, at)
                else:
                    copies.append(pltpu.make_async_copy(
                        ins[n].at[pl.ds(first, count)], out.at[pl.ds(at, count)], sems.at[n]))
                    copies[-1].start()
                    n += 1
                at += count
        table[...] = jnp.zeros_like(table)
        for k, ref in enumerate(vec_refs):
            table[k : k + 1, :shard] = ref[...].astype(f32)
        spot[0][spot[1] : spot[1] + 16, :] = table[...].astype(bf16)
        wait(copies)

    return pl.pallas_call(
        kernel,
        out_shape=[jax.ShapeDtypeStruct((sum(p[2] for p in parts), width), bf16)
                   for parts in (parts_a, parts_b)],
        in_specs=[pl.BlockSpec(memory_space=pltpu.VMEM)] * len(vectors)
        + [pl.BlockSpec(memory_space=pltpu.HBM)] * len(arrays),
        out_specs=[pl.BlockSpec(memory_space=pltpu.VMEM)] * 2,
        scratch_shapes=[pltpu.VMEM((16, width), f32), pltpu.SemaphoreType.DMA((len(arrays),))],
        compiler_params=pltpu.CompilerParams(vmem_limit_bytes=LIMIT * MIB),
        cost_estimate=pl.CostEstimate(flops=0, bytes_accessed=1000, transcendentals=0),
    )(*[x.reshape(1, shard) for x in vectors], *arrays)


def pack_wide(key, recept):
    rows, wide = key.shape
    width = recept.shape[1]
    each = recept.shape[0] * width // wide
    half = (rows + each) // 32 * 16

    def kernel(key_ref, recept_ref, top_ref, low_ref, sems):
        copies = [
            pltpu.make_async_copy(key_ref.at[pl.ds(0, half)], top_ref, sems.at[0]),
            pltpu.make_async_copy(
                key_ref.at[pl.ds(half, rows - half)], low_ref.at[pl.ds(0, rows - half)], sems.at[1])]
        for q in range(wide // width):
            copies.append(pltpu.make_async_copy(
                recept_ref.at[pl.ds(q * each, each)],
                low_ref.at[pl.ds(rows - half, each), pl.ds(q * width, width)], sems.at[2 + q]))
        for c in copies:
            c.start()
        wait(copies)

    return pl.pallas_call(
        kernel,
        out_shape=[jax.ShapeDtypeStruct((n, wide), bf16) for n in (half, rows + each - half)],
        in_specs=[pl.BlockSpec(memory_space=pltpu.HBM)] * 2,
        out_specs=[pl.BlockSpec(memory_space=pltpu.VMEM)] * 2,
        scratch_shapes=[pltpu.SemaphoreType.DMA((2 + wide // width,))],
        compiler_params=pltpu.CompilerParams(vmem_limit_bytes=LIMIT * MIB),
        cost_estimate=pl.CostEstimate(flops=0, bytes_accessed=1000, transcendentals=0),
    )(key, recept)


def recept_blocks(loads, steps, raw, w, info, shard, width, wide):
    each = shard * width // wide
    place = natural(info[0], shard)
    sem = loads.sems.at[loads.used]
    loads.used += 1

    @pl.loop(0, wide // width)
    def _(q):
        for piece, row, rows, m, within in steps:
            pltpu.make_async_copy(
                raw[piece].at[pl.ds(row, rows), pl.ds(pl.multiple_of(q * width, width), width)],
                w.at[pl.ds(pl.multiple_of(place(m) + q * each, each) + within, rows)], sem).start()

    return lambda: pltpu.make_async_copy(w, w, sem).wait()


def time_in(info, stream, last, previous, given, pieces, spots, length, shard):
    tokens, width = stream.shape
    batches = tokens // length
    plans = [plan(pieces, spots[k], shard) for k in "kvr"]
    vplan = plan(pieces, spots["vec"], 16)
    order = relative_order()

    def body(info, small, get, raw, outs, big, put, scratch, loads):
        last_ref, prev_ref = small[:2]
        sum_ref, vec_ref, entry_ref = outs
        in_ref = big[0]
        w, vt = scratch
        place = natural(info[0], shard)
        vcopies = loads.pieces(vplan, raw, vt, lambda m: order.index(m) * 16)
        copies = [loads.pieces(plans[k], raw, w.at[k], place) for k in range(3)]
        wait(vcopies)
        if given is not None:
            vec_ref[...] = small[2][...]
        else:
            for at, m in enumerate(order):
                vec_ref[:, pl.ds(place(m), shard)] = vt[at * 16 : at * 16 + 16, :shard].astype(f32)
        unit, _ = norm(last_ref[...].astype(f32))
        edge = unit * vec_ref[G1 : G1 + 1] + vec_ref[B1 : B1 + 1]
        for b in range(batches):
            entry_ref[b : b + 1, :] = jnp.where(info[1] == 1, prev_ref[b], edge[b : b + 1])
        stream_ref = get(0)

        for b in range(batches):
            def step(i, before):
                r = row_chunk(b, i, length)
                na, _ = norm(stream_ref[r, :].astype(f32))
                xa = na * vec_ref[G1 : G1 + 1] + vec_ref[B1 : B1 + 1]
                xs = down_one(xa, before)
                for k, row in enumerate((MK, MV, MR)):
                    mix = vec_ref[row : row + 1]
                    in_ref[k, r, :] = (xa * mix + xs * (1.0 - mix)).astype(bf16)
                return xa[ROWS - 1 :]
            lax.fori_loop(0, length // ROWS, step, entry_ref[b : b + 1])
        put(0)
        def project(k):
            wait(copies[k])
            @columns(width, STEP)
            def _(n):
                big[1 + k][:, n] = dot_nn(in_ref[k], w[k, :, n]).astype(big[1 + k].dtype)
            put(1 + k)
        project(0)
        project(1)
        keys_ref, vals_ref = big[1], big[2]
        for b in range(batches):
            t = slice(b * length, (b + 1) * length)
            @columns(width, LANES)
            def _(n):
                rate = -jnp.exp(vec_ref[DECAY : DECAY + 1, n])
                at = lax.broadcasted_iota(jnp.int32, (length, 1), 0).astype(f32)
                shifted = keys_ref[t, n] - at * rate
                peak = jnp.max(shifted, axis=0, keepdims=True)
                factor = jnp.exp(shifted - peak)
                sum_ref[b : b + 1, n] = jnp.sum(
                    factor * vals_ref[t, n].astype(f32), axis=0, keepdims=True)
                sum_ref[batches + b : batches + b + 1, n] = jnp.sum(factor, axis=0, keepdims=True)
                sum_ref[2 * batches + b : 2 * batches + b + 1, n] = peak + (length - 1.0) * rate
        project(2)

    extra = [] if given is None else [given]
    return call(
        body, info, [last, previous, *extra], [(stream, None)], flat_pieces(pieces),
        [((3 * batches, width), f32), ((16, width), f32), ((batches, width), f32)],
        [((3, tokens, width), bf16), ((tokens, width), f32)] + [((tokens, width), bf16)] * 2,
        [pltpu.VMEM((3, width, width), bf16), pltpu.VMEM((16 * len(order), width), bf16)],
        len(vplan) + sum(map(len, plans)), 9, 40)


def wkv_terms(kvr_ref, ent_ref, vec_ref, b, t, n, batches, length):
    rate = -jnp.exp(vec_ref[DECAY : DECAY + 1, n])
    at = lax.broadcasted_iota(jnp.int32, (length, 1), 0).astype(f32)
    keys = kvr_ref[0][t, n]
    shifted = keys - at * rate
    peak = jnp.max(shifted, axis=0, keepdims=True)
    factor = jnp.exp(shifted - peak)
    near = (at - 1.0) * rate + peak
    opening = at * rate + ent_ref[2 * batches + b : 2 * batches + b + 1, n]
    reward = vec_ref[FIRST : FIRST + 1, n] + keys
    top = jnp.maximum(jnp.maximum(near, opening), reward)
    return at, factor, jnp.exp(near - top), jnp.exp(opening - top), jnp.exp(reward - top)


def time_out(info, kvr, everyone, state, vec, stream, pieces, spots, length, shard):
    tokens, width = stream.shape
    batches = tokens // length
    stretches = len(everyone)
    relative = isinstance(everyone, list)
    if not relative:
        everyone = [everyone]
    steps = plan(pieces, spots["o"], shard)

    def body(info, small, get, raw, outs, big, put, scratch, loads):
        every_ref, (num_ref, den_ref, exp_ref, vec_ref) = small[:-4], small[-4:]
        if not relative:
            every_ref = [every_ref[0].at[z] for z in range(stretches)]
        ent_ref, mean_ref, log_ref, edge_ref = outs
        gated_ref, wkv_ref, rden_ref, mid_ref, xb_ref = big
        (w,) = scratch
        copies = loads.pieces(steps, raw, w, natural(info[0], shard))
        span = -jnp.exp(vec_ref[DECAY : DECAY + 1, :]) * float(length)

        def merge(upto, b):
            upto_f = upto.astype(f32) if upto is not stretches else float(stretches)
            logits = []
            for j in range(stretches):
                row, z = 2 * batches + b, jnp.bitwise_xor(info[2], j) if relative else jnp.int32(j)
                logit = every_ref[j][row : row + 1, :] + (upto_f - 1.0 - z.astype(f32)) * span
                logits.append(logit if upto is stretches else jnp.where(z < upto, logit, -jnp.inf))
            opening = exp_ref[b] + upto_f * span
            top = opening
            for logit in logits:
                top = jnp.maximum(top, logit)
            start = jnp.exp(opening - top)
            num, den = num_ref[b] * start, den_ref[b] * start
            for j, logit in enumerate(logits):
                weight = jnp.exp(logit - top)
                num = num + weight * every_ref[j][b : b + 1, :]
                den = den + weight * every_ref[j][batches + b : batches + b + 1, :]
            return num, den, top

        for b in range(batches):
            for k, part in enumerate(merge(info[2], b)):
                ent_ref[k * batches + b : k * batches + b + 1, :] = part
            num, den, top = merge(stretches, b)
            mean_ref[b] = num / den
            log_ref[b] = top + jnp.log(den)

        lower = triangle(length, True)
        kvr_ref = [get(k) for k in range(3)]
        for b in range(batches):
            t = slice(b * length, (b + 1) * length)
            @columns(width, LANES)
            def _(n):
                _, factor, p, o, e = wkv_terms(kvr_ref, ent_ref, vec_ref, b, t, n, batches, length)
                vals = kvr_ref[1][t, n].astype(f32)
                num = (two_part(lower, factor * vals) * p
                       + ent_ref[b : b + 1, n] * o + vals * e)
                den = (two_part(lower, factor) * p
                       + ent_ref[batches + b : batches + b + 1, n] * o + e)
                rden = 1.0 / den
                wkv = num * rden
                wkv_ref[t, n] = wkv.astype(bf16)
                rden_ref[t, n] = rden.astype(bf16)
                gated_ref[t, n] = (jax.nn.sigmoid(kvr_ref[2][t, n].astype(f32)) * wkv).astype(bf16)
        put(0)
        put(1)
        put(2)
        wait(copies)
        stream_ref = get(3)
        @columns(width, STEP)
        def _(n):
            mid_ref[:, n] = stream_ref[:, n].astype(f32) + dot_nn(gated_ref[...], w[:, n])
        put(3)
        @pl.loop(0, tokens // ROWS)
        def _(i):
            r = row_chunk(0, i, 0)
            nb, _ = norm(mid_ref[r, :])
            xb_ref[r, :] = (nb * vec_ref[G2 : G2 + 1] + vec_ref[B2 : B2 + 1]).astype(bf16)
        for b in range(batches):
            last = (b + 1) * length
            edge_ref[b : b + 1, :] = xb_ref[last - 16 : last, :].astype(f32)[15:]

    one, low = ((tokens, width), f32), ((tokens, width), bf16)
    return call(
        body, info, [*everyone, *state, vec], [(a, None) for a in (*kvr, stream)], flat_pieces(pieces),
        [((3 * batches, width), f32), ((batches, 1, width), f32), ((batches, 1, width), f32),
         ((batches, width), f32)],
        [low, low, low, one, low],
        [pltpu.VMEM((width, width), bf16)], len(steps), 7, 40)


def key_blocks(loads, steps, raw, w, info, shard, fshard, start=0):
    count = lax.axis_size("seg")
    half = count // 2
    place = natural(info[0], shard)
    first = loads.used
    loads.used += count

    @pl.loop(0, count)
    def _(turn):
        at = lax.rem(turn + start, count)
        m = lax.rem(at, half) * 2 + lax.div(at, half)
        cols = pl.ds(natural(info[0], fshard)(m), fshard)
        dst = pl.ds(pl.multiple_of(at * fshard, fshard), fshard)
        for piece, row, rows, m2, within in steps:
            pltpu.make_async_copy(
                raw[piece].at[pl.ds(row, rows), cols], w.at[pl.ds(place(m2) + within, rows), dst],
                loads.sems.at[first + at]).start()

    def arrive(at):
        block = w.at[:, pl.ds(at * fshard, fshard)]
        pltpu.make_async_copy(block, block, loads.sems.at[first + at]).wait()

    return arrive


def value_blocks(loads, raw, w, fshard, stretches):
    order = relative_order()
    others = [m for m in order if m % 2 == 0 and m]
    each = fshard // stretches
    out = {}
    for at, m in enumerate(order):
        own, gathered = raw[2 * (m % 2)], raw[2 * (m % 2) + 1]
        base = m - m % 2
        if base == 0:
            out[m] = [loads.start(own, w.at[pl.ds(at * fshard, fshard)])]
            continue
        out[m] = [
            loads.start(
                gathered.at[pl.ds((z * len(others) + others.index(base)) * each, each)],
                w.at[pl.ds(at * fshard + z * each, each)])
            for z in range(stretches)
        ]
    return out


def value_copies(stretches):
    count = lax.axis_size("seg")
    return 2 + (count - 2) * stretches


def chan_in(info, xb, edge, previous, vec, pieces_ck, length, shard, fshard):
    tokens, width = xb.shape
    batches = tokens // length
    order = relative_order()
    wide = fshard * len(order)
    steps_k = plan(pieces_ck, 0, shard)
    steps_c = plan(pieces_ck, shard, shard * width // wide)

    def body(info, small, get, raw, outs, big, put, scratch, loads):
        edge_ref, prev_ref, vec_ref = small
        (entry_ref,) = outs
        in_ref, near_ref, far_ref, act_ref, frec_ref = big
        wk, wc = scratch
        half = len(order) // 2
        turn = order[half:] + order[:half]
        arrive = key_blocks(loads, steps_k, raw, wk, info, shard, fshard, half)
        arrive_c = recept_blocks(loads, steps_c, raw, wc, info, shard, width, wide)
        for b in range(batches):
            entry_ref[b : b + 1, :] = jnp.where(info[1] == 1, prev_ref[b], edge_ref[b : b + 1, :])
        xb_ref = get(0)
        for b in range(batches):
            def step(i, before):
                r = row_chunk(b, i, length)
                x = xb_ref[r, :].astype(f32)
                xt = down_one(x, before)
                for k, row in enumerate((CMK, CMR)):
                    mix = vec_ref[row : row + 1]
                    in_ref[k, r, :] = (x * mix + xt * (1.0 - mix)).astype(bf16)
                return x[ROWS - 1 :]
            lax.fori_loop(0, length // ROWS, step, entry_ref[b : b + 1])
        put(0)
        for m in turn:
            at = order.index(m)
            arrive(at)
            hid_ref, lo = (near_ref, at * fshard) if at < half else (far_ref, (at - half) * fshard)
            act = jnp.maximum(dot_nn(in_ref[0], wk[:, at * fshard : (at + 1) * fshard]), 0.0)
            act_ref[:, at * fshard : (at + 1) * fshard] = act.astype(bf16)
            hid_ref[:, lo : lo + fshard] = (act * act).astype(bf16)
            if m == turn[half - 1]:
                put(2)
        put(1)
        put(3)
        arrive_c()
        @columns(width, STEP)
        def _(n):
            frec_ref[:, n] = dot_nn(in_ref[1], wc[:, n]).astype(bf16)

    return call(
        body, info, [edge, previous, vec], [(xb, None)], flat_pieces(pieces_ck),
        [((batches, width), f32)],
        [((2, tokens, width), bf16), ((tokens, wide // 2), bf16), ((tokens, wide // 2), bf16),
         ((tokens, wide), bf16), ((tokens, width), bf16)],
        [pltpu.VMEM((width, wide), bf16), pltpu.VMEM((width, width), bf16)],
        1 + len(order), 11, 40)


def chan_out(info, near, far, frec, mid, cot, cv, fshard):
    tokens, width = mid.shape
    order = relative_order()
    wide = fshard * len(order)
    stretches = lax.axis_size("stretch")

    def body(info, small, get, raw, outs, big, put, scratch, loads):
        out_ref, df_ref, dr_ref = big
        w, fval = scratch
        blocks = value_blocks(loads, raw, w, fshard, stretches)
        half = len(order) // 2
        for k in range(2):
            hid_ref = get(k)
            for m in order[k * half : (k + 1) * half]:
                wait(blocks[m])
            @columns(width, STEP)
            def _(n):
                part = dot_nn(hid_ref[...], w[k * wide // 2 : (k + 1) * wide // 2, n])
                fval[:, n] = part if k == 0 else fval[:, n] + part
        frec_ref, mid_ref, cot_ref = get(2), get(3), get(4)
        @pl.loop(0, tokens // ROWS)
        def _(i):
            r = row_chunk(0, i, 0)
            sig = jax.nn.sigmoid(frec_ref[r, :].astype(f32))
            cots, value = cot_ref[r, :].astype(f32), fval[r, :]
            df_ref[r, :] = (cots * sig).astype(bf16)
            out_ref[r, :] = (mid_ref[r, :] + sig * value).astype(bf16)
            dr_ref[r, :] = (cots * value * sig * (1.0 - sig)).astype(bf16)

    low = ((tokens, width), bf16)
    return call(
        body, info, [], [(a, None) for a in (near, far, frec, mid, cot)], cv, [], [low, low, low],
        [pltpu.VMEM((wide, width), bf16), pltpu.VMEM((tokens, width), f32)],
        value_copies(stretches), 7, 40)


def hidden_back(info, act, dfval, cv, fshard):
    tokens, width = dfval.shape
    order = relative_order()
    wide = fshard * len(order)
    stretches = lax.axis_size("stretch")

    def body(info, small, get, raw, outs, big, put, scratch, loads):
        (dpre_ref,) = big
        (wv,) = scratch
        values = value_blocks(loads, raw, wv, fshard, stretches)
        dfval_ref, act_ref = get(0), get(1)
        for at, m in enumerate(order):
            wait(values[m])
            block = slice(at * fshard, (at + 1) * fshard)
            d = dot_nt(dfval_ref[...], wv[block, :]) * (2.0 * act_ref[:, block].astype(f32))
            dpre_ref[:, block] = d.astype(bf16)
            put(0, (slice(None), pl.ds(at * fshard, fshard)))

    return call(
        body, info, [], [(dfval, None), (act, None)], cv, [], [((tokens, wide), bf16)],
        [pltpu.VMEM((wide, width), bf16)], value_copies(stretches) + len(order), 7, 40)[0]


def chan_back(info, dpre, dfrec, xb, entry, vec, pieces_ck, length, shard, fshard):
    tokens, width = xb.shape
    batches = tokens // length
    order = relative_order()
    wide = fshard * len(order)
    steps_k = plan(pieces_ck, 0, shard)
    steps_c = plan(pieces_ck, shard, shard * width // wide)

    def body(info, small, get, raw, outs, big, put, scratch, loads):
        entry_ref, vec_ref = small
        head_ref, total_ref = outs
        dxt_ref, dxb_ref = big
        wk, wc, df, dr, sum_ref = scratch
        arrive_c = recept_blocks(loads, steps_c, raw, wc, info, shard, width, wide)
        arrive = key_blocks(loads, steps_k, raw, wk, info, shard, fshard)
        dfrec_ref = get(0)
        arrive_c()
        @columns(width, STEP)
        def _(n):
            dr[:, n] = dot_nt(dfrec_ref[...], wc[n, :])
        dpre_ref = get(1)
        half = len(order) // 2
        for k in range(2):
            for at in range(k * half, (k + 1) * half):
                arrive(at)
            part_of = slice(k * wide // 2, (k + 1) * wide // 2)
            @columns(width, STEP)
            def _(n):
                part = dot_nt(dpre_ref[:, part_of], wk[n, part_of])
                df[:, n] = part if k == 0 else df[:, n] + part
        sum_ref[...] = jnp.zeros_like(sum_ref)
        xb_ref = get(2)
        for b in range(batches):
            def step(i, before):
                r = row_chunk(b, i, length)
                x = xb_ref[r, :].astype(f32)
                gap = x - down_one(x, before)
                a, c = df[r, :], dr[r, :]
                ck, cr = vec_ref[CMK : CMK + 1], vec_ref[CMR : CMR + 1]
                dxt_ref[r, :] = (a * (1.0 - ck) + c * (1.0 - cr)).astype(bf16)
                dxb_ref[r, :] = (a * ck + c * cr).astype(bf16)
                sum_ref[0] += fold(a * gap)
                sum_ref[1] += fold(c * gap)
                return x[ROWS - 1 :]
            lax.fori_loop(0, length // ROWS, step, entry_ref[b : b + 1])
            head_ref[b : b + 1, :] = dxt_ref[b * length : b * length + 16, :].astype(f32)[:1]
        column_sums(total_ref, sum_ref)

    low = ((tokens, width), bf16)
    return call(
        body, info, [entry, vec], [(a, None) for a in (dfrec, dpre, xb)], flat_pieces(pieces_ck),
        [((batches, width), f32), ((2, width), f32)], [low, low],
        [pltpu.VMEM((width, wide), bf16), pltpu.VMEM((width, width), bf16),
         pltpu.VMEM((tokens, width), f32), pltpu.VMEM((tokens, width), f32),
         pltpu.VMEM((2, 8, width), f32)],
        1 + len(order), 10, 40)


def mid_back(info, dxt, dxb, after, head, mid, cot, vec, kvr, wkv, rden, ent, pieces, spots, length, shard):
    tokens, width = mid.shape
    batches = tokens // length
    steps = plan(pieces, spots["o"], shard)

    def body(info, small, get, raw, outs, big, put, scratch, loads):
        after_ref, head_ref, vec_ref, ent_ref = small
        dent_ref, total_ref = outs
        dent_ref[2 * batches : 3 * batches, :] = ent_ref[2 * batches :, :]
        dent_ref[3 * batches :, :] = head_ref[...]
        dmid_ref, low_ref, high_ref, rlow_ref, rhigh_ref, gn_ref = big
        w, sum_ref, dgate = scratch
        copies = loads.pieces(steps, raw, w, natural(info[0], shard))
        sum_ref[...] = jnp.zeros_like(sum_ref)
        dxt_ref, dxb_ref, mid_ref, cot_ref = get(0), get(1), get(2), get(3)
        for b in range(batches):
            def step(k, after_row):
                r = row_chunk(b, length // ROWS - 1 - k, length)
                nb, inverse = norm(mid_ref[r, :])
                dx = dxt_ref[r, :].astype(f32)
                d = dxb_ref[r, :].astype(f32) + up_one(dx, after_row)
                back = cot_ref[r, :].astype(f32) + norm_back(d, nb, inverse, vec_ref[G2 : G2 + 1])
                dmid_ref[r, :] = back.astype(bf16)
                low_ref[r, :] = back[:, : width // 2].astype(bf16)
                high_ref[r, :] = back[:, width // 2 :].astype(bf16)
                sum_ref[0] += fold(d * nb)
                sum_ref[1] += fold(d)
                return dx[:1]
            lax.fori_loop(0, length // ROWS, step, after_ref[b : b + 1])
        put(0)
        put(1)
        put(2)
        column_sums(total_ref, sum_ref)
        wait(copies)
        @columns(width, STEP)
        def _(n):
            dgate[:, n] = (dot_nt(low_ref[...], w[n, : width // 2])
                           + dot_nt(high_ref[...], w[n, width // 2 :]))
        kvr_ref = [get(4), None, get(5)]
        wkv_ref, rden_ref = get(6), get(7)
        lanes = min(LANES, width // 2)
        for b, half, q in [(b, h, q) for b in range(batches) for h in range(2)
                           for q in range(width // 2 // lanes)]:
            t = slice(b * length, (b + 1) * length)
            n = slice(half * width // 2 + q * lanes, half * width // 2 + (q + 1) * lanes)
            part, at_half = (rlow_ref, rhigh_ref)[half], slice(q * lanes, (q + 1) * lanes)
            if True:
                _, _, _, o, _ = wkv_terms(kvr_ref, ent_ref, vec_ref, b, t, n, batches, length)
                sig = jax.nn.sigmoid(kvr_ref[2][t, n].astype(f32))
                d = dgate[t, n] * sig
                wkvs = wkv_ref[t, n].astype(f32)
                part[t, at_half] = (d * wkvs * (1.0 - sig)).astype(bf16)
                gn = d * rden_ref[t, n].astype(f32)
                gn_ref[t, n] = gn.astype(bf16)
                go = gn * o
                dent_ref[b : b + 1, n] = jnp.sum(go, axis=0, keepdims=True)
                dent_ref[batches + b : batches + b + 1, n] = -jnp.sum(go * wkvs, axis=0, keepdims=True)

    low, half = ((tokens, width), bf16), ((tokens, width // 2), bf16)
    return call(
        body, info, [after, head, vec, ent], [(a, None) for a in (dxt, dxb, mid, cot, kvr[0], kvr[2], wkv, rden)],
        flat_pieces(pieces), [((4 * batches, width), f32), ((2, width), f32)], [low, half, half, half, half, low],
        [pltpu.VMEM((width, width), bf16), pltpu.VMEM((2, 8, width), f32), pltpu.VMEM((tokens, width), f32)],
        len(steps), 9, 40)


def time_back(info, gn, wkv, kvr, ent, back, sums, state, drec, stream, entry, vec, pieces, spots,
              length, shard):
    tokens, width = stream.shape
    batches = tokens // length
    relative = isinstance(back, list)
    stretches = 4 if relative else len(back)
    if not relative:
        back = [back]
    plans = [plan(pieces, spots[k], shard) for k in "kvr"]

    def body(info, small, get, raw, outs, big, put, scratch, loads):
        back_ref = small[:-7]
        if not relative:
            back_ref = [back_ref[0].at[z] for z in range(stretches)]
        else:
            rows = 4 * batches
            back_ref = [*back_ref[:2], *[back_ref[2].at[pl.ds(k * rows, rows)] for k in range(2)]]
        ent_ref, sums_ref, num_ref, den_ref, exp_ref, entry_ref, vec_ref = small[-7:]
        gnum_ref, gden_ref, gexp_ref, gffn_ref, head_ref, total_ref, extra_ref = outs
        d_ref, dxs_ref, dxa_ref = big
        w, dins, sum_ref, later_ref, loc_ref = scratch
        place = natural(info[0], shard)
        copies = [loads.pieces(plans[k], raw, w.at[k], place) for k in range(3)]
        span = -jnp.exp(vec_ref[DECAY : DECAY + 1, :]) * float(length)
        pos = info[2].astype(f32)
        nums, dens, exps = (slice(k * batches, (k + 1) * batches) for k in range(3))
        zero = jnp.zeros((batches, width), f32)

        def state(ref):
            return jnp.concatenate([ref[b] for b in range(batches)], axis=0)

        later_n = later_d = carry_n = carry_d = grad_n = grad_d = grad_f = zero
        for j in range(stretches):
            there = back_ref[j][exps, :]
            at_z = jnp.bitwise_xor(info[2], j) if relative else jnp.int32(j)
            z = at_z.astype(f32)
            after = at_z > info[2]
            lift = jnp.where(after, jnp.exp(jnp.minimum(
                sums_ref[exps, :] - there + (z - 1.0 - pos) * span, 0.0)), 0.0)
            carry = jnp.where(after, jnp.exp(jnp.minimum(
                ent_ref[exps, :] - there + (z - pos) * span, 0.0)), 0.0)
            raised = jnp.exp(jnp.minimum(state(exp_ref) - there + z * span, 0.0))
            dn, dd = back_ref[j][nums, :], back_ref[j][dens, :]
            grad_f = grad_f + jnp.where(at_z == 0, back_ref[j][3 * batches :, :], 0.0)
            later_n, later_d = later_n + dn * lift, later_d + dd * lift
            carry_n, carry_d = carry_n + dn * carry, carry_d + dd * carry
            grad_n, grad_d = grad_n + dn * raised, grad_d + dd * raised
        later_ref[nums, :], later_ref[dens, :] = later_n, later_d
        grad_e = state(num_ref) * grad_n + state(den_ref) * grad_d
        for b in range(batches):
            gnum_ref[b], gden_ref[b] = grad_n[b : b + 1], grad_d[b : b + 1]
            gexp_ref[b] = grad_e[b : b + 1]
            gffn_ref[b] = grad_f[b : b + 1]
        rate_part = (
            float(length) * (ent_ref[nums, :] * carry_n + ent_ref[dens, :] * carry_d)
            + (length - 1.0) * (later_n * sums_ref[nums, :] + later_d * sums_ref[dens, :]))

        upper = triangle(length, False)
        gn_ref, wkv_ref = get(0), get(1)
        kvr_ref = [get(2), get(3)]
        for b in range(batches):
            t = slice(b * length, (b + 1) * length)
            @columns(width, LANES)
            def _(n):
                at, factor, p, o, e = wkv_terms(kvr_ref, ent_ref, vec_ref, b, t, n, batches, length)
                vals, g = kvr_ref[1][t, n].astype(f32), gn_ref[t, n].astype(f32)
                gd = -g * wkv_ref[t, n].astype(f32)
                direct = e * (g * vals + gd)
                opened = o * (g * ent_ref[b : b + 1, n] + gd * ent_ref[batches + b : batches + b + 1, n])
                rn = two_part(upper, g * p) + later_ref[b : b + 1, n]
                rd = two_part(upper, gd * p) + later_ref[batches + b : batches + b + 1, n]
                chain = factor * (rn * vals + rd)
                d_ref[0, t, n] = (chain + direct).astype(bf16)
                d_ref[1, t, n] = (factor * rn + g * e).astype(bf16)
                loc_ref[b : b + 1, n] = jnp.sum(
                    opened - (at - 1.0) * direct - at * chain, axis=0, keepdims=True)
                loc_ref[batches + b : batches + b + 1, n] = jnp.sum(direct, axis=0, keepdims=True)
        put(0)
        rate_rows = rate_part + loc_ref[:batches, :]
        extra_ref[0:1, :] = jnp.sum(rate_rows, axis=0, keepdims=True) * -jnp.exp(
            vec_ref[DECAY : DECAY + 1, :])
        extra_ref[1:2, :] = jnp.sum(loc_ref[batches:, :], axis=0, keepdims=True)
        for k in range(2):
            wait(copies[k])
            @columns(width, STEP)
            def _(n):
                dins[k, :, n] = dot_nt(d_ref[k], w[k, n, :])
        low_ref, high_ref = get(5), get(6)
        wait(copies[2])
        @columns(width, STEP)
        def _(n):
            dins[2, :, n] = (dot_nt(low_ref[...], w[2, n, : width // 2])
                             + dot_nt(high_ref[...], w[2, n, width // 2 :]))
        sum_ref[...] = jnp.zeros_like(sum_ref)
        stream_ref = get(4)
        for b in range(batches):
            def step(i, before):
                r = row_chunk(b, i, length)
                na, _ = norm(stream_ref[r, :].astype(f32))
                xa = na * vec_ref[G1 : G1 + 1] + vec_ref[B1 : B1 + 1]
                gap = xa - down_one(xa, before)
                dxs = jnp.zeros((ROWS, width), f32)
                dxa = jnp.zeros((ROWS, width), f32)
                for k, row in enumerate((MK, MV, MR)):
                    d, mix = dins[k, r, :], vec_ref[row : row + 1]
                    dxs = dxs + d * (1.0 - mix)
                    dxa = dxa + d * mix
                    sum_ref[k] += fold(d * gap)
                dxs_ref[r, :] = dxs.astype(bf16)
                dxa_ref[r, :] = dxa.astype(bf16)
                return xa[ROWS - 1 :]
            lax.fori_loop(0, length // ROWS, step, entry_ref[b : b + 1])
            head_ref[b : b + 1, :] = dxs_ref[b * length : b * length + 16, :].astype(f32)[:1]
        column_sums(total_ref, sum_ref)

    low = ((tokens, width), bf16)
    return call(
        body, info, [*back, ent, sums, *state, entry, vec],
        [(a, None) for a in (gn, wkv, kvr[0], kvr[1], stream, *drec)], flat_pieces(pieces),
        [((batches, 1, width), f32)] * 4
        + [((batches, width), f32), ((3, width), f32), ((2, width), f32)],
        [((2, tokens, width), bf16), low, low],
        [pltpu.VMEM((3, width, width), bf16), pltpu.VMEM((3, tokens, width), f32),
         pltpu.VMEM((3, 8, width), f32), pltpu.VMEM((2 * batches, width), f32),
         pltpu.VMEM((2 * batches, width), f32)],
        sum(map(len, plans)), 14, 40)


def in_back(info, dxs, dxa, after, dmid, stream, vec, length):
    tokens, width = stream.shape
    batches = tokens // length

    def body(info, small, get, raw, outs, big, put, scratch, loads):
        after_ref, vec_ref = small
        (out_ref,) = big
        (sum_ref,) = scratch
        dxs_ref, dxa_ref, dmid_ref, stream_ref = (get(k) for k in range(4))
        sum_ref[...] = jnp.zeros_like(sum_ref)
        for b in range(batches):
            def step(k, after_row):
                r = row_chunk(b, length // ROWS - 1 - k, length)
                na, inverse = norm(stream_ref[r, :].astype(f32))
                dx = dxs_ref[r, :].astype(f32)
                d = dxa_ref[r, :].astype(f32) + up_one(dx, after_row)
                back = norm_back(d, na, inverse, vec_ref[G1 : G1 + 1])
                out_ref[r, :] = (dmid_ref[r, :].astype(f32) + back).astype(bf16)
                sum_ref[0] += fold(d * na)
                sum_ref[1] += fold(d)
                return dx[:1]
            lax.fori_loop(0, length // ROWS, step, after_ref[b : b + 1])
        column_sums(outs[0], sum_ref)

    return call(
        body, info, [after, vec], [(a, None) for a in (dxs, dxa, dmid, stream)], [],
        [((2, width), f32)], [((tokens, width), bf16)],
        [pltpu.VMEM((2, 8, width), f32)], 0, 6, 40)


def weight_grad(info, arrays, items, layout, us, relative=False, stacked=False, under=()):
    count = lax.axis_size("seg")
    evens = list(range(0, count, 2))
    first = items[0][2]
    lead = first[0] if isinstance(first, list) else first
    tokens, n_wide = arrays[lead[0]].shape[-2:]
    n_wide *= len(first) if isinstance(first, list) else 1
    w = arrays[items[0][0][0]].shape[-1] // {"natural": count, "blocks": len(evens), "joined": len(evens)}[layout]
    pair = 2 if w < 256 else 1
    groups = [evens[1:][k : k + pair] for k in range(0, len(evens) - 1, pair)]
    groups[-1].append(0) if len(groups[-1]) < pair else groups.append([0])
    groups = [g for g in groups if g]
    stretches = lax.axis_size("stretch")
    each_z = w // stretches
    shapes = [(len(evens) * len(items) * w, n_wide)] if stacked else [(len(items) * w, n_wide)] * len(evens)
    shares = [x.shape[0] // len(evens) for x in under]
    if under:
        shapes = [(len(items) * w + sum(shares), n_wide)] * len(evens)

    def body(info, small, get, raw, outs, big, put, scratch, loads):
        x_all, dy_all = scratch
        copies_under, at = [], len(items) * w
        for n, share in enumerate(shares):
            for k in range(len(evens)):
                copies_under.append(loads.start(
                    raw[len(arrays) + n].at[pl.ds(k * share, share)], big[k].at[pl.ds(at, share)]))
            at += share

        def view(spec):
            which, lead = spec
            return raw[which] if lead is None else raw[which].at[lead]

        def columns_of(ref, m):
            if layout == "natural":
                return ref.at[:, pl.ds(natural(info[0], w)(m), w)]
            return ref.at[:, pl.ds(evens.index(m) * w, w)]

        x_loads, dy_loads = {}, {}
        for k, (x, x_sib, dy, dy_sib) in enumerate(items):
            for at, part in ((0, dy), (tokens, dy_sib)):
                if relative:
                    each = n_wide // count
                    for n, m in enumerate(relative_order()):
                        cols = natural(info[0], each)(m if at == 0 else m ^ 1)
                        dy_loads.setdefault(k, []).append(loads.start(
                            view(part).at[:, pl.ds(n * each, each)],
                            dy_all.at[k, pl.ds(at, tokens), pl.ds(cols, each)]))
                    continue
                pieces = part if isinstance(part, list) else [part]
                each = n_wide // len(pieces)
                for n, piece in enumerate(pieces):
                    dy_loads.setdefault(k, []).append(loads.start(
                        view(piece), dy_all.at[k, pl.ds(at, tokens), pl.ds(n * each, each)]))
            for g, ms in enumerate(groups):
                for at, part in ((0, x), (tokens, x_sib)):
                    ref, rows = view(part), pl.ds(at, tokens)
                    if layout == "joined":
                        cols = pl.ds(g * pair * w, len(ms) * w)
                        x_loads.setdefault((k, g), []).append(loads.start(
                            ref.at[:, cols], x_all.at[k, g, rows, pl.ds(0, len(ms) * w)]))
                        continue
                    for n, m in enumerate(ms):
                        x_loads.setdefault((k, g), []).append(loads.start(
                            columns_of(ref, m), x_all.at[k, g, rows, pl.ds(n * w, w)]))

        def need(table, key):
            wait(table.pop(key, ()))

        step = min(512, n_wide)
        for g, ms in enumerate(groups):
            for k in range(len(items)):
                need(x_loads, (k, g))
                for q in range(n_wide // step):
                    need(dy_loads, k)
                    dst = slice(q * step, (q + 1) * step)
                    block = dot_tn(x_all[k, g, :, : len(ms) * w], dy_all[k, :, dst]).astype(bf16)
                    for n, m in enumerate(ms):
                        if not stacked:
                            big[evens.index(m)][k * w : (k + 1) * w, dst] = block[n * w : (n + 1) * w]
                            continue
                        for z in range(stretches):
                            row = ((z * len(evens) + evens.index(m)) * len(items) + k) * each_z
                            big[0][row : row + each_z, dst] = block[n * w + z * each_z : n * w + (z + 1) * each_z]
            if g == 0:
                wait(copies_under)
            for m in ms:
                if not stacked:
                    put(evens.index(m))
                    continue
                rows = len(items) * each_z
                if rows % 16 == 0:
                    for z in range(stretches):
                        put(0, pl.ds((z * len(evens) + evens.index(m)) * rows, rows))

    return call(
        body, info, [], [], [*arrays, *under], [], [(shape, bf16) for shape in shapes],
        [pltpu.VMEM((len(items), len(groups), 2 * tokens, pair * w), bf16),
         pltpu.VMEM((len(items), 2 * tokens, n_wide), bf16)],
        len(items) * (4 + 2 * len(evens) + 2 * count) + len(evens) * (len(under) + stretches), us, 40)


def grad_send(parts):
    return [hop(part, 2 * k) for k, part in enumerate(parts) if k]


def total(terms):
    out = terms[0].astype(f32)
    for t in terms[1:]:
        out = out + t.astype(f32)
    return out


def grad_stack(info, key, recept):
    stretches = lax.axis_size("stretch")
    own, width = recept[0].shape
    each, blocks = own // stretches, key[0].shape[1] // width
    rows = (blocks + 1) * each
    if each % 16:
        wide = total(key).astype(bf16).reshape(stretches, each, blocks, width)
        wide = jnp.swapaxes(wide, 1, 2).reshape(stretches, blocks * each, width)
        narrow = total(recept).astype(bf16).reshape(stretches, each, width)
        return jnp.concatenate([wide, narrow], axis=1).reshape(stretches * rows, width)
    terms = len(key)

    def body(info, small, get, raw, outs, big, put, scratch, loads):
        keys, recepts = scratch
        copies = []
        for z in range(stretches):
            src = pl.ds(z * each, each)
            now = [loads.start(raw[j].at[src], keys.at[j, z]) for j in range(terms)]
            copies.append(now + [loads.start(raw[terms + j].at[src], recepts.at[j, z]) for j in range(terms)])
        for z in range(stretches):
            wait(copies[z])
            for q in range(blocks):
                at = z * rows + q * each
                big[0][at : at + each, :] = total(
                    [keys[j, z, :, q * width : (q + 1) * width] for j in range(terms)]).astype(bf16)
            at = z * rows + blocks * each
            big[0][at : at + each, :] = total([recepts[j, z] for j in range(terms)]).astype(bf16)

    return call(
        body, info, [], [], [*key, *recept], [], [((stretches * rows, width), bf16)],
        [pltpu.VMEM((terms, stretches, each, blocks * width), bf16),
         pltpu.VMEM((terms, stretches, each, width), bf16)],
        stretches * 2 * terms, 4, 24)[0]


def grad_pieces(info, own, got, items, each):
    stretches = lax.axis_size("stretch")
    rows, n_wide = own.shape
    width = each * stretches

    def body(info, small, get, raw, outs, big, put, scratch, loads):
        refs = [get(k) for k in range(1 + len(got))]
        first = items * width
        table = total([r[first : first + 16, :] for r in refs])
        half = n_wide // 2
        table = table[:, :half] + table[:, half:]
        hi = table.astype(bf16)
        lo = (table - hi.astype(f32)).astype(bf16)
        for j in list(range(1, stretches)) + [0]:
            z = jnp.bitwise_xor(info[2], j)
            for k in range(items):
                src = pl.ds(pl.multiple_of(k * width + z * each, each), each)
                big[j][k * each : (k + 1) * each, :] = total([r[src, :] for r in refs]).astype(bf16)
            big[j][items * each :, :half] = hi
            big[j][items * each :, half:] = lo
            put(j)

    return call(
        body, info, [], [(a, None) for a in (own, *got)], [], [],
        [((items * each + 16, n_wide), bf16)] * stretches, [], 0, 3, 24)


def stretch_part(part):
    return lax.psum_scatter(part, "stretch", scatter_dimension=0, tiled=True)


def stretch_items(out, items):
    own = out.shape[0] // items
    return [out[k * own : (k + 1) * own].astype(f32) for k in range(items)]


def vector_rows(table, width):
    me, count = lax.axis_index("seg"), lax.axis_size("seg")
    own = table.shape[1] // count
    table = jnp.pad(table, ((0, 16 - table.shape[0]), (0, 0)))
    rows = []
    for m in range(0, count, 2):
        pair = lax.dynamic_slice_in_dim(table, (me ^ m) // 2 * (2 * own), 2 * own, 1)
        pair = jnp.pad(pair, ((0, 0), (0, width // 2 - 2 * own)))
        hi = pair.astype(bf16)
        rows.append(jnp.concatenate([hi, (pair - hi.astype(f32)).astype(bf16)], axis=1))
    return jnp.concatenate(rows, axis=0)


def vector_read(rows):
    half = rows.shape[1] // 2
    return rows[:, :half].astype(f32) + rows[:, half:].astype(f32)


def vector_own(pair, own):
    second = (lax.axis_index("seg") & 1) != 0
    lo, hi = pair[:, :own], pair[:, own : 2 * own]
    return jnp.where(second, hi, lo) + hop(jnp.where(second, lo, hi), 1)


def vector_finish(table):
    position, count = lax.axis_index("stretch"), lax.axis_size("stretch")
    bit = count // 2
    while bit:
        lo, hi = jnp.split(table, 2, axis=1)
        upper = (position & bit) != 0
        table = jnp.where(upper, hi, lo) + across(jnp.where(upper, lo, hi), bit)
        bit //= 2
    return table


def own_columns(x, me, w):
    ms = [*range(2, lax.axis_size("seg"), 2), 0]
    return jnp.concatenate([lax.dynamic_slice_in_dim(x, (me ^ m) * w, w, 1) for m in ms], axis=1)


def body(
    stream_in, cotangent, previous_mix, previous_ffn, state_num, state_den, state_exp,
    gain_one, bias_one, gain_two, bias_two, mix_key, mix_value, mix_recept,
    time_decay, time_first, chan_mix_key, chan_mix_recept,
    att_key, att_value, att_recept, att_output, chan_key, chan_value, chan_recept,
):
    mine = lax.axis_index("seg")
    position = lax.axis_index("stretch")
    stretches = lax.axis_size("stretch")
    batches, _, length, width = stream_in.shape
    tokens = batches * length
    shard = att_key.shape[0]
    fshard = chan_value.shape[0]
    wide = chan_key.shape[1]
    aligned = shard % 128 == 0
    count = lax.axis_size("seg")
    info = jnp.stack([mine, (position == 0).astype(jnp.int32), position])

    stream = stream_in.reshape(tokens, width)
    cot = cotangent.reshape(tokens, width)
    state = (state_num, state_den, state_exp)
    vectors = [gain_one, bias_one, gain_two, bias_two, mix_key, mix_value, mix_recept,
               time_decay, time_first, chan_mix_key, chan_mix_recept]

    v = Live()
    evens = list(range(0, count, 2))
    spots = {"k": 0, "v": shard, "vec": 2 * shard, "r": 2 * shard + 16, "o": 3 * shard + 16}
    each = fshard // stretches
    v.own_tm = pack(
        [(att_key, 0, shard), (att_value, 0, shard), (None, 0, 16)],
        [(att_recept, 0, shard), (att_output, 0, shard)], vectors, width)
    v.share = lax.dynamic_slice_in_dim(chan_value, position * each, each, 0)
    v.cv = chan_value
    v.last_in = stream_in[:, 0, length - 1]
    v.sync()
    v.shares = lax.all_gather(v.share, "seg", axis=0, tiled=True)
    v.one_tm = first_stage(v.own_tm)
    v.ck = pack_wide(tie(chan_key, *v.own_tm), chan_recept)
    v.tm0 = sibling({0: v.own_tm})
    v.last_in = along(tie(v.last_in, *v.tm0[1]), 1)
    v.sync()
    v.tm6 = second_stage(v.one_tm, v.one_tm)
    v.tm2 = sibling(v.one_tm)
    v.ck0 = sibling({0: v.ck})
    gathered_cv = lax.all_gather(
        jnp.concatenate([lax.dynamic_slice_in_dim(v.shares, (mine ^ m) * each, each, 0) for m in evens[1:]], axis=0),
        "stretch", axis=0, tiled=True)
    v.sync()
    v.tm6_sib = sibling(v.tm6)
    v.sync()

    v.one_ck = first_stage(v.ck)
    tm = {0: v.own_tm, **v.one_tm, **v.tm6, **v.tm0, **v.tm2, **v.tm6_sib}
    given = None
    if not aligned:
        given = lax.all_gather(jnp.stack(vectors), "seg", axis=1, tiled=True).astype(f32)
        given = jnp.pad(given, ((0, 5), (0, 0)))
    v.sums, v.vec, v.entry, v.kvr_in, *v.kvr = time_in(
        info, stream, v.last_in, previous_mix, given, tm, spots, length, shard)
    v.everyone = lax.all_gather(v.sums, "stretch")
    v.tm = tm
    v.drop("own_tm", "one_tm", "tm6", "tm0", "tm2", "tm6_sib", "share", "shares")
    v.sync()

    v.ck6 = second_stage(v.one_ck, v.one_ck)
    v.ent, v.mean, v.log, v.edge_b, v.gated, v.wkv, v.rden, v.mid, v.xb = time_out(
        info, v.kvr, v.everyone, state, v.vec, stream, v.tm, spots, length, shard)
    first_far = far_bits()[0]
    v.ck2 = sibling({first_far: v.one_ck[first_far]})
    v.edge_b = along(v.edge_b, 1)
    v.drop("everyone")
    v.sync()
    v.ck2 = {**v.ck2, **sibling({m: p for m, p in v.one_ck.items() if m != first_far})}
    v.all_ck = {0: v.ck, **v.one_ck, **v.ck6, **v.ck0, **v.ck2, **sibling(v.ck6)}
    v.gathered_cv = gathered_cv
    v.drop("ck", "one_ck", "ck6", "ck0", "ck2")
    v.sync()

    v.entry_b, v.f_in, v.near, v.far, v.act, v.frec = chan_in(
        info, v.xb, v.edge_b, previous_ffn, v.vec, v.all_ck, length, shard, fshard)
    v.all_cv = [v.cv, v.gathered_cv, hop(v.cv, 1), hop(v.gathered_cv, 1)]
    v.drop("cv", "gathered_cv")
    v.sync()
    v.block_out, v.d_fval, v.d_frec = chan_out(
        info, v.near, v.far, v.frec, v.mid, cot, v.all_cv, fshard)
    v.far_sib = hop(v.far, 1)
    v.f_sib = hop(v.f_in, 1)
    v.g_sib = hop(v.gated, 1)
    v.kvr_sib = hop(v.kvr_in, 1)
    v.drop("frec", "far")
    v.sync()

    def pairs(*arrays):
        if aligned:
            return [a for pair in arrays for a in pair]
        return [own_columns(a, mine, shard) for pair in arrays for a in pair]

    layout = "natural" if aligned else "joined"
    flat = tuple((j, None) for j in range(4))
    arrays = [v.near, v.far_sib, v.d_fval, hop(v.d_fval, 1)]
    v.stack_cv = weight_grad(info, arrays, [flat], "blocks", 6, stacked=True)[0]
    v.dfrec_sib = hop(v.d_frec, 1)
    v.drop("near", "far_sib")
    v.sync()

    z_cv = stretch_part(v.stack_cv)
    v.dpre = hidden_back(info, v.act, v.d_fval, v.all_cv, fshard)
    d_frec = tie(v.d_frec, v.dpre)
    if aligned:
        v.parts_c = weight_grad(
            info, [v.f_in, v.f_sib, d_frec, v.dfrec_sib], [((0, 1), (1, 1), (2, None), (3, None))], layout, 3)
    else:
        v.parts_c = weight_grad(
            info, [*pairs((v.f_in[1], v.f_sib[1])), d_frec, v.dfrec_sib], [flat], layout, 3)
    v.got_c = grad_send(v.parts_c)
    dpre_sib = hop(v.dpre, 1)
    v.head_b, v.sums_c, v.dxt, v.dxb = chan_back(
        info, v.dpre, v.d_frec, v.xb, v.entry_b, v.vec, v.all_ck, length, shard, fshard)
    v.next_b = along(v.head_b, -1)
    dpre = tie(v.dpre, v.dxt)
    if aligned:
        v.parts_ck = weight_grad(
            info, [v.f_in, v.f_sib, dpre, dpre_sib], [((0, 0), (1, 0), (2, None), (3, None))], layout, 7, True)
    else:
        v.parts_ck = weight_grad(
            info, [*pairs((v.f_in[0], v.f_sib[0])), dpre, dpre_sib], [flat], layout, 7, True)
    v.drop("all_ck", "all_cv", "xb", "entry_b", "act", "d_fval", "dpre", "stack_cv")
    v.sync()

    v.got_ck = grad_send(v.parts_ck)
    backs, v.sums_m, v.dmid, *lows, gn = mid_back(
        info, v.dxt, v.dxb, v.next_b, v.head_b, v.mid, cot, v.vec, v.kvr, v.wkv, v.rden, v.ent, v.tm, spots,
        length, shard)
    v.dbr, v.drec = lows[:2], lows[2:]
    back = exchange_two(backs)
    *v.grads, v.head_a, v.sums_t, v.extra, v.d_kv, v.dxs, v.dxa = time_back(
        info, gn, v.wkv, v.kvr, v.ent, back, v.sums, state, v.drec, stream, v.entry, v.vec,
        v.tm, spots, length, shard)
    v.dbr_sib = [hop(a, 1) for a in v.dbr]
    v.drec_sib = [hop(a, 1) for a in v.drec]
    dys = [([(at, None), (at + 1, None)], [(at + 2, None), (at + 3, None)]) for at in (0, 4)]
    lows = [*v.dbr, *v.dbr_sib, *v.drec, *v.drec_sib]
    gated = tie(v.gated, v.d_kv)
    if aligned:
        v.parts_or = weight_grad(
            info, [*lows, gated, v.g_sib, v.kvr_in, v.kvr_sib],
            [((8, None), (9, None), *dys[0]), ((10, 2), (11, 2), *dys[1])], layout, 6, stacked=True)
    else:
        xs = pairs((gated, v.g_sib), (v.kvr_in[2], v.kvr_sib[2]))
        v.parts_or = weight_grad(
            info, [*lows, *xs], [((8, None), (9, None), *dys[0]), ((10, None), (11, None), *dys[1])], layout, 6,
            stacked=True)
    v.drop("wkv", "kvr", "ent", "sums", "entry", "tm", "dxt", "dxb", "mid", "rden", "next_b", "head_b")
    v.sync()
    v.dkv_sib = hop(v.d_kv, 1)
    v.next_a = along(v.head_a, -1)
    z_or = stretch_part(v.parts_or[0])
    v.stack = grad_stack(info, [v.parts_ck[0], *v.got_ck], [v.parts_c[0], *v.got_c])
    v.drop("gated", "g_sib", "dbr", "dbr_sib", "drec", "drec_sib", "f_in", "f_sib", "d_frec",
           "parts_ck", "got_ck", "parts_c", "got_c", "parts_or")
    v.z_cv = z_cv
    v.sync()

    v.parts_cv = [v.z_cv[k * each : (k + 1) * each] for k in range(len(evens))]
    z_rest = stretch_part(v.stack)
    v.got_cv = grad_send(v.parts_cv)
    sums_i, v.grad_stream = in_back(info, v.dxs, v.dxa, v.next_a, v.dmid, stream, v.vec, length)
    table = jnp.concatenate([sums_i, v.sums_m, v.sums_t, v.extra, v.sums_c], axis=0)
    under = [vector_rows(table, width)]
    if aligned:
        v.parts_kv = weight_grad(
            info, [v.kvr_in, v.kvr_sib, v.d_kv, v.dkv_sib],
            [tuple((j, k) for j in range(4)) for k in range(2)], layout, 7, under=under)
    else:
        xs = pairs(*[(v.kvr_in[k], v.kvr_sib[k]) for k in range(2)])
        v.parts_kv = weight_grad(
            info, [*xs, v.d_kv, v.dkv_sib],
            [((2 * k, None), (2 * k + 1, None), (4, k), (5, k)) for k in range(2)], layout, 7, under=under)
    v.drop("kvr_in", "kvr_sib", "d_kv", "dkv_sib", "dxs", "dxa", "dmid", "next_a", "stack",
           "sums_m", "sums_t", "extra", "sums_c", "z_cv")
    v.sync()

    v.got_kv = grad_send(v.parts_kv)
    v.heads = lax.all_gather(v.head_a, "stretch")[0]
    v.out_cv = total([v.parts_cv[0], *v.got_cv])
    v.drop("parts_cv", "got_cv")
    v.z_or = z_or
    v.sync()
    rows = shard // stretches
    by_hops = stretches == 4 and rows % 16 == 0
    if by_hops:
        v.pieces = grad_pieces(info, v.parts_kv[0], v.got_kv, 2, rows)
    else:
        whole = total([v.parts_kv[0], *v.got_kv])
        first = 2 * shard
        v.table = vector_read(whole[first:])
        v.part_kv = whole[:first].astype(bf16).reshape(2, stretches, rows, width)
        v.part_kv = jnp.swapaxes(v.part_kv, 0, 1).reshape(first, width)
    parts = [v.z_or[2 * k * rows : 2 * (k + 1) * rows] for k in range(len(evens))]
    v.parts_or = [parts[0], *grad_send(parts)]
    v.drop("parts_kv", "got_kv", "z_or")
    v.sync()
    blocks = wide // width
    out_ck = jnp.concatenate([z_rest[q * rows : (q + 1) * rows] for q in range(blocks)], axis=1).astype(f32)
    out_c = z_rest[blocks * rows : (blocks + 1) * rows].astype(f32)
    if by_hops:
        pieces = [v.pieces[0], *[across(v.pieces[j], j) for j in range(1, stretches)]]
        z_kv = total([p[: 2 * rows] for p in pieces])
        small = sum(vector_read(p[2 * rows : 2 * rows + 11]) for p in pieces)
        small = lax.dynamic_slice_in_dim(vector_own(small, shard), position * rows, rows, 1)
    else:
        z_kv = stretch_part(v.part_kv)
        small = vector_finish(vector_own(v.table[:11], shard))
    out_k, out_v = stretch_items(z_kv, 2)
    out_o, out_r = stretch_items(total(v.parts_or), 2)
    out_cv = v.out_cv
    grad_previous_mix = v.heads
    block_out, grad_stream = v.block_out, v.grad_stream

    shape = stream_in.shape
    return (
        block_out.reshape(shape), grad_stream.reshape(shape), *[small[i] for i in range(11)],
        out_k, out_v, out_r, out_o, out_ck, out_cv, out_c,
        *v.grads[:3], grad_previous_mix[:, None], v.grads[3], v.mean, v.log,
    )


def solution(mesh):
    rows = P(None, "seg", "stretch", None)
    state = P(None, "seg", None)
    both = P(("seg", "stretch"))
    table = P(("seg", "stretch"), None)
    return jax.shard_map(
        body,
        mesh=mesh,
        in_specs=(rows,) * 2 + (state,) * 5 + (P("seg"),) * 11 + (P("seg", None),) * 7,
        out_specs=(rows,) * 2 + (both,) * 11 + (table,) * 7 + (state,) * 7,
        check_vma=False,
    )
```

```python
import jax
import jax.numpy as jnp
from jax import lax
from jax.experimental import pallas as pl
from jax.experimental.pallas import tpu as pltpu
from jax.sharding import PartitionSpec as P

epsilon = 1e-05
bf16 = jnp.bfloat16
f32 = jnp.float32
ROWS = 64
STEP = 512
LANES = 512
LIMIT = 63
MIB = 2**20
G1, B1, G2, B2, MK, MV, MR, DECAY, FIRST, CMK, CMR = range(11)


def hop(value, bit):
    count = lax.axis_size("seg")
    return lax.ppermute(value, "seg", [(i, i ^ bit) for i in range(count)])


def along(value, steps):
    count = lax.axis_size("stretch")
    first, last = (max(0, -steps), min(count, count - steps))
    return lax.ppermute(value, "stretch", [(i, i + steps) for i in range(first, last)])


def across(value, j):
    count = lax.axis_size("stretch")
    return lax.ppermute(value, "stretch", [(i, i ^ j) for i in range(count)])


def exchange(value):
    count = lax.axis_size("stretch")
    if count == 4:
        near, far = across(value, 1), across(value, 2)
        return [value, near, far, across(near, 2)]
    return lax.all_gather(value, "stretch")


def tie(value, *others):
    return lax.optimization_barrier((value, *others))[0]


def exchange_two(value):
    if lax.axis_size("stretch") != 4:
        return lax.all_gather(value, "stretch")
    near = across(value, 1)
    return [value, near, across(jnp.concatenate([value, near], axis=0), 2)]


class Live:
    def __init__(self):
        self.__dict__["held"] = {}

    def __getattr__(self, name):
        return self.held[name]

    def __setattr__(self, name, value):
        self.held[name] = value

    def drop(self, *names):
        for name in names:
            del self.held[name]

    def sync(self):
        self.__dict__["held"] = lax.optimization_barrier(self.held)


def far_bits():
    bits, b = [], 2
    while b < lax.axis_size("seg"):
        bits.append(b)
        b *= 2
    return bits


def relative_order():
    count = lax.axis_size("seg")
    return list(range(0, count, 2)) + list(range(1, count, 2))


def first_stage(own):
    return {b: [hop(part, b) for part in own] for b in far_bits()}


def second_stage(direct, held):
    rest = far_bits()
    held = dict(held)
    for m in sorted(range(0, lax.axis_size("seg"), 2), key=lambda m: (bin(m).count("1"), m)):
        if m == 0 or m in held:
            continue
        bits = [b for b in rest if m & b]
        held[m] = [hop(held[m ^ bits[-1]][0], bits[-1]), hop(held[m ^ bits[0]][1], bits[0])]
    return {m: held[m] for m in held if m not in direct}


def sibling(pieces):
    return {m ^ 1: [hop(p, 1) for p in parts] for m, parts in pieces.items()}


def plan(pieces, first, rows):
    steps, at = [], 0
    for m in relative_order():
        base = 0
        for part in pieces[m]:
            lo, hi = max(first, base), min(first + rows, base + part.shape[0])
            if lo < hi:
                steps.append((at, lo - base, hi - lo, m, lo - first))
            base += part.shape[0]
            at += 1
    return steps


def flat_pieces(pieces):
    return [part for m in relative_order() for part in pieces[m]]


class Loads:
    def __init__(self, sems):
        self.sems, self.used = sems, 0

    def start(self, src, dst):
        copy = pltpu.make_async_copy(src, dst, self.sems.at[self.used])
        self.used += 1
        copy.start()
        return copy

    def pieces(self, steps, refs, target, place):
        return [
            self.start(refs[piece].at[pl.ds(row, count)], target.at[pl.ds(place(m) + within, count)])
            for piece, row, count, m, within in steps
        ]


def wait(copies):
    for c in copies:
        c.wait()


def call(body, info, small, large, raw, outs, big_outs, scratch, copies, us, limit):
    n_small, n_large, n_raw = len(small), len(large), len(raw)
    n_out, n_big = len(outs), len(big_outs)

    def shape_of(array, index):
        return array.shape if index is None else array.shape[1:]

    def kernel(*refs):
        at = 0

        def take(n):
            nonlocal at
            at += n
            return refs[at - n : at]

        (info_ref,), small_refs, large_refs, raw_refs = take(1), take(n_small), take(n_large), take(n_raw)
        out_refs, big_refs = take(n_out), take(n_big)
        buffers, big_buffers, (sems,) = take(n_large), take(n_big), take(1)
        rest = take(len(refs) - at)
        loads = Loads(sems)
        pending = []
        for (array, index), ref, buf in zip(large, large_refs, buffers):
            pending.append(loads.start(ref if index is None else ref.at[index], buf))
        stored = {}

        def get(k):
            if pending[k] is not None:
                pending[k].wait()
                pending[k] = None
            return buffers[k]

        def put(k, part=None):
            src, dst = big_buffers[k], big_refs[k]
            if part is not None:
                src, dst = src.at[part], dst.at[part]
            stored.setdefault(k, []).append(loads.start(src, dst))

        body(info_ref, small_refs, get, raw_refs, out_refs, big_buffers, put, rest, loads)
        for k in range(n_large):
            get(k)
        for k in range(n_big):
            if k not in stored:
                put(k)
        wait([c for copies in stored.values() for c in copies])

    hbm = pl.BlockSpec(memory_space=pltpu.HBM)
    vmem = pl.BlockSpec(memory_space=pltpu.VMEM)
    return pl.pallas_call(
        kernel,
        out_shape=[jax.ShapeDtypeStruct(s, d) for s, d in (*outs, *big_outs)],
        in_specs=[pl.BlockSpec(memory_space=pltpu.SMEM)] + [vmem] * n_small + [hbm] * (n_large + n_raw),
        out_specs=[vmem] * n_out + [hbm] * n_big,
        scratch_shapes=[pltpu.VMEM(shape_of(a, i), a.dtype) for a, i in large]
        + [pltpu.VMEM(s, d) for s, d in big_outs]
        + [pltpu.SemaphoreType.DMA((max(1, n_large + n_big + copies),))]
        + list(scratch),
        compiler_params=pltpu.CompilerParams(vmem_limit_bytes=LIMIT * MIB),
        cost_estimate=pl.CostEstimate(
            flops=0, bytes_accessed=int(us * 1e3), transcendentals=0),
    )(info, *small, *[a for a, _ in large], *raw)


def natural(me, rows):
    return lambda m: pl.multiple_of(jnp.bitwise_xor(me, m) * rows, rows)


def dot_nn(a, b):
    return jnp.dot(a, b, preferred_element_type=f32)


def dot_nt(a, b):
    return lax.dot_general(a, b, (((1,), (1,)), ((), ())), preferred_element_type=f32)


def dot_tn(a, b):
    return lax.dot_general(a, b, (((0,), (0,)), ((), ())), preferred_element_type=f32)


def norm(rows):
    centre = rows - jnp.mean(rows, axis=-1, keepdims=True)
    inverse = lax.rsqrt(jnp.mean(centre * centre, axis=-1, keepdims=True) + epsilon)
    return centre * inverse, inverse


def norm_back(d, unit, inverse, gain):
    q = d * gain
    return inverse * (
        q
        - jnp.mean(q, axis=-1, keepdims=True)
        - unit * jnp.mean(q * unit, axis=-1, keepdims=True)
    )


def down_one(rows, entering):
    at = lax.broadcasted_iota(jnp.int32, rows.shape, 0)
    return jnp.where(at == 0, entering, pltpu.roll(rows, 1, 0))


def up_one(rows, entering):
    at = lax.broadcasted_iota(jnp.int32, rows.shape, 0)
    last = rows.shape[0] - 1
    return jnp.where(at == last, entering, pltpu.roll(rows, last, 0))


def fold(rows):
    total = rows[:8]
    for k in range(8, rows.shape[0], 8):
        total = total + rows[k : k + 8]
    return total


def columns(width, step):
    step = min(step, width)

    def run(body):
        @pl.loop(0, width // step)
        def _(n):
            body(pl.ds(pl.multiple_of(n * step, step), step))

    return run


def row_chunk(b, i, length):
    return pl.ds(pl.multiple_of(b * length + i * ROWS, ROWS), ROWS)


def two_part(mat, value):
    hi = value.astype(bf16)
    lo = (value - hi.astype(f32)).astype(bf16)
    return dot_nn(mat, hi) + dot_nn(mat, lo)


def triangle(length, strictly_before):
    row = lax.broadcasted_iota(jnp.int32, (length, length), 0)
    col = lax.broadcasted_iota(jnp.int32, (length, length), 1)
    keep = (col < row) if strictly_before else (col > row)
    return keep.astype(f32).astype(bf16)


def column_sums(out_ref, sum_ref):
    for k in range(sum_ref.shape[0]):
        out_ref[k : k + 1, :] = jnp.sum(sum_ref[k], axis=0, keepdims=True)


def pack(parts_a, parts_b, vectors, width):
    arrays = [p[0] for p in (*parts_a, *parts_b) if p[0] is not None]
    shard = vectors[0].shape[0]

    def kernel(*refs):
        vec_refs, ins = refs[: len(vectors)], refs[len(vectors) : len(vectors) + len(arrays)]
        outs, (table, sems) = refs[len(vectors) + len(arrays) : -2], refs[-2:]
        copies, n = [], 0
        for out, parts in zip(outs, (parts_a, parts_b)):
            at = 0
            for array, first, count in parts:
                if array is None:
                    spot = (out, at)
                else:
                    copies.append(pltpu.make_async_copy(
                        ins[n].at[pl.ds(first, count)], out.at[pl.ds(at, count)], sems.at[n]))
                    copies[-1].start()
                    n += 1
                at += count
        table[...] = jnp.zeros_like(table)
        for k, ref in enumerate(vec_refs):
            table[k : k + 1, :shard] = ref[...].astype(f32)
        spot[0][spot[1] : spot[1] + 16, :] = table[...].astype(bf16)
        wait(copies)

    return pl.pallas_call(
        kernel,
        out_shape=[jax.ShapeDtypeStruct((sum(p[2] for p in parts), width), bf16)
                   for parts in (parts_a, parts_b)],
        in_specs=[pl.BlockSpec(memory_space=pltpu.VMEM)] * len(vectors)
        + [pl.BlockSpec(memory_space=pltpu.HBM)] * len(arrays),
        out_specs=[pl.BlockSpec(memory_space=pltpu.VMEM)] * 2,
        scratch_shapes=[pltpu.VMEM((16, width), f32), pltpu.SemaphoreType.DMA((len(arrays),))],
        compiler_params=pltpu.CompilerParams(vmem_limit_bytes=LIMIT * MIB),
        cost_estimate=pl.CostEstimate(flops=0, bytes_accessed=1000, transcendentals=0),
    )(*[x.reshape(1, shard) for x in vectors], *arrays)


def pack_wide(key, recept):
    rows, wide = key.shape
    width = recept.shape[1]
    each = recept.shape[0] * width // wide
    half = (rows + each) // 32 * 16

    def kernel(key_ref, recept_ref, top_ref, low_ref, sems):
        copies = [
            pltpu.make_async_copy(key_ref.at[pl.ds(0, half)], top_ref, sems.at[0]),
            pltpu.make_async_copy(
                key_ref.at[pl.ds(half, rows - half)], low_ref.at[pl.ds(0, rows - half)], sems.at[1])]
        for q in range(wide // width):
            copies.append(pltpu.make_async_copy(
                recept_ref.at[pl.ds(q * each, each)],
                low_ref.at[pl.ds(rows - half, each), pl.ds(q * width, width)], sems.at[2 + q]))
        for c in copies:
            c.start()
        wait(copies)

    return pl.pallas_call(
        kernel,
        out_shape=[jax.ShapeDtypeStruct((n, wide), bf16) for n in (half, rows + each - half)],
        in_specs=[pl.BlockSpec(memory_space=pltpu.HBM)] * 2,
        out_specs=[pl.BlockSpec(memory_space=pltpu.VMEM)] * 2,
        scratch_shapes=[pltpu.SemaphoreType.DMA((2 + wide // width,))],
        compiler_params=pltpu.CompilerParams(vmem_limit_bytes=LIMIT * MIB),
        cost_estimate=pl.CostEstimate(flops=0, bytes_accessed=1000, transcendentals=0),
    )(key, recept)


def recept_blocks(loads, steps, raw, w, info, shard, width, wide):
    each = shard * width // wide
    place = natural(info[0], shard)
    sem = loads.sems.at[loads.used]
    loads.used += 1

    @pl.loop(0, wide // width)
    def _(q):
        for piece, row, rows, m, within in steps:
            pltpu.make_async_copy(
                raw[piece].at[pl.ds(row, rows), pl.ds(pl.multiple_of(q * width, width), width)],
                w.at[pl.ds(pl.multiple_of(place(m) + q * each, each) + within, rows)], sem).start()

    return lambda: pltpu.make_async_copy(w, w, sem).wait()


def time_in(info, stream, last, previous, given, pieces, spots, length, shard):
    tokens, width = stream.shape
    batches = tokens // length
    plans = [plan(pieces, spots[k], shard) for k in "kvr"]
    vplan = plan(pieces, spots["vec"], 16)
    order = relative_order()

    def body(info, small, get, raw, outs, big, put, scratch, loads):
        last_ref, prev_ref = small[:2]
        sum_ref, vec_ref, entry_ref = outs
        in_ref = big[0]
        w, vt = scratch
        place = natural(info[0], shard)
        vcopies = loads.pieces(vplan, raw, vt, lambda m: order.index(m) * 16)
        copies = [loads.pieces(plans[k], raw, w.at[k], place) for k in range(3)]
        wait(vcopies)
        if given is not None:
            vec_ref[...] = small[2][...]
        else:
            for at, m in enumerate(order):
                vec_ref[:, pl.ds(place(m), shard)] = vt[at * 16 : at * 16 + 16, :shard].astype(f32)
        unit, _ = norm(last_ref[...].astype(f32))
        edge = unit * vec_ref[G1 : G1 + 1] + vec_ref[B1 : B1 + 1]
        for b in range(batches):
            entry_ref[b : b + 1, :] = jnp.where(info[1] == 1, prev_ref[b], edge[b : b + 1])
        stream_ref = get(0)

        for b in range(batches):
            def step(i, before):
                r = row_chunk(b, i, length)
                na, _ = norm(stream_ref[r, :].astype(f32))
                xa = na * vec_ref[G1 : G1 + 1] + vec_ref[B1 : B1 + 1]
                xs = down_one(xa, before)
                for k, row in enumerate((MK, MV, MR)):
                    mix = vec_ref[row : row + 1]
                    in_ref[k, r, :] = (xa * mix + xs * (1.0 - mix)).astype(bf16)
                return xa[ROWS - 1 :]
            lax.fori_loop(0, length // ROWS, step, entry_ref[b : b + 1])
        put(0)
        def project(k):
            wait(copies[k])
            @columns(width, STEP)
            def _(n):
                big[1 + k][:, n] = dot_nn(in_ref[k], w[k, :, n]).astype(big[1 + k].dtype)
            put(1 + k)
        project(0)
        project(1)
        keys_ref, vals_ref = big[1], big[2]
        for b in range(batches):
            t = slice(b * length, (b + 1) * length)
            @columns(width, LANES)
            def _(n):
                rate = -jnp.exp(vec_ref[DECAY : DECAY + 1, n])
                at = lax.broadcasted_iota(jnp.int32, (length, 1), 0).astype(f32)
                shifted = keys_ref[t, n] - at * rate
                peak = jnp.max(shifted, axis=0, keepdims=True)
                factor = jnp.exp(shifted - peak)
                sum_ref[b : b + 1, n] = jnp.sum(
                    factor * vals_ref[t, n].astype(f32), axis=0, keepdims=True)
                sum_ref[batches + b : batches + b + 1, n] = jnp.sum(factor, axis=0, keepdims=True)
                sum_ref[2 * batches + b : 2 * batches + b + 1, n] = peak + (length - 1.0) * rate
        project(2)

    extra = [] if given is None else [given]
    return call(
        body, info, [last, previous, *extra], [(stream, None)], flat_pieces(pieces),
        [((3 * batches, width), f32), ((16, width), f32), ((batches, width), f32)],
        [((3, tokens, width), bf16)] + [((tokens, width), f32)] * 3,
        [pltpu.VMEM((3, width, width), bf16), pltpu.VMEM((16 * len(order), width), bf16)],
        len(vplan) + sum(map(len, plans)), 9, 40)


def wkv_terms(kvr_ref, ent_ref, vec_ref, b, t, n, batches, length):
    rate = -jnp.exp(vec_ref[DECAY : DECAY + 1, n])
    at = lax.broadcasted_iota(jnp.int32, (length, 1), 0).astype(f32)
    keys = kvr_ref[0][t, n]
    shifted = keys - at * rate
    peak = jnp.max(shifted, axis=0, keepdims=True)
    factor = jnp.exp(shifted - peak)
    near = (at - 1.0) * rate + peak
    opening = at * rate + ent_ref[2 * batches + b : 2 * batches + b + 1, n]
    reward = vec_ref[FIRST : FIRST + 1, n] + keys
    top = jnp.maximum(jnp.maximum(near, opening), reward)
    return at, factor, jnp.exp(near - top), jnp.exp(opening - top), jnp.exp(reward - top)


def time_out(info, kvr, everyone, state, vec, stream, pieces, spots, length, shard):
    tokens, width = stream.shape
    batches = tokens // length
    stretches = len(everyone)
    relative = isinstance(everyone, list)
    if not relative:
        everyone = [everyone]
    steps = plan(pieces, spots["o"], shard)

    def body(info, small, get, raw, outs, big, put, scratch, loads):
        every_ref, (num_ref, den_ref, exp_ref, vec_ref) = small[:-4], small[-4:]
        if not relative:
            every_ref = [every_ref[0].at[z] for z in range(stretches)]
        ent_ref, mean_ref, log_ref, edge_ref = outs
        gated_ref, wkv_ref, rden_ref, mid_ref, xb_ref = big
        (w,) = scratch
        copies = loads.pieces(steps, raw, w, natural(info[0], shard))
        span = -jnp.exp(vec_ref[DECAY : DECAY + 1, :]) * float(length)

        def merge(upto, b):
            upto_f = upto.astype(f32) if upto is not stretches else float(stretches)
            logits = []
            for j in range(stretches):
                row, z = 2 * batches + b, jnp.bitwise_xor(info[2], j) if relative else jnp.int32(j)
                logit = every_ref[j][row : row + 1, :] + (upto_f - 1.0 - z.astype(f32)) * span
                logits.append(logit if upto is stretches else jnp.where(z < upto, logit, -jnp.inf))
            opening = exp_ref[b] + upto_f * span
            top = opening
            for logit in logits:
                top = jnp.maximum(top, logit)
            start = jnp.exp(opening - top)
            num, den = num_ref[b] * start, den_ref[b] * start
            for j, logit in enumerate(logits):
                weight = jnp.exp(logit - top)
                num = num + weight * every_ref[j][b : b + 1, :]
                den = den + weight * every_ref[j][batches + b : batches + b + 1, :]
            return num, den, top

        for b in range(batches):
            for k, part in enumerate(merge(info[2], b)):
                ent_ref[k * batches + b : k * batches + b + 1, :] = part
            num, den, top = merge(stretches, b)
            mean_ref[b] = num / den
            log_ref[b] = top + jnp.log(den)

        lower = triangle(length, True)
        kvr_ref = [get(k) for k in range(3)]
        for b in range(batches):
            t = slice(b * length, (b + 1) * length)
            @columns(width, LANES)
            def _(n):
                _, factor, p, o, e = wkv_terms(kvr_ref, ent_ref, vec_ref, b, t, n, batches, length)
                vals = kvr_ref[1][t, n].astype(f32)
                num = (two_part(lower, factor * vals) * p
                       + ent_ref[b : b + 1, n] * o + vals * e)
                den = (two_part(lower, factor) * p
                       + ent_ref[batches + b : batches + b + 1, n] * o + e)
                rden = 1.0 / den
                wkv = num * rden
                wkv_ref[t, n] = wkv
                rden_ref[t, n] = rden.astype(bf16)
                gated_ref[t, n] = (jax.nn.sigmoid(kvr_ref[2][t, n].astype(f32)) * wkv).astype(bf16)
        put(0)
        put(1)
        put(2)
        wait(copies)
        stream_ref = get(3)
        @columns(width, STEP)
        def _(n):
            mid_ref[:, n] = stream_ref[:, n].astype(f32) + dot_nn(gated_ref[...], w[:, n])
        put(3)
        @pl.loop(0, tokens // ROWS)
        def _(i):
            r = row_chunk(0, i, 0)
            nb, _ = norm(mid_ref[r, :])
            xb_ref[r, :] = nb * vec_ref[G2 : G2 + 1] + vec_ref[B2 : B2 + 1]
        for b in range(batches):
            last = (b + 1) * length
            edge_ref[b : b + 1, :] = xb_ref[last - 1 : last, :]

    one, low = ((tokens, width), f32), ((tokens, width), bf16)
    return call(
        body, info, [*everyone, *state, vec], [(a, None) for a in (*kvr, stream)], flat_pieces(pieces),
        [((3 * batches, width), f32), ((batches, 1, width), f32), ((batches, 1, width), f32),
         ((batches, width), f32)],
        [low, one, low, one, one],
        [pltpu.VMEM((width, width), bf16)], len(steps), 7, 40)


def key_blocks(loads, steps, raw, w, info, shard, fshard, start=0):
    count = lax.axis_size("seg")
    half = count // 2
    place = natural(info[0], shard)
    first = loads.used
    loads.used += count

    @pl.loop(0, count)
    def _(turn):
        at = lax.rem(turn + start, count)
        m = lax.rem(at, half) * 2 + lax.div(at, half)
        cols = pl.ds(natural(info[0], fshard)(m), fshard)
        dst = pl.ds(pl.multiple_of(at * fshard, fshard), fshard)
        for piece, row, rows, m2, within in steps:
            pltpu.make_async_copy(
                raw[piece].at[pl.ds(row, rows), cols], w.at[pl.ds(place(m2) + within, rows), dst],
                loads.sems.at[first + at]).start()

    def arrive(at):
        block = w.at[:, pl.ds(at * fshard, fshard)]
        pltpu.make_async_copy(block, block, loads.sems.at[first + at]).wait()

    return arrive


def value_blocks(loads, raw, w, fshard, stretches):
    order = relative_order()
    others = [m for m in order if m % 2 == 0 and m]
    each = fshard // stretches
    out = {}
    for at, m in enumerate(order):
        own, gathered = raw[2 * (m % 2)], raw[2 * (m % 2) + 1]
        base = m - m % 2
        if base == 0:
            out[m] = [loads.start(own, w.at[pl.ds(at * fshard, fshard)])]
            continue
        out[m] = [
            loads.start(
                gathered.at[pl.ds((z * len(others) + others.index(base)) * each, each)],
                w.at[pl.ds(at * fshard + z * each, each)])
            for z in range(stretches)
        ]
    return out


def value_copies(stretches):
    count = lax.axis_size("seg")
    return 2 + (count - 2) * stretches


def chan_in(info, xb, edge, previous, vec, pieces_ck, length, shard, fshard):
    tokens, width = xb.shape
    batches = tokens // length
    order = relative_order()
    wide = fshard * len(order)
    steps_k = plan(pieces_ck, 0, shard)
    steps_c = plan(pieces_ck, shard, shard * width // wide)

    def body(info, small, get, raw, outs, big, put, scratch, loads):
        edge_ref, prev_ref, vec_ref = small
        (entry_ref,) = outs
        in_ref, near_ref, far_ref, act_ref, frec_ref = big
        wk, wc = scratch
        half = len(order) // 2
        turn = order[half:] + order[:half]
        arrive = key_blocks(loads, steps_k, raw, wk, info, shard, fshard, half)
        arrive_c = recept_blocks(loads, steps_c, raw, wc, info, shard, width, wide)
        for b in range(batches):
            entry_ref[b : b + 1, :] = jnp.where(info[1] == 1, prev_ref[b], edge_ref[b : b + 1, :])
        xb_ref = get(0)
        for b in range(batches):
            def step(i, before):
                r = row_chunk(b, i, length)
                x = xb_ref[r, :].astype(f32)
                xt = down_one(x, before)
                for k, row in enumerate((CMK, CMR)):
                    mix = vec_ref[row : row + 1]
                    in_ref[k, r, :] = (x * mix + xt * (1.0 - mix)).astype(bf16)
                return x[ROWS - 1 :]
            lax.fori_loop(0, length // ROWS, step, entry_ref[b : b + 1])
        put(0)
        for m in turn:
            at = order.index(m)
            arrive(at)
            hid_ref, lo = (near_ref, at * fshard) if at < half else (far_ref, (at - half) * fshard)
            act = jnp.maximum(dot_nn(in_ref[0], wk[:, at * fshard : (at + 1) * fshard]), 0.0)
            act_ref[:, at * fshard : (at + 1) * fshard] = act.astype(bf16)
            hid_ref[:, lo : lo + fshard] = (act * act).astype(bf16)
            if m == turn[half - 1]:
                put(2)
        put(1)
        put(3)
        arrive_c()
        @columns(width, STEP)
        def _(n):
            frec_ref[:, n] = dot_nn(in_ref[1], wc[:, n])

    return call(
        body, info, [edge, previous, vec], [(xb, None)], flat_pieces(pieces_ck),
        [((batches, width), f32)],
        [((2, tokens, width), bf16), ((tokens, wide // 2), bf16), ((tokens, wide // 2), bf16),
         ((tokens, wide), bf16), ((tokens, width), f32)],
        [pltpu.VMEM((width, wide), bf16), pltpu.VMEM((width, width), bf16)],
        1 + len(order), 11, 40)


def chan_out(info, near, far, frec, mid, cot, cv, fshard):
    tokens, width = mid.shape
    order = relative_order()
    wide = fshard * len(order)
    stretches = lax.axis_size("stretch")

    def body(info, small, get, raw, outs, big, put, scratch, loads):
        out_ref, df_ref, dr_ref = big
        w, fval = scratch
        blocks = value_blocks(loads, raw, w, fshard, stretches)
        half = len(order) // 2
        for k in range(2):
            hid_ref = get(k)
            for m in order[k * half : (k + 1) * half]:
                wait(blocks[m])
            @columns(width, STEP)
            def _(n):
                part = dot_nn(hid_ref[...], w[k * wide // 2 : (k + 1) * wide // 2, n])
                fval[:, n] = part if k == 0 else fval[:, n] + part
        frec_ref, mid_ref, cot_ref = get(2), get(3), get(4)
        @pl.loop(0, tokens // ROWS)
        def _(i):
            r = row_chunk(0, i, 0)
            sig = jax.nn.sigmoid(frec_ref[r, :].astype(f32))
            cots, value = cot_ref[r, :].astype(f32), fval[r, :]
            df_ref[r, :] = (cots * sig).astype(bf16)
            out_ref[r, :] = (mid_ref[r, :] + sig * value).astype(bf16)
            dr_ref[r, :] = (cots * value * sig * (1.0 - sig)).astype(bf16)

    low = ((tokens, width), bf16)
    return call(
        body, info, [], [(a, None) for a in (near, far, frec, mid, cot)], cv, [], [low, low, low],
        [pltpu.VMEM((wide, width), bf16), pltpu.VMEM((tokens, width), f32)],
        value_copies(stretches), 7, 40)


def hidden_back(info, act, dfval, cv, fshard):
    tokens, width = dfval.shape
    order = relative_order()
    wide = fshard * len(order)
    stretches = lax.axis_size("stretch")

    def body(info, small, get, raw, outs, big, put, scratch, loads):
        (dpre_ref,) = big
        (wv,) = scratch
        values = value_blocks(loads, raw, wv, fshard, stretches)
        dfval_ref, act_ref = get(0), get(1)
        for at, m in enumerate(order):
            wait(values[m])
            block = slice(at * fshard, (at + 1) * fshard)
            d = dot_nt(dfval_ref[...], wv[block, :]) * (2.0 * act_ref[:, block].astype(f32))
            dpre_ref[:, block] = d.astype(bf16)
            put(0, (slice(None), pl.ds(at * fshard, fshard)))

    return call(
        body, info, [], [(dfval, None), (act, None)], cv, [], [((tokens, wide), bf16)],
        [pltpu.VMEM((wide, width), bf16)], value_copies(stretches) + len(order), 7, 40)[0]


def chan_back(info, dpre, dfrec, xb, entry, vec, pieces_ck, length, shard, fshard):
    tokens, width = xb.shape
    batches = tokens // length
    order = relative_order()
    wide = fshard * len(order)
    steps_k = plan(pieces_ck, 0, shard)
    steps_c = plan(pieces_ck, shard, shard * width // wide)

    def body(info, small, get, raw, outs, big, put, scratch, loads):
        entry_ref, vec_ref = small
        head_ref, total_ref = outs
        dxt_ref, dxb_ref = big
        wk, wc, df, dr, sum_ref = scratch
        arrive_c = recept_blocks(loads, steps_c, raw, wc, info, shard, width, wide)
        arrive = key_blocks(loads, steps_k, raw, wk, info, shard, fshard)
        dfrec_ref = get(0)
        arrive_c()
        @columns(width, STEP)
        def _(n):
            dr[:, n] = dot_nt(dfrec_ref[...], wc[n, :])
        dpre_ref = get(1)
        half = len(order) // 2
        for k in range(2):
            for at in range(k * half, (k + 1) * half):
                arrive(at)
            part_of = slice(k * wide // 2, (k + 1) * wide // 2)
            @columns(width, STEP)
            def _(n):
                part = dot_nt(dpre_ref[:, part_of], wk[n, part_of])
                df[:, n] = part if k == 0 else df[:, n] + part
        sum_ref[...] = jnp.zeros_like(sum_ref)
        xb_ref = get(2)
        for b in range(batches):
            def step(i, before):
                r = row_chunk(b, i, length)
                x = xb_ref[r, :].astype(f32)
                gap = x - down_one(x, before)
                a, c = df[r, :], dr[r, :]
                ck, cr = vec_ref[CMK : CMK + 1], vec_ref[CMR : CMR + 1]
                dxt_ref[r, :] = (a * (1.0 - ck) + c * (1.0 - cr)).astype(bf16)
                dxb_ref[r, :] = (a * ck + c * cr).astype(bf16)
                sum_ref[0] += fold(a * gap)
                sum_ref[1] += fold(c * gap)
                return x[ROWS - 1 :]
            lax.fori_loop(0, length // ROWS, step, entry_ref[b : b + 1])
            head_ref[b : b + 1, :] = dxt_ref[b * length : b * length + 16, :].astype(f32)[:1]
        column_sums(total_ref, sum_ref)

    low = ((tokens, width), bf16)
    return call(
        body, info, [entry, vec], [(a, None) for a in (dfrec, dpre, xb)], flat_pieces(pieces_ck),
        [((batches, width), f32), ((2, width), f32)], [low, low],
        [pltpu.VMEM((width, wide), bf16), pltpu.VMEM((width, width), bf16),
         pltpu.VMEM((tokens, width), f32), pltpu.VMEM((tokens, width), f32),
         pltpu.VMEM((2, 8, width), f32)],
        1 + len(order), 10, 40)


def mid_back(info, dxt, dxb, after, head, mid, cot, vec, kvr, wkv, rden, ent, pieces, spots, length, shard):
    tokens, width = mid.shape
    batches = tokens // length
    steps = plan(pieces, spots["o"], shard)

    def body(info, small, get, raw, outs, big, put, scratch, loads):
        after_ref, head_ref, vec_ref, ent_ref = small
        dent_ref, total_ref = outs
        dent_ref[2 * batches : 3 * batches, :] = ent_ref[2 * batches :, :]
        dent_ref[3 * batches :, :] = head_ref[...]
        dmid_ref, low_ref, high_ref, rlow_ref, rhigh_ref, gn_ref = big
        w, sum_ref, dgate = scratch
        copies = loads.pieces(steps, raw, w, natural(info[0], shard))
        sum_ref[...] = jnp.zeros_like(sum_ref)
        dxt_ref, dxb_ref, mid_ref, cot_ref = get(0), get(1), get(2), get(3)
        for b in range(batches):
            def step(k, after_row):
                r = row_chunk(b, length // ROWS - 1 - k, length)
                nb, inverse = norm(mid_ref[r, :])
                dx = dxt_ref[r, :].astype(f32)
                d = dxb_ref[r, :].astype(f32) + up_one(dx, after_row)
                back = cot_ref[r, :].astype(f32) + norm_back(d, nb, inverse, vec_ref[G2 : G2 + 1])
                dmid_ref[r, :] = back.astype(bf16)
                low_ref[r, :] = back[:, : width // 2].astype(bf16)
                high_ref[r, :] = back[:, width // 2 :].astype(bf16)
                sum_ref[0] += fold(d * nb)
                sum_ref[1] += fold(d)
                return dx[:1]
            lax.fori_loop(0, length // ROWS, step, after_ref[b : b + 1])
        put(0)
        put(1)
        put(2)
        column_sums(total_ref, sum_ref)
        wait(copies)
        @columns(width, STEP)
        def _(n):
            dgate[:, n] = (dot_nt(low_ref[...], w[n, : width // 2])
                           + dot_nt(high_ref[...], w[n, width // 2 :]))
        kvr_ref = [get(4), None, get(5)]
        wkv_ref, rden_ref = get(6), get(7)
        lanes = min(LANES, width // 2)
        for b, half, q in [(b, h, q) for b in range(batches) for h in range(2)
                           for q in range(width // 2 // lanes)]:
            t = slice(b * length, (b + 1) * length)
            n = slice(half * width // 2 + q * lanes, half * width // 2 + (q + 1) * lanes)
            part, at_half = (rlow_ref, rhigh_ref)[half], slice(q * lanes, (q + 1) * lanes)
            if True:
                _, _, _, o, _ = wkv_terms(kvr_ref, ent_ref, vec_ref, b, t, n, batches, length)
                sig = jax.nn.sigmoid(kvr_ref[2][t, n].astype(f32))
                d = dgate[t, n] * sig
                wkvs = wkv_ref[t, n].astype(f32)
                part[t, at_half] = (d * wkvs * (1.0 - sig)).astype(bf16)
                gn = d * rden_ref[t, n].astype(f32)
                gn_ref[t, n] = gn.astype(bf16)
                go = gn * o
                dent_ref[b : b + 1, n] = jnp.sum(go, axis=0, keepdims=True)
                dent_ref[batches + b : batches + b + 1, n] = -jnp.sum(go * wkvs, axis=0, keepdims=True)

    low, half = ((tokens, width), bf16), ((tokens, width // 2), bf16)
    return call(
        body, info, [after, head, vec, ent], [(a, None) for a in (dxt, dxb, mid, cot, kvr[0], kvr[2], wkv, rden)],
        flat_pieces(pieces), [((4 * batches, width), f32), ((2, width), f32)], [low, half, half, half, half, low],
        [pltpu.VMEM((width, width), bf16), pltpu.VMEM((2, 8, width), f32), pltpu.VMEM((tokens, width), f32)],
        len(steps), 9, 40)


def time_back(info, gn, wkv, kvr, ent, back, sums, state, drec, stream, entry, vec, pieces, spots,
              length, shard):
    tokens, width = stream.shape
    batches = tokens // length
    relative = isinstance(back, list)
    stretches = 4 if relative else len(back)
    if not relative:
        back = [back]
    plans = [plan(pieces, spots[k], shard) for k in "kvr"]

    def body(info, small, get, raw, outs, big, put, scratch, loads):
        back_ref = small[:-7]
        if not relative:
            back_ref = [back_ref[0].at[z] for z in range(stretches)]
        else:
            rows = 4 * batches
            back_ref = [*back_ref[:2], *[back_ref[2].at[pl.ds(k * rows, rows)] for k in range(2)]]
        ent_ref, sums_ref, num_ref, den_ref, exp_ref, entry_ref, vec_ref = small[-7:]
        gnum_ref, gden_ref, gexp_ref, gffn_ref, head_ref, total_ref, extra_ref = outs
        d_ref, dxs_ref, dxa_ref = big
        w, dins, sum_ref, later_ref, loc_ref = scratch
        place = natural(info[0], shard)
        copies = [loads.pieces(plans[k], raw, w.at[k], place) for k in range(3)]
        span = -jnp.exp(vec_ref[DECAY : DECAY + 1, :]) * float(length)
        pos = info[2].astype(f32)
        nums, dens, exps = (slice(k * batches, (k + 1) * batches) for k in range(3))
        zero = jnp.zeros((batches, width), f32)

        def state(ref):
            return jnp.concatenate([ref[b] for b in range(batches)], axis=0)

        later_n = later_d = carry_n = carry_d = grad_n = grad_d = grad_f = zero
        for j in range(stretches):
            there = back_ref[j][exps, :]
            at_z = jnp.bitwise_xor(info[2], j) if relative else jnp.int32(j)
            z = at_z.astype(f32)
            after = at_z > info[2]
            lift = jnp.where(after, jnp.exp(jnp.minimum(
                sums_ref[exps, :] - there + (z - 1.0 - pos) * span, 0.0)), 0.0)
            carry = jnp.where(after, jnp.exp(jnp.minimum(
                ent_ref[exps, :] - there + (z - pos) * span, 0.0)), 0.0)
            raised = jnp.exp(jnp.minimum(state(exp_ref) - there + z * span, 0.0))
            dn, dd = back_ref[j][nums, :], back_ref[j][dens, :]
            grad_f = grad_f + jnp.where(at_z == 0, back_ref[j][3 * batches :, :], 0.0)
            later_n, later_d = later_n + dn * lift, later_d + dd * lift
            carry_n, carry_d = carry_n + dn * carry, carry_d + dd * carry
            grad_n, grad_d = grad_n + dn * raised, grad_d + dd * raised
        later_ref[nums, :], later_ref[dens, :] = later_n, later_d
        grad_e = state(num_ref) * grad_n + state(den_ref) * grad_d
        for b in range(batches):
            gnum_ref[b], gden_ref[b] = grad_n[b : b + 1], grad_d[b : b + 1]
            gexp_ref[b] = grad_e[b : b + 1]
            gffn_ref[b] = grad_f[b : b + 1]
        rate_part = (
            float(length) * (ent_ref[nums, :] * carry_n + ent_ref[dens, :] * carry_d)
            + (length - 1.0) * (later_n * sums_ref[nums, :] + later_d * sums_ref[dens, :]))

        upper = triangle(length, False)
        gn_ref, wkv_ref = get(0), get(1)
        kvr_ref = [get(2), get(3)]
        for b in range(batches):
            t = slice(b * length, (b + 1) * length)
            @columns(width, LANES)
            def _(n):
                at, factor, p, o, e = wkv_terms(kvr_ref, ent_ref, vec_ref, b, t, n, batches, length)
                vals, g = kvr_ref[1][t, n].astype(f32), gn_ref[t, n].astype(f32)
                gd = -g * wkv_ref[t, n].astype(f32)
                direct = e * (g * vals + gd)
                opened = o * (g * ent_ref[b : b + 1, n] + gd * ent_ref[batches + b : batches + b + 1, n])
                rn = two_part(upper, g * p) + later_ref[b : b + 1, n]
                rd = two_part(upper, gd * p) + later_ref[batches + b : batches + b + 1, n]
                chain = factor * (rn * vals + rd)
                d_ref[0, t, n] = (chain + direct).astype(bf16)
                d_ref[1, t, n] = (factor * rn + g * e).astype(bf16)
                loc_ref[b : b + 1, n] = jnp.sum(
                    opened - (at - 1.0) * direct - at * chain, axis=0, keepdims=True)
                loc_ref[batches + b : batches + b + 1, n] = jnp.sum(direct, axis=0, keepdims=True)
        put(0)
        rate_rows = rate_part + loc_ref[:batches, :]
        extra_ref[0:1, :] = jnp.sum(rate_rows, axis=0, keepdims=True) * -jnp.exp(
            vec_ref[DECAY : DECAY + 1, :])
        extra_ref[1:2, :] = jnp.sum(loc_ref[batches:, :], axis=0, keepdims=True)
        for k in range(2):
            wait(copies[k])
            @columns(width, STEP)
            def _(n):
                dins[k, :, n] = dot_nt(d_ref[k], w[k, n, :])
        low_ref, high_ref = get(5), get(6)
        wait(copies[2])
        @columns(width, STEP)
        def _(n):
            dins[2, :, n] = (dot_nt(low_ref[...], w[2, n, : width // 2])
                             + dot_nt(high_ref[...], w[2, n, width // 2 :]))
        sum_ref[...] = jnp.zeros_like(sum_ref)
        stream_ref = get(4)
        for b in range(batches):
            def step(i, before):
                r = row_chunk(b, i, length)
                na, _ = norm(stream_ref[r, :].astype(f32))
                xa = na * vec_ref[G1 : G1 + 1] + vec_ref[B1 : B1 + 1]
                gap = xa - down_one(xa, before)
                dxs = jnp.zeros((ROWS, width), f32)
                dxa = jnp.zeros((ROWS, width), f32)
                for k, row in enumerate((MK, MV, MR)):
                    d, mix = dins[k, r, :], vec_ref[row : row + 1]
                    dxs = dxs + d * (1.0 - mix)
                    dxa = dxa + d * mix
                    sum_ref[k] += fold(d * gap)
                dxs_ref[r, :] = dxs.astype(bf16)
                dxa_ref[r, :] = dxa.astype(bf16)
                return xa[ROWS - 1 :]
            lax.fori_loop(0, length // ROWS, step, entry_ref[b : b + 1])
            head_ref[b : b + 1, :] = dxs_ref[b * length : b * length + 16, :].astype(f32)[:1]
        column_sums(total_ref, sum_ref)

    low = ((tokens, width), bf16)
    return call(
        body, info, [*back, ent, sums, *state, entry, vec],
        [(a, None) for a in (gn, wkv, kvr[0], kvr[1], stream, *drec)], flat_pieces(pieces),
        [((batches, 1, width), f32)] * 4
        + [((batches, width), f32), ((3, width), f32), ((2, width), f32)],
        [((2, tokens, width), bf16), low, low],
        [pltpu.VMEM((3, width, width), bf16), pltpu.VMEM((3, tokens, width), f32),
         pltpu.VMEM((3, 8, width), f32), pltpu.VMEM((2 * batches, width), f32),
         pltpu.VMEM((2 * batches, width), f32)],
        sum(map(len, plans)), 14, 40)


def in_back(info, dxs, dxa, after, dmid, stream, vec, length):
    tokens, width = stream.shape
    batches = tokens // length

    def body(info, small, get, raw, outs, big, put, scratch, loads):
        after_ref, vec_ref = small
        (out_ref,) = big
        (sum_ref,) = scratch
        dxs_ref, dxa_ref, dmid_ref, stream_ref = (get(k) for k in range(4))
        sum_ref[...] = jnp.zeros_like(sum_ref)
        for b in range(batches):
            def step(k, after_row):
                r = row_chunk(b, length // ROWS - 1 - k, length)
                na, inverse = norm(stream_ref[r, :].astype(f32))
                dx = dxs_ref[r, :].astype(f32)
                d = dxa_ref[r, :].astype(f32) + up_one(dx, after_row)
                back = norm_back(d, na, inverse, vec_ref[G1 : G1 + 1])
                out_ref[r, :] = (dmid_ref[r, :].astype(f32) + back).astype(bf16)
                sum_ref[0] += fold(d * na)
                sum_ref[1] += fold(d)
                return dx[:1]
            lax.fori_loop(0, length // ROWS, step, after_ref[b : b + 1])
        column_sums(outs[0], sum_ref)

    return call(
        body, info, [after, vec], [(a, None) for a in (dxs, dxa, dmid, stream)], [],
        [((2, width), f32)], [((tokens, width), bf16)],
        [pltpu.VMEM((2, 8, width), f32)], 0, 6, 40)


def weight_grad(info, arrays, items, layout, us, relative=False, stacked=False, under=()):
    count = lax.axis_size("seg")
    evens = list(range(0, count, 2))
    first = items[0][2]
    lead = first[0] if isinstance(first, list) else first
    tokens, n_wide = arrays[lead[0]].shape[-2:]
    n_wide *= len(first) if isinstance(first, list) else 1
    w = arrays[items[0][0][0]].shape[-1] // {"natural": count, "blocks": len(evens), "joined": len(evens)}[layout]
    pair = 2 if w < 256 else 1
    groups = [evens[1:][k : k + pair] for k in range(0, len(evens) - 1, pair)]
    groups[-1].append(0) if len(groups[-1]) < pair else groups.append([0])
    groups = [g for g in groups if g]
    stretches = lax.axis_size("stretch")
    each_z = w // stretches
    shapes = [(len(evens) * len(items) * w, n_wide)] if stacked else [(len(items) * w, n_wide)] * len(evens)
    shares = [x.shape[0] // len(evens) for x in under]
    if under:
        shapes = [(len(items) * w + sum(shares), n_wide)] * len(evens)

    def body(info, small, get, raw, outs, big, put, scratch, loads):
        x_all, dy_all = scratch
        copies_under, at = [], len(items) * w
        for n, share in enumerate(shares):
            for k in range(len(evens)):
                copies_under.append(loads.start(
                    raw[len(arrays) + n].at[pl.ds(k * share, share)], big[k].at[pl.ds(at, share)]))
            at += share

        def view(spec):
            which, lead = spec
            return raw[which] if lead is None else raw[which].at[lead]

        def columns_of(ref, m):
            if layout == "natural":
                return ref.at[:, pl.ds(natural(info[0], w)(m), w)]
            return ref.at[:, pl.ds(evens.index(m) * w, w)]

        x_loads, dy_loads = {}, {}
        for k, (x, x_sib, dy, dy_sib) in enumerate(items):
            for at, part in ((0, dy), (tokens, dy_sib)):
                if relative:
                    each = n_wide // count
                    for n, m in enumerate(relative_order()):
                        cols = natural(info[0], each)(m if at == 0 else m ^ 1)
                        dy_loads.setdefault(k, []).append(loads.start(
                            view(part).at[:, pl.ds(n * each, each)],
                            dy_all.at[k, pl.ds(at, tokens), pl.ds(cols, each)]))
                    continue
                pieces = part if isinstance(part, list) else [part]
                each = n_wide // len(pieces)
                for n, piece in enumerate(pieces):
                    dy_loads.setdefault(k, []).append(loads.start(
                        view(piece), dy_all.at[k, pl.ds(at, tokens), pl.ds(n * each, each)]))
            for g, ms in enumerate(groups):
                for at, part in ((0, x), (tokens, x_sib)):
                    ref, rows = view(part), pl.ds(at, tokens)
                    if layout == "joined":
                        cols = pl.ds(g * pair * w, len(ms) * w)
                        x_loads.setdefault((k, g), []).append(loads.start(
                            ref.at[:, cols], x_all.at[k, g, rows, pl.ds(0, len(ms) * w)]))
                        continue
                    for n, m in enumerate(ms):
                        x_loads.setdefault((k, g), []).append(loads.start(
                            columns_of(ref, m), x_all.at[k, g, rows, pl.ds(n * w, w)]))

        def need(table, key):
            wait(table.pop(key, ()))

        step = min(512, n_wide)
        for g, ms in enumerate(groups):
            for k in range(len(items)):
                need(x_loads, (k, g))
                for q in range(n_wide // step):
                    need(dy_loads, k)
                    dst = slice(q * step, (q + 1) * step)
                    block = dot_tn(x_all[k, g, :, : len(ms) * w], dy_all[k, :, dst]).astype(bf16)
                    for n, m in enumerate(ms):
                        if not stacked:
                            big[evens.index(m)][k * w : (k + 1) * w, dst] = block[n * w : (n + 1) * w]
                            continue
                        for z in range(stretches):
                            row = ((z * len(evens) + evens.index(m)) * len(items) + k) * each_z
                            big[0][row : row + each_z, dst] = block[n * w + z * each_z : n * w + (z + 1) * each_z]
            if g == 0:
                wait(copies_under)
            for m in ms:
                if not stacked:
                    put(evens.index(m))
                    continue
                rows = len(items) * each_z
                if rows % 16 == 0:
                    for z in range(stretches):
                        put(0, pl.ds((z * len(evens) + evens.index(m)) * rows, rows))

    return call(
        body, info, [], [], [*arrays, *under], [], [(shape, bf16) for shape in shapes],
        [pltpu.VMEM((len(items), len(groups), 2 * tokens, pair * w), bf16),
         pltpu.VMEM((len(items), 2 * tokens, n_wide), bf16)],
        len(items) * (4 + 2 * len(evens) + 2 * count) + len(evens) * (len(under) + stretches), us, 40)


def grad_send(parts):
    return [hop(part, 2 * k) for k, part in enumerate(parts) if k]


def total(terms):
    out = terms[0].astype(f32)
    for t in terms[1:]:
        out = out + t.astype(f32)
    return out


def grad_stack(info, key, recept):
    stretches = lax.axis_size("stretch")
    own, width = recept[0].shape
    each, blocks = own // stretches, key[0].shape[1] // width
    rows = (blocks + 1) * each
    if each % 16:
        wide = total(key).astype(bf16).reshape(stretches, each, blocks, width)
        wide = jnp.swapaxes(wide, 1, 2).reshape(stretches, blocks * each, width)
        narrow = total(recept).astype(bf16).reshape(stretches, each, width)
        return jnp.concatenate([wide, narrow], axis=1).reshape(stretches * rows, width)
    terms = len(key)

    def body(info, small, get, raw, outs, big, put, scratch, loads):
        keys, recepts = scratch
        copies = []
        for z in range(stretches):
            src = pl.ds(z * each, each)
            now = [loads.start(raw[j].at[src], keys.at[j, z]) for j in range(terms)]
            copies.append(now + [loads.start(raw[terms + j].at[src], recepts.at[j, z]) for j in range(terms)])
        for z in range(stretches):
            wait(copies[z])
            for q in range(blocks):
                at = z * rows + q * each
                big[0][at : at + each, :] = total(
                    [keys[j, z, :, q * width : (q + 1) * width] for j in range(terms)]).astype(bf16)
            at = z * rows + blocks * each
            big[0][at : at + each, :] = total([recepts[j, z] for j in range(terms)]).astype(bf16)

    return call(
        body, info, [], [], [*key, *recept], [], [((stretches * rows, width), bf16)],
        [pltpu.VMEM((terms, stretches, each, blocks * width), bf16),
         pltpu.VMEM((terms, stretches, each, width), bf16)],
        stretches * 2 * terms, 4, 24)[0]


def grad_pieces(info, own, got, items, each):
    stretches = lax.axis_size("stretch")
    rows, n_wide = own.shape
    width = each * stretches

    def body(info, small, get, raw, outs, big, put, scratch, loads):
        refs = [get(k) for k in range(1 + len(got))]
        first = items * width
        table = total([r[first : first + 16, :] for r in refs])
        half = n_wide // 2
        table = table[:, :half] + table[:, half:]
        hi = table.astype(bf16)
        lo = (table - hi.astype(f32)).astype(bf16)
        for j in list(range(1, stretches)) + [0]:
            z = jnp.bitwise_xor(info[2], j)
            for k in range(items):
                src = pl.ds(pl.multiple_of(k * width + z * each, each), each)
                big[j][k * each : (k + 1) * each, :] = total([r[src, :] for r in refs]).astype(bf16)
            big[j][items * each :, :half] = hi
            big[j][items * each :, half:] = lo
            put(j)

    return call(
        body, info, [], [(a, None) for a in (own, *got)], [], [],
        [((items * each + 16, n_wide), bf16)] * stretches, [], 0, 3, 24)


def stretch_part(part):
    return lax.psum_scatter(part, "stretch", scatter_dimension=0, tiled=True)


def stretch_items(out, items):
    own = out.shape[0] // items
    return [out[k * own : (k + 1) * own].astype(f32) for k in range(items)]


def vector_rows(table, width):
    me, count = lax.axis_index("seg"), lax.axis_size("seg")
    own = table.shape[1] // count
    table = jnp.pad(table, ((0, 16 - table.shape[0]), (0, 0)))
    rows = []
    for m in range(0, count, 2):
        pair = lax.dynamic_slice_in_dim(table, (me ^ m) // 2 * (2 * own), 2 * own, 1)
        pair = jnp.pad(pair, ((0, 0), (0, width // 2 - 2 * own)))
        hi = pair.astype(bf16)
        rows.append(jnp.concatenate([hi, (pair - hi.astype(f32)).astype(bf16)], axis=1))
    return jnp.concatenate(rows, axis=0)


def vector_read(rows):
    half = rows.shape[1] // 2
    return rows[:, :half].astype(f32) + rows[:, half:].astype(f32)


def vector_own(pair, own):
    second = (lax.axis_index("seg") & 1) != 0
    lo, hi = pair[:, :own], pair[:, own : 2 * own]
    return jnp.where(second, hi, lo) + hop(jnp.where(second, lo, hi), 1)


def vector_finish(table):
    position, count = lax.axis_index("stretch"), lax.axis_size("stretch")
    bit = count // 2
    while bit:
        lo, hi = jnp.split(table, 2, axis=1)
        upper = (position & bit) != 0
        table = jnp.where(upper, hi, lo) + across(jnp.where(upper, lo, hi), bit)
        bit //= 2
    return table


def own_columns(x, me, w):
    ms = [*range(2, lax.axis_size("seg"), 2), 0]
    return jnp.concatenate([lax.dynamic_slice_in_dim(x, (me ^ m) * w, w, 1) for m in ms], axis=1)


def body(
    stream_in, cotangent, previous_mix, previous_ffn, state_num, state_den, state_exp,
    gain_one, bias_one, gain_two, bias_two, mix_key, mix_value, mix_recept,
    time_decay, time_first, chan_mix_key, chan_mix_recept,
    att_key, att_value, att_recept, att_output, chan_key, chan_value, chan_recept,
):
    mine = lax.axis_index("seg")
    position = lax.axis_index("stretch")
    stretches = lax.axis_size("stretch")
    batches, _, length, width = stream_in.shape
    tokens = batches * length
    shard = att_key.shape[0]
    fshard = chan_value.shape[0]
    wide = chan_key.shape[1]
    aligned = shard % 128 == 0
    count = lax.axis_size("seg")
    info = jnp.stack([mine, (position == 0).astype(jnp.int32), position])

    stream = stream_in.reshape(tokens, width)
    cot = cotangent.reshape(tokens, width)
    state = (state_num, state_den, state_exp)
    vectors = [gain_one, bias_one, gain_two, bias_two, mix_key, mix_value, mix_recept,
               time_decay, time_first, chan_mix_key, chan_mix_recept]

    v = Live()
    evens = list(range(0, count, 2))
    spots = {"k": 0, "v": shard, "vec": 2 * shard, "r": 2 * shard + 16, "o": 3 * shard + 16}
    each = fshard // stretches
    v.own_tm = pack(
        [(att_key, 0, shard), (att_value, 0, shard), (None, 0, 16)],
        [(att_recept, 0, shard), (att_output, 0, shard)], vectors, width)
    v.share = lax.dynamic_slice_in_dim(chan_value, position * each, each, 0)
    v.cv = chan_value
    v.last_in = stream_in[:, 0, length - 1]
    v.sync()
    v.shares = lax.all_gather(v.share, "seg", axis=0, tiled=True)
    v.one_tm = first_stage(v.own_tm)
    v.ck = pack_wide(tie(chan_key, *v.own_tm), chan_recept)
    v.tm0 = sibling({0: v.own_tm})
    v.last_in = along(tie(v.last_in, *v.tm0[1]), 1)
    v.sync()
    v.tm6 = second_stage(v.one_tm, v.one_tm)
    v.tm2 = sibling(v.one_tm)
    v.ck0 = sibling({0: v.ck})
    gathered_cv = lax.all_gather(
        jnp.concatenate([lax.dynamic_slice_in_dim(v.shares, (mine ^ m) * each, each, 0) for m in evens[1:]], axis=0),
        "stretch", axis=0, tiled=True)
    v.sync()
    v.tm6_sib = sibling(v.tm6)
    v.sync()

    v.one_ck = first_stage(v.ck)
    tm = {0: v.own_tm, **v.one_tm, **v.tm6, **v.tm0, **v.tm2, **v.tm6_sib}
    given = None
    if not aligned:
        given = lax.all_gather(jnp.stack(vectors), "seg", axis=1, tiled=True).astype(f32)
        given = jnp.pad(given, ((0, 5), (0, 0)))
    v.sums, v.vec, v.entry, v.kvr_in, *v.kvr = time_in(
        info, stream, v.last_in, previous_mix, given, tm, spots, length, shard)
    v.everyone = lax.all_gather(v.sums, "stretch")
    v.tm = tm
    v.drop("own_tm", "one_tm", "tm6", "tm0", "tm2", "tm6_sib", "share", "shares")
    v.sync()

    v.ck6 = second_stage(v.one_ck, v.one_ck)
    v.ent, v.mean, v.log, v.edge_b, v.gated, v.wkv, v.rden, v.mid, v.xb = time_out(
        info, v.kvr, v.everyone, state, v.vec, stream, v.tm, spots, length, shard)
    first_far = far_bits()[0]
    v.ck2 = sibling({first_far: v.one_ck[first_far]})
    v.edge_b = along(v.edge_b, 1)
    v.drop("everyone")
    v.sync()
    v.ck2 = {**v.ck2, **sibling({m: p for m, p in v.one_ck.items() if m != first_far})}
    v.all_ck = {0: v.ck, **v.one_ck, **v.ck6, **v.ck0, **v.ck2, **sibling(v.ck6)}
    v.gathered_cv = gathered_cv
    v.drop("ck", "one_ck", "ck6", "ck0", "ck2")
    v.sync()

    v.entry_b, v.f_in, v.near, v.far, v.act, v.frec = chan_in(
        info, v.xb, v.edge_b, previous_ffn, v.vec, v.all_ck, length, shard, fshard)
    v.all_cv = [v.cv, v.gathered_cv, hop(v.cv, 1), hop(v.gathered_cv, 1)]
    v.drop("cv", "gathered_cv")
    v.sync()
    v.block_out, v.d_fval, v.d_frec = chan_out(
        info, v.near, v.far, v.frec, v.mid, cot, v.all_cv, fshard)
    v.far_sib = hop(v.far, 1)
    v.f_sib = hop(v.f_in, 1)
    v.g_sib = hop(v.gated, 1)
    v.kvr_sib = hop(v.kvr_in, 1)
    v.drop("frec", "far")
    v.sync()

    def pairs(*arrays):
        if aligned:
            return [a for pair in arrays for a in pair]
        return [own_columns(a, mine, shard) for pair in arrays for a in pair]

    layout = "natural" if aligned else "joined"
    flat = tuple((j, None) for j in range(4))
    arrays = [v.near, v.far_sib, v.d_fval, hop(v.d_fval, 1)]
    v.stack_cv = weight_grad(info, arrays, [flat], "blocks", 6, stacked=True)[0]
    v.dfrec_sib = hop(v.d_frec, 1)
    v.drop("near", "far_sib")
    v.sync()

    z_cv = stretch_part(v.stack_cv)
    v.dpre = hidden_back(info, v.act, v.d_fval, v.all_cv, fshard)
    d_frec = tie(v.d_frec, v.dpre)
    if aligned:
        v.parts_c = weight_grad(
            info, [v.f_in, v.f_sib, d_frec, v.dfrec_sib], [((0, 1), (1, 1), (2, None), (3, None))], layout, 3)
    else:
        v.parts_c = weight_grad(
            info, [*pairs((v.f_in[1], v.f_sib[1])), d_frec, v.dfrec_sib], [flat], layout, 3)
    v.got_c = grad_send(v.parts_c)
    dpre_sib = hop(v.dpre, 1)
    v.head_b, v.sums_c, v.dxt, v.dxb = chan_back(
        info, v.dpre, v.d_frec, v.xb, v.entry_b, v.vec, v.all_ck, length, shard, fshard)
    v.next_b = along(v.head_b, -1)
    dpre = tie(v.dpre, v.dxt)
    if aligned:
        v.parts_ck = weight_grad(
            info, [v.f_in, v.f_sib, dpre, dpre_sib], [((0, 0), (1, 0), (2, None), (3, None))], layout, 7, True)
    else:
        v.parts_ck = weight_grad(
            info, [*pairs((v.f_in[0], v.f_sib[0])), dpre, dpre_sib], [flat], layout, 7, True)
    v.drop("all_ck", "all_cv", "xb", "entry_b", "act", "d_fval", "dpre", "stack_cv")
    v.sync()

    v.got_ck = grad_send(v.parts_ck)
    backs, v.sums_m, v.dmid, *lows, gn = mid_back(
        info, v.dxt, v.dxb, v.next_b, v.head_b, v.mid, cot, v.vec, v.kvr, v.wkv, v.rden, v.ent, v.tm, spots,
        length, shard)
    v.dbr, v.drec = lows[:2], lows[2:]
    back = exchange_two(backs)
    *v.grads, v.head_a, v.sums_t, v.extra, v.d_kv, v.dxs, v.dxa = time_back(
        info, gn, v.wkv, v.kvr, v.ent, back, v.sums, state, v.drec, stream, v.entry, v.vec,
        v.tm, spots, length, shard)
    v.dbr_sib = [hop(a, 1) for a in v.dbr]
    v.drec_sib = [hop(a, 1) for a in v.drec]
    dys = [([(at, None), (at + 1, None)], [(at + 2, None), (at + 3, None)]) for at in (0, 4)]
    lows = [*v.dbr, *v.dbr_sib, *v.drec, *v.drec_sib]
    gated = tie(v.gated, v.d_kv)
    if aligned:
        v.parts_or = weight_grad(
            info, [*lows, gated, v.g_sib, v.kvr_in, v.kvr_sib],
            [((8, None), (9, None), *dys[0]), ((10, 2), (11, 2), *dys[1])], layout, 6, stacked=True)
    else:
        xs = pairs((gated, v.g_sib), (v.kvr_in[2], v.kvr_sib[2]))
        v.parts_or = weight_grad(
            info, [*lows, *xs], [((8, None), (9, None), *dys[0]), ((10, None), (11, None), *dys[1])], layout, 6,
            stacked=True)
    v.drop("wkv", "kvr", "ent", "sums", "entry", "tm", "dxt", "dxb", "mid", "rden", "next_b", "head_b")
    v.sync()
    v.dkv_sib = hop(v.d_kv, 1)
    v.next_a = along(v.head_a, -1)
    z_or = stretch_part(v.parts_or[0])
    v.stack = grad_stack(info, [v.parts_ck[0], *v.got_ck], [v.parts_c[0], *v.got_c])
    v.drop("gated", "g_sib", "dbr", "dbr_sib", "drec", "drec_sib", "f_in", "f_sib", "d_frec",
           "parts_ck", "got_ck", "parts_c", "got_c", "parts_or")
    v.z_cv = z_cv
    v.sync()

    v.parts_cv = [v.z_cv[k * each : (k + 1) * each] for k in range(len(evens))]
    z_rest = stretch_part(v.stack)
    v.got_cv = grad_send(v.parts_cv)
    sums_i, v.grad_stream = in_back(info, v.dxs, v.dxa, v.next_a, v.dmid, stream, v.vec, length)
    table = jnp.concatenate([sums_i, v.sums_m, v.sums_t, v.extra, v.sums_c], axis=0)
    under = [vector_rows(table, width)]
    if aligned:
        v.parts_kv = weight_grad(
            info, [v.kvr_in, v.kvr_sib, v.d_kv, v.dkv_sib],
            [tuple((j, k) for j in range(4)) for k in range(2)], layout, 7, under=under)
    else:
        xs = pairs(*[(v.kvr_in[k], v.kvr_sib[k]) for k in range(2)])
        v.parts_kv = weight_grad(
            info, [*xs, v.d_kv, v.dkv_sib],
            [((2 * k, None), (2 * k + 1, None), (4, k), (5, k)) for k in range(2)], layout, 7, under=under)
    v.drop("kvr_in", "kvr_sib", "d_kv", "dkv_sib", "dxs", "dxa", "dmid", "next_a", "stack",
           "sums_m", "sums_t", "extra", "sums_c", "z_cv")
    v.sync()

    v.got_kv = grad_send(v.parts_kv)
    v.heads = lax.all_gather(v.head_a, "stretch")[0]
    v.out_cv = total([v.parts_cv[0], *v.got_cv])
    v.drop("parts_cv", "got_cv")
    v.z_or = z_or
    v.sync()
    rows = shard // stretches
    by_hops = stretches == 4 and rows % 16 == 0
    if by_hops:
        v.pieces = grad_pieces(info, v.parts_kv[0], v.got_kv, 2, rows)
    else:
        whole = total([v.parts_kv[0], *v.got_kv])
        first = 2 * shard
        v.table = vector_read(whole[first:])
        v.part_kv = whole[:first].astype(bf16).reshape(2, stretches, rows, width)
        v.part_kv = jnp.swapaxes(v.part_kv, 0, 1).reshape(first, width)
    parts = [v.z_or[2 * k * rows : 2 * (k + 1) * rows] for k in range(len(evens))]
    v.parts_or = [parts[0], *grad_send(parts)]
    v.drop("parts_kv", "got_kv", "z_or")
    v.sync()
    blocks = wide // width
    out_ck = jnp.concatenate([z_rest[q * rows : (q + 1) * rows] for q in range(blocks)], axis=1).astype(f32)
    out_c = z_rest[blocks * rows : (blocks + 1) * rows].astype(f32)
    if by_hops:
        pieces = [v.pieces[0], *[across(v.pieces[j], j) for j in range(1, stretches)]]
        z_kv = total([p[: 2 * rows] for p in pieces])
        small = sum(vector_read(p[2 * rows : 2 * rows + 11]) for p in pieces)
        small = lax.dynamic_slice_in_dim(vector_own(small, shard), position * rows, rows, 1)
    else:
        z_kv = stretch_part(v.part_kv)
        small = vector_finish(vector_own(v.table[:11], shard))
    out_k, out_v = stretch_items(z_kv, 2)
    out_o, out_r = stretch_items(total(v.parts_or), 2)
    out_cv = v.out_cv
    grad_previous_mix = v.heads
    block_out, grad_stream = v.block_out, v.grad_stream

    shape = stream_in.shape
    return (
        block_out.reshape(shape), grad_stream.reshape(shape), *[small[i] for i in range(11)],
        out_k, out_v, out_r, out_o, out_ck, out_cv, out_c,
        *v.grads[:3], grad_previous_mix[:, None], v.grads[3], v.mean, v.log,
    )


def solution(mesh):
    rows = P(None, "seg", "stretch", None)
    state = P(None, "seg", None)
    both = P(("seg", "stretch"))
    table = P(("seg", "stretch"), None)
    return jax.shard_map(
        body,
        mesh=mesh,
        in_specs=(rows,) * 2 + (state,) * 5 + (P("seg"),) * 11 + (P("seg", None),) * 7,
        out_specs=(rows,) * 2 + (both,) * 11 + (table,) * 7 + (state,) * 7,
        check_vma=False,
    )
```

```python
import jax
import jax.numpy as jnp
from jax import lax
from jax.experimental import pallas as pl
from jax.experimental.pallas import tpu as pltpu
from jax.sharding import PartitionSpec as P

epsilon = 1e-05
bf16 = jnp.bfloat16
f32 = jnp.float32
ROWS = 64
STEP = 512
LANES = 512
LIMIT = 63
MIB = 2**20
G1, B1, G2, B2, MK, MV, MR, DECAY, FIRST, CMK, CMR = range(11)


def hop(value, bit):
    count = lax.axis_size("seg")
    return lax.ppermute(value, "seg", [(i, i ^ bit) for i in range(count)])


def along(value, steps):
    count = lax.axis_size("stretch")
    first, last = (max(0, -steps), min(count, count - steps))
    return lax.ppermute(value, "stretch", [(i, i + steps) for i in range(first, last)])


def across(value, j):
    count = lax.axis_size("stretch")
    return lax.ppermute(value, "stretch", [(i, i ^ j) for i in range(count)])


def exchange(value):
    count = lax.axis_size("stretch")
    if count == 4:
        near, far = across(value, 1), across(value, 2)
        return [value, near, far, across(near, 2)]
    return lax.all_gather(value, "stretch")


def tie(value, *others):
    return lax.optimization_barrier((value, *others))[0]


def exchange_two(value):
    if lax.axis_size("stretch") != 4:
        return lax.all_gather(value, "stretch")
    near = across(value, 1)
    return [value, near, across(jnp.concatenate([value, near], axis=0), 2)]


class Live:
    def __init__(self):
        self.__dict__["held"] = {}

    def __getattr__(self, name):
        return self.held[name]

    def __setattr__(self, name, value):
        self.held[name] = value

    def drop(self, *names):
        for name in names:
            del self.held[name]

    def sync(self):
        self.__dict__["held"] = lax.optimization_barrier(self.held)


def far_bits():
    bits, b = [], 2
    while b < lax.axis_size("seg"):
        bits.append(b)
        b *= 2
    return bits


def relative_order():
    count = lax.axis_size("seg")
    return list(range(0, count, 2)) + list(range(1, count, 2))


def first_stage(own):
    return {b: [hop(part, b) for part in own] for b in far_bits()}


def second_stage(direct, held):
    rest = far_bits()
    held = dict(held)
    for m in sorted(range(0, lax.axis_size("seg"), 2), key=lambda m: (bin(m).count("1"), m)):
        if m == 0 or m in held:
            continue
        bits = [b for b in rest if m & b]
        held[m] = [hop(held[m ^ bits[-1]][0], bits[-1]), hop(held[m ^ bits[0]][1], bits[0])]
    return {m: held[m] for m in held if m not in direct}


def sibling(pieces):
    return {m ^ 1: [hop(p, 1) for p in parts] for m, parts in pieces.items()}


def plan(pieces, first, rows):
    steps, at = [], 0
    for m in relative_order():
        base = 0
        for part in pieces[m]:
            lo, hi = max(first, base), min(first + rows, base + part.shape[0])
            if lo < hi:
                steps.append((at, lo - base, hi - lo, m, lo - first))
            base += part.shape[0]
            at += 1
    return steps


def flat_pieces(pieces):
    return [part for m in relative_order() for part in pieces[m]]


class Loads:
    def __init__(self, sems):
        self.sems, self.used = sems, 0

    def start(self, src, dst):
        copy = pltpu.make_async_copy(src, dst, self.sems.at[self.used])
        self.used += 1
        copy.start()
        return copy

    def pieces(self, steps, refs, target, place):
        return [
            self.start(refs[piece].at[pl.ds(row, count)], target.at[pl.ds(place(m) + within, count)])
            for piece, row, count, m, within in steps
        ]


def wait(copies):
    for c in copies:
        c.wait()


def call(body, info, small, large, raw, outs, big_outs, scratch, copies, us, limit, late=()):
    n_small, n_large, n_raw = len(small), len(large), len(raw)
    n_out, n_big = len(outs), len(big_outs)

    def shape_of(array, index):
        return array.shape if index is None else array.shape[1:]

    def kernel(*refs):
        at = 0

        def take(n):
            nonlocal at
            at += n
            return refs[at - n : at]

        (info_ref,), small_refs, large_refs, raw_refs = take(1), take(n_small), take(n_large), take(n_raw)
        out_refs, big_refs = take(n_out), take(n_big)
        buffers, big_buffers, (sems,) = take(n_large), take(n_big), take(1)
        rest = take(len(refs) - at)
        loads = Loads(sems)
        pending = []
        for k, ((array, index), ref, buf) in enumerate(zip(large, large_refs, buffers)):
            src = ref if index is None else ref.at[index]
            pending.append((src, buf) if k in late else loads.start(src, buf))

        def start_late():
            for k in late:
                pending[k] = loads.start(*pending[k])

        loads.start_late = start_late
        stored = {}

        def get(k):
            if pending[k] is not None:
                pending[k].wait()
                pending[k] = None
            return buffers[k]

        def put(k, part=None):
            src, dst = big_buffers[k], big_refs[k]
            if part is not None:
                src, dst = src.at[part], dst.at[part]
            stored.setdefault(k, []).append(loads.start(src, dst))

        body(info_ref, small_refs, get, raw_refs, out_refs, big_buffers, put, rest, loads)
        for k in range(n_large):
            get(k)
        for k in range(n_big):
            if k not in stored:
                put(k)
        wait([c for copies in stored.values() for c in copies])

    hbm = pl.BlockSpec(memory_space=pltpu.HBM)
    vmem = pl.BlockSpec(memory_space=pltpu.VMEM)
    return pl.pallas_call(
        kernel,
        out_shape=[jax.ShapeDtypeStruct(s, d) for s, d in (*outs, *big_outs)],
        in_specs=[pl.BlockSpec(memory_space=pltpu.SMEM)] + [vmem] * n_small + [hbm] * (n_large + n_raw),
        out_specs=[vmem] * n_out + [hbm] * n_big,
        scratch_shapes=[pltpu.VMEM(shape_of(a, i), a.dtype) for a, i in large]
        + [pltpu.VMEM(s, d) for s, d in big_outs]
        + [pltpu.SemaphoreType.DMA((max(1, n_large + n_big + copies),))]
        + list(scratch),
        compiler_params=pltpu.CompilerParams(vmem_limit_bytes=LIMIT * MIB),
        cost_estimate=pl.CostEstimate(
            flops=0, bytes_accessed=int(us * 1e3), transcendentals=0),
    )(info, *small, *[a for a, _ in large], *raw)


def natural(me, rows):
    return lambda m: pl.multiple_of(jnp.bitwise_xor(me, m) * rows, rows)


def dot_nn(a, b):
    return jnp.dot(a, b, preferred_element_type=f32)


def dot_nt(a, b):
    return lax.dot_general(a, b, (((1,), (1,)), ((), ())), preferred_element_type=f32)


def dot_tn(a, b):
    return lax.dot_general(a, b, (((0,), (0,)), ((), ())), preferred_element_type=f32)


def norm(rows):
    centre = rows - jnp.mean(rows, axis=-1, keepdims=True)
    inverse = lax.rsqrt(jnp.mean(centre * centre, axis=-1, keepdims=True) + epsilon)
    return centre * inverse, inverse


def norm_back(d, unit, inverse, gain):
    q = d * gain
    return inverse * (
        q
        - jnp.mean(q, axis=-1, keepdims=True)
        - unit * jnp.mean(q * unit, axis=-1, keepdims=True)
    )


def down_one(rows, entering):
    at = lax.broadcasted_iota(jnp.int32, rows.shape, 0)
    return jnp.where(at == 0, entering, pltpu.roll(rows, 1, 0))


def up_one(rows, entering):
    at = lax.broadcasted_iota(jnp.int32, rows.shape, 0)
    last = rows.shape[0] - 1
    return jnp.where(at == last, entering, pltpu.roll(rows, last, 0))


def fold(rows):
    total = rows[:8]
    for k in range(8, rows.shape[0], 8):
        total = total + rows[k : k + 8]
    return total


def columns(width, step):
    step = min(step, width)

    def run(body):
        @pl.loop(0, width // step)
        def _(n):
            body(pl.ds(pl.multiple_of(n * step, step), step))

    return run


def row_chunk(b, i, length):
    return pl.ds(pl.multiple_of(b * length + i * ROWS, ROWS), ROWS)


def two_part(mat, value):
    hi = value.astype(bf16)
    lo = (value - hi.astype(f32)).astype(bf16)
    return dot_nn(mat, hi) + dot_nn(mat, lo)


def triangle(length, strictly_before):
    row = lax.broadcasted_iota(jnp.int32, (length, length), 0)
    col = lax.broadcasted_iota(jnp.int32, (length, length), 1)
    keep = (col < row) if strictly_before else (col > row)
    return keep.astype(f32).astype(bf16)


def column_sums(out_ref, sum_ref):
    for k in range(sum_ref.shape[0]):
        out_ref[k : k + 1, :] = jnp.sum(sum_ref[k], axis=0, keepdims=True)


def pack(parts_a, parts_b, vectors, width):
    arrays = [p[0] for p in (*parts_a, *parts_b) if p[0] is not None]
    shard = vectors[0].shape[0]

    def kernel(*refs):
        vec_refs, ins = refs[: len(vectors)], refs[len(vectors) : len(vectors) + len(arrays)]
        outs, (table, sems) = refs[len(vectors) + len(arrays) : -2], refs[-2:]
        copies, n = [], 0
        for out, parts in zip(outs, (parts_a, parts_b)):
            at = 0
            for array, first, count in parts:
                if array is None:
                    spot = (out, at)
                else:
                    copies.append(pltpu.make_async_copy(
                        ins[n].at[pl.ds(first, count)], out.at[pl.ds(at, count)], sems.at[n]))
                    copies[-1].start()
                    n += 1
                at += count
        table[...] = jnp.zeros_like(table)
        for k, ref in enumerate(vec_refs):
            table[k : k + 1, :shard] = ref[...].astype(f32)
        spot[0][spot[1] : spot[1] + 16, :] = table[...].astype(bf16)
        wait(copies)

    return pl.pallas_call(
        kernel,
        out_shape=[jax.ShapeDtypeStruct((sum(p[2] for p in parts), width), bf16)
                   for parts in (parts_a, parts_b)],
        in_specs=[pl.BlockSpec(memory_space=pltpu.VMEM)] * len(vectors)
        + [pl.BlockSpec(memory_space=pltpu.HBM)] * len(arrays),
        out_specs=[pl.BlockSpec(memory_space=pltpu.VMEM)] * 2,
        scratch_shapes=[pltpu.VMEM((16, width), f32), pltpu.SemaphoreType.DMA((len(arrays),))],
        compiler_params=pltpu.CompilerParams(vmem_limit_bytes=LIMIT * MIB),
        cost_estimate=pl.CostEstimate(flops=0, bytes_accessed=1000, transcendentals=0),
    )(*[x.reshape(1, shard) for x in vectors], *arrays)


def pack_wide(key, recept):
    rows, wide = key.shape
    width = recept.shape[1]
    each = recept.shape[0] * width // wide
    half = (rows + each) // 32 * 16

    def kernel(key_ref, recept_ref, top_ref, low_ref, sems):
        copies = [
            pltpu.make_async_copy(key_ref.at[pl.ds(0, half)], top_ref, sems.at[0]),
            pltpu.make_async_copy(
                key_ref.at[pl.ds(half, rows - half)], low_ref.at[pl.ds(0, rows - half)], sems.at[1])]
        for q in range(wide // width):
            copies.append(pltpu.make_async_copy(
                recept_ref.at[pl.ds(q * each, each)],
                low_ref.at[pl.ds(rows - half, each), pl.ds(q * width, width)], sems.at[2 + q]))
        for c in copies:
            c.start()
        wait(copies)

    return pl.pallas_call(
        kernel,
        out_shape=[jax.ShapeDtypeStruct((n, wide), bf16) for n in (half, rows + each - half)],
        in_specs=[pl.BlockSpec(memory_space=pltpu.HBM)] * 2,
        out_specs=[pl.BlockSpec(memory_space=pltpu.VMEM)] * 2,
        scratch_shapes=[pltpu.SemaphoreType.DMA((2 + wide // width,))],
        compiler_params=pltpu.CompilerParams(vmem_limit_bytes=LIMIT * MIB),
        cost_estimate=pl.CostEstimate(flops=0, bytes_accessed=1000, transcendentals=0),
    )(key, recept)


def recept_blocks(loads, steps, raw, w, info, shard, width, wide):
    each = shard * width // wide
    place = natural(info[0], shard)
    sem = loads.sems.at[loads.used]
    loads.used += 1

    @pl.loop(0, wide // width)
    def _(q):
        for piece, row, rows, m, within in steps:
            pltpu.make_async_copy(
                raw[piece].at[pl.ds(row, rows), pl.ds(pl.multiple_of(q * width, width), width)],
                w.at[pl.ds(pl.multiple_of(place(m) + q * each, each) + within, rows)], sem).start()

    return lambda: pltpu.make_async_copy(w, w, sem).wait()


def time_in(info, stream, last, previous, given, pieces, spots, length, shard):
    tokens, width = stream.shape
    batches = tokens // length
    plans = [plan(pieces, spots[k], shard) for k in "kvr"]
    vplan = plan(pieces, spots["vec"], 16)
    order = relative_order()

    def body(info, small, get, raw, outs, big, put, scratch, loads):
        last_ref, prev_ref = small[:2]
        sum_ref, vec_ref, entry_ref = outs
        in_ref = big[0]
        w, vt = scratch
        place = natural(info[0], shard)
        vcopies = loads.pieces(vplan, raw, vt, lambda m: order.index(m) * 16)
        copies = [loads.pieces(plans[k], raw, w.at[k], place) for k in range(3)]
        wait(vcopies)
        if given is not None:
            vec_ref[...] = small[2][...]
        else:
            for at, m in enumerate(order):
                vec_ref[:, pl.ds(place(m), shard)] = vt[at * 16 : at * 16 + 16, :shard].astype(f32)
        unit, _ = norm(last_ref[...].astype(f32))
        edge = unit * vec_ref[G1 : G1 + 1] + vec_ref[B1 : B1 + 1]
        for b in range(batches):
            entry_ref[b : b + 1, :] = jnp.where(info[1] == 1, prev_ref[b], edge[b : b + 1])
        stream_ref = get(0)

        for b in range(batches):
            def step(i, before):
                r = row_chunk(b, i, length)
                na, _ = norm(stream_ref[r, :].astype(f32))
                xa = na * vec_ref[G1 : G1 + 1] + vec_ref[B1 : B1 + 1]
                xs = down_one(xa, before)
                for k, row in enumerate((MK, MV, MR)):
                    mix = vec_ref[row : row + 1]
                    in_ref[k, r, :] = (xa * mix + xs * (1.0 - mix)).astype(bf16)
                return xa[ROWS - 1 :]
            lax.fori_loop(0, length // ROWS, step, entry_ref[b : b + 1])
        put(0)
        def project(k):
            wait(copies[k])
            @columns(width, STEP)
            def _(n):
                big[1 + k][:, n] = dot_nn(in_ref[k], w[k, :, n]).astype(big[1 + k].dtype)
            put(1 + k)
        project(0)
        project(1)
        keys_ref, vals_ref = big[1], big[2]
        for b in range(batches):
            t = slice(b * length, (b + 1) * length)
            @columns(width, LANES)
            def _(n):
                rate = -jnp.exp(vec_ref[DECAY : DECAY + 1, n])
                at = lax.broadcasted_iota(jnp.int32, (length, 1), 0).astype(f32)
                shifted = keys_ref[t, n] - at * rate
                peak = jnp.max(shifted, axis=0, keepdims=True)
                factor = jnp.exp(shifted - peak)
                sum_ref[b : b + 1, n] = jnp.sum(
                    factor * vals_ref[t, n].astype(f32), axis=0, keepdims=True)
                sum_ref[batches + b : batches + b + 1, n] = jnp.sum(factor, axis=0, keepdims=True)
                sum_ref[2 * batches + b : 2 * batches + b + 1, n] = peak + (length - 1.0) * rate
        project(2)

    extra = [] if given is None else [given]
    return call(
        body, info, [last, previous, *extra], [(stream, None)], flat_pieces(pieces),
        [((3 * batches, width), f32), ((16, width), f32), ((batches, width), f32)],
        [((3, tokens, width), bf16)] + [((tokens, width), f32)] * 3,
        [pltpu.VMEM((3, width, width), bf16), pltpu.VMEM((16 * len(order), width), bf16)],
        len(vplan) + sum(map(len, plans)), 9, 40)


def wkv_terms(kvr_ref, ent_ref, vec_ref, b, t, n, batches, length):
    rate = -jnp.exp(vec_ref[DECAY : DECAY + 1, n])
    at = lax.broadcasted_iota(jnp.int32, (length, 1), 0).astype(f32)
    keys = kvr_ref[0][t, n]
    shifted = keys - at * rate
    peak = jnp.max(shifted, axis=0, keepdims=True)
    factor = jnp.exp(shifted - peak)
    near = (at - 1.0) * rate + peak
    opening = at * rate + ent_ref[2 * batches + b : 2 * batches + b + 1, n]
    reward = vec_ref[FIRST : FIRST + 1, n] + keys
    top = jnp.maximum(jnp.maximum(near, opening), reward)
    return at, factor, jnp.exp(near - top), jnp.exp(opening - top), jnp.exp(reward - top)


def time_out(info, kvr, everyone, state, vec, stream, pieces, spots, length, shard):
    tokens, width = stream.shape
    batches = tokens // length
    stretches = len(everyone)
    relative = isinstance(everyone, list)
    if not relative:
        everyone = [everyone]
    steps = plan(pieces, spots["o"], shard)

    def body(info, small, get, raw, outs, big, put, scratch, loads):
        every_ref, (num_ref, den_ref, exp_ref, vec_ref) = small[:-4], small[-4:]
        if not relative:
            every_ref = [every_ref[0].at[z] for z in range(stretches)]
        ent_ref, mean_ref, log_ref, edge_ref = outs
        gated_ref, wkv_ref, rden_ref, mid_ref, xb_ref = big
        (w,) = scratch
        copies = loads.pieces(steps, raw, w, natural(info[0], shard))
        span = -jnp.exp(vec_ref[DECAY : DECAY + 1, :]) * float(length)

        def merge(upto, b):
            upto_f = upto.astype(f32) if upto is not stretches else float(stretches)
            logits = []
            for j in range(stretches):
                row, z = 2 * batches + b, jnp.bitwise_xor(info[2], j) if relative else jnp.int32(j)
                logit = every_ref[j][row : row + 1, :] + (upto_f - 1.0 - z.astype(f32)) * span
                logits.append(logit if upto is stretches else jnp.where(z < upto, logit, -jnp.inf))
            opening = exp_ref[b] + upto_f * span
            top = opening
            for logit in logits:
                top = jnp.maximum(top, logit)
            start = jnp.exp(opening - top)
            num, den = num_ref[b] * start, den_ref[b] * start
            for j, logit in enumerate(logits):
                weight = jnp.exp(logit - top)
                num = num + weight * every_ref[j][b : b + 1, :]
                den = den + weight * every_ref[j][batches + b : batches + b + 1, :]
            return num, den, top

        for b in range(batches):
            for k, part in enumerate(merge(info[2], b)):
                ent_ref[k * batches + b : k * batches + b + 1, :] = part
            num, den, top = merge(stretches, b)
            mean_ref[b] = num / den
            log_ref[b] = top + jnp.log(den)

        lower = triangle(length, True)
        kvr_ref = [get(k) for k in range(3)]
        for b in range(batches):
            t = slice(b * length, (b + 1) * length)
            @columns(width, LANES)
            def _(n):
                _, factor, p, o, e = wkv_terms(kvr_ref, ent_ref, vec_ref, b, t, n, batches, length)
                vals = kvr_ref[1][t, n].astype(f32)
                num = (two_part(lower, factor * vals) * p
                       + ent_ref[b : b + 1, n] * o + vals * e)
                den = (two_part(lower, factor) * p
                       + ent_ref[batches + b : batches + b + 1, n] * o + e)
                rden = 1.0 / den
                wkv = num * rden
                wkv_ref[t, n] = wkv
                rden_ref[t, n] = rden.astype(bf16)
                gated_ref[t, n] = (jax.nn.sigmoid(kvr_ref[2][t, n].astype(f32)) * wkv).astype(bf16)
        put(0)
        put(1)
        put(2)
        wait(copies)
        stream_ref = get(3)
        @columns(width, STEP)
        def _(n):
            mid_ref[:, n] = stream_ref[:, n].astype(f32) + dot_nn(gated_ref[...], w[:, n])
        put(3)
        @pl.loop(0, tokens // ROWS)
        def _(i):
            r = row_chunk(0, i, 0)
            nb, _ = norm(mid_ref[r, :])
            xb_ref[r, :] = nb * vec_ref[G2 : G2 + 1] + vec_ref[B2 : B2 + 1]
        for b in range(batches):
            last = (b + 1) * length
            edge_ref[b : b + 1, :] = xb_ref[last - 1 : last, :]

    one, low = ((tokens, width), f32), ((tokens, width), bf16)
    return call(
        body, info, [*everyone, *state, vec], [(a, None) for a in (*kvr, stream)], flat_pieces(pieces),
        [((3 * batches, width), f32), ((batches, 1, width), f32), ((batches, 1, width), f32),
         ((batches, width), f32)],
        [low, one, low, one, one],
        [pltpu.VMEM((width, width), bf16)], len(steps), 7, 40)


def key_blocks(loads, steps, raw, w, info, shard, fshard, start=0):
    count = lax.axis_size("seg")
    half = count // 2
    place = natural(info[0], shard)
    first = loads.used
    loads.used += count

    @pl.loop(0, count)
    def _(turn):
        at = lax.rem(turn + start, count)
        m = lax.rem(at, half) * 2 + lax.div(at, half)
        cols = pl.ds(natural(info[0], fshard)(m), fshard)
        dst = pl.ds(pl.multiple_of(at * fshard, fshard), fshard)
        for piece, row, rows, m2, within in steps:
            pltpu.make_async_copy(
                raw[piece].at[pl.ds(row, rows), cols], w.at[pl.ds(place(m2) + within, rows), dst],
                loads.sems.at[first + at]).start()

    def arrive(at):
        block = w.at[:, pl.ds(at * fshard, fshard)]
        pltpu.make_async_copy(block, block, loads.sems.at[first + at]).wait()

    return arrive


def value_blocks(loads, raw, w, fshard, stretches, after_first=None):
    order = relative_order()
    others = [m for m in order if m % 2 == 0 and m]
    each = fshard // stretches
    out = {}
    for at, m in enumerate(order):
        own, gathered = raw[2 * (m % 2)], raw[2 * (m % 2) + 1]
        base = m - m % 2
        if base == 0:
            out[m] = [loads.start(own, w.at[pl.ds(at * fshard, fshard)])]
            if at == 0 and after_first is not None:
                after_first()
            continue
        out[m] = [
            loads.start(
                gathered.at[pl.ds((z * len(others) + others.index(base)) * each, each)],
                w.at[pl.ds(at * fshard + z * each, each)])
            for z in range(stretches)
        ]
    return out


def value_copies(stretches):
    count = lax.axis_size("seg")
    return 2 + (count - 2) * stretches


def chan_in(info, xb, edge, previous, vec, pieces_ck, length, shard, fshard):
    tokens, width = xb.shape
    batches = tokens // length
    order = relative_order()
    wide = fshard * len(order)
    steps_k = plan(pieces_ck, 0, shard)
    steps_c = plan(pieces_ck, shard, shard * width // wide)

    def body(info, small, get, raw, outs, big, put, scratch, loads):
        edge_ref, prev_ref, vec_ref = small
        (entry_ref,) = outs
        in_ref, near_ref, far_ref, act_ref, frec_ref = big
        wk, wc = scratch
        half = len(order) // 2
        turn = order[half:] + order[:half]
        arrive = key_blocks(loads, steps_k, raw, wk, info, shard, fshard, half)
        arrive_c = recept_blocks(loads, steps_c, raw, wc, info, shard, width, wide)
        for b in range(batches):
            entry_ref[b : b + 1, :] = jnp.where(info[1] == 1, prev_ref[b], edge_ref[b : b + 1, :])
        xb_ref = get(0)
        for b in range(batches):
            def step(i, before):
                r = row_chunk(b, i, length)
                x = xb_ref[r, :].astype(f32)
                xt = down_one(x, before)
                for k, row in enumerate((CMK, CMR)):
                    mix = vec_ref[row : row + 1]
                    in_ref[k, r, :] = (x * mix + xt * (1.0 - mix)).astype(bf16)
                return x[ROWS - 1 :]
            lax.fori_loop(0, length // ROWS, step, entry_ref[b : b + 1])
        put(0)
        for m in turn:
            at = order.index(m)
            arrive(at)
            hid_ref, lo = (near_ref, at * fshard) if at < half else (far_ref, (at - half) * fshard)
            act = jnp.maximum(dot_nn(in_ref[0], wk[:, at * fshard : (at + 1) * fshard]), 0.0)
            act_ref[:, at * fshard : (at + 1) * fshard] = act.astype(bf16)
            hid_ref[:, lo : lo + fshard] = (act * act).astype(bf16)
            if m == turn[half - 1]:
                put(2)
        put(1)
        put(3)
        arrive_c()
        @columns(width, STEP)
        def _(n):
            frec_ref[:, n] = dot_nn(in_ref[1], wc[:, n])

    return call(
        body, info, [edge, previous, vec], [(xb, None)], flat_pieces(pieces_ck),
        [((batches, width), f32)],
        [((2, tokens, width), bf16), ((tokens, wide // 2), bf16), ((tokens, wide // 2), bf16),
         ((tokens, wide), bf16), ((tokens, width), f32)],
        [pltpu.VMEM((width, wide), bf16), pltpu.VMEM((width, width), bf16)],
        1 + len(order), 11, 40)


def chan_out(info, near, far, frec, mid, cot, cv, fshard):
    tokens, width = mid.shape
    order = relative_order()
    wide = fshard * len(order)
    stretches = lax.axis_size("stretch")

    def body(info, small, get, raw, outs, big, put, scratch, loads):
        out_ref, df_ref, dr_ref = big
        w, fval = scratch
        blocks = value_blocks(loads, raw, w, fshard, stretches)
        loads.start_late()
        half = len(order) // 2
        for k in range(2):
            hid_ref = get(k)
            for m in order[k * half : (k + 1) * half]:
                wait(blocks[m])
            @columns(width, STEP)
            def _(n):
                part = dot_nn(hid_ref[...], w[k * wide // 2 : (k + 1) * wide // 2, n])
                fval[:, n] = part if k == 0 else fval[:, n] + part
        frec_ref, mid_ref, cot_ref = get(2), get(3), get(4)
        @pl.loop(0, tokens // ROWS)
        def _(i):
            r = row_chunk(0, i, 0)
            sig = jax.nn.sigmoid(frec_ref[r, :].astype(f32))
            cots, value = cot_ref[r, :].astype(f32), fval[r, :]
            df_ref[r, :] = (cots * sig).astype(bf16)
            out_ref[r, :] = (mid_ref[r, :] + sig * value).astype(bf16)
            dr_ref[r, :] = (cots * value * sig * (1.0 - sig)).astype(bf16)

    low = ((tokens, width), bf16)
    return call(
        body, info, [], [(a, None) for a in (near, far, frec, mid, cot)], cv, [], [low, low, low],
        [pltpu.VMEM((wide, width), bf16), pltpu.VMEM((tokens, width), f32)],
        value_copies(stretches), 7, 40, late=(2, 3, 4))


def hidden_back(info, act, dfval, cv, fshard):
    tokens, width = dfval.shape
    order = relative_order()
    wide = fshard * len(order)
    stretches = lax.axis_size("stretch")

    def body(info, small, get, raw, outs, big, put, scratch, loads):
        (dpre_ref,) = big
        (wv,) = scratch
        values = value_blocks(loads, raw, wv, fshard, stretches, loads.start_late)
        dfval_ref, act_ref = get(0), get(1)
        for at, m in enumerate(order):
            wait(values[m])
            block = slice(at * fshard, (at + 1) * fshard)
            d = dot_nt(dfval_ref[...], wv[block, :]) * (2.0 * act_ref[:, block].astype(f32))
            dpre_ref[:, block] = d.astype(bf16)
            put(0, (slice(None), pl.ds(at * fshard, fshard)))

    return call(
        body, info, [], [(dfval, None), (act, None)], cv, [], [((tokens, wide), bf16)],
        [pltpu.VMEM((wide, width), bf16)], value_copies(stretches) + len(order), 7, 40, late=(1,))[0]


def chan_back(info, dpre, dfrec, xb, entry, vec, pieces_ck, length, shard, fshard):
    tokens, width = xb.shape
    batches = tokens // length
    order = relative_order()
    wide = fshard * len(order)
    steps_k = plan(pieces_ck, 0, shard)
    steps_c = plan(pieces_ck, shard, shard * width // wide)

    def body(info, small, get, raw, outs, big, put, scratch, loads):
        entry_ref, vec_ref = small
        head_ref, total_ref = outs
        dxt_ref, dxb_ref = big
        wk, wc, df, dr, sum_ref = scratch
        arrive_c = recept_blocks(loads, steps_c, raw, wc, info, shard, width, wide)
        arrive = key_blocks(loads, steps_k, raw, wk, info, shard, fshard)
        loads.start_late()
        dfrec_ref = get(0)
        arrive_c()
        @columns(width, STEP)
        def _(n):
            dr[:, n] = dot_nt(dfrec_ref[...], wc[n, :])
        dpre_ref = get(1)
        half = len(order) // 2
        for k in range(2):
            for at in range(k * half, (k + 1) * half):
                arrive(at)
            part_of = slice(k * wide // 2, (k + 1) * wide // 2)
            @columns(width, STEP)
            def _(n):
                part = dot_nt(dpre_ref[:, part_of], wk[n, part_of])
                df[:, n] = part if k == 0 else df[:, n] + part
        sum_ref[...] = jnp.zeros_like(sum_ref)
        xb_ref = get(2)
        for b in range(batches):
            def step(i, before):
                r = row_chunk(b, i, length)
                x = xb_ref[r, :].astype(f32)
                gap = x - down_one(x, before)
                a, c = df[r, :], dr[r, :]
                ck, cr = vec_ref[CMK : CMK + 1], vec_ref[CMR : CMR + 1]
                dxt_ref[r, :] = (a * (1.0 - ck) + c * (1.0 - cr)).astype(bf16)
                dxb_ref[r, :] = (a * ck + c * cr).astype(bf16)
                sum_ref[0] += fold(a * gap)
                sum_ref[1] += fold(c * gap)
                return x[ROWS - 1 :]
            lax.fori_loop(0, length // ROWS, step, entry_ref[b : b + 1])
            head_ref[b : b + 1, :] = dxt_ref[b * length : b * length + 16, :].astype(f32)[:1]
        column_sums(total_ref, sum_ref)

    low = ((tokens, width), bf16)
    return call(
        body, info, [entry, vec], [(a, None) for a in (dfrec, dpre, xb)], flat_pieces(pieces_ck),
        [((batches, width), f32), ((2, width), f32)], [low, low],
        [pltpu.VMEM((width, wide), bf16), pltpu.VMEM((width, width), bf16),
         pltpu.VMEM((tokens, width), f32), pltpu.VMEM((tokens, width), f32),
         pltpu.VMEM((2, 8, width), f32)],
        1 + len(order), 10, 40, late=(2,))


def mid_back(info, dxt, dxb, after, head, mid, cot, vec, kvr, wkv, rden, ent, pieces, spots, length, shard):
    tokens, width = mid.shape
    batches = tokens // length
    steps = plan(pieces, spots["o"], shard)

    def body(info, small, get, raw, outs, big, put, scratch, loads):
        after_ref, head_ref, vec_ref, ent_ref = small
        dent_ref, total_ref = outs
        dent_ref[2 * batches : 3 * batches, :] = ent_ref[2 * batches :, :]
        dent_ref[3 * batches :, :] = head_ref[...]
        dmid_ref, low_ref, high_ref, rlow_ref, rhigh_ref, gn_ref = big
        w, sum_ref, dgate = scratch
        copies = loads.pieces(steps, raw, w, natural(info[0], shard))
        sum_ref[...] = jnp.zeros_like(sum_ref)
        dxt_ref, dxb_ref, mid_ref, cot_ref = get(0), get(1), get(2), get(3)
        for b in range(batches):
            def step(k, after_row):
                r = row_chunk(b, length // ROWS - 1 - k, length)
                nb, inverse = norm(mid_ref[r, :])
                dx = dxt_ref[r, :].astype(f32)
                d = dxb_ref[r, :].astype(f32) + up_one(dx, after_row)
                back = cot_ref[r, :].astype(f32) + norm_back(d, nb, inverse, vec_ref[G2 : G2 + 1])
                dmid_ref[r, :] = back.astype(bf16)
                low_ref[r, :] = back[:, : width // 2].astype(bf16)
                high_ref[r, :] = back[:, width // 2 :].astype(bf16)
                sum_ref[0] += fold(d * nb)
                sum_ref[1] += fold(d)
                return dx[:1]
            lax.fori_loop(0, length // ROWS, step, after_ref[b : b + 1])
        put(0)
        put(1)
        put(2)
        column_sums(total_ref, sum_ref)
        wait(copies)
        @columns(width, STEP)
        def _(n):
            dgate[:, n] = (dot_nt(low_ref[...], w[n, : width // 2])
                           + dot_nt(high_ref[...], w[n, width // 2 :]))
        kvr_ref = [get(4), None, get(5)]
        wkv_ref, rden_ref = get(6), get(7)
        lanes = min(LANES, width // 2)
        for b, half, q in [(b, h, q) for b in range(batches) for h in range(2)
                           for q in range(width // 2 // lanes)]:
            t = slice(b * length, (b + 1) * length)
            n = slice(half * width // 2 + q * lanes, half * width // 2 + (q + 1) * lanes)
            part, at_half = (rlow_ref, rhigh_ref)[half], slice(q * lanes, (q + 1) * lanes)
            if True:
                _, _, _, o, _ = wkv_terms(kvr_ref, ent_ref, vec_ref, b, t, n, batches, length)
                sig = jax.nn.sigmoid(kvr_ref[2][t, n].astype(f32))
                d = dgate[t, n] * sig
                wkvs = wkv_ref[t, n].astype(f32)
                part[t, at_half] = (d * wkvs * (1.0 - sig)).astype(bf16)
                gn = d * rden_ref[t, n].astype(f32)
                gn_ref[t, n] = gn.astype(bf16)
                go = gn * o
                dent_ref[b : b + 1, n] = jnp.sum(go, axis=0, keepdims=True)
                dent_ref[batches + b : batches + b + 1, n] = -jnp.sum(go * wkvs, axis=0, keepdims=True)

    low, half = ((tokens, width), bf16), ((tokens, width // 2), bf16)
    return call(
        body, info, [after, head, vec, ent], [(a, None) for a in (dxt, dxb, mid, cot, kvr[0], kvr[2], wkv, rden)],
        flat_pieces(pieces), [((4 * batches, width), f32), ((2, width), f32)], [low, half, half, half, half, low],
        [pltpu.VMEM((width, width), bf16), pltpu.VMEM((2, 8, width), f32), pltpu.VMEM((tokens, width), f32)],
        len(steps), 9, 40)


def time_back(info, gn, wkv, kvr, ent, back, sums, state, drec, stream, entry, vec, pieces, spots,
              length, shard):
    tokens, width = stream.shape
    batches = tokens // length
    relative = isinstance(back, list)
    stretches = 4 if relative else len(back)
    if not relative:
        back = [back]
    plans = [plan(pieces, spots[k], shard) for k in "kvr"]

    def body(info, small, get, raw, outs, big, put, scratch, loads):
        back_ref = small[:-7]
        if not relative:
            back_ref = [back_ref[0].at[z] for z in range(stretches)]
        else:
            rows = 4 * batches
            back_ref = [*back_ref[:2], *[back_ref[2].at[pl.ds(k * rows, rows)] for k in range(2)]]
        ent_ref, sums_ref, num_ref, den_ref, exp_ref, entry_ref, vec_ref = small[-7:]
        gnum_ref, gden_ref, gexp_ref, gffn_ref, head_ref, total_ref, extra_ref = outs
        d_ref, dxs_ref, dxa_ref = big
        w, dins, sum_ref, later_ref, loc_ref = scratch
        place = natural(info[0], shard)
        copies = [loads.pieces(plans[k], raw, w.at[k], place) for k in range(3)]
        span = -jnp.exp(vec_ref[DECAY : DECAY + 1, :]) * float(length)
        pos = info[2].astype(f32)
        nums, dens, exps = (slice(k * batches, (k + 1) * batches) for k in range(3))
        zero = jnp.zeros((batches, width), f32)

        def state(ref):
            return jnp.concatenate([ref[b] for b in range(batches)], axis=0)

        later_n = later_d = carry_n = carry_d = grad_n = grad_d = grad_f = zero
        for j in range(stretches):
            there = back_ref[j][exps, :]
            at_z = jnp.bitwise_xor(info[2], j) if relative else jnp.int32(j)
            z = at_z.astype(f32)
            after = at_z > info[2]
            lift = jnp.where(after, jnp.exp(jnp.minimum(
                sums_ref[exps, :] - there + (z - 1.0 - pos) * span, 0.0)), 0.0)
            carry = jnp.where(after, jnp.exp(jnp.minimum(
                ent_ref[exps, :] - there + (z - pos) * span, 0.0)), 0.0)
            raised = jnp.exp(jnp.minimum(state(exp_ref) - there + z * span, 0.0))
            dn, dd = back_ref[j][nums, :], back_ref[j][dens, :]
            grad_f = grad_f + jnp.where(at_z == 0, back_ref[j][3 * batches :, :], 0.0)
            later_n, later_d = later_n + dn * lift, later_d + dd * lift
            carry_n, carry_d = carry_n + dn * carry, carry_d + dd * carry
            grad_n, grad_d = grad_n + dn * raised, grad_d + dd * raised
        later_ref[nums, :], later_ref[dens, :] = later_n, later_d
        grad_e = state(num_ref) * grad_n + state(den_ref) * grad_d
        for b in range(batches):
            gnum_ref[b], gden_ref[b] = grad_n[b : b + 1], grad_d[b : b + 1]
            gexp_ref[b] = grad_e[b : b + 1]
            gffn_ref[b] = grad_f[b : b + 1]
        rate_part = (
            float(length) * (ent_ref[nums, :] * carry_n + ent_ref[dens, :] * carry_d)
            + (length - 1.0) * (later_n * sums_ref[nums, :] + later_d * sums_ref[dens, :]))

        upper = triangle(length, False)
        gn_ref, wkv_ref = get(0), get(1)
        kvr_ref = [get(2), get(3)]
        for b in range(batches):
            t = slice(b * length, (b + 1) * length)
            @columns(width, LANES)
            def _(n):
                at, factor, p, o, e = wkv_terms(kvr_ref, ent_ref, vec_ref, b, t, n, batches, length)
                vals, g = kvr_ref[1][t, n].astype(f32), gn_ref[t, n].astype(f32)
                gd = -g * wkv_ref[t, n].astype(f32)
                direct = e * (g * vals + gd)
                opened = o * (g * ent_ref[b : b + 1, n] + gd * ent_ref[batches + b : batches + b + 1, n])
                rn = two_part(upper, g * p) + later_ref[b : b + 1, n]
                rd = two_part(upper, gd * p) + later_ref[batches + b : batches + b + 1, n]
                chain = factor * (rn * vals + rd)
                d_ref[0, t, n] = (chain + direct).astype(bf16)
                d_ref[1, t, n] = (factor * rn + g * e).astype(bf16)
                loc_ref[b : b + 1, n] = jnp.sum(
                    opened - (at - 1.0) * direct - at * chain, axis=0, keepdims=True)
                loc_ref[batches + b : batches + b + 1, n] = jnp.sum(direct, axis=0, keepdims=True)
        put(0)
        rate_rows = rate_part + loc_ref[:batches, :]
        extra_ref[0:1, :] = jnp.sum(rate_rows, axis=0, keepdims=True) * -jnp.exp(
            vec_ref[DECAY : DECAY + 1, :])
        extra_ref[1:2, :] = jnp.sum(loc_ref[batches:, :], axis=0, keepdims=True)
        for k in range(2):
            wait(copies[k])
            @columns(width, STEP)
            def _(n):
                dins[k, :, n] = dot_nt(d_ref[k], w[k, n, :])
        low_ref, high_ref = get(5), get(6)
        wait(copies[2])
        @columns(width, STEP)
        def _(n):
            dins[2, :, n] = (dot_nt(low_ref[...], w[2, n, : width // 2])
                             + dot_nt(high_ref[...], w[2, n, width // 2 :]))
        sum_ref[...] = jnp.zeros_like(sum_ref)
        stream_ref = get(4)
        for b in range(batches):
            def step(i, before):
                r = row_chunk(b, i, length)
                na, _ = norm(stream_ref[r, :].astype(f32))
                xa = na * vec_ref[G1 : G1 + 1] + vec_ref[B1 : B1 + 1]
                gap = xa - down_one(xa, before)
                dxs = jnp.zeros((ROWS, width), f32)
                dxa = jnp.zeros((ROWS, width), f32)
                for k, row in enumerate((MK, MV, MR)):
                    d, mix = dins[k, r, :], vec_ref[row : row + 1]
                    dxs = dxs + d * (1.0 - mix)
                    dxa = dxa + d * mix
                    sum_ref[k] += fold(d * gap)
                dxs_ref[r, :] = dxs.astype(bf16)
                dxa_ref[r, :] = dxa.astype(bf16)
                return xa[ROWS - 1 :]
            lax.fori_loop(0, length // ROWS, step, entry_ref[b : b + 1])
            head_ref[b : b + 1, :] = dxs_ref[b * length : b * length + 16, :].astype(f32)[:1]
        column_sums(total_ref, sum_ref)

    low = ((tokens, width), bf16)
    return call(
        body, info, [*back, ent, sums, *state, entry, vec],
        [(a, None) for a in (gn, wkv, kvr[0], kvr[1], stream, *drec)], flat_pieces(pieces),
        [((batches, 1, width), f32)] * 4
        + [((batches, width), f32), ((3, width), f32), ((2, width), f32)],
        [((2, tokens, width), bf16), low, low],
        [pltpu.VMEM((3, width, width), bf16), pltpu.VMEM((3, tokens, width), f32),
         pltpu.VMEM((3, 8, width), f32), pltpu.VMEM((2 * batches, width), f32),
         pltpu.VMEM((2 * batches, width), f32)],
        sum(map(len, plans)), 14, 40)


def in_back(info, dxs, dxa, after, dmid, stream, vec, length):
    tokens, width = stream.shape
    batches = tokens // length

    def body(info, small, get, raw, outs, big, put, scratch, loads):
        after_ref, vec_ref = small
        (out_ref,) = big
        (sum_ref,) = scratch
        dxs_ref, dxa_ref, dmid_ref, stream_ref = (get(k) for k in range(4))
        sum_ref[...] = jnp.zeros_like(sum_ref)
        for b in range(batches):
            def step(k, after_row):
                r = row_chunk(b, length // ROWS - 1 - k, length)
                na, inverse = norm(stream_ref[r, :].astype(f32))
                dx = dxs_ref[r, :].astype(f32)
                d = dxa_ref[r, :].astype(f32) + up_one(dx, after_row)
                back = norm_back(d, na, inverse, vec_ref[G1 : G1 + 1])
                out_ref[r, :] = (dmid_ref[r, :].astype(f32) + back).astype(bf16)
                sum_ref[0] += fold(d * na)
                sum_ref[1] += fold(d)
                return dx[:1]
            lax.fori_loop(0, length // ROWS, step, after_ref[b : b + 1])
        column_sums(outs[0], sum_ref)

    return call(
        body, info, [after, vec], [(a, None) for a in (dxs, dxa, dmid, stream)], [],
        [((2, width), f32)], [((tokens, width), bf16)],
        [pltpu.VMEM((2, 8, width), f32)], 0, 6, 40)


def weight_grad(info, arrays, items, layout, us, relative=False, stacked=False, under=()):
    count = lax.axis_size("seg")
    evens = list(range(0, count, 2))
    first = items[0][2]
    lead = first[0] if isinstance(first, list) else first
    tokens, n_wide = arrays[lead[0]].shape[-2:]
    n_wide *= len(first) if isinstance(first, list) else 1
    w = arrays[items[0][0][0]].shape[-1] // {"natural": count, "blocks": len(evens), "joined": len(evens)}[layout]
    pair = 2 if w < 256 else 1
    groups = [evens[1:][k : k + pair] for k in range(0, len(evens) - 1, pair)]
    groups[-1].append(0) if len(groups[-1]) < pair else groups.append([0])
    groups = [g for g in groups if g]
    stretches = lax.axis_size("stretch")
    each_z = w // stretches
    shapes = [(len(evens) * len(items) * w, n_wide)] if stacked else [(len(items) * w, n_wide)] * len(evens)
    shares = [x.shape[0] // len(evens) for x in under]
    if under:
        shapes = [(len(items) * w + sum(shares), n_wide)] * len(evens)

    def body(info, small, get, raw, outs, big, put, scratch, loads):
        x_all, dy_all = scratch
        copies_under, at = [], len(items) * w
        for n, share in enumerate(shares):
            for k in range(len(evens)):
                copies_under.append(loads.start(
                    raw[len(arrays) + n].at[pl.ds(k * share, share)], big[k].at[pl.ds(at, share)]))
            at += share

        def view(spec):
            which, lead = spec
            return raw[which] if lead is None else raw[which].at[lead]

        def columns_of(ref, m):
            if layout == "natural":
                return ref.at[:, pl.ds(natural(info[0], w)(m), w)]
            return ref.at[:, pl.ds(evens.index(m) * w, w)]

        x_loads, dy_loads = {}, {}
        for k, (x, x_sib, dy, dy_sib) in enumerate(items):
            for at, part in ((0, dy), (tokens, dy_sib)):
                if relative:
                    each = n_wide // count
                    for n, m in enumerate(relative_order()):
                        cols = natural(info[0], each)(m if at == 0 else m ^ 1)
                        dy_loads.setdefault(k, []).append(loads.start(
                            view(part).at[:, pl.ds(n * each, each)],
                            dy_all.at[k, pl.ds(at, tokens), pl.ds(cols, each)]))
                    continue
                pieces = part if isinstance(part, list) else [part]
                each = n_wide // len(pieces)
                for n, piece in enumerate(pieces):
                    dy_loads.setdefault(k, []).append(loads.start(
                        view(piece), dy_all.at[k, pl.ds(at, tokens), pl.ds(n * each, each)]))
            for g, ms in enumerate(groups):
                for at, part in ((0, x), (tokens, x_sib)):
                    ref, rows = view(part), pl.ds(at, tokens)
                    if layout == "joined":
                        cols = pl.ds(g * pair * w, len(ms) * w)
                        x_loads.setdefault((k, g), []).append(loads.start(
                            ref.at[:, cols], x_all.at[k, g, rows, pl.ds(0, len(ms) * w)]))
                        continue
                    for n, m in enumerate(ms):
                        x_loads.setdefault((k, g), []).append(loads.start(
                            columns_of(ref, m), x_all.at[k, g, rows, pl.ds(n * w, w)]))

        def need(table, key):
            wait(table.pop(key, ()))

        step = min(512, n_wide)
        for g, ms in enumerate(groups):
            for k in range(len(items)):
                need(x_loads, (k, g))
                for q in range(n_wide // step):
                    need(dy_loads, k)
                    dst = slice(q * step, (q + 1) * step)
                    block = dot_tn(x_all[k, g, :, : len(ms) * w], dy_all[k, :, dst]).astype(bf16)
                    for n, m in enumerate(ms):
                        if not stacked:
                            big[evens.index(m)][k * w : (k + 1) * w, dst] = block[n * w : (n + 1) * w]
                            continue
                        for z in range(stretches):
                            row = ((z * len(evens) + evens.index(m)) * len(items) + k) * each_z
                            big[0][row : row + each_z, dst] = block[n * w + z * each_z : n * w + (z + 1) * each_z]
            if g == 0:
                wait(copies_under)
            for m in ms:
                if not stacked:
                    put(evens.index(m))
                    continue
                rows = len(items) * each_z
                if rows % 16 == 0:
                    for z in range(stretches):
                        put(0, pl.ds((z * len(evens) + evens.index(m)) * rows, rows))

    return call(
        body, info, [], [], [*arrays, *under], [], [(shape, bf16) for shape in shapes],
        [pltpu.VMEM((len(items), len(groups), 2 * tokens, pair * w), bf16),
         pltpu.VMEM((len(items), 2 * tokens, n_wide), bf16)],
        len(items) * (4 + 2 * len(evens) + 2 * count) + len(evens) * (len(under) + stretches), us, 40)


def grad_send(parts):
    return [hop(part, 2 * k) for k, part in enumerate(parts) if k]


def total(terms):
    out = terms[0].astype(f32)
    for t in terms[1:]:
        out = out + t.astype(f32)
    return out


def grad_stack(info, key, recept):
    stretches = lax.axis_size("stretch")
    own, width = recept[0].shape
    each, blocks = own // stretches, key[0].shape[1] // width
    rows = (blocks + 1) * each
    if each % 16:
        wide = total(key).astype(bf16).reshape(stretches, each, blocks, width)
        wide = jnp.swapaxes(wide, 1, 2).reshape(stretches, blocks * each, width)
        narrow = total(recept).astype(bf16).reshape(stretches, each, width)
        return jnp.concatenate([wide, narrow], axis=1).reshape(stretches * rows, width)
    terms = len(key)

    def body(info, small, get, raw, outs, big, put, scratch, loads):
        keys, recepts = scratch
        copies = []
        for z in range(stretches):
            src = pl.ds(z * each, each)
            now = [loads.start(raw[j].at[src], keys.at[j, z]) for j in range(terms)]
            copies.append(now + [loads.start(raw[terms + j].at[src], recepts.at[j, z]) for j in range(terms)])
        for z in range(stretches):
            wait(copies[z])
            for q in range(blocks):
                at = z * rows + q * each
                big[0][at : at + each, :] = total(
                    [keys[j, z, :, q * width : (q + 1) * width] for j in range(terms)]).astype(bf16)
            at = z * rows + blocks * each
            big[0][at : at + each, :] = total([recepts[j, z] for j in range(terms)]).astype(bf16)

    return call(
        body, info, [], [], [*key, *recept], [], [((stretches * rows, width), bf16)],
        [pltpu.VMEM((terms, stretches, each, blocks * width), bf16),
         pltpu.VMEM((terms, stretches, each, width), bf16)],
        stretches * 2 * terms, 4, 24)[0]


def grad_pieces(info, own, got, items, each):
    stretches = lax.axis_size("stretch")
    rows, n_wide = own.shape
    width = each * stretches

    def body(info, small, get, raw, outs, big, put, scratch, loads):
        refs = [get(k) for k in range(1 + len(got))]
        first = items * width
        table = total([r[first : first + 16, :] for r in refs])
        half = n_wide // 2
        table = table[:, :half] + table[:, half:]
        hi = table.astype(bf16)
        lo = (table - hi.astype(f32)).astype(bf16)
        for j in list(range(1, stretches)) + [0]:
            z = jnp.bitwise_xor(info[2], j)
            for k in range(items):
                src = pl.ds(pl.multiple_of(k * width + z * each, each), each)
                big[j][k * each : (k + 1) * each, :] = total([r[src, :] for r in refs]).astype(bf16)
            big[j][items * each :, :half] = hi
            big[j][items * each :, half:] = lo
            put(j)

    return call(
        body, info, [], [(a, None) for a in (own, *got)], [], [],
        [((items * each + 16, n_wide), bf16)] * stretches, [], 0, 3, 24)


def stretch_part(part):
    return lax.psum_scatter(part, "stretch", scatter_dimension=0, tiled=True)


def stretch_items(out, items):
    own = out.shape[0] // items
    return [out[k * own : (k + 1) * own].astype(f32) for k in range(items)]


def vector_rows(table, width):
    me, count = lax.axis_index("seg"), lax.axis_size("seg")
    own = table.shape[1] // count
    table = jnp.pad(table, ((0, 16 - table.shape[0]), (0, 0)))
    rows = []
    for m in range(0, count, 2):
        pair = lax.dynamic_slice_in_dim(table, (me ^ m) // 2 * (2 * own), 2 * own, 1)
        pair = jnp.pad(pair, ((0, 0), (0, width // 2 - 2 * own)))
        hi = pair.astype(bf16)
        rows.append(jnp.concatenate([hi, (pair - hi.astype(f32)).astype(bf16)], axis=1))
    return jnp.concatenate(rows, axis=0)


def vector_read(rows):
    half = rows.shape[1] // 2
    return rows[:, :half].astype(f32) + rows[:, half:].astype(f32)


def vector_own(pair, own):
    second = (lax.axis_index("seg") & 1) != 0
    lo, hi = pair[:, :own], pair[:, own : 2 * own]
    return jnp.where(second, hi, lo) + hop(jnp.where(second, lo, hi), 1)


def vector_finish(table):
    position, count = lax.axis_index("stretch"), lax.axis_size("stretch")
    bit = count // 2
    while bit:
        lo, hi = jnp.split(table, 2, axis=1)
        upper = (position & bit) != 0
        table = jnp.where(upper, hi, lo) + across(jnp.where(upper, lo, hi), bit)
        bit //= 2
    return table


def own_columns(x, me, w):
    ms = [*range(2, lax.axis_size("seg"), 2), 0]
    return jnp.concatenate([lax.dynamic_slice_in_dim(x, (me ^ m) * w, w, 1) for m in ms], axis=1)


def body(
    stream_in, cotangent, previous_mix, previous_ffn, state_num, state_den, state_exp,
    gain_one, bias_one, gain_two, bias_two, mix_key, mix_value, mix_recept,
    time_decay, time_first, chan_mix_key, chan_mix_recept,
    att_key, att_value, att_recept, att_output, chan_key, chan_value, chan_recept,
):
    mine = lax.axis_index("seg")
    position = lax.axis_index("stretch")
    stretches = lax.axis_size("stretch")
    batches, _, length, width = stream_in.shape
    tokens = batches * length
    shard = att_key.shape[0]
    fshard = chan_value.shape[0]
    wide = chan_key.shape[1]
    aligned = shard % 128 == 0
    count = lax.axis_size("seg")
    info = jnp.stack([mine, (position == 0).astype(jnp.int32), position])

    stream = stream_in.reshape(tokens, width)
    cot = cotangent.reshape(tokens, width)
    state = (state_num, state_den, state_exp)
    vectors = [gain_one, bias_one, gain_two, bias_two, mix_key, mix_value, mix_recept,
               time_decay, time_first, chan_mix_key, chan_mix_recept]

    v = Live()
    evens = list(range(0, count, 2))
    spots = {"k": 0, "v": shard, "vec": 2 * shard, "r": 2 * shard + 16, "o": 3 * shard + 16}
    each = fshard // stretches
    v.own_tm = pack(
        [(att_key, 0, shard), (att_value, 0, shard), (None, 0, 16)],
        [(att_recept, 0, shard), (att_output, 0, shard)], vectors, width)
    v.share = lax.dynamic_slice_in_dim(chan_value, position * each, each, 0)
    v.cv = chan_value
    v.last_in = stream_in[:, 0, length - 1]
    v.sync()
    v.shares = lax.all_gather(v.share, "seg", axis=0, tiled=True)
    v.one_tm = first_stage(v.own_tm)
    v.ck = pack_wide(tie(chan_key, *v.own_tm), chan_recept)
    v.tm0 = sibling({0: v.own_tm})
    v.last_in = along(tie(v.last_in, *v.tm0[1]), 1)
    v.sync()
    v.tm6 = second_stage(v.one_tm, v.one_tm)
    v.tm2 = sibling(v.one_tm)
    v.ck0 = sibling({0: v.ck})
    gathered_cv = lax.all_gather(
        jnp.concatenate([lax.dynamic_slice_in_dim(v.shares, (mine ^ m) * each, each, 0) for m in evens[1:]], axis=0),
        "stretch", axis=0, tiled=True)
    v.sync()
    v.tm6_sib = sibling(v.tm6)
    v.sync()

    v.one_ck = first_stage(v.ck)
    tm = {0: v.own_tm, **v.one_tm, **v.tm6, **v.tm0, **v.tm2, **v.tm6_sib}
    given = None
    if not aligned:
        given = lax.all_gather(jnp.stack(vectors), "seg", axis=1, tiled=True).astype(f32)
        given = jnp.pad(given, ((0, 5), (0, 0)))
    v.sums, v.vec, v.entry, v.kvr_in, *v.kvr = time_in(
        info, stream, v.last_in, previous_mix, given, tm, spots, length, shard)
    v.everyone = lax.all_gather(v.sums, "stretch")
    v.tm = tm
    v.drop("own_tm", "one_tm", "tm6", "tm0", "tm2", "tm6_sib", "share", "shares")
    v.sync()

    v.ck6 = second_stage(v.one_ck, v.one_ck)
    v.ent, v.mean, v.log, v.edge_b, v.gated, v.wkv, v.rden, v.mid, v.xb = time_out(
        info, v.kvr, v.everyone, state, v.vec, stream, v.tm, spots, length, shard)
    first_far = far_bits()[0]
    v.ck2 = sibling({first_far: v.one_ck[first_far]})
    v.edge_b = along(v.edge_b, 1)
    v.drop("everyone")
    v.sync()
    v.ck2 = {**v.ck2, **sibling({m: p for m, p in v.one_ck.items() if m != first_far})}
    v.all_ck = {0: v.ck, **v.one_ck, **v.ck6, **v.ck0, **v.ck2, **sibling(v.ck6)}
    v.gathered_cv = gathered_cv
    v.drop("ck", "one_ck", "ck6", "ck0", "ck2")
    v.sync()

    v.entry_b, v.f_in, v.near, v.far, v.act, v.frec = chan_in(
        info, v.xb, v.edge_b, previous_ffn, v.vec, v.all_ck, length, shard, fshard)
    v.all_cv = [v.cv, v.gathered_cv, hop(v.cv, 1), hop(v.gathered_cv, 1)]
    v.drop("cv", "gathered_cv")
    v.sync()
    v.block_out, v.d_fval, v.d_frec = chan_out(
        info, v.near, v.far, v.frec, v.mid, cot, v.all_cv, fshard)
    v.far_sib = hop(v.far, 1)
    v.f_sib = hop(v.f_in, 1)
    v.g_sib = hop(v.gated, 1)
    v.kvr_sib = hop(v.kvr_in, 1)
    v.drop("frec", "far")
    v.sync()

    def pairs(*arrays):
        if aligned:
            return [a for pair in arrays for a in pair]
        return [own_columns(a, mine, shard) for pair in arrays for a in pair]

    layout = "natural" if aligned else "joined"
    flat = tuple((j, None) for j in range(4))
    arrays = [v.near, v.far_sib, v.d_fval, hop(v.d_fval, 1)]
    v.stack_cv = weight_grad(info, arrays, [flat], "blocks", 6, stacked=True)[0]
    v.dfrec_sib = hop(v.d_frec, 1)
    v.drop("near", "far_sib")
    v.sync()

    z_cv = stretch_part(v.stack_cv)
    v.dpre = hidden_back(info, v.act, v.d_fval, v.all_cv, fshard)
    d_frec = tie(v.d_frec, v.dpre)
    if aligned:
        v.parts_c = weight_grad(
            info, [v.f_in, v.f_sib, d_frec, v.dfrec_sib], [((0, 1), (1, 1), (2, None), (3, None))], layout, 3)
    else:
        v.parts_c = weight_grad(
            info, [*pairs((v.f_in[1], v.f_sib[1])), d_frec, v.dfrec_sib], [flat], layout, 3)
    v.got_c = grad_send(v.parts_c)
    dpre_sib = hop(v.dpre, 1)
    v.head_b, v.sums_c, v.dxt, v.dxb = chan_back(
        info, v.dpre, v.d_frec, v.xb, v.entry_b, v.vec, v.all_ck, length, shard, fshard)
    v.next_b = along(v.head_b, -1)
    dpre = tie(v.dpre, v.dxt)
    if aligned:
        v.parts_ck = weight_grad(
            info, [v.f_in, v.f_sib, dpre, dpre_sib], [((0, 0), (1, 0), (2, None), (3, None))], layout, 7, True)
    else:
        v.parts_ck = weight_grad(
            info, [*pairs((v.f_in[0], v.f_sib[0])), dpre, dpre_sib], [flat], layout, 7, True)
    v.drop("all_ck", "all_cv", "xb", "entry_b", "act", "d_fval", "dpre", "stack_cv")
    v.sync()

    v.got_ck = grad_send(v.parts_ck)
    backs, v.sums_m, v.dmid, *lows, gn = mid_back(
        info, v.dxt, v.dxb, v.next_b, v.head_b, v.mid, cot, v.vec, v.kvr, v.wkv, v.rden, v.ent, v.tm, spots,
        length, shard)
    v.dbr, v.drec = lows[:2], lows[2:]
    back = exchange_two(backs)
    *v.grads, v.head_a, v.sums_t, v.extra, v.d_kv, v.dxs, v.dxa = time_back(
        info, gn, v.wkv, v.kvr, v.ent, back, v.sums, state, v.drec, stream, v.entry, v.vec,
        v.tm, spots, length, shard)
    v.dbr_sib = [hop(a, 1) for a in v.dbr]
    v.drec_sib = [hop(a, 1) for a in v.drec]
    dys = [([(at, None), (at + 1, None)], [(at + 2, None), (at + 3, None)]) for at in (0, 4)]
    lows = [*v.dbr, *v.dbr_sib, *v.drec, *v.drec_sib]
    gated = tie(v.gated, v.d_kv)
    if aligned:
        v.parts_or = weight_grad(
            info, [*lows, gated, v.g_sib, v.kvr_in, v.kvr_sib],
            [((8, None), (9, None), *dys[0]), ((10, 2), (11, 2), *dys[1])], layout, 6, stacked=True)
    else:
        xs = pairs((gated, v.g_sib), (v.kvr_in[2], v.kvr_sib[2]))
        v.parts_or = weight_grad(
            info, [*lows, *xs], [((8, None), (9, None), *dys[0]), ((10, None), (11, None), *dys[1])], layout, 6,
            stacked=True)
    v.drop("wkv", "kvr", "ent", "sums", "entry", "tm", "dxt", "dxb", "mid", "rden", "next_b", "head_b")
    v.sync()
    v.dkv_sib = hop(v.d_kv, 1)
    v.next_a = along(v.head_a, -1)
    z_or = stretch_part(v.parts_or[0])
    v.stack = grad_stack(info, [v.parts_ck[0], *v.got_ck], [v.parts_c[0], *v.got_c])
    v.drop("gated", "g_sib", "dbr", "dbr_sib", "drec", "drec_sib", "f_in", "f_sib", "d_frec",
           "parts_ck", "got_ck", "parts_c", "got_c", "parts_or")
    v.z_cv = z_cv
    v.sync()

    v.parts_cv = [v.z_cv[k * each : (k + 1) * each] for k in range(len(evens))]
    z_rest = stretch_part(v.stack)
    v.got_cv = grad_send(v.parts_cv)
    sums_i, v.grad_stream = in_back(info, v.dxs, v.dxa, v.next_a, v.dmid, stream, v.vec, length)
    table = jnp.concatenate([sums_i, v.sums_m, v.sums_t, v.extra, v.sums_c], axis=0)
    under = [vector_rows(table, width)]
    if aligned:
        v.parts_kv = weight_grad(
            info, [v.kvr_in, v.kvr_sib, v.d_kv, v.dkv_sib],
            [tuple((j, k) for j in range(4)) for k in range(2)], layout, 7, under=under)
    else:
        xs = pairs(*[(v.kvr_in[k], v.kvr_sib[k]) for k in range(2)])
        v.parts_kv = weight_grad(
            info, [*xs, v.d_kv, v.dkv_sib],
            [((2 * k, None), (2 * k + 1, None), (4, k), (5, k)) for k in range(2)], layout, 7, under=under)
    v.drop("kvr_in", "kvr_sib", "d_kv", "dkv_sib", "dxs", "dxa", "dmid", "next_a", "stack",
           "sums_m", "sums_t", "extra", "sums_c", "z_cv")
    v.sync()

    v.got_kv = grad_send(v.parts_kv)
    v.heads = lax.all_gather(v.head_a, "stretch")[0]
    v.out_cv = total([v.parts_cv[0], *v.got_cv])
    v.drop("parts_cv", "got_cv")
    v.z_or = z_or
    v.sync()
    rows = shard // stretches
    by_hops = stretches == 4 and rows % 16 == 0
    if by_hops:
        v.pieces = grad_pieces(info, v.parts_kv[0], v.got_kv, 2, rows)
    else:
        whole = total([v.parts_kv[0], *v.got_kv])
        first = 2 * shard
        v.table = vector_read(whole[first:])
        v.part_kv = whole[:first].astype(bf16).reshape(2, stretches, rows, width)
        v.part_kv = jnp.swapaxes(v.part_kv, 0, 1).reshape(first, width)
    parts = [v.z_or[2 * k * rows : 2 * (k + 1) * rows] for k in range(len(evens))]
    v.parts_or = [parts[0], *grad_send(parts)]
    v.drop("parts_kv", "got_kv", "z_or")
    v.sync()
    blocks = wide // width
    out_ck = jnp.concatenate([z_rest[q * rows : (q + 1) * rows] for q in range(blocks)], axis=1).astype(f32)
    out_c = z_rest[blocks * rows : (blocks + 1) * rows].astype(f32)
    if by_hops:
        pieces = [v.pieces[0], *[across(v.pieces[j], j) for j in range(1, stretches)]]
        z_kv = total([p[: 2 * rows] for p in pieces])
        small = sum(vector_read(p[2 * rows : 2 * rows + 11]) for p in pieces)
        small = lax.dynamic_slice_in_dim(vector_own(small, shard), position * rows, rows, 1)
    else:
        z_kv = stretch_part(v.part_kv)
        small = vector_finish(vector_own(v.table[:11], shard))
    out_k, out_v = stretch_items(z_kv, 2)
    out_o, out_r = stretch_items(total(v.parts_or), 2)
    out_cv = v.out_cv
    grad_previous_mix = v.heads
    block_out, grad_stream = v.block_out, v.grad_stream

    shape = stream_in.shape
    return (
        block_out.reshape(shape), grad_stream.reshape(shape), *[small[i] for i in range(11)],
        out_k, out_v, out_r, out_o, out_ck, out_cv, out_c,
        *v.grads[:3], grad_previous_mix[:, None], v.grads[3], v.mean, v.log,
    )


def solution(mesh):
    rows = P(None, "seg", "stretch", None)
    state = P(None, "seg", None)
    both = P(("seg", "stretch"))
    table = P(("seg", "stretch"), None)
    return jax.shard_map(
        body,
        mesh=mesh,
        in_specs=(rows,) * 2 + (state,) * 5 + (P("seg"),) * 11 + (P("seg", None),) * 7,
        out_specs=(rows,) * 2 + (both,) * 11 + (table,) * 7 + (state,) * 7,
        check_vma=False,
    )
```
